32 devices in a mesh: expert: 8 (over y, x, core), fsdp: 4 (over z).
Axes of the slice: x: 2, y: 2, z: 4, core: 2. Of those that a mesh axis runs over, the one named last changes fastest.
Arguments:
- inputs: bfloat16 [12288, 2048], P(('expert', 'fsdp')), may hold values from -6 to 6
- query_weight: bfloat16 [2048, 2048], P('fsdp'), may hold values from -0.125 to 0.125
- key_weight: bfloat16 [2048, 2048], P('fsdp'), may hold values from -0.125 to 0.125
- value_weight: bfloat16 [2048, 2048], P('fsdp'), may hold values from -0.125 to 0.125
- output_weight: bfloat16 [2048, 2048], P('fsdp'), may hold values from -4 to 4
- router_weight: bfloat16 [2048, 64], P('fsdp'), may hold values from -0.0625 to 0.0625
- first_gain: bfloat16 [2048], P('fsdp'), may hold values from 0.5 to 1.5
- query_gain: bfloat16 [2048], P('fsdp'), may hold values from 0.25 to 1.75
- key_gain: bfloat16 [2048], P('fsdp'), may hold values from 0.25 to 1.75
- second_gain: bfloat16 [2048], P('fsdp'), may hold values from 0.5 to 1.5
- gate_weight: bfloat16 [128, 2048, 512], P(('expert', 'fsdp')), may hold values from -0.125 to 0.125
- up_weight: bfloat16 [128, 2048, 512], P(('expert', 'fsdp')), may hold values from -0.125 to 0.125
- down_weight: bfloat16 [128, 512, 2048], P(('expert', 'fsdp')), may hold values from -6 to 6
- routes: int32 [12288, 8], P(('expert', 'fsdp')), may hold values from 0 to 63, all different within a row; in each aligned block of 384 rows (0 to 383, 384 to 767, ...) at most 56 rows name the same one
- lengths: int32 [8, 2], P('expert'), may hold values from 192 to 1344, as said below
- dealing: int32 [12288], P('expert'), may hold values from 0 to 1535, as said below
- cotangent: bfloat16 [12288, 2048], P(('expert', 'fsdp')), may hold values from -6 to 6
Outputs:
- block_output: bfloat16 [12288, 2048], P(('expert', 'fsdp'))
- input_gradient: bfloat16 [12288, 2048], P(('expert', 'fsdp'))
- query_gradient: float32 [2048, 2048], P('fsdp')
- key_gradient: float32 [2048, 2048], P('fsdp')
- value_gradient: float32 [2048, 2048], P('fsdp')
- output_gradient: float32 [2048, 2048], P('fsdp')
- router_gradient: float32 [2048, 64], P('fsdp')
- first_gain_gradient: float32 [2048], P('fsdp')
- query_gain_gradient: float32 [2048], P('fsdp')
- key_gain_gradient: float32 [2048], P('fsdp')
- second_gain_gradient: float32 [2048], P('fsdp')
- gate_gradient: float32 [128, 2048, 512], P(('expert', 'fsdp'))
- up_gradient: float32 [128, 2048, 512], P(('expert', 'fsdp'))
- down_gradient: float32 [128, 512, 2048], P(('expert', 'fsdp'))
The draws below stay inside these ranges and needn't reach their ends.
Inputs may be any that keep to these rules, and one draw needn't show every extreme that they name: `routes`: in each aligned block of 384 rows (the rows of one device) no expert is named by more than 56 rows, and in some block one is named by exactly 56. `lengths`: each row sums to 1536: one entry, the shorter sequence, is 192 to 384, the other is the rest. `dealing`: within each group of 1536 rows, every place from 0 to 1535 once.
All inputs are finite; a program needn't handle non-finite values.
Results may differ from the reference program's by a relative error of at most 0.025.
Values may be sent and summed in bfloat16 or wider, within the bound.
A program may use at most 576 MiB of HBM per device.

```python
import math
from functools import partial
import jax
import jax.numpy as jnp
import numpy as np
from jax import lax

D = 2048
HEADS = 16
HD = 128
FF = 1024
EXPERTS = 64
TOP = 8
TOK_DEV = 384
GROUP_TOK = 1536
TOKENS = 12288
SHORT_MIN = 192
UNITS = 128
CAP = 56
N_EXPERT = 8
N_FSDP = 4


def draw_lengths(key, part):
    key = jax.random.fold_in(key, 11)
    length_key, switch_key = jax.random.split(key)
    shorter = jax.random.randint(length_key, (N_EXPERT,), SHORT_MIN, 2 * SHORT_MIN + 1)
    switch = jax.random.randint(switch_key, (N_EXPERT,), 0, 2)
    longer = GROUP_TOK - shorter
    leading = jnp.where(switch == 1, shorter, longer)
    trailing = jnp.where(switch == 1, longer, shorter)
    return jnp.stack([leading, trailing], axis=1).astype(jnp.int32)


def shuffle(subkey):
    return jax.random.permutation(subkey, GROUP_TOK)


def draw_dealing(key, part):
    key = jax.random.fold_in(key, 23)
    subkeys = jax.random.split(key, N_EXPERT)
    orders = jax.vmap(shuffle)(subkeys)
    return orders.reshape(-1).astype(jnp.int32)


def shard_levels(key, shape, shards, smallest, high):
    factor_of, own = 1.0, jax.random.fold_in(key, 6)
    for dim, shards_of in shards:
        draws = jnp.exp(jax.random.uniform(jax.random.fold_in(own, dim), (shards_of,), jnp.float32, smallest / len(shards), high / len(shards)))
        factor_of = factor_of * jnp.repeat(draws, shape[dim] // shards_of).reshape([-1 if axis == dim else 1 for axis in range(len(shape))])
    return factor_of


def routed_block(stream_key, own, number, rows, amount, top, most, slope):
    ranking = jax.random.permutation(stream_key, amount)
    crowded, common = portions_of(amount, rows * top, most, slope, True), portions_of(amount, rows * top, most, slope, False)
    places = jnp.arange(amount)

    def named(sizes, rotation):
        used = int((sizes > 0).sum())
        fixed = max(1, used // 4)
        moved = fixed + (places - fixed + rotation * (used - fixed)) % max(1, amount - fixed)
        return jnp.zeros((amount,), jnp.int32).at[ranking[jnp.where(places < fixed, places, moved)]].set(jnp.asarray(sizes, jnp.int32))

    sizes = jnp.where(number % 4 == 0, named(crowded, number // 4), named(common, number - number // 4 - 1))
    mixed = jax.random.permutation(jax.random.fold_in(own, 3), amount)
    source_of, receiver = mixed[0:amount // 2 * 2:2], mixed[1:amount // 2 * 2:2]
    slack = jnp.minimum(sizes[source_of] - 1, most - sizes[receiver]) // 2
    slack = jnp.where((source_of == ranking[0]) | (receiver == ranking[0]) | (sizes[receiver] == 0), 0, jnp.maximum(slack, 0))
    moved = jax.random.randint(jax.random.fold_in(own, 4), (amount // 2,), 0, 1 << 20) % (slack + 1)
    sizes = sizes.at[source_of].add(-moved).at[receiver].add(moved)
    items = jnp.searchsorted(jnp.cumsum(sizes), jnp.arange(rows * top), side="right").astype(jnp.int32)
    table = items.reshape(top, rows).T
    table = table[jax.random.permutation(jax.random.fold_in(own, 1), rows)]
    rotation = jax.random.randint(jax.random.fold_in(own, 2), (rows, 1), 0, top)
    return jnp.take_along_axis(table, (jnp.arange(top)[None, :] + rotation) % top, axis=1)


def portions_of(number_of, total, limit, skew, full):
    weights = [(1 << 20) // math.isqrt(grade ** skew) + 1 for grade in range(1, number_of + 1)]
    largest = limit if full else min(limit, max(-(-total // number_of), total * weights[0] // sum(weights)))
    least = 1 if total - largest >= number_of - 1 else 0
    counts, spare = [largest] + [least] * (number_of - 1), total - largest - least * (number_of - 1)
    while spare > 0:
        candidates = [i for i in range(1, number_of) if counts[i] < largest] or [i for i in range(1, number_of) if counts[i] < limit]
        mass, budget = sum([weights[i] for i in candidates]), spare
        for i in candidates:
            extra = min(limit - counts[i], max(1, budget * weights[i] // mass), spare)
            counts[i] = counts[i] + extra
            spare = spare - extra
    return np.array(counts)


def gaussian(stream_key, dims, width, most, cuts=(), kind=jnp.bfloat16):
    values = jax.random.normal(stream_key, dims, jnp.float32) * width
    if len(cuts) > 0:
        values = shard_levels(stream_key, dims, cuts, -0.22, 0.18) * values
    return jnp.clip(values, min=-most, max=most).astype(kind)


def setup_inputs(seed: int = 0) -> dict:
    key_list = jax.random.split(jax.random.key(seed), 18)
    inputs = gaussian(key_list[0], (TOKENS, D), 1.0, 6.0, ((0, 32),))
    query_weight = gaussian(key_list[1], (D, D), D ** -0.5, 0.125, ((0, 4),))
    key_weight = gaussian(key_list[2], (D, D), D ** -0.5, 0.125, ((0, 4),))
    value_weight = gaussian(key_list[3], (D, D), D ** -0.5, 0.125, ((0, 4),))
    output_weight = gaussian(key_list[4], (D, D), ((GROUP_TOK / (8 * D)) ** 0.5), 4.0, ((0, 4),))
    router_weight = gaussian(key_list[5], (D, EXPERTS), (4 * D) ** -0.5, 0.0625, ((0, 4),))
    first_gain = jnp.clip(1.0 + 0.1 * jax.random.normal(key_list[6], (D,), jnp.float32), 0.5, 1.5).astype(jnp.bfloat16)
    query_gain = jnp.clip(1.0 + 0.15 * jax.random.normal(key_list[7], (D,), jnp.float32), 0.25, 1.75).astype(jnp.bfloat16)
    key_gain = jnp.clip(1.0 + 0.15 * jax.random.normal(key_list[8], (D,), jnp.float32), 0.25, 1.75).astype(jnp.bfloat16)
    second_gain = jnp.clip(1.0 + 0.1 * jax.random.normal(key_list[9], (D,), jnp.float32), 0.5, 1.5).astype(jnp.bfloat16)
    gate_weight = gaussian(key_list[10], (UNITS, D, FF // 2), D ** -0.5, 0.125, ((0, 32),))
    up_weight = gaussian(key_list[11], (UNITS, D, FF // 2), D ** -0.5, 0.125, ((0, 32),))
    down_weight = gaussian(key_list[12], (UNITS, FF // 2, D), (32 / FF ** 0.5), 6.0, ((0, 32),))
    routes_keys = jax.random.split(jax.random.fold_in(key_list[13], 1), TOKENS // TOK_DEV)
    routes_turns = jax.random.permutation(jax.random.fold_in(key_list[13], 3), TOKENS // TOK_DEV)
    routes = jax.vmap(lambda own, number: routed_block(jax.random.fold_in(key_list[13], 2), own, number, TOK_DEV, EXPERTS, TOP, CAP, 1))(routes_keys, routes_turns).reshape((TOKENS, TOP))
    lengths = draw_lengths(jax.random.fold_in(key_list[17], 71), 0)
    dealing = draw_dealing(jax.random.fold_in(key_list[17], 71), 0)
    cotangent = gaussian(key_list[16], (TOKENS, D), 1.0, 6.0, ((0, 32),))
    return dict(inputs=inputs, query_weight=query_weight, key_weight=key_weight, value_weight=value_weight, output_weight=output_weight, router_weight=router_weight, first_gain=first_gain, query_gain=query_gain, key_gain=key_gain, second_gain=second_gain, gate_weight=gate_weight, up_weight=up_weight, down_weight=down_weight, routes=routes, lengths=lengths, dealing=dealing, cotangent=cotangent)


@jax.custom_vjp
def low(v):
    return lax.optimization_barrier(v.astype(jnp.bfloat16)).astype(jnp.float32)

@jax.custom_vjp
def low_back(v):
    return v

def low_keep(v):
    return (low(v), None)

def low_pass(kept, grad):
    return (grad,)

def back_keep(v):
    return (v, None)

def back_low(kept, grad):
    return (low(grad),)
low.defvjp(low_keep, low_pass)
low_back.defvjp(back_keep, back_low)
EPSILON = 1e-05
THETA = 10000.0
HIGHEST = lax.Precision.HIGHEST
MASKED = -1e+30

def rms_scale(vector, scaling):
    return vector * lax.rsqrt(lax.optimization_barrier(jnp.mean(vector * vector, axis=-1, keepdims=True)) + EPSILON) * scaling

def rotate(heads_in, cosine, sine_wave):
    middle = heads_in.shape[-1] // 2
    former = heads_in[..., :middle]
    latter = heads_in[..., middle:]
    return jnp.concatenate([former * cosine - latter * sine_wave, latter * cosine + former * sine_wave], axis=-1)

def places(lengths_row, stream):
    seq_ends = jnp.cumsum(lengths_row)
    before = (seq_ends[None, :] <= stream[:, None]).astype(jnp.int32)
    seq_ids = lax.optimization_barrier(jnp.sum(before, axis=1))
    offset = lax.optimization_barrier(jnp.sum(before * lengths_row[None, :], axis=1))
    return (seq_ids, stream - offset)

def angles(positions, head_width):
    exponent = jnp.arange(0, head_width, 2).astype(jnp.float32) / head_width
    phases = positions.astype(jnp.float32)[:, None] * (THETA ** (-exponent))[None, :]
    return (jnp.cos(phases)[:, None, :], jnp.sin(phases)[:, None, :])

def group_attention(group_in, stream, lengths_row, attention_set):
    query_weight, key_weight, value_weight, output_weight, first_gain, query_gain, key_gain = attention_set
    seq_ids, positions = places(lengths_row, stream)
    cosine, sine_wave = angles(positions, HD)
    normed = low(rms_scale(group_in, first_gain))
    query_raw = low_back(jnp.dot(normed, query_weight, precision=HIGHEST))
    key_raw = low_back(jnp.dot(normed, key_weight, precision=HIGHEST))
    values = low(low_back(jnp.dot(normed, value_weight, precision=HIGHEST))).reshape(-1, HEADS, HD)
    queries = low(low_back(rotate(rms_scale(query_raw, query_gain).reshape(-1, HEADS, HD), cosine, sine_wave)))
    key_rows = low(low_back(rotate(rms_scale(key_raw, key_gain).reshape(-1, HEADS, HD), cosine, sine_wave)))
    scores = low_back(jnp.einsum('qhd,khd->hqk', queries, key_rows, precision=HIGHEST) * HD ** (-0.5))
    allowed = (seq_ids[:, None] == seq_ids[None, :]) & (positions[None, :] <= positions[:, None])
    scores = jnp.where(allowed[None], scores, MASKED)
    probability = low(jax.nn.softmax(scores, axis=-1))
    blended = low(low_back(jnp.einsum('hqk,khd->qhd', probability, values, precision=HIGHEST))).reshape(-1, D)
    return group_in + low_back(jnp.dot(blended, output_weight, precision=HIGHEST))

def slot_table(routes):
    devices = N_EXPERT * N_FSDP
    per_device = TOK_DEV * TOP
    expert_ids = routes.reshape(devices, per_device)
    onehot = (expert_ids[:, :, None] == jnp.arange(EXPERTS, dtype=jnp.int32)[None, None, :]).astype(jnp.int32)
    slot_index = lax.optimization_barrier(jnp.sum(jnp.cumsum(onehot, axis=1) * onehot, axis=2)) - 1
    device_ids = jnp.arange(devices, dtype=jnp.int32)[:, None]
    target = ((expert_ids * devices + device_ids) * CAP + slot_index).reshape(-1)
    assigned = jnp.arange(devices * per_device, dtype=jnp.int32)
    filled = jnp.full((EXPERTS * devices * CAP,), devices * per_device, jnp.int32).at[target].set(assigned)
    return filled.reshape(EXPERTS, devices * CAP)

def expert_pair(normed_pad, gating_pad, element):
    table_row, gate_pair, up_pair, down_pair = element
    token_ids = table_row // TOP
    summed = jnp.zeros((table_row.shape[0], D), jnp.float32)
    for which_half in range(2):
        arrived = low_back(normed_pad[token_ids])
        gate_pre = low_back(jnp.dot(arrived, gate_pair[which_half], precision=HIGHEST))
        up_pre = low_back(jnp.dot(arrived, up_pair[which_half], precision=HIGHEST))
        activation = low(jax.nn.silu(gate_pre) * up_pre)
        summed = summed + low(low_back(jnp.dot(activation, down_pair[which_half], precision=HIGHEST)))
    return summed * gating_pad[table_row][:, None]

def expert_part(hidden, routes, table, expert_set):
    router_weight, second_gain, gate_weight, up_weight, down_weight = expert_set
    normed = low(rms_scale(hidden, second_gain))
    logits = low_back(jnp.dot(normed, router_weight, precision=HIGHEST))
    chance = jax.nn.softmax(logits, axis=-1)
    gating = jnp.take_along_axis(chance, routes, axis=1)
    normed_pad = jnp.concatenate([normed, jnp.zeros((1, D), jnp.float32)], axis=0)
    gating_pad = jnp.concatenate([gating.reshape(-1), jnp.zeros((1,), jnp.float32)])
    gate_pairs = gate_weight.reshape(EXPERTS, 2, D, FF // 2)
    up_pairs = up_weight.reshape(EXPERTS, 2, D, FF // 2)
    down_pairs = down_weight.reshape(EXPERTS, 2, FF // 2, D)
    outputs = lax.map(jax.checkpoint(partial(expert_pair, normed_pad, gating_pad)), (table, gate_pairs, up_pairs, down_pairs))
    token_ids = (table // TOP).reshape(-1)
    combined = jnp.zeros((TOKENS + 1, D), jnp.float32).at[token_ids].add(outputs.reshape(-1, D))
    return hidden + combined[:TOKENS]

def reference(inputs, query_weight, key_weight, value_weight, output_weight, router_weight, first_gain, query_gain, key_gain, second_gain, gate_weight, up_weight, down_weight, routes, lengths, dealing, cotangent):
    table = slot_table(routes)
    attention_set = tuple((array_in.astype(jnp.float32) for array_in in (query_weight, key_weight, value_weight, output_weight, first_gain, query_gain, key_gain)))
    expert_set = tuple((array_in.astype(jnp.float32) for array_in in (router_weight, second_gain, gate_weight, up_weight, down_weight)))

    def forward(block_in, attention_params, expert_params):
        advance = jax.checkpoint(group_attention)

        def visit(running, element):
            return (running, advance(element[0], element[1], element[2], attention_params))
        finished, hidden = lax.scan(visit, jnp.zeros((), jnp.float32), (block_in.reshape(N_EXPERT, GROUP_TOK, D), dealing.reshape(N_EXPERT, GROUP_TOK), lengths))
        return expert_part(hidden.reshape(TOKENS, D), routes, table, expert_params)
    result, pullback = jax.vjp(forward, inputs.astype(jnp.float32), attention_set, expert_set)
    input_grad, attention_grads, expert_grads = pullback(cotangent.astype(jnp.float32))
    return (result.astype(jnp.bfloat16), input_grad.astype(jnp.bfloat16), attention_grads[0], attention_grads[1], attention_grads[2], attention_grads[3], expert_grads[0], attention_grads[4], attention_grads[5], attention_grads[6], expert_grads[1], expert_grads[2], expert_grads[3], expert_grads[4])
```

```python
import jax
import jax.numpy as jnp
from jax import lax
from jax.sharding import PartitionSpec as P

HEADS = 16
CAP = 56
EPSILON = 1e-05
THETA = 10000.0
MASKED = -1e30
BF = jnp.bfloat16
F32 = jnp.float32


def dot(a, b):
    return jnp.dot(a, b, preferred_element_type=F32)


def contract(spec, *operands):
    return jnp.einsum(spec, *operands, preferred_element_type=F32)


def rms_scale(vector, scaling):
    return vector * lax.rsqrt(jnp.mean(vector * vector, axis=-1, keepdims=True) + EPSILON) * scaling


def rotate(heads_in, cosine, sine_wave):
    middle = heads_in.shape[-1] // 2
    former = heads_in[..., :middle]
    latter = heads_in[..., middle:]
    return jnp.concatenate(
        [former * cosine - latter * sine_wave, latter * cosine + former * sine_wave], axis=-1
    )


def places(lengths_row, stream):
    seq_ends = jnp.cumsum(lengths_row)
    before = (seq_ends[None, :] <= stream[:, None]).astype(jnp.int32)
    offset = jnp.sum(before * lengths_row[None, :], axis=1)
    return offset, stream - offset


def angles(positions, head_width):
    exponent = jnp.arange(0, head_width, 2).astype(F32) / head_width
    phases = positions.astype(F32)[:, None] * (THETA ** (-exponent))[None, :]
    return (jnp.cos(phases)[:, None, :], jnp.sin(phases)[:, None, :])


def attend(element, allowed, inv_root):
    queries, key_rows, values = element
    scores = contract("qd,kd->qk", queries, key_rows) * inv_root
    scores = jnp.where(allowed, scores, MASKED)
    highest = jnp.max(scores, axis=-1, keepdims=True)
    powers = jnp.exp(scores - highest)
    summed = jnp.sum(powers, axis=-1, keepdims=True)
    probability = (powers / summed).astype(BF)
    blended = dot(probability, values).astype(BF)
    return blended, highest + jnp.log(summed)


def attend_back(element, allowed, inv_root):
    queries, key_rows, values, blended_grad, log_total = element
    scores = contract("qd,kd->qk", queries, key_rows) * inv_root
    scores = jnp.where(allowed, scores, MASKED)
    probability = jnp.exp(scores - log_total)
    prob_slope = contract("qd,kd->qk", blended_grad, values)
    row_dot = jnp.sum(probability * prob_slope, axis=-1, keepdims=True)
    score_slope = (probability * (prob_slope - row_dot)).astype(BF)
    query_part = dot(score_slope, key_rows) * inv_root
    key_part = contract("qk,qd->kd", score_slope, queries) * inv_root
    value_part = contract("qk,qd->kd", probability.astype(BF), blended_grad)
    return query_part.astype(BF), key_part.astype(BF), value_part.astype(BF)


def by_head(matrix, head_count):
    return jnp.moveaxis(matrix.reshape(matrix.shape[0], head_count, -1), 1, 0)


def join_heads(stacked):
    return jnp.moveaxis(stacked, 0, 1).reshape(stacked.shape[1], -1)


def gather_line(array, axis=0):
    return lax.all_gather(array, "fsdp", axis=axis, tiled=True)


def swap_plane(rows):
    return lax.all_to_all(rows, "expert", split_axis=0, concat_axis=0, tiled=True)


def per_device(
    inputs,
    query_weight,
    key_weight,
    value_weight,
    output_weight,
    router_weight,
    first_gain,
    query_gain,
    key_gain,
    second_gain,
    gate_weight,
    up_weight,
    down_weight,
    routes,
    lengths,
    dealing,
    cotangent,
):
    planes, line = lax.axis_size("expert"), lax.axis_size("fsdp")
    plane_at, line_at = lax.axis_index("expert"), lax.axis_index("fsdp")
    tokens, width = inputs.shape
    group = line * tokens
    own_heads = HEADS // line
    head_size = width // HEADS
    own_width = own_heads * head_size
    inv_root = head_size ** (-0.5)
    weight_rows = query_weight.shape[0]
    slice_rows = weight_rows // planes
    units = gate_weight.shape[0]
    local = max(1, units // 2)
    halves = units // local
    expert_count = router_weight.shape[1]

    block_in = gather_line(inputs)
    incoming_low = gather_line(cotangent)
    small = gather_line(jnp.stack([first_gain, second_gain]), axis=1).astype(F32)
    gain_first, gain_second = small[0], small[1]
    full_router = gather_line(router_weight)
    routes_all = gather_line(routes)

    def own_slice(weight):
        return lax.dynamic_slice_in_dim(weight, plane_at * slice_rows, slice_rows, 0)

    sent = jnp.stack([own_slice(w) for w in (query_weight, key_weight, value_weight)], axis=1)
    sent = jnp.moveaxis(sent.reshape(slice_rows, 3, line, own_width), 2, 0)
    swapped = lax.all_to_all(sent, "fsdp", split_axis=0, concat_axis=0, tiled=True)
    columns = lax.all_gather(swapped, "expert", axis=1, tiled=True).reshape(width, 3 * own_width)
    full_output = lax.all_gather(
        own_slice(output_weight), ("fsdp", "expert"), axis=0, tiled=True
    )

    seq_start, positions = places(lengths[0], dealing)
    allowed = (dealing[None, :] >= seq_start[:, None]) & (dealing[None, :] <= dealing[:, None])
    cosine, sine_wave = angles(positions, head_size)
    per_plane = expert_count // planes
    first_local = (line_at * units) // 2
    member = jnp.sum(
        (routes_all[:, :, None] == jnp.arange(expert_count, dtype=jnp.int32)).astype(F32), axis=1
    ).reshape(line, tokens, expert_count)
    earlier = jnp.tril(jnp.ones((tokens, tokens), BF), -1)
    rank = contract("ts,bse->bte", earlier, member.astype(BF))
    coded = jnp.where(member > 0, rank, -1.0).reshape(line, tokens, planes, per_plane)
    coded = lax.dynamic_slice_in_dim(coded, first_local, local, 3)
    slot_of = jnp.moveaxis(coded, 3, 0)[..., None] == jnp.arange(CAP).astype(F32)
    slot_of = slot_of.astype(BF)

    def dispatch(rows):
        blocks = rows.reshape(line, tokens, width)
        arrived = []
        for n in range(local):
            chosen = contract("btps,btd->pbsd", slot_of[n], blocks).astype(BF)
            arrived.append(swap_plane(chosen.reshape(planes, line * CAP, width)))
        return jnp.stack(arrived).reshape(local, planes * line * CAP, width)

    def combine(rows):
        total = 0.0
        for n in range(local):
            returned = swap_plane(rows[n].reshape(planes, line * CAP, width))
            returned = returned.reshape(planes, line, CAP, width)
            total = total + contract("btps,pbsd->btd", slot_of[n], returned)
        return total.reshape(group, width)

    block_full = block_in.astype(F32)
    normed_low = rms_scale(block_full, gain_first).astype(BF)
    raw = dot(normed_low, columns).reshape(group, 3, own_width)
    query_raw, key_raw, value_low = raw[:, 0], raw[:, 1], raw[:, 2].astype(BF)
    squares = lax.psum(
        jnp.stack([jnp.sum(query_raw * query_raw, axis=-1), jnp.sum(key_raw * key_raw, axis=-1)]),
        "fsdp",
    )
    scales = lax.rsqrt(squares / width + EPSILON)[:, :, None]
    gains = (query_gain.astype(F32), key_gain.astype(F32))

    def turn(matrix, sine):
        shaped = matrix.reshape(group, own_heads, head_size)
        return rotate(shaped, cosine, sine).reshape(group, own_width)

    query_low = turn(query_raw * scales[0] * gains[0], sine_wave).astype(BF)
    key_low = turn(key_raw * scales[1] * gains[1], sine_wave).astype(BF)
    query_heads, key_heads, value_heads = (
        by_head(m, own_heads) for m in (query_low, key_low, value_low)
    )
    blended_heads, log_total = lax.map(
        lambda element: attend(element, allowed, inv_root), (query_heads, key_heads, value_heads)
    )
    blended_own = join_heads(blended_heads)
    blended = gather_line(blended_own, axis=1)
    hidden = block_full + dot(blended, full_output)
    normed_second, second_back = jax.vjp(rms_scale, hidden, gain_second)
    expert_in = normed_second.astype(BF)

    arrived = dispatch(expert_in)
    arrived_slopes = dispatch(incoming_low)
    chance = jax.nn.softmax(contract("nrd,de->nre", arrived, full_router), axis=-1)
    expert_ids = ((plane_at * line + line_at) * units) // 2 + jnp.arange(local)
    named = (expert_ids[:, None, None] == jnp.arange(expert_count)).astype(F32)
    gating = jnp.sum(chance * named, axis=-1, keepdims=True)
    gates = gate_weight.reshape(local, halves, width, -1)
    ups = up_weight.reshape(local, halves, width, -1)
    downs = down_weight.reshape(local, halves, -1, width)
    gate_pre = contract("nrd,nhdf->nhrf", arrived, gates)
    up_pre = contract("nrd,nhdf->nhrf", arrived, ups)
    squashed = jax.nn.sigmoid(gate_pre)
    swished = gate_pre * squashed
    activation = (swished * up_pre).astype(BF)
    joined = contract("nhrf,nhfd->nrd", activation, downs)
    incoming_rows = arrived_slopes.astype(F32)
    gating_slope = jnp.sum(incoming_rows * joined, axis=-1, keepdims=True)
    weighted = (gating * joined).astype(BF)
    unit_slope = (gating * incoming_rows).astype(BF)
    logit_slope = (gating_slope * gating * (named - chance)).astype(BF)
    activation_slope = contract("nrd,nhfd->nhrf", unit_slope, downs)
    down_gradient = contract("nhrf,nrd->nhfd", activation, unit_slope)
    gate_slope = (
        activation_slope * up_pre * squashed * (1.0 + gate_pre * (1.0 - squashed))
    ).astype(BF)
    up_slope = (activation_slope * swished).astype(BF)
    gate_gradient = contract("nrd,nhrf->nhdf", arrived, gate_slope)
    up_gradient = contract("nrd,nhrf->nhdf", arrived, up_slope)
    row_slope = (
        contract("nhrf,nhdf->nrd", gate_slope, gates)
        + contract("nhrf,nhdf->nrd", up_slope, ups)
        + contract("nre,de->nrd", logit_slope, full_router)
    ).astype(BF)
    router_grad = contract("nrd,nre->de", arrived, logit_slope)

    slope_part = combine(row_slope).astype(BF)
    output_part = combine(weighted).astype(BF)
    mixed = lax.psum_scatter(output_part, "fsdp", scatter_dimension=0, tiled=True)
    hidden_own = lax.dynamic_slice_in_dim(hidden, line_at * tokens, tokens, 0)
    block_output = (hidden_own + mixed.astype(F32)).astype(BF)
    slope_share = lax.psum_scatter(slope_part, "fsdp", scatter_dimension=0, tiled=True)
    expert_in_slope = gather_line(slope_share).astype(F32)
    hidden_part, second_gain_grad = second_back(expert_in_slope)
    hidden_slope = incoming_low.astype(F32) + hidden_part
    attention_slope = hidden_slope.astype(BF)

    output_grad = contract("tc,td->cd", blended_own, attention_slope)
    blended_slope = contract("td,cd->tc", attention_slope, output_weight).astype(BF)
    parts = lax.map(
        lambda element: attend_back(element, allowed, inv_root),
        (query_heads, key_heads, value_heads, by_head(blended_slope, own_heads), log_total),
    )
    query_slope, key_slope, value_slope = (join_heads(part) for part in parts)
    turned = [turn(slope.astype(F32), -sine_wave) for slope in (query_slope, key_slope)]
    raws = (query_raw, key_raw)
    gain_grads = [
        jnp.sum(turned[i] * raws[i] * scales[i], axis=0) for i in range(2)
    ]
    scaled = [turned[i] * gains[i] for i in range(2)]
    dots = lax.psum(
        jnp.stack([jnp.sum(scaled[i] * raws[i], axis=-1) for i in range(2)]), "fsdp"
    )[:, :, None]
    raw_slopes = [
        (scales[i] * scaled[i] - raws[i] * (scales[i] ** 3 * dots[i] / width)).astype(BF)
        for i in range(2)
    ]
    joint = jnp.concatenate(raw_slopes + [value_slope], axis=1)
    normed_part = contract("tc,dc->td", joint, columns).astype(BF)
    normed_slope = lax.psum_scatter(normed_part, "fsdp", scatter_dimension=0, tiled=True)
    block_own = inputs.astype(F32)
    input_part, first_gain_grad = jax.vjp(rms_scale, block_own, gain_first)[1](
        normed_slope.astype(F32)
    )
    hidden_slope_own = lax.dynamic_slice_in_dim(hidden_slope, line_at * tokens, tokens, 0)
    input_gradient = (hidden_slope_own + input_part).astype(BF)

    joint_grad = contract("td,tc->dc", normed_low, joint).astype(BF)
    joint_grad = joint_grad.reshape(line, planes, slice_rows, 3, own_width)
    shared = lax.psum_scatter(joint_grad, "expert", scatter_dimension=1, tiled=False)
    shared = lax.all_to_all(shared, "fsdp", split_axis=0, concat_axis=0, tiled=True)
    shared = jnp.moveaxis(shared, 0, 2)
    shared = jnp.moveaxis(shared, 1, 0).reshape(3, slice_rows, width)
    weight_grads = lax.all_gather(shared, "expert", axis=1, tiled=True).astype(F32)
    output_total = lax.psum(output_grad.astype(BF), "expert").astype(F32)
    own_second = lax.dynamic_slice_in_dim(second_gain_grad, line_at * weight_rows, weight_rows, 0)
    own_gains = lax.psum(jnp.stack([gain_grads[0], gain_grads[1], own_second]), "expert")
    first_total = lax.psum(first_gain_grad, ("expert", "fsdp"))
    first_total = lax.dynamic_slice_in_dim(first_total, line_at * weight_rows, weight_rows, 0)
    router_share = lax.psum_scatter(
        router_grad.astype(BF), "fsdp", scatter_dimension=0, tiled=True
    )
    router_total = lax.psum(router_share, "expert").astype(F32)
    return (
        block_output,
        input_gradient,
        weight_grads[0],
        weight_grads[1],
        weight_grads[2],
        output_total,
        router_total,
        first_total,
        own_gains[0],
        own_gains[1],
        own_gains[2],
        gate_gradient.reshape(gate_weight.shape),
        up_gradient.reshape(up_weight.shape),
        down_gradient.reshape(down_weight.shape),
    )


def solution(mesh):
    both = ("expert", "fsdp")
    rows, cube, shard, gain = P(both, None), P(both, None, None), P("fsdp", None), P("fsdp")
    return jax.shard_map(
        per_device,
        mesh=mesh,
        in_specs=(rows,)
        + (shard,) * 5
        + (gain,) * 4
        + (cube,) * 3
        + (rows, P("expert", None), P("expert"), rows),
        out_specs=(rows, rows) + (shard,) * 5 + (gain,) * 4 + (cube,) * 3,
        check_vma=False,
    )
```

```python
import functools

import jax
import jax.numpy as jnp
from jax import lax
from jax.experimental import pallas as pl
from jax.experimental.pallas import tpu as pltpu
from jax.sharding import PartitionSpec as P

HEADS = 16
CAP = 56
EPSILON = 1e-05
THETA = 10000.0
MASKED = -1e30
LOG2E = 1.4426950408889634
BF = jnp.bfloat16
F32 = jnp.float32
MESH = pl.DeviceIdType.MESH
MIB = 1 << 20
CHUNKS = 2


def dot(a, b):
    return jnp.dot(a, b, preferred_element_type=F32)


def dot_nt(a, b):
    return lax.dot_general(a, b, (((1,), (1,)), ((), ())), preferred_element_type=F32)


def dot_tn(a, b):
    return lax.dot_general(a, b, (((0,), (0,)), ((), ())), preferred_element_type=F32)


def contract(spec, *operands):
    return jnp.einsum(spec, *operands, preferred_element_type=F32)


def shape_of(dims, dtype):
    return jax.ShapeDtypeStruct(dims, dtype)


def cost(flops, moved):
    return pl.CostEstimate(flops=int(flops), bytes_accessed=int(moved), transcendentals=0)


def params(mib, **kwargs):
    return pltpu.CompilerParams(vmem_limit_bytes=mib * MIB, **kwargs)


def places(lengths_row, stream):
    seq_ends = jnp.cumsum(lengths_row)
    before = (seq_ends[None, :] <= stream[:, None]).astype(jnp.int32)
    offset = jnp.sum(before * lengths_row[None, :], axis=1)
    return offset, stream - offset


def angles(positions, head_width):
    exponent = jnp.arange(0, head_width, 2).astype(F32) / head_width
    phases = positions.astype(F32)[:, None] * (THETA ** (-exponent))[None, :]
    return jnp.cos(phases), jnp.sin(phases)


def gather_kernel(
    planes, line, pieces, x_ref, small_ref, sent_ref,
    all_ref, small_all, columns_ref, swapped_ref,
    x_send, x_recv, s_send, s_recv, z_send, z_recv, p_send, p_recv, own_sem,
):
    e, f = lax.axis_index("expert"), lax.axis_index("fsdp")
    barrier = pltpu.get_barrier_semaphore()
    for d in range(1, line):
        pl.semaphore_signal(
            barrier, inc=1, device_id={"fsdp": lax.rem(f + d, line)}, device_id_type=MESH
        )
    for d in range(1, planes):
        pl.semaphore_signal(
            barrier, inc=1, device_id={"expert": lax.rem(e + d, planes)}, device_id_type=MESH
        )
    pl.semaphore_wait(barrier, line + planes - 2)
    rows = x_ref.shape[0]
    part = rows // pieces
    small_rows = small_ref.shape[0]

    swaps, smalls = [], []
    for d in range(1, line):
        to = lax.rem(f + d, line)
        swaps.append(pltpu.make_async_remote_copy(
            src_ref=sent_ref.at[to], dst_ref=swapped_ref.at[f],
            send_sem=z_send.at[d - 1], recv_sem=z_recv.at[d - 1],
            device_id={"fsdp": to}, device_id_type=MESH,
        ))
        smalls.append(pltpu.make_async_remote_copy(
            src_ref=small_ref, dst_ref=small_all.at[pl.ds(f * small_rows, small_rows)],
            send_sem=s_send.at[d - 1], recv_sem=s_recv.at[d - 1],
            device_id={"fsdp": to}, device_id_type=MESH,
        ))
    for copy in swaps:
        copy.start()

    def hop(direction, step, c):
        origin = f - direction * step
        place = pl.ds(origin * rows + c * part, part)
        source = x_ref.at[pl.ds(c * part, part)] if step == 0 else all_ref.at[place]
        side = 0 if direction == 1 else 1
        return pltpu.make_async_remote_copy(
            src_ref=source, dst_ref=all_ref.at[place],
            send_sem=x_send.at[side, step, c], recv_sem=x_recv.at[side, step, c],
            device_id={"fsdp": f + direction}, device_id_type=MESH,
        )

    def sends(direction, step):
        origin, to = f - direction * step, f + direction
        return (origin >= 0) & (origin < line) & (to >= 0) & (to < line)

    def receives(direction, step):
        origin = f - direction * (step + 1)
        return (origin >= 0) & (origin < line)

    for direction in (1, -1):
        @pl.when(sends(direction, 0))
        def _(direction=direction):
            for c in range(pieces):
                hop(direction, 0, c).start()

    for copy in smalls:
        copy.start()
    locals_ = [
        pltpu.make_async_copy(x_ref, all_ref.at[pl.ds(f * rows, rows)], own_sem.at[0]),
        pltpu.make_async_copy(
            small_ref, small_all.at[pl.ds(f * small_rows, small_rows)], own_sem.at[1]
        ),
        pltpu.make_async_copy(sent_ref.at[f], swapped_ref.at[f], own_sem.at[2]),
    ]
    for copy in locals_:
        copy.start()
    for copy in swaps:
        copy.wait_recv()
    locals_[2].wait()
    spread = []
    for d in range(1, planes):
        spread.append(pltpu.make_async_remote_copy(
            src_ref=swapped_ref, dst_ref=columns_ref.at[:, e],
            send_sem=p_send.at[d - 1], recv_sem=p_recv.at[d - 1],
            device_id={"expert": lax.rem(e + d, planes)}, device_id_type=MESH,
        ))
        spread[-1].start()
    own = pltpu.make_async_copy(swapped_ref, columns_ref.at[:, e], own_sem.at[3])
    own.start()

    for step in range(line - 1):
        for c in range(pieces):
            for direction in (1, -1):
                @pl.when(receives(direction, step))
                def _(direction=direction, step=step, c=c):
                    origin = f - direction * (step + 1)
                    place = pl.ds(origin * rows + c * part, part)
                    side = 0 if direction == 1 else 1
                    pltpu.make_async_remote_copy(
                        src_ref=all_ref.at[place], dst_ref=all_ref.at[place],
                        send_sem=x_send.at[side, step, c], recv_sem=x_recv.at[side, step, c],
                        device_id={"fsdp": f - direction}, device_id_type=MESH,
                    ).wait_recv()
                if step < line - 2:
                    @pl.when(sends(direction, step + 1))
                    def _(direction=direction, step=step, c=c):
                        hop(direction, step + 1, c).start()
    for step in range(line - 1):
        for direction in (1, -1):
            @pl.when(sends(direction, step))
            def _(direction=direction, step=step):
                for c in range(pieces):
                    hop(direction, step, c).wait_send()
    for copy in swaps:
        copy.wait_send()
    for copy in smalls + spread:
        copy.wait()
    for copy in locals_[:2] + [own]:
        copy.wait()


def gather_start(block, small, sent, planes, line):
    rows, width = block.shape
    pieces = 4
    anywhere = pl.BlockSpec(memory_space=pl.ANY)
    sems = pltpu.SemaphoreType.DMA
    return pl.pallas_call(
        functools.partial(gather_kernel, planes, line, pieces),
        out_shape=(
            shape_of((line * rows, width), BF),
            shape_of((line * small.shape[0], small.shape[1]), BF),
            shape_of((line, planes) + sent.shape[1:], BF),
            shape_of(sent.shape, BF),
        ),
        in_specs=[anywhere] * 3,
        out_specs=[anywhere] * 4,
        scratch_shapes=[
            sems((2, line - 1, pieces)), sems((2, line - 1, pieces)),
            sems((line - 1,)), sems((line - 1,)), sems((line - 1,)), sems((line - 1,)),
            sems((planes - 1,)), sems((planes - 1,)), sems((4,)),
        ],
        compiler_params=pltpu.CompilerParams(collective_id=0, has_side_effects=True),
        name="gather_start",
    )(block, small, sent)


def line_sum_kernel(line, pieces, lag, p_ref, o_ref, right_in, left_in, send_sem, recv_sem):
    f = lax.axis_index("fsdp")
    barrier = pltpu.get_barrier_semaphore()
    last = line - 1

    @pl.when(f > 0)
    def _():
        pl.semaphore_signal(barrier, inc=1, device_id={"fsdp": f - 1}, device_id_type=MESH)

    @pl.when(f < last)
    def _():
        pl.semaphore_signal(barrier, inc=1, device_id={"fsdp": f + 1}, device_id_type=MESH)

    pl.semaphore_wait(barrier, jnp.where((f > 0) & (f < last), 2, 1))
    part = p_ref.shape[0] // pieces

    def copy(side, source, c):
        buffer = right_in if side == 0 else left_in
        place = pl.ds(c * part, part)
        return pltpu.make_async_remote_copy(
            src_ref=(p_ref if source else buffer).at[place], dst_ref=buffer.at[place],
            send_sem=send_sem.at[side, c], recv_sem=recv_sem.at[side, c],
            device_id={"fsdp": f + 1 if side == 0 else f - 1}, device_id_type=MESH,
        )

    def first(side):
        def body(c, carry):
            copy(side, True, c).start()
            return carry

        lax.fori_loop(0, pieces, body, 0)

    @pl.when(f == 0)
    def _():
        first(0)

    @pl.when(f == last)
    def _():
        first(1)

    def arrive(side, c):
        place = pl.ds(pl.multiple_of(c * part, part), part)
        buffer = right_in if side == 0 else left_in
        origin, end = (0, last) if side == 0 else (last, 0)
        leads = (2 * f <= last) if side == 0 else (2 * f > last)

        @pl.when(f == origin)
        def _():
            o_ref[place, :] = p_ref[place, :].astype(F32)

        @pl.when(f != origin)
        def _():
            copy(side, False, c).wait_recv()
            came = buffer[place, :].astype(F32)

            @pl.when(f != end)
            def _():
                buffer[place, :] = (came + p_ref[place, :].astype(F32)).astype(BF)
                copy(side, False, c).start()

            @pl.when(leads)
            def _():
                o_ref[place, :] = came + p_ref[place, :].astype(F32)

            @pl.when(jnp.logical_not(leads))
            def _():
                o_ref[place, :] += came

    def body(s, carry):
        for side in range(2):
            c = s - lag * (f if side == 0 else last - f)

            @pl.when((c >= 0) & (c < pieces))
            def _(side=side, c=c):
                arrive(side, c)

        return carry

    lax.fori_loop(0, pieces + lag * last, body, 0)

    def drain(c, carry):
        @pl.when(f < last)
        def _():
            copy(0, True, c).wait_send()

        @pl.when(f > 0)
        def _():
            copy(1, True, c).wait_send()

        return carry

    lax.fori_loop(0, pieces, drain, 0)


def line_sum(part, line, height=32, lag=2):
    rows, width = part.shape
    pieces = rows // height
    return pl.pallas_call(
        functools.partial(line_sum_kernel, line, pieces, lag),
        out_shape=shape_of((rows, width), F32),
        in_specs=[pl.BlockSpec(memory_space=pltpu.VMEM)],
        out_specs=pl.BlockSpec(memory_space=pltpu.VMEM),
        scratch_shapes=[
            pltpu.VMEM((rows, width), BF),
            pltpu.VMEM((rows, width), BF),
            pltpu.SemaphoreType.DMA((2, pieces)),
            pltpu.SemaphoreType.DMA((2, pieces)),
        ],
        compiler_params=params(48, collective_id=1, has_side_effects=True),
        cost_estimate=cost(0, 260 * MIB),
        name="line_sum",
    )(part)


def finish_kernel(
    planes, line, height, lag, p_ref, a_ref, x_ref, gain_ref, slope_ref, gains_ref,
    o_ref, a_out, gains_out,
    right_in, left_in, a_own, a_half, a_in, a_sum, a_cols, gain_part, gain_in, gain_own, gain_all,
    z_send, z_recv, h_send, h_recv, r_send, r_recv, s_send, s_recv, g_send, g_recv,
    w_send, w_recv, n_send, n_recv, m_send, m_recv, own_sem,
):
    e, f = lax.axis_index("expert"), lax.axis_index("fsdp")
    chips, last = planes // 2, line - 1
    c, k = e // 2, e % 2
    mate = e + 1 - 2 * k
    barrier = pltpu.get_barrier_semaphore()

    def greet(**device):
        pl.semaphore_signal(barrier, inc=1, device_id=device, device_id_type=MESH)

    for d in range(1, planes):
        greet(expert=lax.rem(e + d, planes))
    for d in range(1, line):
        greet(fsdp=lax.rem(f + d, line))
    pl.semaphore_wait(barrier, planes - 1 + last)

    rows = p_ref.shape[0] // line
    pieces = rows // height

    def remote(source, target, send, recv, **device):
        return pltpu.make_async_remote_copy(
            src_ref=source, dst_ref=target, send_sem=send, recv_sem=recv,
            device_id=device, device_id_type=MESH,
        )

    to_mate = [remote(a_ref.at[:, :, 1 - k], a_half, h_send.at[0], h_recv.at[0], expert=mate)]
    own_half = [pltpu.make_async_copy(a_ref.at[:, :, k], a_own, own_sem.at[0])]
    for copy in to_mate + own_half:
        copy.start()

    def place_of(side, s):
        target = last - s // pieces if side == 0 else s // pieces
        return target, pl.ds(pl.multiple_of(target * rows + lax.rem(s, pieces) * height, height), height)

    def copy_line(side, source, s):
        buffer = right_in if side == 0 else left_in
        place = place_of(side, s)[1]
        return remote(
            (p_ref if source else buffer).at[place], buffer.at[place],
            z_send.at[side, s], z_recv.at[side, s], fsdp=f + 1 if side == 0 else f - 1,
        )

    def first(side):
        def body(s, carry):
            copy_line(side, True, s).start()
            return carry

        lax.fori_loop(0, last * pieces, body, 0)

    @pl.when(f == 0)
    def _():
        first(0)

    @pl.when(f == last)
    def _():
        first(1)

    def arrive(side, s):
        buffer = right_in if side == 0 else left_in
        target, place = place_of(side, s)
        copy_line(side, False, s).wait_recv()

        @pl.when(target != f)
        def _():
            buffer[place, :] = (buffer[place, :].astype(F32) + p_ref[place, :].astype(F32)).astype(BF)
            copy_line(side, False, s).start()

    def body(s, carry):
        right = s - lag * f
        left = s - lag * (last - f)

        @pl.when((f > 0) & (right >= 0) & (right < (last - f + 1) * pieces))
        def _():
            arrive(0, right)

        @pl.when((f < last) & (left >= 0) & (left < (f + 1) * pieces))
        def _():
            arrive(1, left)

        return carry

    total = last * pieces + lag * last
    stops = [total // 8, total // 2, (total * 5) // 8]
    lax.fori_loop(0, stops[0], body, 0)

    for copy in own_half:
        copy.wait()
    for copy in to_mate:
        copy.wait_recv()

    def add_half(i, carry):
        for j in range(chips):
            a_own[i, j] = (a_own[i, j].astype(F32) + a_half[i, j].astype(F32)).astype(BF)
        return carry

    lax.fori_loop(0, line, add_half, 0)
    shares = []
    for d in range(1, chips):
        to = lax.rem(c + d, chips)
        shares.append(remote(
            a_own.at[:, to], a_in.at[d - 1], r_send.at[d - 1], r_recv.at[d - 1],
            expert=to * 2 + k,
        ))
    for copy in shares:
        copy.start()
    lax.fori_loop(stops[0], stops[1], body, 0)

    for copy in shares:
        copy.wait_recv()

    def add_shares(i, carry):
        summed = a_own[i, c].astype(F32)
        for d in range(1, chips):
            summed = summed + a_in[d - 1, i].astype(F32)
        a_sum[i] = summed.astype(BF)
        return carry

    lax.fori_loop(0, line, add_shares, 0)
    swaps = []
    for d in range(1, line):
        to = lax.rem(f + d, line)
        swaps.append(remote(
            a_sum.at[to], a_cols.at[f], s_send.at[d - 1], s_recv.at[d - 1], fsdp=to
        ))
    for copy in swaps:
        copy.start()
    a_cols[f] = a_sum[f]
    lax.fori_loop(stops[1], stops[2], body, 0)

    for copy in swaps:
        copy.wait_recv()
    spread = [remote(a_cols, a_out.at[:, e], g_send.at[0], g_recv.at[0], expert=mate)]
    for d in range(1, chips):
        to = lax.rem(c + d, chips) * 2 + k
        spread.append(remote(a_cols, a_out.at[:, e], g_send.at[d], g_recv.at[d], expert=to))
    own_out = pltpu.make_async_copy(a_cols, a_out.at[:, e], own_sem.at[1])
    for copy in spread + [own_out]:
        copy.start()
    lax.fori_loop(stops[2], total, body, 0)

    gain = gain_ref[...]
    width = gain.shape[1]
    gain_part[...] = jnp.zeros_like(gain_part)

    def tile(i, carry):
        place = pl.ds(pl.multiple_of(i * height, height), height)
        mine = pl.ds(pl.multiple_of(f * rows + i * height, height), height)
        right = jnp.where(f > 0, right_in[mine, :].astype(F32), 0.0)
        left = jnp.where(f < last, left_in[mine, :].astype(F32), 0.0)
        slope = p_ref[mine, :].astype(F32) + right + left
        x = x_ref[place, :].astype(F32)
        scale = lax.rsqrt(jnp.mean(x * x, axis=-1, keepdims=True) + EPSILON)
        gain_part[0:1, :] += jnp.sum(slope * x * scale, axis=0, keepdims=True)
        slope = slope * gain
        along = jnp.sum(slope * x, axis=-1, keepdims=True) / width
        part = scale * slope - x * (scale * scale * scale * along)
        o_ref[place, :] = (slope_ref[place, :] + part).astype(BF)
        return carry

    lax.fori_loop(0, pieces, tile, 0)

    lanes = gains_ref.shape[1]

    def share_of(which):
        return gain_part.at[:, pl.ds(pl.multiple_of(which * lanes, lanes), lanes)]

    to_shards = []
    for d in range(1, line):
        to = lax.rem(f + d, line)
        to_shards.append(remote(
            share_of(to), gain_in.at[d - 1], n_send.at[d - 1], n_recv.at[d - 1], fsdp=to
        ))
    for copy in to_shards:
        copy.start()
    for copy in to_shards:
        copy.wait_recv()
    summed = share_of(f)[...] + gains_ref[...]
    for d in range(1, line):
        summed = summed + gain_in[d - 1]
    gain_own[...] = summed
    to_plane = []
    for d in range(1, planes):
        to_plane.append(remote(
            gain_own, gain_all.at[d - 1], m_send.at[d - 1], m_recv.at[d - 1],
            expert=lax.rem(e + d, planes),
        ))
    for copy in to_plane:
        copy.start()

    passed = []
    for d in range(1, chips):
        spread[d].wait_recv()
        source = lax.rem(c + chips - d, chips) * 2 + k
        passed.append(remote(
            a_out.at[:, source], a_out.at[:, source], w_send.at[d - 1], w_recv.at[d - 1],
            expert=mate,
        ))
        passed[-1].start()
    for copy in to_plane:
        copy.wait_recv()
    total_gain = gain_own[...]
    for d in range(1, planes):
        total_gain = total_gain + gain_all[d - 1]
    gains_out[...] = total_gain
    spread[0].wait_recv()
    for copy in passed:
        copy.wait()
    for copy in spread + to_shards + to_plane:
        copy.wait_send()
    own_out.wait()
    for copy in to_mate + shares + swaps:
        copy.wait_send()

    def drain(side, source, count):
        def one(s, carry):
            copy_line(side, source, s).wait_send()
            return carry

        lax.fori_loop(0, count, one, 0)

    @pl.when(f < last)
    def _():
        drain(0, True, (last - f) * pieces)

    @pl.when(f > 0)
    def _():
        drain(1, True, f * pieces)


def finish(part, a, block, gain, slope, gains, planes, line, height=32, lag=2):
    group, width = part.shape
    tokens = group // line
    chips, last = planes // 2, line - 1
    items = last * (tokens // height)
    rows, lanes = a.shape[2:]
    share = gains.shape[1]
    vmem = pl.BlockSpec(memory_space=pltpu.VMEM)
    anywhere = pl.BlockSpec(memory_space=pl.ANY)
    sems = pltpu.SemaphoreType.DMA
    return pl.pallas_call(
        functools.partial(finish_kernel, planes, line, height, lag),
        out_shape=(
            shape_of((tokens, width), BF), shape_of(a.shape, BF), shape_of(gains.shape, F32),
        ),
        in_specs=[vmem, anywhere, vmem, vmem, vmem, vmem],
        out_specs=(vmem, anywhere, vmem),
        scratch_shapes=[
            pltpu.VMEM((group, width), BF), pltpu.VMEM((group, width), BF),
            pltpu.VMEM((line, chips, rows, lanes), BF), pltpu.VMEM((line, chips, rows, lanes), BF),
            pltpu.VMEM((chips - 1, line, rows, lanes), BF),
            pltpu.VMEM((line, rows, lanes), BF), pltpu.VMEM((line, rows, lanes), BF),
            pltpu.VMEM((8, width), F32), pltpu.VMEM((last, 8, share), F32),
            pltpu.VMEM((8, share), F32), pltpu.VMEM((planes - 1, 8, share), F32),
            sems((2, items)), sems((2, items)), sems((1,)), sems((1,)),
            sems((chips - 1,)), sems((chips - 1,)), sems((last,)), sems((last,)),
            sems((chips,)), sems((chips,)), sems((chips - 1,)), sems((chips - 1,)),
            sems((last,)), sems((last,)), sems((planes - 1,)), sems((planes - 1,)),
            sems((2,)),
        ],
        compiler_params=params(60, collective_id=2, has_side_effects=True),
        cost_estimate=cost(0, 400 * MIB),
        name="finish",
    )(part, a.reshape(line, chips, 2, rows, lanes), block, gain, slope, gains)


def swap_plane(rows):
    return lax.all_to_all(rows, "expert", split_axis=0, concat_axis=0, tiled=True)


def small_line_sum(array, line):
    total = array
    for d in range(1, line):
        total = total + lax.ppermute(array, "fsdp", [(i, (i + d) % line) for i in range(line)])
    return total


def as_row(column, second):
    lane = lax.broadcasted_iota(jnp.int32, (column.shape[0], 128), 1)
    return jnp.where(lane == 0, column, second).T[:2, :]


def as_column(row):
    return jnp.broadcast_to(row, (128, row.shape[1])).T


def project_kernel(x_ref, gain_ref, columns_ref, normed_ref, raw_ref, value_ref, squares_ref):
    x = x_ref[...].astype(F32)
    scale = lax.rsqrt(jnp.mean(x * x, axis=-1, keepdims=True) + EPSILON)
    normed = (x * scale * gain_ref[...]).astype(BF)
    normed_ref[...] = normed
    own = value_ref.shape[1]
    query = dot(normed, columns_ref[:, :own])
    key = dot(normed, columns_ref[:, own:2 * own])
    value_ref[...] = dot(normed, columns_ref[:, 2 * own:]).astype(BF)
    raw_ref[:, :own] = query
    raw_ref[:, own:] = key
    squares_ref[...] = as_row(
        jnp.sum(query * query, axis=-1, keepdims=True), jnp.sum(key * key, axis=-1, keepdims=True)
    )


def project(block, gain, columns, tile):
    group, width = block.shape
    own = columns.shape[1] // 3
    rows = lambda count: pl.BlockSpec((tile, count), lambda i: (i, 0))
    return pl.pallas_call(
        project_kernel,
        grid=(group // tile,),
        out_shape=(
            shape_of((group, width), BF), shape_of((group, 2 * own), F32),
            shape_of((group, own), BF), shape_of((2, group), F32),
        ),
        in_specs=[
            rows(width), pl.BlockSpec((1, width), lambda i: (0, 0)),
            pl.BlockSpec((width, 3 * own), lambda i: (0, 0)),
        ],
        out_specs=(rows(width), rows(2 * own), rows(own), pl.BlockSpec((2, tile), lambda i: (0, i))),
        compiler_params=params(48),
        cost_estimate=cost(6 * group * width * own, 14 * group * own),
        name="project",
    )(block, gain, columns)


def scales_of(squares_ref, width):
    scales = lax.rsqrt(squares_ref[...] / width + EPSILON)
    return [as_column(scales[i:i + 1, :]) for i in range(2)]


def turn_kernel(width, raw_ref, squares_ref, gain_ref, cos_ref, sin_ref, q_ref, k_ref):
    own = q_ref.shape[1]
    scales = scales_of(squares_ref, width)
    cosine, sine = cos_ref[...], sin_ref[...]
    for which, out in enumerate((q_ref, k_ref)):
        for j in range(0, own, 128):
            place = slice(which * own + j, which * own + j + 128)
            v = raw_ref[:, place] * scales[which] * gain_ref[:, place]
            out[:, j:j + 128] = (v * cosine + pltpu.roll(v, 64, 1) * sine).astype(BF)


def turn(raw, squares, gain, cosine, sine, width, tile):
    group, double = raw.shape
    own = double // 2
    rows = lambda count: pl.BlockSpec((tile, count), lambda i: (i, 0))
    return pl.pallas_call(
        functools.partial(turn_kernel, width),
        grid=(group // tile,),
        out_shape=(shape_of((group, own), BF),) * 2,
        in_specs=[
            rows(double), pl.BlockSpec((2, tile), lambda i: (0, i)),
            pl.BlockSpec((1, double), lambda i: (0, 0)), rows(128), rows(128),
        ],
        out_specs=(rows(own), rows(own)),
        compiler_params=params(32),
        cost_estimate=cost(20 * group * double, 8 * group * double),
        name="turn",
    )(raw, squares, gain, cosine, sine)


def turn_back_kernel(
    width, dq_ref, dk_ref, raw_ref, squares_ref, gain_ref, cos_ref, sin_ref, dots_ref, grad_ref
):
    own = dq_ref.shape[1]
    scales = scales_of(squares_ref, width)
    cosine, sine = cos_ref[...], sin_ref[...]

    @pl.when(pl.program_id(0) == 0)
    def _():
        grad_ref[...] = jnp.zeros_like(grad_ref)

    dots = []
    for which, slope in enumerate((dq_ref, dk_ref)):
        total = 0.0
        for j in range(0, own, 128):
            place = slice(which * own + j, which * own + j + 128)
            v = slope[:, j:j + 128].astype(F32)
            turned = (v * cosine - pltpu.roll(v, 64, 1) * sine) * raw_ref[:, place]
            total = total + jnp.sum(turned * gain_ref[:, place], axis=-1, keepdims=True)
            grad_ref[:, place] += jnp.sum(turned * scales[which], axis=0, keepdims=True)
        dots.append(total)
    dots_ref[...] = as_row(*dots)


def turn_back(dq, dk, raw, squares, gain, cosine, sine, width, tile):
    group, double = raw.shape
    own = double // 2
    rows = lambda count: pl.BlockSpec((tile, count), lambda i: (i, 0))
    pair = pl.BlockSpec((2, tile), lambda i: (0, i))
    flat = pl.BlockSpec((1, double), lambda i: (0, 0))
    return pl.pallas_call(
        functools.partial(turn_back_kernel, width),
        grid=(group // tile,),
        out_shape=(shape_of((2, group), F32), shape_of((1, double), F32)),
        in_specs=[rows(own), rows(own), rows(double), pair, flat, rows(128), rows(128)],
        out_specs=(pair, flat),
        compiler_params=params(32),
        cost_estimate=cost(20 * group * double, 8 * group * double),
        name="turn_back",
    )(dq, dk, raw, squares, gain, cosine, sine)


def join_kernel(
    width, dq_ref, dk_ref, dv_ref, raw_ref, squares_ref, dots_ref, gain_ref, cos_ref, sin_ref,
    columns_ref, joint_ref, part_ref,
):
    own = dq_ref.shape[1]
    scales = scales_of(squares_ref, width)
    dots = [as_column(dots_ref[i:i + 1, :]) for i in range(2)]
    cosine, sine = cos_ref[...], sin_ref[...]
    for which, slope in enumerate((dq_ref, dk_ref)):
        scale = scales[which]
        factor = scale * scale * scale * dots[which] / width
        for j in range(0, own, 128):
            place = slice(which * own + j, which * own + j + 128)
            v = slope[:, j:j + 128].astype(F32)
            turned = (v * cosine - pltpu.roll(v, 64, 1) * sine) * gain_ref[:, place]
            joint_ref[:, place] = (scale * turned - raw_ref[:, place] * factor).astype(BF)
    joint_ref[:, 2 * own:] = dv_ref[...]
    part_ref[...] = dot_nt(joint_ref[...], columns_ref[...]).astype(BF)


def join_slopes(dq, dk, dv, raw, squares, dots, gain, cosine, sine, columns, tile):
    group, double = raw.shape
    own = double // 2
    width = columns.shape[0]
    rows = lambda count: pl.BlockSpec((tile, count), lambda i: (i, 0))
    pair = pl.BlockSpec((2, tile), lambda i: (0, i))
    flat = pl.BlockSpec((1, double), lambda i: (0, 0))
    return pl.pallas_call(
        functools.partial(join_kernel, width),
        grid=(group // tile,),
        out_shape=(shape_of((group, 3 * own), BF), shape_of((group, width), BF)),
        in_specs=[
            rows(own), rows(own), rows(own), rows(double), pair, pair, flat, rows(128), rows(128),
            pl.BlockSpec((width, 3 * own), lambda i: (0, 0)),
        ],
        out_specs=(rows(3 * own), rows(width)),
        compiler_params=params(48),
        cost_estimate=cost(6 * group * width * own, 8 * group * width),
        name="join_slopes",
    )(dq, dk, dv, raw, squares, dots, gain, cosine, sine, columns)


def allowed_scores(queries, key_rows, start_ref, place_ref, key_place_ref, inv_root):
    scores = dot_nt(key_rows, queries) * (inv_root * LOG2E)
    key_place = key_place_ref[...]
    allowed = (key_place >= start_ref[...]) & (key_place <= place_ref[...])
    return jnp.where(allowed, scores, MASKED)


def attend_kernel(inv_root, q_ref, k_ref, v_ref, start_ref, place_ref, kp_ref, o_ref, log_ref):
    scores = allowed_scores(q_ref[...], k_ref[...], start_ref, place_ref, kp_ref, inv_root)
    highest = jnp.max(scores, axis=0, keepdims=True)
    powers = jnp.exp2(scores - highest)
    summed = jnp.sum(powers, axis=0, keepdims=True)
    blended = dot_tn(v_ref[...], powers.astype(BF)) / summed
    o_ref[...] = blended.T.astype(BF)
    log_ref[...] = (highest + jnp.log2(summed))[None]


def attend(query, key, value, start_row, place_row, place_column, heads, tile):
    group, own_width = query.shape
    size = own_width // heads
    kernel = functools.partial(attend_kernel, size ** (-0.5))
    whole = pl.BlockSpec((group, size), lambda h, i: (0, h))
    row = pl.BlockSpec((1, tile), lambda h, i: (0, i))
    return pl.pallas_call(
        kernel,
        grid=(heads, group // tile),
        out_shape=(shape_of((group, own_width), BF), shape_of((heads, 1, group), F32)),
        in_specs=[
            pl.BlockSpec((tile, size), lambda h, i: (i, h)), whole, whole, row, row,
            pl.BlockSpec((group, 1), lambda h, i: (0, 0)),
        ],
        out_specs=(
            pl.BlockSpec((tile, size), lambda h, i: (i, h)),
            pl.BlockSpec((1, 1, tile), lambda h, i: (h, 0, i)),
        ),
        compiler_params=params(48),
        cost_estimate=cost(4 * heads * group * group * size * 4, 8 * group * own_width),
        name="attend",
    )(query, key, value, start_row, place_row, place_column)


def attend_back_kernel(
    inv_root, q_ref, k_ref, v_ref, g_ref, log_ref, start_ref, place_ref, kp_ref,
    dq_ref, dk_ref, dv_ref, dk_sum, dv_sum,
):
    i = pl.program_id(1)
    queries, key_rows, slope = q_ref[...], k_ref[...], g_ref[...]
    scores = allowed_scores(queries, key_rows, start_ref, place_ref, kp_ref, inv_root)
    probability = jnp.exp2(scores - log_ref[0])
    prob_slope = dot_nt(v_ref[...], slope)
    product = probability * prob_slope
    row_dot = jnp.sum(product, axis=0, keepdims=True)
    score_slope = (product - probability * row_dot).astype(BF)
    dq_ref[...] = (dot_tn(key_rows, score_slope) * inv_root).T.astype(BF)
    key_part = dot(score_slope, queries) * inv_root
    value_part = dot(probability.astype(BF), slope)

    @pl.when(i == 0)
    def _():
        dk_sum[...] = key_part
        dv_sum[...] = value_part

    @pl.when(i > 0)
    def _():
        dk_sum[...] += key_part
        dv_sum[...] += value_part

    @pl.when(i == pl.num_programs(1) - 1)
    def _():
        dk_ref[...] = dk_sum[...].astype(BF)
        dv_ref[...] = dv_sum[...].astype(BF)


def attend_back(query, key, value, slope, log_total, start_row, place_row, place_column, heads, tile):
    group, own_width = query.shape
    size = own_width // heads
    whole = pl.BlockSpec((group, size), lambda h, i: (0, h))
    row = pl.BlockSpec((1, tile), lambda h, i: (0, i))
    tiled = pl.BlockSpec((tile, size), lambda h, i: (i, h))
    return pl.pallas_call(
        functools.partial(attend_back_kernel, size ** (-0.5)),
        grid=(heads, group // tile),
        out_shape=(shape_of((group, own_width), BF),) * 3,
        in_specs=[
            tiled, whole, whole, tiled, pl.BlockSpec((1, 1, tile), lambda h, i: (h, 0, i)),
            row, row, pl.BlockSpec((group, 1), lambda h, i: (0, 0)),
        ],
        out_specs=(tiled, whole, whole),
        scratch_shapes=[pltpu.VMEM((group, size), F32)] * 2,
        compiler_params=params(56),
        cost_estimate=cost(10 * heads * group * group * size * 3, 16 * group * own_width),
        name="attend_back",
    )(query, key, value, slope, log_total, start_row, place_row, place_column)


def hide_kernel(x_ref, attended_ref, gain_ref, hidden_ref, normed_ref):
    hidden = x_ref[...].astype(F32) + attended_ref[...]
    hidden_ref[...] = hidden
    scale = lax.rsqrt(jnp.mean(hidden * hidden, axis=-1, keepdims=True) + EPSILON)
    normed_ref[...] = (hidden * scale * gain_ref[...]).astype(BF)


def hide(block, attended, gain, offset, tile):
    count, width = attended.shape
    rows = pl.BlockSpec((tile, width), lambda i: (i, 0))
    return pl.pallas_call(
        hide_kernel,
        grid=(count // tile,),
        out_shape=(shape_of((count, width), F32), shape_of((count, width), BF)),
        in_specs=[
            pl.BlockSpec((tile, width), lambda i: (i + offset // tile, 0)), rows,
            pl.BlockSpec((1, width), lambda i: (0, 0)),
        ],
        out_specs=(rows, rows),
        compiler_params=params(48),
        cost_estimate=cost(8 * count * width, 12 * count * width),
        name="hide",
    )(block, attended, gain)


def hide_back_kernel(
    slope_ref, hidden_ref, incoming_ref, gain_ref, weight_ref, total_ref, low_ref, blend_ref, grad_ref
):
    slope, hidden = slope_ref[...], hidden_ref[...]
    scale = lax.rsqrt(jnp.mean(hidden * hidden, axis=-1, keepdims=True) + EPSILON)
    part = jnp.sum(slope * hidden * scale, axis=0, keepdims=True)

    @pl.when(pl.program_id(0) == 0)
    def _():
        grad_ref[...] = part

    @pl.when(pl.program_id(0) > 0)
    def _():
        grad_ref[...] += part

    slope = slope * gain_ref[...]
    along = jnp.sum(slope * hidden, axis=-1, keepdims=True) / hidden.shape[1]
    total = incoming_ref[...].astype(F32) + (
        scale * slope - hidden * (scale * scale * scale * along)
    )
    total_ref[...] = total
    low = total.astype(BF)
    low_ref[...] = low
    blend_ref[...] = dot_nt(low, weight_ref[...]).astype(BF)


def hide_back(slope, hidden, incoming, gain, weight, offset, tile):
    count, width = slope.shape
    own = weight.shape[0]
    rows = pl.BlockSpec((tile, width), lambda i: (i, 0))
    flat = pl.BlockSpec((1, width), lambda i: (0, 0))
    return pl.pallas_call(
        hide_back_kernel,
        grid=(count // tile,),
        out_shape=(
            shape_of((count, width), F32), shape_of((count, width), BF),
            shape_of((count, own), BF), shape_of((1, width), F32),
        ),
        in_specs=[
            rows, rows, pl.BlockSpec((tile, width), lambda i: (i + offset // tile, 0)), flat,
            pl.BlockSpec((own, width), lambda i: (0, 0)),
        ],
        out_specs=(rows, rows, pl.BlockSpec((tile, own), lambda i: (i, 0)), flat),
        compiler_params=params(56),
        cost_estimate=cost(2 * count * width * own, 18 * count * width),
        name="hide_back",
    )(slope, hidden, incoming, gain, weight)


def joint_grad_kernel(normed_ref, joint_ref, router_ref, o_ref):
    size = joint_ref.shape[1]
    o_ref[:, :size] = dot(normed_ref[...].T, joint_ref[...]).astype(BF)
    o_ref[:, size:] = router_ref[...]


def joint_grad(normed, joint, router):
    group, width = normed.shape
    size, extra = joint.shape[1], router.shape[1]
    tile = 512
    return pl.pallas_call(
        joint_grad_kernel,
        grid=(width // tile,),
        out_shape=shape_of((width, size + extra), BF),
        in_specs=[
            pl.BlockSpec((group, tile), lambda j: (0, j)),
            pl.BlockSpec((group, size), lambda j: (0, 0)),
            pl.BlockSpec((tile, extra), lambda j: (j, 0)),
        ],
        out_specs=pl.BlockSpec((tile, size + extra), lambda j: (j, 0)),
        compiler_params=params(56),
        cost_estimate=cost(2 * group * width * size, 6 * group * width),
        name="joint_grad",
    )(normed, joint, router)


def dispatch_kernel(slots, code_ref, rows_ref, o_ref, select):
    pairs = code_ref.shape[0]

    @pl.when(pl.program_id(0) == 0)
    def _():
        for i in range(pairs):
            row = code_ref[i:i + 1, :]
            slot = lax.broadcasted_iota(jnp.int32, (slots, row.shape[1]), 0).astype(F32)
            select[i * slots:(i + 1) * slots, :] = (slot == row).astype(BF)

    chosen = dot(select[...], rows_ref[...]).astype(BF)
    o_ref[...] = chosen.reshape(o_ref.shape)


def dispatch(codes, rows, planes, local, slots):
    pairs = planes * local
    count, width = rows.shape
    tile = 512
    return pl.pallas_call(
        functools.partial(dispatch_kernel, slots),
        grid=(width // tile,),
        out_shape=shape_of((planes, local, slots, width), BF),
        in_specs=[
            pl.BlockSpec((pairs, count), lambda j: (0, 0)),
            pl.BlockSpec((count, tile), lambda j: (0, j)),
        ],
        out_specs=pl.BlockSpec((planes, local, slots, tile), lambda j: (0, 0, 0, j)),
        scratch_shapes=[pltpu.VMEM((pairs * slots, count), BF)],
        compiler_params=params(48),
        cost_estimate=cost(2 * pairs * slots * count * width, 2 * pairs * slots * width * 2),
        name="dispatch",
    )(codes, rows)


def combine_kernel(slots, code_ref, rows_ref, o_ref, select):
    pairs = code_ref.shape[1]

    @pl.when(pl.program_id(0) == 0)
    def _():
        total = pairs * slots
        lane = lax.broadcasted_iota(jnp.int32, (pairs, total), 1)
        start = lax.broadcasted_iota(jnp.int32, (pairs, total), 0) * slots
        within = (lane >= start) & (lane < start + slots)
        spread = dot(code_ref[...], within.astype(BF))
        slot = jnp.sum(jnp.where(within, lane - start, 0), axis=0, keepdims=True)
        select[...] = (spread == slot.astype(F32)).astype(BF)

    rows = rows_ref[...].reshape(pairs * slots, rows_ref.shape[-1])
    o_ref[...] = dot(select[...], rows).astype(BF)


def combine(codes, rows):
    planes, local, slots, width = rows.shape
    pairs = planes * local
    count = codes.shape[0]
    tile = 512
    return pl.pallas_call(
        functools.partial(combine_kernel, slots),
        grid=(width // tile,),
        out_shape=shape_of((count, width), BF),
        in_specs=[
            pl.BlockSpec((count, pairs), lambda j: (0, 0)),
            pl.BlockSpec((planes, local, slots, tile), lambda j: (0, 0, 0, j)),
        ],
        out_specs=pl.BlockSpec((count, tile), lambda j: (0, j)),
        scratch_shapes=[pltpu.VMEM((count, pairs * slots), BF)],
        compiler_params=params(56),
        cost_estimate=cost(2 * pairs * slots * count * width, 2 * pairs * slots * width * 2),
        name="combine",
    )(codes, rows)


def expert_kernel(
    halves, x_ref, c_ref, gate_ref, up_ref, down_ref, router_ref, named_ref,
    weighted_ref, slope_ref, act_ref, gslope_ref, uslope_ref, logit_ref,
):
    width = x_ref.shape[-1]
    x = x_ref[...].reshape(-1, width)
    c = c_ref[...].reshape(-1, width).astype(F32)
    router = router_ref[...]
    logits = dot(x, router)
    powers = jnp.exp(logits - jnp.max(logits, axis=-1, keepdims=True))
    chance = powers / jnp.sum(powers, axis=-1, keepdims=True)
    named = named_ref[0]
    gating = jnp.sum(chance * named, axis=-1, keepdims=True)
    joined = None
    kept = []
    for h in range(halves):
        gate_pre = dot(x, gate_ref[h])
        up_pre = dot(x, up_ref[h])
        squashed = jax.nn.sigmoid(gate_pre)
        swished = gate_pre * squashed
        activation = swished * up_pre
        act_ref[h] = (gating * activation).astype(BF)
        part = dot(activation.astype(BF), down_ref[h])
        joined = part if joined is None else joined + part
        kept.append((up_pre * squashed * (1.0 + gate_pre * (1.0 - squashed)), swished))
    gating_slope = jnp.sum(c * joined, axis=-1, keepdims=True)
    weighted_ref[...] = (gating * joined).astype(BF).reshape(weighted_ref.shape)
    unit_slope = (gating * c).astype(BF)
    logit_slope = (gating_slope * gating * (named - chance)).astype(BF)
    logit_ref[...] = logit_slope[None]
    slope = dot_nt(logit_slope, router)
    for h in range(halves):
        activation_slope = dot_nt(unit_slope, down_ref[h])
        gate_slope = (activation_slope * kept[h][0]).astype(BF)
        up_slope = (activation_slope * kept[h][1]).astype(BF)
        gslope_ref[h] = gate_slope
        uslope_ref[h] = up_slope
        slope = slope + dot_nt(gate_slope, gate_ref[h]) + dot_nt(up_slope, up_ref[h])
    slope_ref[...] = slope.astype(BF).reshape(slope_ref.shape)


def experts(x, c, gates, ups, downs, router, named, halves):
    planes, local, slots, width = x.shape
    hidden = gates.shape[-1]
    sources = max(1, 448 // slots)
    tile = sources * slots
    steps = planes // sources
    count = planes * slots
    expert_total = router.shape[1]
    units = local * halves
    row_spec = pl.BlockSpec((sources, 1, slots, width), lambda n, t: (t, n, 0, 0))
    unit_spec = pl.BlockSpec((halves, tile, hidden), lambda n, t: (n, t, 0))
    once = pl.Buffered(1)
    wide = pl.BlockSpec((halves, width, hidden), lambda n, t: (n, 0, 0), pipeline_mode=once)
    tall = pl.BlockSpec((halves, hidden, width), lambda n, t: (n, 0, 0), pipeline_mode=once)
    return pl.pallas_call(
        functools.partial(expert_kernel, halves),
        grid=(local, steps),
        out_shape=(
            shape_of(x.shape, BF), shape_of(x.shape, BF),
            shape_of((units, count, hidden), BF), shape_of((units, count, hidden), BF),
            shape_of((units, count, hidden), BF), shape_of((local, count, expert_total), BF),
        ),
        in_specs=[
            row_spec, row_spec, wide, wide, tall,
            pl.BlockSpec((width, expert_total), lambda n, t: (0, 0)),
            pl.BlockSpec((1, 1, expert_total), lambda n, t: (n, 0, 0)),
        ],
        out_specs=(
            row_spec, row_spec, unit_spec, unit_spec, unit_spec,
            pl.BlockSpec((1, tile, expert_total), lambda n, t: (n, t, 0)),
        ),
        compiler_params=params(62),
        cost_estimate=cost(12 * units * count * hidden * width, 10 * local * count * width),
        name="experts",
    )(x, c, gates, ups, downs, router, named)


def wide_grad_kernel(x0_ref, x1_ref, g0_ref, g1_ref, u0_ref, u1_ref, dg_ref, du_ref):
    tile = x0_ref.shape[-1]
    x0 = x0_ref[...].reshape(-1, tile).T
    x1 = x1_ref[...].reshape(-1, tile).T
    dg_ref[0] = dot(x0, g0_ref[0]) + dot(x1, g1_ref[0])
    du_ref[0] = dot(x0, u0_ref[0]) + dot(x1, u1_ref[0])


def wide_grad(xs, gslopes, uslopes, halves):
    planes, local, slots, width = xs[0].shape
    units, count, hidden = gslopes[0].shape
    tile = 1024 if planes * slots <= 1024 else 512
    x_spec = pl.BlockSpec((planes, 1, slots, tile), lambda u, j: (0, u // halves, 0, j))
    s_spec = pl.BlockSpec((1, count, hidden), lambda u, j: (u, 0, 0))
    o_spec = pl.BlockSpec((1, tile, hidden), lambda u, j: (u, j, 0))
    out = shape_of((units, width, hidden), F32)
    return pl.pallas_call(
        wide_grad_kernel,
        grid=(units, width // tile),
        out_shape=(out, out),
        in_specs=[x_spec] * 2 + [s_spec] * 4,
        out_specs=(o_spec, o_spec),
        compiler_params=params(60),
        cost_estimate=cost(8 * units * count * hidden * width, 8 * units * hidden * width),
        name="wide_grad",
    )(*xs, *gslopes, *uslopes)


def down_grad_kernel(a0_ref, a1_ref, c0_ref, c1_ref, d_ref):
    tile = c0_ref.shape[-1]
    d_ref[0] = dot(a0_ref[0].T, c0_ref[...].reshape(-1, tile)) + dot(
        a1_ref[0].T, c1_ref[...].reshape(-1, tile)
    )


def down_grad(acts, cs, halves):
    planes, local, slots, width = cs[0].shape
    units, count, hidden = acts[0].shape
    tile = 1024 if planes * slots <= 1024 else 512
    c_spec = pl.BlockSpec((planes, 1, slots, tile), lambda u, j: (0, u // halves, 0, j))
    a_spec = pl.BlockSpec((1, count, hidden), lambda u, j: (u, 0, 0))
    return pl.pallas_call(
        down_grad_kernel,
        grid=(units, width // tile),
        out_shape=shape_of((units, hidden, width), F32),
        in_specs=[a_spec] * 2 + [c_spec] * 2,
        out_specs=pl.BlockSpec((1, hidden, tile), lambda u, j: (u, 0, j)),
        compiler_params=params(60),
        cost_estimate=cost(4 * units * count * hidden * width, 4 * units * hidden * width),
        name="down_grad",
    )(*acts, *cs)


def per_device(
    inputs,
    query_weight,
    key_weight,
    value_weight,
    output_weight,
    router_weight,
    first_gain,
    query_gain,
    key_gain,
    second_gain,
    gate_weight,
    up_weight,
    down_weight,
    routes,
    lengths,
    dealing,
    cotangent,
):
    planes, line = lax.axis_size("expert"), lax.axis_size("fsdp")
    plane_at, line_at = lax.axis_index("expert"), lax.axis_index("fsdp")
    tokens, width = inputs.shape
    group = line * tokens
    own_heads = HEADS // line
    head_size = width // HEADS
    own_width = own_heads * head_size
    weight_rows = query_weight.shape[0]
    slice_rows = weight_rows // planes
    units = gate_weight.shape[0]
    local = max(1, units // 2)
    halves = units // local
    expert_count = router_weight.shape[1]
    blocks = line // CHUNKS
    chunk_rows = blocks * tokens
    slots = blocks * CAP

    def own_slice(weight):
        return lax.dynamic_slice_in_dim(weight, plane_at * slice_rows, slice_rows, 0)

    sent = jnp.stack([own_slice(w) for w in (query_weight, key_weight, value_weight)], axis=1)
    sent = jnp.moveaxis(sent.reshape(slice_rows, 3, line, own_width), 2, 0)
    sent = sent.reshape(line, slice_rows, 3 * own_width)
    top_count = routes.shape[1]
    packed = [router_weight, first_gain, second_gain, routes.astype(BF)]
    sizes = [array.size for array in packed]
    fill = -sum(sizes) % (16 * 128)
    small = jnp.concatenate([array.reshape(-1) for array in packed] + [jnp.zeros((fill,), BF)])
    block_in, small_all, columns, _ = gather_start(
        inputs, small.reshape(-1, 128), sent, planes, line
    )
    columns = columns.reshape(width, 3 * own_width)
    small_all = small_all.reshape(line, -1)
    ends = [sum(sizes[:i]) for i in range(5)]
    full_router, gain_first, gain_second, routes_all = (
        small_all[:, ends[i]:ends[i + 1]] for i in range(4)
    )
    full_router = full_router.reshape(width, expert_count)
    gain_first, gain_second = (g.reshape(width).astype(F32) for g in (gain_first, gain_second))
    routes_all = routes_all.reshape(line, tokens, top_count).astype(jnp.int32)
    block_in, later = lax.optimization_barrier((block_in, cotangent))
    incoming_low = lax.all_gather(later, "fsdp", axis=0, tiled=True)

    seq_start, positions = places(lengths[0], dealing)
    start_row, place_row, place_column = seq_start[None, :], dealing[None, :], dealing[:, None]
    cosine, sine = angles(positions, head_size)
    per_plane = expert_count // planes
    first_local = (line_at * units) // 2
    member = jnp.sum(
        (routes_all[..., None] == jnp.arange(expert_count, dtype=jnp.int32)).astype(F32), axis=2
    )
    earlier = jnp.tril(jnp.ones((tokens, tokens), BF), -1)
    rank = contract("ts,bse->bte", earlier, member.astype(BF))
    rank = rank + ((jnp.arange(line) % blocks) * CAP).astype(F32)[:, None, None]
    coded = jnp.where(member > 0, rank, -1.0).reshape(line, tokens, planes, per_plane)
    coded = lax.dynamic_slice_in_dim(coded, first_local, local, 3)
    coded = coded.reshape(CHUNKS, chunk_rows, planes * local)
    by_token = [coded[k].astype(BF) for k in range(CHUNKS)]
    by_pair = [coded[k].T for k in range(CHUNKS)]

    def chunk(array, k):
        return lax.slice_in_dim(array, k * chunk_rows, (k + 1) * chunk_rows)

    def own_rows(parts):
        start = (line_at % blocks) * tokens
        picked = [lax.dynamic_slice_in_dim(part, start, tokens, 0) for part in parts]
        result = picked[0]
        for k in range(1, CHUNKS):
            result = jnp.where(line_at // blocks == k, picked[k], result)
        return result

    normed_low, raw, value_low, squares = project(block_in, gain_first[None], columns, tokens)
    squares = small_line_sum(squares, line)
    both_gains = jnp.concatenate([query_gain, key_gain])[None].astype(F32)
    rotary = (jnp.concatenate([cosine, cosine], -1), jnp.concatenate([-sine, sine], -1))
    query_low, key_low = turn(raw, squares, both_gains, *rotary, width, tokens)
    blended, log_total = attend(
        query_low, key_low, value_low, start_row, place_row, place_column, own_heads, tokens
    )
    attention_part = dot(blended, output_weight).astype(BF)

    named = (
        (((plane_at * line + line_at) * units) // 2 + jnp.arange(local))[:, None, None]
        == jnp.arange(expert_count)
    ).astype(F32)
    slope_rows = [
        dispatch(by_pair[k], chunk(incoming_low, k), planes, local, slots) for k in range(CHUNKS)
    ]
    attention_parts = [chunk(attention_part, k) for k in range(CHUNKS)]
    slope_rows[0], slope_rows[1], attention_parts[0] = lax.optimization_barrier(
        (slope_rows[0], slope_rows[1], attention_parts[0])
    )
    hidden, arrived, arrived_slopes = [], [], []
    for k in range(CHUNKS):
        if k:
            slope_rows[k], attention_parts[k], rows = lax.optimization_barrier(
                (slope_rows[k], attention_parts[k], rows)
            )
            arrived.append(swap_plane(rows))
            slope_rows[k], _ = lax.optimization_barrier((slope_rows[k], arrived[-1]))
        arrived_slopes.append(swap_plane(slope_rows[k]))
        attended = line_sum(attention_parts[k], line)
        held, normed = hide(block_in, attended, gain_second[None], k * chunk_rows, tokens)
        hidden.append(held)
        rows = dispatch(by_pair[k], normed, planes, local, slots)
        rows, arrived_slopes[k] = lax.optimization_barrier((rows, arrived_slopes[k]))
    arrived.append(swap_plane(rows))
    weighted, row_slopes, acts, gslopes, uslopes, logit_slopes = [], [], [], [], [], []
    for k in range(CHUNKS):
        results = experts(
            arrived[k], arrived_slopes[k], gate_weight, up_weight, down_weight, full_router,
            named, halves,
        )
        for store, result in zip(
            (weighted, row_slopes, acts, gslopes, uslopes, logit_slopes), results
        ):
            store.append(result)
    returned = []
    behind = arrived[-1]
    for k in range(CHUNKS):
        rows, _ = lax.optimization_barrier((row_slopes[k], behind))
        behind = swap_plane(rows)
        returned.append(behind)
    hidden_slopes, attention_slopes, blended_slopes, second_gain_grad = [], [], [], 0.0
    mixed_rows = []
    for k in range(CHUNKS):
        part = combine(by_token[k], returned[k])
        if k:
            part, _ = lax.optimization_barrier((part, summed))
        summed = line_sum(part, line)
        results = hide_back(
            summed, hidden[k], incoming_low, gain_second[None], output_weight, k * chunk_rows, tokens
        )
        hidden_slopes.append(results[0])
        attention_slopes.append(results[1])
        blended_slopes.append(results[2])
        second_gain_grad = second_gain_grad + results[3]
        rows, _, _ = lax.optimization_barrier((weighted[k], behind, summed))
        behind = swap_plane(rows)
        mixed_rows.append(behind)
    slopes = attend_back(
        query_low, key_low, value_low, jnp.concatenate(blended_slopes), log_total, start_row,
        place_row, place_column, own_heads, tokens,
    )
    slopes, acts, gslopes, uslopes, logit_slopes, mixed_rows, attention_slopes = (
        lax.optimization_barrier(
            (slopes, acts, gslopes, uslopes, logit_slopes, mixed_rows, attention_slopes)
        )
    )
    attention_slope = jnp.concatenate(attention_slopes)
    gate_gradient, up_gradient = wide_grad(arrived, gslopes, uslopes, halves)
    down_gradient = down_grad(acts, arrived_slopes, halves)
    router_grad = sum(
        contract(
            "ensd,nesq->dq", arrived[k],
            logit_slopes[k].reshape(local, planes, slots, expert_count),
        )
        for k in range(CHUNKS)
    )
    output_part = jnp.concatenate(
        [combine(by_token[k], mixed_rows[k]) for k in range(CHUNKS)]
    )

    output_grad = contract("tc,td->cd", blended, attention_slope).astype(BF)
    output_share = lax.psum_scatter(output_grad, "expert", scatter_dimension=0, tiled=True)
    output_total = lax.all_gather(output_share, "expert", axis=0, tiled=True).astype(F32)
    dots, gain_grads = turn_back(*slopes[:2], raw, squares, both_gains, *rotary, width, tokens)
    dots = small_line_sum(dots, line)
    joint, normed_part = join_slopes(
        *slopes, raw, squares, dots, both_gains, *rotary, columns, tokens
    )
    router_lanes = -expert_count % 128
    router_pad = jnp.pad(router_grad.astype(BF), ((0, 0), (0, router_lanes)))
    joint_total = joint_grad(normed_low, joint, router_pad)
    mine = line_at * weight_rows
    second_own = lax.dynamic_slice_in_dim(second_gain_grad, mine, weight_rows, 1)
    gain_rows = jnp.concatenate(
        [
            jnp.zeros((1, weight_rows), F32), second_own, gain_grads.reshape(2, own_width),
            jnp.zeros((4, weight_rows), F32),
        ]
    )
    input_gradient, totals, gain_totals = finish(
        normed_part, joint_total.reshape(line, planes, slice_rows, -1), inputs, gain_first[None],
        own_rows(hidden_slopes), gain_rows, planes, line,
    )
    mixed = lax.psum_scatter(output_part, "fsdp", scatter_dimension=0, tiled=True)
    block_output = (own_rows(hidden) + mixed.astype(F32)).astype(BF)
    totals = totals.reshape(line, weight_rows, -1)
    weight_grads = [
        jnp.moveaxis(totals[:, :, i * own_width:(i + 1) * own_width], 0, 1)
        .reshape(weight_rows, width)
        .astype(F32)
        for i in range(3)
    ]
    router_total = jnp.sum(
        totals[:, :, 3 * own_width:3 * own_width + expert_count].astype(F32), axis=0
    )
    return (
        block_output,
        input_gradient,
        *weight_grads,
        output_total,
        router_total,
        gain_totals[0],
        gain_totals[2],
        gain_totals[3],
        gain_totals[1],
        gate_gradient,
        up_gradient,
        down_gradient,
    )


def solution(mesh):
    both = ("expert", "fsdp")
    rows, cube, shard, gain = P(both, None), P(both, None, None), P("fsdp", None), P("fsdp")
    return jax.shard_map(
        per_device,
        mesh=mesh,
        in_specs=(rows,)
        + (shard,) * 5
        + (gain,) * 4
        + (cube,) * 3
        + (rows, P("expert", None), P("expert"), rows),
        out_specs=(rows, rows) + (shard,) * 5 + (gain,) * 4 + (cube,) * 3,
        check_vma=False,
    )
```

```python
import functools

import jax
import jax.numpy as jnp
from jax import lax
from jax.experimental import pallas as pl
from jax.experimental.pallas import tpu as pltpu
from jax.sharding import PartitionSpec as P

HEADS = 16
CAP = 56
EPSILON = 1e-05
THETA = 10000.0
MASKED = -1e30
LOG2E = 1.4426950408889634
BF = jnp.bfloat16
F32 = jnp.float32
MESH = pl.DeviceIdType.MESH
MIB = 1 << 20
CHUNKS = 2


def dot(a, b):
    return jnp.dot(a, b, preferred_element_type=F32)


def dot_nt(a, b):
    return lax.dot_general(a, b, (((1,), (1,)), ((), ())), preferred_element_type=F32)


def dot_tn(a, b):
    return lax.dot_general(a, b, (((0,), (0,)), ((), ())), preferred_element_type=F32)


def contract(spec, *operands):
    return jnp.einsum(spec, *operands, preferred_element_type=F32)


def shape_of(dims, dtype):
    return jax.ShapeDtypeStruct(dims, dtype)


def cost(flops, moved):
    return pl.CostEstimate(flops=int(flops) // 64, bytes_accessed=int(moved) // 64, transcendentals=0)


def params(mib, **kwargs):
    return pltpu.CompilerParams(vmem_limit_bytes=mib * MIB, **kwargs)


def places(lengths_row, stream):
    seq_ends = jnp.cumsum(lengths_row)
    before = (seq_ends[None, :] <= stream[:, None]).astype(jnp.int32)
    offset = jnp.sum(before * lengths_row[None, :], axis=1)
    return offset, stream - offset


def angles(positions, head_width):
    exponent = jnp.arange(0, head_width, 2).astype(F32) / head_width
    phases = positions.astype(F32)[:, None] * (THETA ** (-exponent))[None, :]
    return jnp.cos(phases), jnp.sin(phases)


def gather_kernel(
    planes, line, pieces, x_ref, c_ref, small_ref, sent_ref,
    x_all, c_all, small_all, columns_ref, swapped_ref,
    x_send, x_recv, s_send, s_recv, z_send, z_recv, p_send, p_recv, own_sem,
):
    e, f = lax.axis_index("expert"), lax.axis_index("fsdp")
    barrier = pltpu.get_barrier_semaphore()
    for d in range(1, line):
        pl.semaphore_signal(
            barrier, inc=1, device_id={"fsdp": lax.rem(f + d, line)}, device_id_type=MESH
        )
    for d in range(1, planes):
        pl.semaphore_signal(
            barrier, inc=1, device_id={"expert": lax.rem(e + d, planes)}, device_id_type=MESH
        )
    pl.semaphore_wait(barrier, line + planes - 2)
    rows = x_ref.shape[0]
    part = rows // pieces
    small_rows = small_ref.shape[0]

    swaps, smalls = [], []
    for d in range(1, line):
        to = lax.rem(f + d, line)
        swaps.append(pltpu.make_async_remote_copy(
            src_ref=sent_ref.at[to], dst_ref=swapped_ref.at[f],
            send_sem=z_send.at[d - 1], recv_sem=z_recv.at[d - 1],
            device_id={"fsdp": to}, device_id_type=MESH,
        ))
        smalls.append(pltpu.make_async_remote_copy(
            src_ref=small_ref, dst_ref=small_all.at[pl.ds(f * small_rows, small_rows)],
            send_sem=s_send.at[d - 1], recv_sem=s_recv.at[d - 1],
            device_id={"fsdp": to}, device_id_type=MESH,
        ))
    for copy in swaps:
        copy.start()

    def hop(direction, step, c):
        own_ref, all_ref = (x_ref, x_all) if c < pieces else (c_ref, c_all)
        origin = f - direction * step
        place = pl.ds(origin * rows + c % pieces * part, part)
        source = own_ref.at[pl.ds(c % pieces * part, part)] if step == 0 else all_ref.at[place]
        side = 0 if direction == 1 else 1
        return pltpu.make_async_remote_copy(
            src_ref=source, dst_ref=all_ref.at[place],
            send_sem=x_send.at[side, step, c], recv_sem=x_recv.at[side, step, c],
            device_id={"fsdp": f + direction}, device_id_type=MESH,
        )

    def sends(direction, step):
        origin, to = f - direction * step, f + direction
        return (origin >= 0) & (origin < line) & (to >= 0) & (to < line)

    def receives(direction, step):
        origin = f - direction * (step + 1)
        return (origin >= 0) & (origin < line)

    for direction in (1, -1):
        @pl.when(sends(direction, 0))
        def _(direction=direction):
            for c in range(2 * pieces):
                hop(direction, 0, c).start()

    for copy in smalls:
        copy.start()
    locals_ = [
        pltpu.make_async_copy(x_ref, x_all.at[pl.ds(f * rows, rows)], own_sem.at[0]),
        pltpu.make_async_copy(c_ref, c_all.at[pl.ds(f * rows, rows)], own_sem.at[4]),
        pltpu.make_async_copy(
            small_ref, small_all.at[pl.ds(f * small_rows, small_rows)], own_sem.at[1]
        ),
        pltpu.make_async_copy(sent_ref.at[f], swapped_ref.at[f], own_sem.at[2]),
    ]
    for copy in locals_:
        copy.start()
    for copy in swaps:
        copy.wait_recv()
    locals_[3].wait()
    spread = []
    for d in range(1, planes):
        spread.append(pltpu.make_async_remote_copy(
            src_ref=swapped_ref, dst_ref=columns_ref.at[:, e],
            send_sem=p_send.at[d - 1], recv_sem=p_recv.at[d - 1],
            device_id={"expert": lax.rem(e + d, planes)}, device_id_type=MESH,
        ))
        spread[-1].start()
    own = pltpu.make_async_copy(swapped_ref, columns_ref.at[:, e], own_sem.at[3])
    own.start()

    for step in range(line - 1):
        for c in range(2 * pieces):
            for direction in (1, -1):
                @pl.when(receives(direction, step))
                def _(direction=direction, step=step, c=c):
                    origin = f - direction * (step + 1)
                    all_ref = x_all if c < pieces else c_all
                    place = pl.ds(origin * rows + c % pieces * part, part)
                    side = 0 if direction == 1 else 1
                    pltpu.make_async_remote_copy(
                        src_ref=all_ref.at[place], dst_ref=all_ref.at[place],
                        send_sem=x_send.at[side, step, c], recv_sem=x_recv.at[side, step, c],
                        device_id={"fsdp": f - direction}, device_id_type=MESH,
                    ).wait_recv()
                if step < line - 2:
                    @pl.when(sends(direction, step + 1))
                    def _(direction=direction, step=step, c=c):
                        hop(direction, step + 1, c).start()
    for step in range(line - 1):
        for direction in (1, -1):
            @pl.when(sends(direction, step))
            def _(direction=direction, step=step):
                for c in range(2 * pieces):
                    hop(direction, step, c).wait_send()
    for copy in swaps:
        copy.wait_send()
    for copy in smalls + spread:
        copy.wait()
    for copy in locals_[:3] + [own]:
        copy.wait()


def gather_start(block, half, small, sent, planes, line):
    rows, width = block.shape
    pieces = 4
    anywhere = pl.BlockSpec(memory_space=pl.ANY)
    sems = pltpu.SemaphoreType.DMA
    return pl.pallas_call(
        functools.partial(gather_kernel, planes, line, pieces),
        out_shape=(
            shape_of((line * rows, width), BF),
            shape_of((line * rows, half.shape[1]), BF),
            shape_of((line * small.shape[0], small.shape[1]), BF),
            shape_of((line, planes) + sent.shape[1:], BF),
            shape_of(sent.shape, BF),
        ),
        in_specs=[anywhere] * 4,
        out_specs=[anywhere] * 5,
        scratch_shapes=[
            sems((2, line - 1, 2 * pieces)), sems((2, line - 1, 2 * pieces)),
            sems((line - 1,)), sems((line - 1,)), sems((line - 1,)), sems((line - 1,)),
            sems((planes - 1,)), sems((planes - 1,)), sems((5,)),
        ],
        compiler_params=pltpu.CompilerParams(collective_id=0, has_side_effects=True),
        name="gather_start",
    )(block, half, small, sent)


def line_steps(line, pieces, lag, p_ref, o_ref, right_in, left_in, send_sem, recv_sem):
    f = lax.axis_index("fsdp")
    last = line - 1
    part = p_ref.shape[0] // pieces

    def greet():
        barrier = pltpu.get_barrier_semaphore()

        @pl.when(f > 0)
        def _():
            pl.semaphore_signal(barrier, inc=1, device_id={"fsdp": f - 1}, device_id_type=MESH)

        @pl.when(f < last)
        def _():
            pl.semaphore_signal(barrier, inc=1, device_id={"fsdp": f + 1}, device_id_type=MESH)

    neighbours = jnp.where((f > 0) & (f < last), 2, 1)

    def copy(side, source, c):
        buffer = right_in if side == 0 else left_in
        place = pl.ds(c * part, part)
        return pltpu.make_async_remote_copy(
            src_ref=(p_ref if source else buffer).at[place], dst_ref=buffer.at[place],
            send_sem=send_sem.at[side, c], recv_sem=recv_sem.at[side, c],
            device_id={"fsdp": f + 1 if side == 0 else f - 1}, device_id_type=MESH,
        )

    def enter():
        for side in range(2):
            @pl.when(f == (0 if side == 0 else last))
            def _(side=side):
                def one(c, carry):
                    copy(side, True, c).start()
                    return carry

                lax.fori_loop(0, pieces, one, 0)

    def arrive(side, c):
        place = pl.ds(pl.multiple_of(c * part, part), part)
        buffer = right_in if side == 0 else left_in
        origin, end = (0, last) if side == 0 else (last, 0)
        leads = (2 * f <= last) if side == 0 else (2 * f > last)

        @pl.when(f == origin)
        def _():
            o_ref[place, :] = p_ref[place, :].astype(F32)

        @pl.when(f != origin)
        def _():
            copy(side, False, c).wait_recv()
            came = buffer[place, :].astype(F32)

            @pl.when(f != end)
            def _():
                buffer[place, :] = (came + p_ref[place, :].astype(F32)).astype(BF)
                copy(side, False, c).start()

            @pl.when(leads)
            def _():
                o_ref[place, :] = came + p_ref[place, :].astype(F32)

            @pl.when(jnp.logical_not(leads))
            def _():
                o_ref[place, :] += came

    def body(s, carry):
        for side in range(2):
            c = s - lag * (f if side == 0 else last - f)

            @pl.when((c >= 0) & (c < pieces))
            def _(side=side, c=c):
                arrive(side, c)

        return carry

    def drain():
        def one(c, carry):
            @pl.when(f < last)
            def _():
                copy(0, True, c).wait_send()

            @pl.when(f > 0)
            def _():
                copy(1, True, c).wait_send()

            return carry

        lax.fori_loop(0, pieces, one, 0)

    return greet, neighbours, enter, body, drain, pieces + lag * last


def line_sum_kernel(line, pieces, lag, p_ref, o_ref, right_in, left_in, send_sem, recv_sem):
    greet, neighbours, enter, body, drain, total = line_steps(
        line, pieces, lag, p_ref, o_ref, right_in, left_in, send_sem, recv_sem
    )
    greet()
    pl.semaphore_wait(pltpu.get_barrier_semaphore(), neighbours)
    enter()
    lax.fori_loop(0, total, body, 0)
    drain()


def line_scratch(rows, width, pieces):
    return [
        pltpu.VMEM((rows, width), BF),
        pltpu.VMEM((rows, width), BF),
        pltpu.SemaphoreType.DMA((2, pieces)),
        pltpu.SemaphoreType.DMA((2, pieces)),
    ]


def line_sum(part, line, height=32, lag=2):
    rows, width = part.shape
    pieces = rows // height
    return pl.pallas_call(
        functools.partial(line_sum_kernel, line, pieces, lag),
        out_shape=shape_of((rows, width), F32),
        in_specs=[pl.BlockSpec(memory_space=pltpu.VMEM)],
        out_specs=pl.BlockSpec(memory_space=pltpu.VMEM),
        scratch_shapes=line_scratch(rows, width, pieces),
        compiler_params=params(48, collective_id=1, has_side_effects=True),
        cost_estimate=cost(0, 260 * MIB),
        name="line_sum",
    )(part)


def line_swap_kernel(
    planes, line, pieces, lag, p_ref, rows_ref, o_ref, swapped_ref,
    right_in, left_in, send_sem, recv_sem, w_send, w_recv, own_sem,
):
    e = lax.axis_index("expert")
    greet, neighbours, enter, body, drain, total = line_steps(
        line, pieces, lag, p_ref, o_ref, right_in, left_in, send_sem, recv_sem
    )
    greet()
    barrier = pltpu.get_barrier_semaphore()
    for d in range(1, planes):
        pl.semaphore_signal(
            barrier, inc=1, device_id={"expert": lax.rem(e + d, planes)}, device_id_type=MESH
        )
    pl.semaphore_wait(barrier, neighbours + planes - 1)
    enter()
    swaps = []
    for d in range(1, planes):
        to = lax.rem(e + d, planes)
        swaps.append(pltpu.make_async_remote_copy(
            src_ref=rows_ref.at[to], dst_ref=swapped_ref.at[e],
            send_sem=w_send.at[d - 1], recv_sem=w_recv.at[d - 1],
            device_id={"expert": to}, device_id_type=MESH,
        ))
    own = pltpu.make_async_copy(rows_ref.at[e], swapped_ref.at[e], own_sem.at[0])
    for copy in swaps + [own]:
        copy.start()
    lax.fori_loop(0, total, body, 0)
    drain()
    for copy in swaps + [own]:
        copy.wait()


def line_swap(part, rows_sent, line, identity, height=32, lag=2):
    rows, width = part.shape
    planes = rows_sent.shape[0]
    pieces = rows // height
    sems = pltpu.SemaphoreType.DMA
    vmem, anywhere = pl.BlockSpec(memory_space=pltpu.VMEM), pl.BlockSpec(memory_space=pl.ANY)
    return pl.pallas_call(
        functools.partial(line_swap_kernel, planes, line, pieces, lag),
        out_shape=(shape_of((rows, width), F32), shape_of(rows_sent.shape, BF)),
        in_specs=[vmem, anywhere],
        out_specs=(vmem, anywhere),
        scratch_shapes=line_scratch(rows, width, pieces)
        + [sems((planes - 1,)), sems((planes - 1,)), sems((1,))],
        compiler_params=params(48, collective_id=identity, has_side_effects=True),
        cost_estimate=cost(0, 300 * MIB),
        name="line_swap",
    )(part, rows_sent)


def finish_kernel(
    planes, line, height, lag, p_ref, a_ref, b_ref, x_ref, gain_ref, slope_ref, gains_ref,
    o_ref, a_out, b_out, gains_out,
    right_in, left_in, a_own, a_half, a_in, a_sum, a_cols, b_own, b_half, b_in, b_sum, gain_part, gain_in, gain_own, gain_all,
    z_send, z_recv, h_send, h_recv, r_send, r_recv, s_send, s_recv, g_send, g_recv,
    w_send, w_recv, n_send, n_recv, m_send, m_recv, own_sem, slope_own,
):
    e, f = lax.axis_index("expert"), lax.axis_index("fsdp")
    chips, last = planes // 2, line - 1
    c, k = e // 2, e % 2
    mate = e + 1 - 2 * k
    barrier = pltpu.get_barrier_semaphore()

    def greet(**device):
        pl.semaphore_signal(barrier, inc=1, device_id=device, device_id_type=MESH)

    for d in range(1, planes):
        greet(expert=lax.rem(e + d, planes))
    for d in range(1, line):
        greet(fsdp=lax.rem(f + d, line))
    pl.semaphore_wait(barrier, planes - 1 + last)

    rows = p_ref.shape[0] // line
    pieces = rows // height

    def remote(source, target, send, recv, **device):
        return pltpu.make_async_remote_copy(
            src_ref=source, dst_ref=target, send_sem=send, recv_sem=recv,
            device_id=device, device_id_type=MESH,
        )

    to_mate = [
        remote(a_ref.at[:, :, 1 - k], a_half, h_send.at[0], h_recv.at[0], expert=mate),
        remote(b_ref.at[:, 1 - k], b_half, h_send.at[1], h_recv.at[1], expert=mate),
    ]
    own_half = [
        pltpu.make_async_copy(a_ref.at[:, :, k], a_own, own_sem.at[0]),
        pltpu.make_async_copy(b_ref.at[:, k], b_own, own_sem.at[1]),
    ]
    slope_load = pltpu.make_async_copy(
        slope_ref.at[pl.ds(pl.multiple_of(f * rows, rows), rows)], slope_own, own_sem.at[4]
    )
    for copy in to_mate + own_half + [slope_load]:
        copy.start()

    def place_of(side, s):
        target = last - s // pieces if side == 0 else s // pieces
        return target, pl.ds(pl.multiple_of(target * rows + lax.rem(s, pieces) * height, height), height)

    def copy_line(side, source, s):
        buffer = right_in if side == 0 else left_in
        place = place_of(side, s)[1]
        return remote(
            (p_ref if source else buffer).at[place], buffer.at[place],
            z_send.at[side, s], z_recv.at[side, s], fsdp=f + 1 if side == 0 else f - 1,
        )

    def first(side):
        def body(s, carry):
            copy_line(side, True, s).start()
            return carry

        lax.fori_loop(0, last * pieces, body, 0)

    @pl.when(f == 0)
    def _():
        first(0)

    @pl.when(f == last)
    def _():
        first(1)

    def arrive(side, s):
        buffer = right_in if side == 0 else left_in
        target, place = place_of(side, s)
        copy_line(side, False, s).wait_recv()

        @pl.when(target != f)
        def _():
            buffer[place, :] = (buffer[place, :].astype(F32) + p_ref[place, :].astype(F32)).astype(BF)
            copy_line(side, False, s).start()

    def body(s, carry):
        right = s - lag * f
        left = s - lag * (last - f)

        @pl.when((f > 0) & (right >= 0) & (right < (last - f + 1) * pieces))
        def _():
            arrive(0, right)

        @pl.when((f < last) & (left >= 0) & (left < (f + 1) * pieces))
        def _():
            arrive(1, left)

        return carry

    total = last * pieces + lag * last
    stops = [total // 8, total // 2, (total * 5) // 8]
    lax.fori_loop(0, stops[0], body, 0)

    for copy in own_half:
        copy.wait()
    for copy in to_mate:
        copy.wait_recv()

    def add_half(i, carry):
        for j in range(chips):
            a_own[i, j] = (a_own[i, j].astype(F32) + a_half[i, j].astype(F32)).astype(BF)
        return carry

    lax.fori_loop(0, line, add_half, 0)
    for j in range(chips):
        b_own[j] = (b_own[j].astype(F32) + b_half[j].astype(F32)).astype(BF)
    shares = []
    for d in range(1, chips):
        to = lax.rem(c + d, chips)
        shares.append(remote(
            a_own.at[:, to], a_in.at[d - 1], r_send.at[0, d - 1], r_recv.at[0, d - 1],
            expert=to * 2 + k,
        ))
        shares.append(remote(
            b_own.at[to], b_in.at[d - 1], r_send.at[1, d - 1], r_recv.at[1, d - 1],
            expert=to * 2 + k,
        ))
    for copy in shares:
        copy.start()
    lax.fori_loop(stops[0], stops[1], body, 0)

    for copy in shares:
        copy.wait_recv()

    def add_shares(i, carry):
        summed = a_own[i, c].astype(F32)
        for d in range(1, chips):
            summed = summed + a_in[d - 1, i].astype(F32)
        a_sum[i] = summed.astype(BF)
        return carry

    lax.fori_loop(0, line, add_shares, 0)
    summed = b_own[c].astype(F32)
    for d in range(1, chips):
        summed = summed + b_in[d - 1].astype(F32)
    b_sum[...] = summed.astype(BF)
    swaps = []
    for d in range(1, line):
        to = lax.rem(f + d, line)
        swaps.append(remote(
            a_sum.at[to], a_cols.at[f], s_send.at[d - 1], s_recv.at[d - 1], fsdp=to
        ))
    for copy in swaps:
        copy.start()
    a_cols[f] = a_sum[f]
    lax.fori_loop(stops[1], stops[2], body, 0)

    for copy in swaps:
        copy.wait_recv()
    spread = [[
        remote(a_cols, a_out.at[:, e], g_send.at[0, 0], g_recv.at[0, 0], expert=mate),
        remote(b_sum, b_out.at[e], g_send.at[1, 0], g_recv.at[1, 0], expert=mate),
    ]]
    for d in range(1, chips):
        to = lax.rem(c + d, chips) * 2 + k
        spread.append([
            remote(a_cols, a_out.at[:, e], g_send.at[0, d], g_recv.at[0, d], expert=to),
            remote(b_sum, b_out.at[e], g_send.at[1, d], g_recv.at[1, d], expert=to),
        ])
    own_out = [
        pltpu.make_async_copy(a_cols, a_out.at[:, e], own_sem.at[2]),
        pltpu.make_async_copy(b_sum, b_out.at[e], own_sem.at[3]),
    ]
    for copy in sum(spread, own_out):
        copy.start()
    lax.fori_loop(stops[2], total, body, 0)

    gain = gain_ref[...]
    width = gain.shape[1]
    gain_part[...] = jnp.zeros_like(gain_part)
    slope_load.wait()

    def tile(i, carry):
        place = pl.ds(pl.multiple_of(i * height, height), height)
        mine = pl.ds(pl.multiple_of(f * rows + i * height, height), height)
        right = jnp.where(f > 0, right_in[mine, :].astype(F32), 0.0)
        left = jnp.where(f < last, left_in[mine, :].astype(F32), 0.0)
        slope = p_ref[mine, :].astype(F32) + right + left
        x = x_ref[place, :].astype(F32)
        scale = lax.rsqrt(jnp.mean(x * x, axis=-1, keepdims=True) + EPSILON)
        gain_part[0:1, :] += jnp.sum(slope * x * scale, axis=0, keepdims=True)
        slope = slope * gain
        along = jnp.sum(slope * x, axis=-1, keepdims=True) / width
        part = scale * slope - x * (scale * scale * scale * along)
        o_ref[place, :] = (slope_own[place, :] + part).astype(BF)
        return carry

    lax.fori_loop(0, pieces, tile, 0)

    lanes = gains_ref.shape[1]

    def share_of(which):
        return gain_part.at[:, pl.ds(pl.multiple_of(which * lanes, lanes), lanes)]

    to_shards = []
    for d in range(1, line):
        to = lax.rem(f + d, line)
        to_shards.append(remote(
            share_of(to), gain_in.at[d - 1], n_send.at[d - 1], n_recv.at[d - 1], fsdp=to
        ))
    for copy in to_shards:
        copy.start()
    for copy in to_shards:
        copy.wait_recv()
    summed = share_of(f)[...] + gains_ref[...]
    for d in range(1, line):
        summed = summed + gain_in[d - 1]
    gain_own[...] = summed
    to_plane = []
    for d in range(1, planes):
        to_plane.append(remote(
            gain_own, gain_all.at[d - 1], m_send.at[d - 1], m_recv.at[d - 1],
            expert=lax.rem(e + d, planes),
        ))
    for copy in to_plane:
        copy.start()

    passed = []
    for d in range(1, chips):
        for copy in spread[d]:
            copy.wait_recv()
        source = lax.rem(c + chips - d, chips) * 2 + k
        pair = [
            remote(
                a_out.at[:, source], a_out.at[:, source], w_send.at[0, d - 1], w_recv.at[0, d - 1],
                expert=mate,
            ),
            remote(
                b_out.at[source], b_out.at[source], w_send.at[1, d - 1], w_recv.at[1, d - 1],
                expert=mate,
            ),
        ]
        for copy in pair:
            copy.start()
        passed += pair
    for copy in to_plane:
        copy.wait_recv()
    total_gain = gain_own[...]
    for d in range(1, planes):
        total_gain = total_gain + gain_all[d - 1]
    gains_out[...] = total_gain
    for copy in spread[0]:
        copy.wait_recv()
    for copy in passed + own_out:
        copy.wait()
    for copy in sum(spread, to_shards + to_plane):
        copy.wait_send()
    for copy in to_mate + shares + swaps:
        copy.wait_send()

    def drain(side, source, count):
        def one(s, carry):
            copy_line(side, source, s).wait_send()
            return carry

        lax.fori_loop(0, count, one, 0)

    @pl.when(f < last)
    def _():
        drain(0, True, (last - f) * pieces)

    @pl.when(f > 0)
    def _():
        drain(1, True, f * pieces)


def finish(part, a, b, block, gain, slope, gains, planes, line, height=32, lag=2):
    group, width = part.shape
    tokens = group // line
    chips, last = planes // 2, line - 1
    items = last * (tokens // height)
    rows, lanes = a.shape[2:]
    share = gains.shape[1]
    vmem = pl.BlockSpec(memory_space=pltpu.VMEM)
    anywhere = pl.BlockSpec(memory_space=pl.ANY)
    sems = pltpu.SemaphoreType.DMA
    return pl.pallas_call(
        functools.partial(finish_kernel, planes, line, height, lag),
        out_shape=(
            shape_of((tokens, width), BF), shape_of(a.shape, BF), shape_of(b.shape, BF),
            shape_of(gains.shape, F32),
        ),
        in_specs=[vmem, anywhere, anywhere, vmem, vmem, anywhere, vmem],
        out_specs=(vmem, anywhere, anywhere, vmem),
        scratch_shapes=[
            pltpu.VMEM((group, width), BF), pltpu.VMEM((group, width), BF),
            pltpu.VMEM((line, chips, rows, lanes), BF), pltpu.VMEM((line, chips, rows, lanes), BF),
            pltpu.VMEM((chips - 1, line, rows, lanes), BF),
            pltpu.VMEM((line, rows, lanes), BF), pltpu.VMEM((line, rows, lanes), BF),
            pltpu.VMEM((chips, rows, width), BF), pltpu.VMEM((chips, rows, width), BF),
            pltpu.VMEM((chips - 1, rows, width), BF), pltpu.VMEM((rows, width), BF),
            pltpu.VMEM((8, width), F32), pltpu.VMEM((last, 8, share), F32),
            pltpu.VMEM((8, share), F32), pltpu.VMEM((planes - 1, 8, share), F32),
            sems((2, items)), sems((2, items)), sems((2,)), sems((2,)),
            sems((2, chips - 1)), sems((2, chips - 1)), sems((last,)), sems((last,)),
            sems((2, chips)), sems((2, chips)), sems((2, chips - 1)), sems((2, chips - 1)),
            sems((last,)), sems((last,)), sems((planes - 1,)), sems((planes - 1,)),
            sems((5,)), pltpu.VMEM((tokens, width), F32),
        ],
        compiler_params=params(60, collective_id=2, has_side_effects=True),
        cost_estimate=cost(0, 400 * MIB),
        name="finish",
    )(
        part, a.reshape(line, chips, 2, rows, lanes), b.reshape(chips, 2, rows, width), block, gain,
        slope, gains,
    )


def swap_plane(rows):
    return lax.all_to_all(rows, "expert", split_axis=0, concat_axis=0, tiled=True)


def small_line_sum(array, line):
    total = array
    for d in range(1, line):
        total = total + lax.ppermute(array, "fsdp", [(i, (i + d) % line) for i in range(line)])
    return total


def as_row(column, second):
    lane = lax.broadcasted_iota(jnp.int32, (column.shape[0], 128), 1)
    return jnp.where(lane == 0, column, second).T[:2, :]


def as_column(row):
    return jnp.broadcast_to(row, (128, row.shape[1])).T


def project_kernel(x_ref, gain_ref, columns_ref, normed_ref, raw_ref, value_ref, squares_ref):
    x = x_ref[...].astype(F32)
    scale = lax.rsqrt(jnp.mean(x * x, axis=-1, keepdims=True) + EPSILON)
    normed = (x * scale * gain_ref[...]).astype(BF)
    normed_ref[...] = normed
    own = value_ref.shape[1]
    query = dot(normed, columns_ref[:, :own])
    key = dot(normed, columns_ref[:, own:2 * own])
    value_ref[...] = dot(normed, columns_ref[:, 2 * own:]).astype(BF)
    raw_ref[:, :own] = query
    raw_ref[:, own:] = key
    squares_ref[...] = as_row(
        jnp.sum(query * query, axis=-1, keepdims=True), jnp.sum(key * key, axis=-1, keepdims=True)
    )


def project(block, gain, columns, tile):
    group, width = block.shape
    own = columns.shape[1] // 3
    rows = lambda count: pl.BlockSpec((tile, count), lambda i: (i, 0))
    return pl.pallas_call(
        project_kernel,
        grid=(group // tile,),
        out_shape=(
            shape_of((group, width), BF), shape_of((group, 2 * own), F32),
            shape_of((group, own), BF), shape_of((2, group), F32),
        ),
        in_specs=[
            rows(width), pl.BlockSpec((1, width), lambda i: (0, 0)),
            pl.BlockSpec((width, 3 * own), lambda i: (0, 0)),
        ],
        out_specs=(rows(width), rows(2 * own), rows(own), pl.BlockSpec((2, tile), lambda i: (0, i))),
        compiler_params=params(48),
        cost_estimate=cost(6 * group * width * own, 14 * group * own),
        name="project",
    )(block, gain, columns)


def scales_of(squares_ref, width):
    scales = lax.rsqrt(squares_ref[...] / width + EPSILON)
    return [as_column(scales[i:i + 1, :]) for i in range(2)]


def turn_kernel(width, raw_ref, squares_ref, gain_ref, cos_ref, sin_ref, q_ref, k_ref):
    own = q_ref.shape[1]
    scales = scales_of(squares_ref, width)
    cosine, sine = cos_ref[...], sin_ref[...]
    for which, out in enumerate((q_ref, k_ref)):
        for j in range(0, own, 128):
            place = slice(which * own + j, which * own + j + 128)
            v = raw_ref[:, place] * scales[which] * gain_ref[:, place]
            out[:, j:j + 128] = (v * cosine + pltpu.roll(v, 64, 1) * sine).astype(BF)


def turn(raw, squares, gain, cosine, sine, width, tile):
    group, double = raw.shape
    own = double // 2
    rows = lambda count: pl.BlockSpec((tile, count), lambda i: (i, 0))
    return pl.pallas_call(
        functools.partial(turn_kernel, width),
        grid=(group // tile,),
        out_shape=(shape_of((group, own), BF),) * 2,
        in_specs=[
            rows(double), pl.BlockSpec((2, tile), lambda i: (0, i)),
            pl.BlockSpec((1, double), lambda i: (0, 0)), rows(128), rows(128),
        ],
        out_specs=(rows(own), rows(own)),
        compiler_params=params(32),
        cost_estimate=cost(20 * group * double, 8 * group * double),
        name="turn",
    )(raw, squares, gain, cosine, sine)


def turn_back_kernel(
    width, dq_ref, dk_ref, raw_ref, squares_ref, gain_ref, cos_ref, sin_ref, dots_ref, grad_ref
):
    own = dq_ref.shape[1]
    scales = scales_of(squares_ref, width)
    cosine, sine = cos_ref[...], sin_ref[...]

    @pl.when(pl.program_id(0) == 0)
    def _():
        grad_ref[...] = jnp.zeros_like(grad_ref)

    dots = []
    for which, slope in enumerate((dq_ref, dk_ref)):
        total = 0.0
        for j in range(0, own, 128):
            place = slice(which * own + j, which * own + j + 128)
            v = slope[:, j:j + 128].astype(F32)
            turned = (v * cosine - pltpu.roll(v, 64, 1) * sine) * raw_ref[:, place]
            total = total + jnp.sum(turned * gain_ref[:, place], axis=-1, keepdims=True)
            grad_ref[:, place] += jnp.sum(turned * scales[which], axis=0, keepdims=True)
        dots.append(total)
    dots_ref[...] = as_row(*dots)


def turn_back(dq, dk, raw, squares, gain, cosine, sine, width, tile):
    group, double = raw.shape
    own = double // 2
    rows = lambda count: pl.BlockSpec((tile, count), lambda i: (i, 0))
    pair = pl.BlockSpec((2, tile), lambda i: (0, i))
    flat = pl.BlockSpec((1, double), lambda i: (0, 0))
    return pl.pallas_call(
        functools.partial(turn_back_kernel, width),
        grid=(group // tile,),
        out_shape=(shape_of((2, group), F32), shape_of((1, double), F32)),
        in_specs=[rows(own), rows(own), rows(double), pair, flat, rows(128), rows(128)],
        out_specs=(pair, flat),
        compiler_params=params(32),
        cost_estimate=cost(20 * group * double, 8 * group * double),
        name="turn_back",
    )(dq, dk, raw, squares, gain, cosine, sine)


def join_kernel(
    width, dq_ref, dk_ref, dv_ref, raw_ref, squares_ref, dots_ref, gain_ref, cos_ref, sin_ref,
    columns_ref, joint_ref, part_ref,
):
    own = dq_ref.shape[1]
    scales = scales_of(squares_ref, width)
    dots = [as_column(dots_ref[i:i + 1, :]) for i in range(2)]
    cosine, sine = cos_ref[...], sin_ref[...]
    for which, slope in enumerate((dq_ref, dk_ref)):
        scale = scales[which]
        factor = scale * scale * scale * dots[which] / width
        for j in range(0, own, 128):
            place = slice(which * own + j, which * own + j + 128)
            v = slope[:, j:j + 128].astype(F32)
            turned = (v * cosine - pltpu.roll(v, 64, 1) * sine) * gain_ref[:, place]
            joint_ref[:, place] = (scale * turned - raw_ref[:, place] * factor).astype(BF)
    joint_ref[:, 2 * own:] = dv_ref[...]
    part_ref[...] = dot_nt(joint_ref[...], columns_ref[...]).astype(BF)


def join_slopes(dq, dk, dv, raw, squares, dots, gain, cosine, sine, columns, tile):
    group, double = raw.shape
    own = double // 2
    width = columns.shape[0]
    rows = lambda count: pl.BlockSpec((tile, count), lambda i: (i, 0))
    pair = pl.BlockSpec((2, tile), lambda i: (0, i))
    flat = pl.BlockSpec((1, double), lambda i: (0, 0))
    return pl.pallas_call(
        functools.partial(join_kernel, width),
        grid=(group // tile,),
        out_shape=(shape_of((group, 3 * own), BF), shape_of((group, width), BF)),
        in_specs=[
            rows(own), rows(own), rows(own), rows(double), pair, pair, flat, rows(128), rows(128),
            pl.BlockSpec((width, 3 * own), lambda i: (0, 0)),
        ],
        out_specs=(rows(3 * own), rows(width)),
        compiler_params=params(48),
        cost_estimate=cost(6 * group * width * own, 8 * group * width),
        name="join_slopes",
    )(dq, dk, dv, raw, squares, dots, gain, cosine, sine, columns)


def allowed_scores(queries, key_rows, start_ref, place_ref, key_place_ref, inv_root):
    scores = dot_nt(key_rows, queries) * (inv_root * LOG2E)
    key_place = key_place_ref[...]
    allowed = (key_place >= start_ref[...]) & (key_place <= place_ref[...])
    return jnp.where(allowed, scores, MASKED)


def attend_kernel(inv_root, q_ref, k_ref, v_ref, start_ref, place_ref, kp_ref, o_ref, log_ref):
    scores = allowed_scores(q_ref[...], k_ref[...], start_ref, place_ref, kp_ref, inv_root)
    highest = jnp.max(scores, axis=0, keepdims=True)
    powers = jnp.exp2(scores - highest)
    summed = jnp.sum(powers, axis=0, keepdims=True)
    blended = dot_tn(v_ref[...], powers.astype(BF)) / summed
    o_ref[...] = blended.T.astype(BF)
    log_ref[...] = (highest + jnp.log2(summed))[None]


def attend(query, key, value, start_row, place_row, place_column, heads, tile):
    group, own_width = query.shape
    size = own_width // heads
    kernel = functools.partial(attend_kernel, size ** (-0.5))
    whole = pl.BlockSpec((group, size), lambda h, i: (0, h))
    row = pl.BlockSpec((1, tile), lambda h, i: (0, i))
    return pl.pallas_call(
        kernel,
        grid=(heads, group // tile),
        out_shape=(shape_of((group, own_width), BF), shape_of((heads, 1, group), F32)),
        in_specs=[
            pl.BlockSpec((tile, size), lambda h, i: (i, h)), whole, whole, row, row,
            pl.BlockSpec((group, 1), lambda h, i: (0, 0)),
        ],
        out_specs=(
            pl.BlockSpec((tile, size), lambda h, i: (i, h)),
            pl.BlockSpec((1, 1, tile), lambda h, i: (h, 0, i)),
        ),
        compiler_params=params(48),
        cost_estimate=cost(4 * heads * group * group * size * 4, 8 * group * own_width),
        name="attend",
    )(query, key, value, start_row, place_row, place_column)


def attend_back_kernel(
    inv_root, q_ref, k_ref, v_ref, g_ref, log_ref, start_ref, place_ref, kp_ref,
    dq_ref, dk_ref, dv_ref, dk_sum, dv_sum,
):
    i = pl.program_id(1)
    queries, key_rows, slope = q_ref[...], k_ref[...], g_ref[...]
    scores = allowed_scores(queries, key_rows, start_ref, place_ref, kp_ref, inv_root)
    probability = jnp.exp2(scores - log_ref[0])
    prob_slope = dot_nt(v_ref[...], slope)
    product = probability * prob_slope
    row_dot = jnp.sum(product, axis=0, keepdims=True)
    score_slope = (product - probability * row_dot).astype(BF)
    dq_ref[...] = (dot_tn(key_rows, score_slope) * inv_root).T.astype(BF)
    key_part = dot(score_slope, queries) * inv_root
    value_part = dot(probability.astype(BF), slope)

    @pl.when(i == 0)
    def _():
        dk_sum[...] = key_part
        dv_sum[...] = value_part

    @pl.when(i > 0)
    def _():
        dk_sum[...] += key_part
        dv_sum[...] += value_part

    @pl.when(i == pl.num_programs(1) - 1)
    def _():
        dk_ref[...] = dk_sum[...].astype(BF)
        dv_ref[...] = dv_sum[...].astype(BF)


def attend_back(query, key, value, slope, log_total, start_row, place_row, place_column, heads, tile):
    group, own_width = query.shape
    size = own_width // heads
    whole = pl.BlockSpec((group, size), lambda h, i: (0, h))
    row = pl.BlockSpec((1, tile), lambda h, i: (0, i))
    tiled = pl.BlockSpec((tile, size), lambda h, i: (i, h))
    return pl.pallas_call(
        functools.partial(attend_back_kernel, size ** (-0.5)),
        grid=(heads, group // tile),
        out_shape=(shape_of((group, own_width), BF),) * 3,
        in_specs=[
            tiled, whole, whole, tiled, pl.BlockSpec((1, 1, tile), lambda h, i: (h, 0, i)),
            row, row, pl.BlockSpec((group, 1), lambda h, i: (0, 0)),
        ],
        out_specs=(tiled, whole, whole),
        scratch_shapes=[pltpu.VMEM((group, size), F32)] * 2,
        compiler_params=params(56),
        cost_estimate=cost(10 * heads * group * group * size * 3, 16 * group * own_width),
        name="attend_back",
    )(query, key, value, slope, log_total, start_row, place_row, place_column)


def hide_kernel(x_ref, attended_ref, gain_ref, kept_ref, hidden_ref, normed_ref):
    hidden = x_ref[...].astype(F32) + attended_ref[...]
    hidden_ref[...] = hidden
    scale = lax.rsqrt(jnp.mean(hidden * hidden, axis=-1, keepdims=True) + EPSILON)
    normed_ref[...] = (hidden * scale * gain_ref[...]).astype(BF)


def hide(block, attended, gain, offset, tile, kept):
    count, width = attended.shape
    rows = pl.BlockSpec((tile, width), lambda i: (i, 0))
    placed = pl.BlockSpec((tile, width), lambda i: (i + offset // tile, 0))
    return pl.pallas_call(
        hide_kernel,
        grid=(count // tile,),
        out_shape=(shape_of(block.shape, F32), shape_of((count, width), BF)),
        in_specs=[
            placed, rows, pl.BlockSpec((1, width), lambda i: (0, 0)),
            pl.BlockSpec(memory_space=pl.ANY),
        ],
        out_specs=(placed, rows),
        input_output_aliases={3: 0} if offset else {},
        compiler_params=params(48),
        cost_estimate=cost(8 * count * width, 12 * count * width),
        name="hide",
    )(block, attended, gain, kept)


def hide_back_kernel(
    slope_ref, hidden_ref, ca_ref, cb_ref, gain_ref, weight_ref, kept0, kept1, kept2,
    total_ref, low_ref, blend_ref, grad_ref,
):
    slope, hidden = slope_ref[...].astype(F32), hidden_ref[...]
    scale = lax.rsqrt(jnp.mean(hidden * hidden, axis=-1, keepdims=True) + EPSILON)
    part = jnp.sum(slope * hidden * scale, axis=0, keepdims=True)

    @pl.when(pl.program_id(0) == 0)
    def _():
        grad_ref[...] = part

    @pl.when(pl.program_id(0) > 0)
    def _():
        grad_ref[...] += part

    slope = slope * gain_ref[...]
    along = jnp.sum(slope * hidden, axis=-1, keepdims=True) / hidden.shape[1]
    incoming = jnp.concatenate([ca_ref[...], cb_ref[...]], axis=1).astype(F32)
    total = incoming + (
        scale * slope - hidden * (scale * scale * scale * along)
    )
    total_ref[...] = total
    low = total.astype(BF)
    low_ref[...] = low
    blend_ref[...] = dot_nt(low, weight_ref[...]).astype(BF)


def hide_back(slope, hidden, incoming, gain, weight, offset, tile, kept):
    count, width = slope.shape
    group = hidden.shape[0]
    own = weight.shape[0]
    flat = pl.BlockSpec((1, width), lambda i: (0, 0))

    def placed(size):
        return pl.BlockSpec((tile, size), lambda i: (i + offset // tile, 0))

    return pl.pallas_call(
        hide_back_kernel,
        grid=(count // tile,),
        out_shape=(
            shape_of((group, width), F32), shape_of((group, width), BF),
            shape_of((group, own), BF), shape_of((1, width), F32),
        ),
        in_specs=[
            pl.BlockSpec((tile, width), lambda i: (i, 0)), placed(width), placed(width // 2),
            placed(width // 2), flat, pl.BlockSpec((own, width), lambda i: (0, 0)),
        ]
        + [pl.BlockSpec(memory_space=pl.ANY)] * 3,
        out_specs=(placed(width), placed(width), placed(own), flat),
        input_output_aliases={6: 0, 7: 1, 8: 2} if offset else {},
        compiler_params=params(56),
        cost_estimate=cost(2 * count * width * own, 18 * count * width),
        name="hide_back",
    )(slope, hidden, *incoming, gain, weight, *kept)


def joint_grad_kernel(normed_ref, joint_ref, router_ref, o_ref):
    size = joint_ref.shape[1]
    o_ref[:, :size] = dot(normed_ref[...].T, joint_ref[...]).astype(BF)
    o_ref[:, size:] = router_ref[...]


def joint_grad(normed, joint, router):
    group, width = normed.shape
    size, extra = joint.shape[1], router.shape[1]
    tile = 512
    return pl.pallas_call(
        joint_grad_kernel,
        grid=(width // tile,),
        out_shape=shape_of((width, size + extra), BF),
        in_specs=[
            pl.BlockSpec((group, tile), lambda j: (0, j)),
            pl.BlockSpec((group, size), lambda j: (0, 0)),
            pl.BlockSpec((tile, extra), lambda j: (j, 0)),
        ],
        out_specs=pl.BlockSpec((tile, size + extra), lambda j: (j, 0)),
        compiler_params=params(56),
        cost_estimate=cost(2 * group * width * size, 6 * group * width),
        name="joint_grad",
    )(normed, joint, router)


def dispatch_kernel(slots, code_ref, rows_ref, o_ref, select):
    pairs = code_ref.shape[1]

    @pl.when(pl.program_id(1) == 0)
    def _():
        for i in range(pairs):
            row = code_ref[0, i:i + 1, :]
            slot = lax.broadcasted_iota(jnp.int32, (slots, row.shape[1]), 0).astype(F32)
            select[i * slots:(i + 1) * slots, :] = (slot == row).astype(BF)

    chosen = dot(select[...], rows_ref[...]).astype(BF)
    o_ref[...] = chosen.reshape(o_ref.shape)


def dispatch(codes, rows, planes, local, slots):
    chunks, pairs, count = codes.shape
    width = rows.shape[1]
    tile = 512
    return pl.pallas_call(
        functools.partial(dispatch_kernel, slots),
        grid=(chunks, width // tile),
        out_shape=shape_of((planes, local, chunks * slots, width), BF),
        in_specs=[
            pl.BlockSpec((1, pairs, count), lambda k, j: (k, 0, 0)),
            pl.BlockSpec((count, tile), lambda k, j: (k, j)),
        ],
        out_specs=pl.BlockSpec((planes, local, slots, tile), lambda k, j: (0, 0, k, j)),
        scratch_shapes=[pltpu.VMEM((pairs * slots, count), BF)],
        compiler_params=params(48),
        cost_estimate=cost(2 * pairs * slots * chunks * count * width, 4 * pairs * slots * width),
        name="dispatch",
    )(codes, rows)


def combine_kernel(slots, code_ref, rows_ref, o_ref, select):
    pairs = code_ref.shape[2]

    @pl.when(pl.program_id(1) == 0)
    def _():
        total = pairs * slots
        lane = lax.broadcasted_iota(jnp.int32, (pairs, total), 1)
        start = lax.broadcasted_iota(jnp.int32, (pairs, total), 0) * slots
        within = (lane >= start) & (lane < start + slots)
        spread = dot(code_ref[0], within.astype(BF))
        slot = jnp.sum(jnp.where(within, lane - start, 0), axis=0, keepdims=True)
        select[...] = (spread == slot.astype(F32)).astype(BF)

    rows = rows_ref[...].reshape(pairs * slots, rows_ref.shape[-1])
    o_ref[...] = dot(select[...], rows).astype(BF)


def combine(codes, rows, slots):
    planes, local, _, width = rows.shape
    chunks, count, pairs = codes.shape
    tile = 512
    return pl.pallas_call(
        functools.partial(combine_kernel, slots),
        grid=(chunks, width // tile),
        out_shape=shape_of((chunks * count, width), BF),
        in_specs=[
            pl.BlockSpec((1, count, pairs), lambda k, j: (k, 0, 0)),
            pl.BlockSpec((planes, local, slots, tile), lambda k, j: (0, 0, k, j)),
        ],
        out_specs=pl.BlockSpec((count, tile), lambda k, j: (k, j)),
        scratch_shapes=[pltpu.VMEM((count, pairs * slots), BF)],
        compiler_params=params(56),
        cost_estimate=cost(2 * pairs * slots * chunks * count * width, 4 * pairs * slots * width),
        name="combine",
    )(codes, rows)


def expert_kernel(
    halves, x_ref, ca_ref, cb_ref, gate_ref, up_ref, down_ref, router_ref, named_ref, kept_ref,
    weighted_ref, slope_ref, act_ref, gslope_ref, uslope_ref, logit_ref,
):
    width = x_ref.shape[-1]
    x = x_ref[...].reshape(-1, width)
    c = jnp.concatenate(
        [ref[...].reshape(-1, width // 2) for ref in (ca_ref, cb_ref)], axis=1
    ).astype(F32)
    router = router_ref[...]
    logits = dot(x, router)
    powers = jnp.exp(logits - jnp.max(logits, axis=-1, keepdims=True))
    chance = powers / jnp.sum(powers, axis=-1, keepdims=True)
    named = named_ref[0]
    gating = jnp.sum(chance * named, axis=-1, keepdims=True)
    joined = None
    kept = []
    for h in range(halves):
        gate_pre = dot(x, gate_ref[h])
        up_pre = dot(x, up_ref[h])
        squashed = jax.nn.sigmoid(gate_pre)
        swished = gate_pre * squashed
        activation = swished * up_pre
        act_ref[h] = (gating * activation).astype(BF)
        part = dot(activation.astype(BF), down_ref[h])
        joined = part if joined is None else joined + part
        kept.append((up_pre * squashed * (1.0 + gate_pre * (1.0 - squashed)), swished))
    gating_slope = jnp.sum(c * joined, axis=-1, keepdims=True)
    weighted_ref[...] = (gating * joined).astype(BF).reshape(weighted_ref.shape)
    unit_slope = (gating * c).astype(BF)
    logit_slope = (gating_slope * gating * (named - chance)).astype(BF)
    logit_ref[...] = logit_slope[None]
    slope = dot_nt(logit_slope, router)
    for h in range(halves):
        activation_slope = dot_nt(unit_slope, down_ref[h])
        gate_slope = (activation_slope * kept[h][0]).astype(BF)
        up_slope = (activation_slope * kept[h][1]).astype(BF)
        gslope_ref[h] = gate_slope
        uslope_ref[h] = up_slope
        slope = slope + dot_nt(gate_slope, gate_ref[h]) + dot_nt(up_slope, up_ref[h])
    slope_ref[...] = slope.astype(BF).reshape(slope_ref.shape)


def experts(x, cs, at, gates, ups, downs, router, named, halves, kept):
    planes, local, slots, width = x.shape
    hidden = gates.shape[-1]
    sources = max(1, 448 // slots)
    tile = sources * slots
    steps = planes // sources
    count = planes * slots
    expert_total = router.shape[1]
    units = local * halves
    row_spec = pl.BlockSpec((sources, 1, slots, width), lambda n, t: (t, n, 0, 0))
    half_spec = pl.BlockSpec((sources, 1, slots, width // 2), lambda n, t: (t, n, at, 0))
    unit_spec = pl.BlockSpec((halves, tile, hidden), lambda n, t: (n, t, 0))
    once = pl.Buffered(1)
    wide = pl.BlockSpec((halves, width, hidden), lambda n, t: (n, 0, 0), pipeline_mode=once)
    tall = pl.BlockSpec((halves, hidden, width), lambda n, t: (n, 0, 0), pipeline_mode=once)
    return pl.pallas_call(
        functools.partial(expert_kernel, halves),
        grid=(local, steps),
        out_shape=(
            shape_of((planes, local, CHUNKS * slots, width), BF), shape_of(x.shape, BF),
            shape_of((units, count, hidden), BF), shape_of((units, count, hidden), BF),
            shape_of((units, count, hidden), BF), shape_of((local, count, expert_total), BF),
        ),
        in_specs=[
            row_spec, half_spec, half_spec, wide, wide, tall,
            pl.BlockSpec((width, expert_total), lambda n, t: (0, 0)),
            pl.BlockSpec((1, 1, expert_total), lambda n, t: (n, 0, 0)),
            pl.BlockSpec(memory_space=pl.ANY),
        ],
        out_specs=(
            pl.BlockSpec((sources, 1, slots, width), lambda n, t: (t, n, at, 0)), row_spec, unit_spec, unit_spec, unit_spec,
            pl.BlockSpec((1, tile, expert_total), lambda n, t: (n, t, 0)),
        ),
        input_output_aliases={8: 0} if at else {},
        compiler_params=params(62),
        cost_estimate=cost(12 * units * count * hidden * width, 10 * local * count * width),
        name="experts",
    )(x, *cs, gates, ups, downs, router, named, kept)


def wide_grad_kernel(x0_ref, x1_ref, g0_ref, g1_ref, dg_ref):
    tile = x0_ref.shape[-1]
    dg_ref[0] = dot(x0_ref[...].reshape(-1, tile).T, g0_ref[0]) + dot(
        x1_ref[...].reshape(-1, tile).T, g1_ref[0]
    )


def wide_grad(xs, slopes, halves):
    planes, local, slots, width = xs[0].shape
    units, count, hidden = slopes[0].shape
    tile = 1024 if planes * slots <= 1024 else 512
    x_spec = pl.BlockSpec((planes, 1, slots, tile), lambda u, j: (0, u // halves, 0, j))
    s_spec = pl.BlockSpec((1, count, hidden), lambda u, j: (u, 0, 0))
    return pl.pallas_call(
        wide_grad_kernel,
        grid=(units, width // tile),
        out_shape=shape_of((units, width, hidden), F32),
        in_specs=[x_spec] * 2 + [s_spec] * 2,
        out_specs=pl.BlockSpec((1, tile, hidden), lambda u, j: (u, j, 0)),
        compiler_params=params(60),
        cost_estimate=cost(4 * units * count * hidden * width, 4 * units * hidden * width),
        name="wide_grad",
    )(*xs, *slopes)


def down_grad_kernel(a0_ref, a1_ref, ca_ref, cb_ref, d_ref):
    tile, slots = ca_ref.shape[-1], ca_ref.shape[2] // 2

    def part(c_ref):
        d_ref[0] = dot(a0_ref[0].T, c_ref[:, :, :slots].reshape(-1, tile)) + dot(
            a1_ref[0].T, c_ref[:, :, slots:].reshape(-1, tile)
        )

    first = pl.program_id(1) < pl.num_programs(1) // 2
    pl.when(first)(lambda: part(ca_ref))
    pl.when(jnp.logical_not(first))(lambda: part(cb_ref))


def down_grad(acts, cs, halves):
    planes, local, double, half = cs[0].shape
    units, count, hidden = acts[0].shape
    tile = half if planes * double <= 2048 else 512
    steps = half // tile
    a_spec = pl.BlockSpec((1, count, hidden), lambda u, j: (u, 0, 0))
    shape = (planes, 1, double, tile)
    return pl.pallas_call(
        down_grad_kernel,
        grid=(units, 2 * steps),
        out_shape=shape_of((units, hidden, 2 * half), F32),
        in_specs=[
            a_spec, a_spec,
            pl.BlockSpec(shape, lambda u, j: (0, u // halves, 0, jnp.minimum(j, steps - 1))),
            pl.BlockSpec(shape, lambda u, j: (0, u // halves, 0, jnp.maximum(j - steps, 0))),
        ],
        out_specs=pl.BlockSpec((1, hidden, tile), lambda u, j: (u, 0, j)),
        compiler_params=params(60),
        cost_estimate=cost(8 * units * count * hidden * half, 8 * units * hidden * half),
        name="down_grad",
    )(*acts, *cs)


def per_device(
    inputs,
    query_weight,
    key_weight,
    value_weight,
    output_weight,
    router_weight,
    first_gain,
    query_gain,
    key_gain,
    second_gain,
    gate_weight,
    up_weight,
    down_weight,
    routes,
    lengths,
    dealing,
    cotangent,
):
    planes, line = lax.axis_size("expert"), lax.axis_size("fsdp")
    plane_at, line_at = lax.axis_index("expert"), lax.axis_index("fsdp")
    tokens, width = inputs.shape
    group = line * tokens
    own_heads = HEADS // line
    head_size = width // HEADS
    own_width = own_heads * head_size
    weight_rows = query_weight.shape[0]
    slice_rows = weight_rows // planes
    units = gate_weight.shape[0]
    local = max(1, units // 2)
    halves = units // local
    expert_count = router_weight.shape[1]
    blocks = line // CHUNKS
    chunk_rows = blocks * tokens
    slots = blocks * CAP

    def own_slice(weight):
        return lax.dynamic_slice_in_dim(weight, plane_at * slice_rows, slice_rows, 0)

    sent = jnp.stack([own_slice(w) for w in (query_weight, key_weight, value_weight)], axis=1)
    sent = jnp.moveaxis(sent.reshape(slice_rows, 3, line, own_width), 2, 0)
    sent = sent.reshape(line, slice_rows, 3 * own_width)
    top_count = routes.shape[1]
    packed = [router_weight, first_gain, second_gain, routes.astype(BF)]
    sizes = [array.size for array in packed]
    fill = -sum(sizes) % (16 * 128)
    small = jnp.concatenate([array.reshape(-1) for array in packed] + [jnp.zeros((fill,), BF)])
    first_half, second_half = jnp.split(cotangent, 2, axis=1)
    block_in, first_half, small_all, columns, _ = gather_start(
        inputs, first_half, small.reshape(-1, 128), sent, planes, line
    )
    columns = columns.reshape(width, 3 * own_width)
    small_all = small_all.reshape(line, -1)
    ends = [sum(sizes[:i]) for i in range(5)]
    full_router, gain_first, gain_second, routes_all = (
        small_all[:, ends[i]:ends[i + 1]] for i in range(4)
    )
    full_router = full_router.reshape(width, expert_count)
    gain_first, gain_second = (g.reshape(width).astype(F32) for g in (gain_first, gain_second))
    routes_all = routes_all.reshape(line, tokens, top_count).astype(jnp.int32)
    second_half, _ = lax.optimization_barrier((second_half, block_in))
    incoming = [first_half, lax.all_gather(second_half, "fsdp", axis=0, tiled=True)]

    seq_start, positions = places(lengths[0], dealing)
    start_row, place_row, place_column = seq_start[None, :], dealing[None, :], dealing[:, None]
    cosine, sine = angles(positions, head_size)
    per_plane = expert_count // planes
    first_local = (line_at * units) // 2
    member = jnp.sum(
        (routes_all[..., None] == jnp.arange(expert_count, dtype=jnp.int32)).astype(F32), axis=2
    )
    earlier = jnp.tril(jnp.ones((tokens, tokens), BF), -1)
    rank = contract("ts,bse->bte", earlier, member.astype(BF))
    rank = rank + ((jnp.arange(line) % blocks) * CAP).astype(F32)[:, None, None]
    coded = jnp.where(member > 0, rank, -1.0).reshape(line, tokens, planes, per_plane)
    coded = lax.dynamic_slice_in_dim(coded, first_local, local, 3)
    coded = coded.reshape(CHUNKS, chunk_rows, planes * local)
    by_token = coded.astype(BF)
    by_pair = jnp.swapaxes(coded, 1, 2)

    def chunk(array, k):
        return lax.slice_in_dim(array, k * chunk_rows, (k + 1) * chunk_rows)

    rows = dispatch(by_pair, incoming[0], planes, local, slots)
    normed_low, raw, value_low, squares = project(block_in, gain_first[None], columns, tokens)
    squares = small_line_sum(squares, line)
    both_gains = jnp.concatenate([query_gain, key_gain])[None].astype(F32)
    rotary = (jnp.concatenate([cosine, cosine], -1), jnp.concatenate([-sine, sine], -1))
    query_low, key_low = turn(raw, squares, both_gains, *rotary, width, tokens)
    blended, log_total = attend(
        query_low, key_low, value_low, start_row, place_row, place_column, own_heads, tokens
    )
    attention_part = dot(blended, output_weight).astype(BF)

    named = (
        (((plane_at * line + line_at) * units) // 2 + jnp.arange(local))[:, None, None]
        == jnp.arange(expert_count)
    ).astype(F32)
    attention_parts = [chunk(attention_part, k) for k in range(CHUNKS)]
    arrived_slopes = [swap_plane(rows)]
    rows = dispatch(by_pair, incoming[1], planes, local, slots)
    attended, swapped = line_swap(attention_parts[0], rows, line, 4)
    arrived_slopes.append(swapped)
    hidden, arrived = block_in, []
    for k in range(CHUNKS):
        hidden, normed = hide(block_in, attended, gain_second[None], k * chunk_rows, tokens, hidden)
        rows = dispatch(by_pair[k:k + 1], normed, planes, local, slots)
        if k + 1 < CHUNKS:
            attended, swapped = line_swap(attention_parts[k + 1], rows, line, 3)
            arrived.append(swapped)
        else:
            rows, arrived_slopes[0] = lax.optimization_barrier((rows, arrived_slopes[0]))
            arrived.append(swap_plane(rows))
    weighted = arrived_slopes[0]
    row_slopes, acts, gslopes, uslopes, logit_slopes = [], [], [], [], []
    for k in range(CHUNKS):
        results = experts(
            arrived[k], arrived_slopes, k, gate_weight, up_weight, down_weight, full_router,
            named, halves, weighted,
        )
        weighted = results[0]
        for store, result in zip((row_slopes, acts, gslopes, uslopes, logit_slopes), results[1:]):
            store.append(result)
    returned = []
    behind = arrived[-1]
    for k in range(CHUNKS):
        rows, _ = lax.optimization_barrier((row_slopes[k], behind))
        behind = swap_plane(rows)
        returned.append(behind)

    second_gain_grad = 0.0
    kept = (block_in,) * 3
    for k in range(CHUNKS):
        returned[k], _ = lax.optimization_barrier((returned[k], summed if k else row_slopes[-1]))
        part = combine(by_token[k:k + 1], returned[k], slots)
        if k:
            rows, _ = lax.optimization_barrier((weighted, returned[k]))
            mixed_rows = swap_plane(rows)
        summed = line_sum(part, line)
        *kept, gain_part = hide_back(
            summed, hidden, incoming, gain_second[None], output_weight, k * chunk_rows, tokens, kept
        )
        second_gain_grad = second_gain_grad + gain_part
    hidden_slope, attention_slope, blended_slope = kept
    slopes = attend_back(
        query_low, key_low, value_low, blended_slope, log_total, start_row,
        place_row, place_column, own_heads, tokens,
    )
    dots, gain_grads = turn_back(*slopes[:2], raw, squares, both_gains, *rotary, width, tokens)
    dots = small_line_sum(dots, line)
    mixed_rows, _ = lax.optimization_barrier((mixed_rows, gain_grads))
    mixed = combine(by_token, mixed_rows, slots)
    acts, gslopes, uslopes, logit_slopes, attention_slope, _ = lax.optimization_barrier(
        (acts, gslopes, uslopes, logit_slopes, attention_slope, mixed)
    )
    mixed = lax.psum_scatter(mixed, "fsdp", scatter_dimension=0, tiled=True)
    expert_grads = [
        wide_grad(arrived, gslopes, halves),
        wide_grad(arrived, uslopes, halves),
        down_grad(acts, arrived_slopes, halves),
    ]
    router_grad = sum(
        contract(
            "ensd,nesq->dq", arrived[k],
            logit_slopes[k].reshape(local, planes, slots, expert_count),
        )
        for k in range(CHUNKS)
    )
    output_grad = contract("tc,td->cd", blended, attention_slope).astype(BF)
    dots, _ = lax.optimization_barrier((dots, expert_grads))
    joint, normed_part = join_slopes(
        *slopes, raw, squares, dots, both_gains, *rotary, columns, tokens
    )
    router_lanes = -expert_count % 128
    router_pad = jnp.pad(router_grad.astype(BF), ((0, 0), (0, router_lanes)))
    joint_total = joint_grad(normed_low, joint, router_pad)
    mine = line_at * weight_rows
    second_own = lax.dynamic_slice_in_dim(second_gain_grad, mine, weight_rows, 1)
    gain_rows = jnp.concatenate(
        [
            jnp.zeros((1, weight_rows), F32), second_own, gain_grads.reshape(2, own_width),
            jnp.zeros((4, weight_rows), F32),
        ]
    )
    input_gradient, totals, output_total, gain_totals = finish(
        normed_part, joint_total.reshape(line, planes, slice_rows, -1),
        output_grad.reshape(planes, slice_rows, width), inputs, gain_first[None],
        hidden_slope, gain_rows, planes, line,
    )
    hidden_own = lax.dynamic_slice_in_dim(hidden, line_at * tokens, tokens, 0)
    block_output = (hidden_own + mixed.astype(F32)).astype(BF)
    output_total = output_total.reshape(weight_rows, width).astype(F32)
    totals = totals.reshape(line, weight_rows, -1)
    weight_grads = [
        jnp.moveaxis(totals[:, :, i * own_width:(i + 1) * own_width], 0, 1)
        .reshape(weight_rows, width)
        .astype(F32)
        for i in range(3)
    ]
    router_total = jnp.sum(
        totals[:, :, 3 * own_width:3 * own_width + expert_count].astype(F32), axis=0
    )
    return (
        block_output,
        input_gradient,
        *weight_grads,
        output_total,
        router_total,
        gain_totals[0],
        gain_totals[2],
        gain_totals[3],
        gain_totals[1],
        *expert_grads,
    )


def solution(mesh):
    both = ("expert", "fsdp")
    rows, cube, shard, gain = P(both, None), P(both, None, None), P("fsdp", None), P("fsdp")
    return jax.shard_map(
        per_device,
        mesh=mesh,
        in_specs=(rows,)
        + (shard,) * 5
        + (gain,) * 4
        + (cube,) * 3
        + (rows, P("expert", None), P("expert"), rows),
        out_specs=(rows, rows) + (shard,) * 5 + (gain,) * 4 + (cube,) * 3,
        check_vma=False,
    )
```

```python
import functools

import jax
import jax.numpy as jnp
from jax import lax
from jax.experimental import pallas as pl
from jax.experimental.pallas import tpu as pltpu
from jax.sharding import PartitionSpec as P

HEADS = 16
CAP = 56
EPSILON = 1e-05
THETA = 10000.0
MASKED = -1e30
LOG2E = 1.4426950408889634
BF = jnp.bfloat16
F32 = jnp.float32
MESH = pl.DeviceIdType.MESH
MIB = 1 << 20
CHUNKS = 2


def dot(a, b):
    return jnp.dot(a, b, preferred_element_type=F32)


def dot_nt(a, b):
    return lax.dot_general(a, b, (((1,), (1,)), ((), ())), preferred_element_type=F32)


def dot_tn(a, b):
    return lax.dot_general(a, b, (((0,), (0,)), ((), ())), preferred_element_type=F32)


def contract(spec, *operands):
    return jnp.einsum(spec, *operands, preferred_element_type=F32)


def shape_of(dims, dtype):
    return jax.ShapeDtypeStruct(dims, dtype)


def cost(flops, moved):
    return pl.CostEstimate(flops=int(flops) // 64, bytes_accessed=int(moved) // 64, transcendentals=0)


def params(mib, **kwargs):
    return pltpu.CompilerParams(vmem_limit_bytes=mib * MIB, **kwargs)


def places(lengths_row, stream):
    seq_ends = jnp.cumsum(lengths_row)
    before = (seq_ends[None, :] <= stream[:, None]).astype(jnp.int32)
    offset = jnp.sum(before * lengths_row[None, :], axis=1)
    return offset, stream - offset


def angles(positions, head_width):
    exponent = jnp.arange(0, head_width, 2).astype(F32) / head_width
    phases = positions.astype(F32)[:, None] * (THETA ** (-exponent))[None, :]
    return jnp.cos(phases), jnp.sin(phases)


def gather_kernel(
    planes, line, pieces, x_ref, c_ref, small_ref, sent_ref,
    x_all, c_all, small_all, columns_ref, swapped_ref,
    x_send, x_recv, s_send, s_recv, z_send, z_recv, p_send, p_recv, own_sem,
):
    e, f = lax.axis_index("expert"), lax.axis_index("fsdp")
    barrier = pltpu.get_barrier_semaphore()
    for d in range(1, line):
        pl.semaphore_signal(
            barrier, inc=1, device_id={"fsdp": lax.rem(f + d, line)}, device_id_type=MESH
        )
    for d in range(1, planes):
        pl.semaphore_signal(
            barrier, inc=1, device_id={"expert": lax.rem(e + d, planes)}, device_id_type=MESH
        )
    pl.semaphore_wait(barrier, line + planes - 2)
    rows = x_ref.shape[0]
    part = rows // pieces
    small_rows = small_ref.shape[0]

    swaps, smalls = [], []
    for d in range(1, line):
        to = lax.rem(f + d, line)
        swaps.append(pltpu.make_async_remote_copy(
            src_ref=sent_ref.at[to], dst_ref=swapped_ref.at[f],
            send_sem=z_send.at[d - 1], recv_sem=z_recv.at[d - 1],
            device_id={"fsdp": to}, device_id_type=MESH,
        ))
        smalls.append(pltpu.make_async_remote_copy(
            src_ref=small_ref, dst_ref=small_all.at[pl.ds(f * small_rows, small_rows)],
            send_sem=s_send.at[d - 1], recv_sem=s_recv.at[d - 1],
            device_id={"fsdp": to}, device_id_type=MESH,
        ))
    for copy in swaps:
        copy.start()

    def hop(direction, step, c):
        own_ref, all_ref = (x_ref, x_all) if c < pieces else (c_ref, c_all)
        origin = f - direction * step
        place = pl.ds(origin * rows + c % pieces * part, part)
        cut = pl.ds(0, all_ref.shape[1])
        source = own_ref.at[pl.ds(c % pieces * part, part), cut] if step == 0 else all_ref.at[place]
        side = 0 if direction == 1 else 1
        return pltpu.make_async_remote_copy(
            src_ref=source, dst_ref=all_ref.at[place],
            send_sem=x_send.at[side, step, c], recv_sem=x_recv.at[side, step, c],
            device_id={"fsdp": f + direction}, device_id_type=MESH,
        )

    def sends(direction, step):
        origin, to = f - direction * step, f + direction
        return (origin >= 0) & (origin < line) & (to >= 0) & (to < line)

    def receives(direction, step):
        origin = f - direction * (step + 1)
        return (origin >= 0) & (origin < line)

    for direction in (1, -1):
        @pl.when(sends(direction, 0))
        def _(direction=direction):
            for c in range(2 * pieces):
                hop(direction, 0, c).start()

    for copy in smalls:
        copy.start()
    locals_ = [
        pltpu.make_async_copy(x_ref, x_all.at[pl.ds(f * rows, rows)], own_sem.at[0]),
        pltpu.make_async_copy(
            c_ref.at[:, pl.ds(0, c_all.shape[1])], c_all.at[pl.ds(f * rows, rows)], own_sem.at[4]
        ),
        pltpu.make_async_copy(
            small_ref, small_all.at[pl.ds(f * small_rows, small_rows)], own_sem.at[1]
        ),
        pltpu.make_async_copy(sent_ref.at[f], swapped_ref.at[f], own_sem.at[2]),
    ]
    for copy in locals_:
        copy.start()
    for copy in swaps:
        copy.wait_recv()
    locals_[3].wait()
    spread = []
    for d in range(1, planes):
        spread.append(pltpu.make_async_remote_copy(
            src_ref=swapped_ref, dst_ref=columns_ref.at[:, e],
            send_sem=p_send.at[d - 1], recv_sem=p_recv.at[d - 1],
            device_id={"expert": lax.rem(e + d, planes)}, device_id_type=MESH,
        ))
        spread[-1].start()
    own = pltpu.make_async_copy(swapped_ref, columns_ref.at[:, e], own_sem.at[3])
    own.start()

    for step in range(line - 1):
        for c in range(2 * pieces):
            for direction in (1, -1):
                @pl.when(receives(direction, step))
                def _(direction=direction, step=step, c=c):
                    origin = f - direction * (step + 1)
                    all_ref = x_all if c < pieces else c_all
                    place = pl.ds(origin * rows + c % pieces * part, part)
                    side = 0 if direction == 1 else 1
                    pltpu.make_async_remote_copy(
                        src_ref=all_ref.at[place], dst_ref=all_ref.at[place],
                        send_sem=x_send.at[side, step, c], recv_sem=x_recv.at[side, step, c],
                        device_id={"fsdp": f - direction}, device_id_type=MESH,
                    ).wait_recv()
                if step < line - 2:
                    @pl.when(sends(direction, step + 1))
                    def _(direction=direction, step=step, c=c):
                        hop(direction, step + 1, c).start()
    for step in range(line - 1):
        for direction in (1, -1):
            @pl.when(sends(direction, step))
            def _(direction=direction, step=step):
                for c in range(2 * pieces):
                    hop(direction, step, c).wait_send()
    for copy in swaps:
        copy.wait_send()
    for copy in smalls + spread:
        copy.wait()
    for copy in locals_[:3] + [own]:
        copy.wait()


def gather_start(block, half, small, sent, planes, line):
    rows, width = block.shape
    pieces = 4
    anywhere = pl.BlockSpec(memory_space=pl.ANY)
    sems = pltpu.SemaphoreType.DMA
    return pl.pallas_call(
        functools.partial(gather_kernel, planes, line, pieces),
        out_shape=(
            shape_of((line * rows, width), BF),
            shape_of((line * rows, half.shape[1] // 2), BF),
            shape_of((line * small.shape[0], small.shape[1]), BF),
            shape_of((line, planes) + sent.shape[1:], BF),
            shape_of(sent.shape, BF),
        ),
        in_specs=[anywhere] * 4,
        out_specs=[anywhere] * 5,
        scratch_shapes=[
            sems((2, line - 1, 2 * pieces)), sems((2, line - 1, 2 * pieces)),
            sems((line - 1,)), sems((line - 1,)), sems((line - 1,)), sems((line - 1,)),
            sems((planes - 1,)), sems((planes - 1,)), sems((5,)),
        ],
        compiler_params=pltpu.CompilerParams(collective_id=0, has_side_effects=True),
        name="gather_start",
    )(block, half, small, sent)


def line_steps(line, pieces, lag, p_ref, o_ref, right_in, left_in, send_sem, recv_sem):
    f = lax.axis_index("fsdp")
    last = line - 1
    part = p_ref.shape[0] // pieces

    def greet():
        barrier = pltpu.get_barrier_semaphore()

        @pl.when(f > 0)
        def _():
            pl.semaphore_signal(barrier, inc=1, device_id={"fsdp": f - 1}, device_id_type=MESH)

        @pl.when(f < last)
        def _():
            pl.semaphore_signal(barrier, inc=1, device_id={"fsdp": f + 1}, device_id_type=MESH)

    neighbours = jnp.where((f > 0) & (f < last), 2, 1)

    def copy(side, source, c):
        buffer = right_in if side == 0 else left_in
        place = pl.ds(c * part, part)
        return pltpu.make_async_remote_copy(
            src_ref=(p_ref if source else buffer).at[place], dst_ref=buffer.at[place],
            send_sem=send_sem.at[side, c], recv_sem=recv_sem.at[side, c],
            device_id={"fsdp": f + 1 if side == 0 else f - 1}, device_id_type=MESH,
        )

    def enter():
        for side in range(2):
            @pl.when(f == (0 if side == 0 else last))
            def _(side=side):
                def one(c, carry):
                    copy(side, True, c).start()
                    return carry

                lax.fori_loop(0, pieces, one, 0)

    def arrive(side, c):
        place = pl.ds(pl.multiple_of(c * part, part), part)
        buffer = right_in if side == 0 else left_in
        origin, end = (0, last) if side == 0 else (last, 0)
        leads = (2 * f <= last) if side == 0 else (2 * f > last)

        @pl.when(f == origin)
        def _():
            o_ref[place, :] = p_ref[place, :].astype(F32)

        @pl.when(f != origin)
        def _():
            copy(side, False, c).wait_recv()
            came = buffer[place, :].astype(F32)

            @pl.when(f != end)
            def _():
                buffer[place, :] = (came + p_ref[place, :].astype(F32)).astype(BF)
                copy(side, False, c).start()

            @pl.when(leads)
            def _():
                o_ref[place, :] = came + p_ref[place, :].astype(F32)

            @pl.when(jnp.logical_not(leads))
            def _():
                o_ref[place, :] += came

    def body(s, carry):
        for side in range(2):
            c = s - lag * (f if side == 0 else last - f)

            @pl.when((c >= 0) & (c < pieces))
            def _(side=side, c=c):
                arrive(side, c)

        return carry

    def drain():
        def one(c, carry):
            @pl.when(f < last)
            def _():
                copy(0, True, c).wait_send()

            @pl.when(f > 0)
            def _():
                copy(1, True, c).wait_send()

            return carry

        lax.fori_loop(0, pieces, one, 0)

    return greet, neighbours, enter, body, drain, pieces + lag * last


def line_sum_kernel(line, pieces, lag, p_ref, o_ref, right_in, left_in, send_sem, recv_sem):
    greet, neighbours, enter, body, drain, total = line_steps(
        line, pieces, lag, p_ref, o_ref, right_in, left_in, send_sem, recv_sem
    )
    greet()
    pl.semaphore_wait(pltpu.get_barrier_semaphore(), neighbours)
    enter()
    lax.fori_loop(0, total, body, 0)
    drain()


def line_scratch(rows, width, pieces):
    return [
        pltpu.VMEM((rows, width), BF),
        pltpu.VMEM((rows, width), BF),
        pltpu.SemaphoreType.DMA((2, pieces)),
        pltpu.SemaphoreType.DMA((2, pieces)),
    ]


def line_sum(part, line, height=32, lag=2):
    rows, width = part.shape
    pieces = rows // height
    return pl.pallas_call(
        functools.partial(line_sum_kernel, line, pieces, lag),
        out_shape=shape_of((rows, width), F32),
        in_specs=[pl.BlockSpec(memory_space=pltpu.VMEM)],
        out_specs=pl.BlockSpec(memory_space=pltpu.VMEM),
        scratch_shapes=line_scratch(rows, width, pieces),
        compiler_params=params(48, collective_id=1, has_side_effects=True),
        cost_estimate=cost(0, 260 * MIB),
        name="line_sum",
    )(part)


def line_swap_kernel(
    planes, line, pieces, lag, p_ref, rows_ref, o_ref, swapped_ref,
    right_in, left_in, send_sem, recv_sem, w_send, w_recv, own_sem,
):
    e = lax.axis_index("expert")
    greet, neighbours, enter, body, drain, total = line_steps(
        line, pieces, lag, p_ref, o_ref, right_in, left_in, send_sem, recv_sem
    )
    greet()
    barrier = pltpu.get_barrier_semaphore()
    for d in range(1, planes):
        pl.semaphore_signal(
            barrier, inc=1, device_id={"expert": lax.rem(e + d, planes)}, device_id_type=MESH
        )
    pl.semaphore_wait(barrier, neighbours + planes - 1)
    enter()
    swaps = []
    for d in range(1, planes):
        to = lax.rem(e + d, planes)
        swaps.append(pltpu.make_async_remote_copy(
            src_ref=rows_ref.at[to], dst_ref=swapped_ref.at[e],
            send_sem=w_send.at[d - 1], recv_sem=w_recv.at[d - 1],
            device_id={"expert": to}, device_id_type=MESH,
        ))
    own = pltpu.make_async_copy(rows_ref.at[e], swapped_ref.at[e], own_sem.at[0])
    for copy in swaps + [own]:
        copy.start()
    lax.fori_loop(0, total, body, 0)
    drain()
    for copy in swaps + [own]:
        copy.wait()


def line_swap(part, rows_sent, line, identity, height=32, lag=2):
    rows, width = part.shape
    planes = rows_sent.shape[0]
    pieces = rows // height
    sems = pltpu.SemaphoreType.DMA
    vmem, anywhere = pl.BlockSpec(memory_space=pltpu.VMEM), pl.BlockSpec(memory_space=pl.ANY)
    return pl.pallas_call(
        functools.partial(line_swap_kernel, planes, line, pieces, lag),
        out_shape=(shape_of((rows, width), F32), shape_of(rows_sent.shape, BF)),
        in_specs=[vmem, anywhere],
        out_specs=(vmem, anywhere),
        scratch_shapes=line_scratch(rows, width, pieces)
        + [sems((planes - 1,)), sems((planes - 1,)), sems((1,))],
        compiler_params=params(48, collective_id=identity, has_side_effects=True),
        cost_estimate=cost(0, 300 * MIB),
        name="line_swap",
    )(part, rows_sent)


def finish_kernel(
    planes, line, height, lag, p_ref, a_ref, b_ref, x_ref, gain_ref, slope_ref, gains_ref,
    o_ref, a_out, b_out, gains_out,
    right_in, left_in, a_own, a_half, a_in, a_sum, a_cols, b_own, b_half, b_in, b_sum, gain_part, gain_in, gain_own, gain_all,
    z_send, z_recv, h_send, h_recv, r_send, r_recv, s_send, s_recv, g_send, g_recv,
    w_send, w_recv, n_send, n_recv, m_send, m_recv, own_sem, slope_own,
):
    e, f = lax.axis_index("expert"), lax.axis_index("fsdp")
    chips, last = planes // 2, line - 1
    c, k = e // 2, e % 2
    mate = e + 1 - 2 * k
    barrier = pltpu.get_barrier_semaphore()

    def greet(**device):
        pl.semaphore_signal(barrier, inc=1, device_id=device, device_id_type=MESH)

    for d in range(1, planes):
        greet(expert=lax.rem(e + d, planes))
    for d in range(1, line):
        greet(fsdp=lax.rem(f + d, line))
    pl.semaphore_wait(barrier, planes - 1 + last)

    rows = p_ref.shape[0] // line
    pieces = rows // height
    ahead = 4

    def remote(source, target, send, recv, **device):
        return pltpu.make_async_remote_copy(
            src_ref=source, dst_ref=target, send_sem=send, recv_sem=recv,
            device_id=device, device_id_type=MESH,
        )

    lanes_a = a_ref.shape[-1]
    cut = lanes_a // 128 * 9 // 13 * 128
    spans = (pl.ds(0, cut), pl.ds(cut, lanes_a - cut))

    to_mate = [
        remote(
            a_ref.at[:, :, 1 - k, :, span], a_half.at[:, :, :, span], h_send.at[i], h_recv.at[i],
            expert=mate,
        )
        for i, span in enumerate(spans)
    ]
    to_mate.append(remote(b_ref.at[:, 1 - k], b_half, h_send.at[2], h_recv.at[2], expert=mate))
    own_half = [
        pltpu.make_async_copy(a_ref.at[:, :, k], a_own, own_sem.at[0]),
        pltpu.make_async_copy(b_ref.at[:, k], b_own, own_sem.at[1]),
    ]
    slope_load = pltpu.make_async_copy(
        slope_ref.at[pl.ds(pl.multiple_of(f * rows, rows), rows)], slope_own, own_sem.at[4]
    )
    for copy in to_mate + own_half + [slope_load]:
        copy.start()

    def place_of(side, s):
        target = last - s // pieces if side == 0 else s // pieces
        return target, pl.ds(pl.multiple_of(target * rows + lax.rem(s, pieces) * height, height), height)

    def copy_line(side, source, s):
        buffer = right_in if side == 0 else left_in
        place = place_of(side, s)[1]
        return remote(
            (p_ref if source else buffer).at[place], buffer.at[place],
            z_send.at[side, s], z_recv.at[side, s], fsdp=f + 1 if side == 0 else f - 1,
        )

    def begin(side, s):
        @pl.when(s >= ahead)
        def _():
            copy_line(side, True, s - ahead).wait_send()

        copy_line(side, True, s).start()

    def arrive(side, s):
        buffer = right_in if side == 0 else left_in
        target, place = place_of(side, s)
        copy_line(side, False, s).wait_recv()

        @pl.when(target != f)
        def _():
            buffer[place, :] = (buffer[place, :].astype(F32) + p_ref[place, :].astype(F32)).astype(BF)
            copy_line(side, False, s).start()

    def body(s, carry):
        right = s - lag * f
        left = s - lag * (last - f)

        @pl.when((f == 0) & (s < last * pieces))
        def _():
            begin(0, s)

        @pl.when((f == last) & (s < last * pieces))
        def _():
            begin(1, s)

        @pl.when((f > 0) & (right >= 0) & (right < (last - f + 1) * pieces))
        def _():
            arrive(0, right)

        @pl.when((f < last) & (left >= 0) & (left < (f + 1) * pieces))
        def _():
            arrive(1, left)

        return carry

    total = last * pieces + lag * last
    shares, swaps, spread = [], [], []
    sent = []

    def add_pairs():
        for copy in own_half:
            copy.wait()
        for copy in to_mate:
            copy.wait_recv()

        def one(i, carry):
            for j in range(chips):
                a_own[i, j] = (a_own[i, j].astype(F32) + a_half[i, j].astype(F32)).astype(BF)
            return carry

        lax.fori_loop(0, line, one, 0)
        for j in range(chips):
            b_own[j] = (b_own[j].astype(F32) + b_half[j].astype(F32)).astype(BF)

    def share(which):
        span = spans[which]
        mine = []
        for d in range(1, chips):
            to = lax.rem(c + d, chips)
            mine.append(remote(
                a_own.at[:, to, :, span], a_in.at[d - 1, :, :, span],
                r_send.at[which, d - 1], r_recv.at[which, d - 1], expert=to * 2 + k,
            ))
            if which:
                mine.append(remote(
                    b_own.at[to], b_in.at[d - 1], r_send.at[2, d - 1], r_recv.at[2, d - 1],
                    expert=to * 2 + k,
                ))
        for copy in mine:
            copy.start()
        shares.append(mine)

    def swap(which):
        span = spans[which]

        def one(i, carry):
            summed = a_own[i, c, :, span].astype(F32)
            for d in range(1, chips):
                summed = summed + a_in[d - 1, i, :, span].astype(F32)
            a_sum[i, :, span] = summed.astype(BF)
            return carry

        lax.fori_loop(0, line, one, 0)
        if which:
            summed = b_own[c].astype(F32)
            for d in range(1, chips):
                summed = summed + b_in[d - 1].astype(F32)
            b_sum[...] = summed.astype(BF)
        mine = []
        for d in range(1, line):
            to = lax.rem(f + d, line)
            mine.append(remote(
                a_sum.at[to, :, span], a_cols.at[f, :, span],
                s_send.at[which, d - 1], s_recv.at[which, d - 1], fsdp=to,
            ))
        for copy in mine:
            copy.start()
        a_cols[f, :, span] = a_sum[f, :, span]
        swaps.append(mine)

    def spread_out(which):
        span = spans[which]
        for copy in swaps[which]:
            copy.wait_recv()
        mine = []
        for d in range(chips):
            to = lax.rem(c + d, chips) * 2 + k if d else mate
            pair = [remote(
                a_cols.at[:, :, span], a_out.at[:, e, :, span],
                g_send.at[which, d], g_recv.at[which, d], expert=to,
            )]
            if which:
                pair.append(remote(
                    b_sum, b_out.at[e], g_send.at[2, d], g_recv.at[2, d], expert=to
                ))
            for copy in pair:
                copy.start()
            mine.append(pair)
        spread.append(mine)

    def pass_on(which):
        span = spans[which]
        for d in range(1, chips):
            for copy in spread[which][d]:
                copy.wait_recv()
            source = lax.rem(c + chips - d, chips) * 2 + k
            place = a_out.at[:, source, :, span]
            pair = [remote(
                place, place, w_send.at[which, d - 1], w_recv.at[which, d - 1], expert=mate
            )]
            if which:
                place = b_out.at[source]
                pair.append(remote(
                    place, place, w_send.at[2, d - 1], w_recv.at[2, d - 1], expert=mate
                ))
            for copy in pair:
                copy.start()
            sent.extend(pair)

    stops = [total // 10, total * 3 // 10, total // 2, total * 3 // 5, total * 3 // 4, total]
    lax.fori_loop(0, stops[0], body, 0)
    add_pairs()
    share(0)
    lax.fori_loop(stops[0], stops[1], body, 0)
    for copy in shares[0]:
        copy.wait_recv()
    share(1)
    swap(0)
    lax.fori_loop(stops[1], stops[2], body, 0)
    spread_out(0)
    lax.fori_loop(stops[2], stops[3], body, 0)
    for copy in shares[1]:
        copy.wait_recv()
    swap(1)
    lax.fori_loop(stops[3], stops[4], body, 0)
    spread_out(1)
    lax.fori_loop(stops[4], stops[5], body, 0)
    own_out = [
        pltpu.make_async_copy(a_cols, a_out.at[:, e], own_sem.at[2]),
        pltpu.make_async_copy(b_sum, b_out.at[e], own_sem.at[3]),
    ]
    for copy in own_out:
        copy.start()
    pass_on(0)

    gain = gain_ref[...]
    width = gain.shape[1]
    gain_part[...] = jnp.zeros_like(gain_part)
    slope_load.wait()

    def tile(i, carry):
        place = pl.ds(pl.multiple_of(i * height, height), height)
        mine = pl.ds(pl.multiple_of(f * rows + i * height, height), height)
        right = jnp.where(f > 0, right_in[mine, :].astype(F32), 0.0)
        left = jnp.where(f < last, left_in[mine, :].astype(F32), 0.0)
        slope = p_ref[mine, :].astype(F32) + right + left
        x = x_ref[place, :].astype(F32)
        scale = lax.rsqrt(jnp.mean(x * x, axis=-1, keepdims=True) + EPSILON)
        gain_part[0:1, :] += jnp.sum(slope * x * scale, axis=0, keepdims=True)
        slope = slope * gain
        along = jnp.sum(slope * x, axis=-1, keepdims=True) / width
        part = scale * slope - x * (scale * scale * scale * along)
        o_ref[place, :] = (slope_own[place, :] + part).astype(BF)
        return carry

    lax.fori_loop(0, pieces, tile, 0)

    lanes = gains_ref.shape[1]

    def share_of(which):
        return gain_part.at[:, pl.ds(pl.multiple_of(which * lanes, lanes), lanes)]

    to_shards = []
    for d in range(1, line):
        to = lax.rem(f + d, line)
        to_shards.append(remote(
            share_of(to), gain_in.at[d - 1], n_send.at[d - 1], n_recv.at[d - 1], fsdp=to
        ))
    for copy in to_shards:
        copy.start()
    for copy in to_shards:
        copy.wait_recv()
    summed = share_of(f)[...] + gains_ref[...]
    for d in range(1, line):
        summed = summed + gain_in[d - 1]
    gain_own[...] = summed
    to_plane = []
    for d in range(1, planes):
        to_plane.append(remote(
            gain_own, gain_all.at[d - 1], m_send.at[d - 1], m_recv.at[d - 1],
            expert=lax.rem(e + d, planes),
        ))
    for copy in to_plane:
        copy.start()

    pass_on(1)
    for copy in to_plane:
        copy.wait_recv()
    total_gain = gain_own[...]
    for d in range(1, planes):
        total_gain = total_gain + gain_all[d - 1]
    gains_out[...] = total_gain
    for mine in spread:
        for copy in mine[0]:
            copy.wait_recv()
    for copy in sent + own_out:
        copy.wait()
    for mine in spread:
        for copy in sum(mine, []):
            copy.wait_send()
    for copy in to_shards + to_plane + to_mate + sum(shares + swaps, []):
        copy.wait_send()

    def drain(side, start, stop):
        def one(s, carry):
            copy_line(side, True, s).wait_send()
            return carry

        lax.fori_loop(start, stop, one, 0)

    for side, origin in ((0, 0), (1, last)):
        count = ((last - f) if side == 0 else f) * pieces

        @pl.when(f == origin)
        def _(side=side):
            drain(side, last * pieces - ahead, last * pieces)

        @pl.when(f != origin)
        def _(side=side, count=count):
            drain(side, 0, count)


def finish(part, a, b, block, gain, slope, gains, planes, line, height=32, lag=2):
    group, width = part.shape
    tokens = group // line
    chips, last = planes // 2, line - 1
    items = last * (tokens // height)
    rows, lanes = a.shape[2:]
    share = gains.shape[1]
    vmem = pl.BlockSpec(memory_space=pltpu.VMEM)
    anywhere = pl.BlockSpec(memory_space=pl.ANY)
    sems = pltpu.SemaphoreType.DMA
    return pl.pallas_call(
        functools.partial(finish_kernel, planes, line, height, lag),
        out_shape=(
            shape_of((tokens, width), BF), shape_of(a.shape, BF), shape_of(b.shape, BF),
            shape_of(gains.shape, F32),
        ),
        in_specs=[vmem, anywhere, anywhere, vmem, vmem, anywhere, vmem],
        out_specs=(vmem, anywhere, anywhere, vmem),
        scratch_shapes=[
            pltpu.VMEM((group, width), BF), pltpu.VMEM((group, width), BF),
            pltpu.VMEM((line, chips, rows, lanes), BF), pltpu.VMEM((line, chips, rows, lanes), BF),
            pltpu.VMEM((chips - 1, line, rows, lanes), BF),
            pltpu.VMEM((line, rows, lanes), BF), pltpu.VMEM((line, rows, lanes), BF),
            pltpu.VMEM((chips, rows, width), BF), pltpu.VMEM((chips, rows, width), BF),
            pltpu.VMEM((chips - 1, rows, width), BF), pltpu.VMEM((rows, width), BF),
            pltpu.VMEM((8, width), F32), pltpu.VMEM((last, 8, share), F32),
            pltpu.VMEM((8, share), F32), pltpu.VMEM((planes - 1, 8, share), F32),
            sems((2, items)), sems((2, items)), sems((3,)), sems((3,)),
            sems((3, chips - 1)), sems((3, chips - 1)), sems((2, last)), sems((2, last)),
            sems((3, chips)), sems((3, chips)), sems((3, chips - 1)), sems((3, chips - 1)),
            sems((last,)), sems((last,)), sems((planes - 1,)), sems((planes - 1,)),
            sems((5,)), pltpu.VMEM((tokens, width), F32),
        ],
        compiler_params=params(60, collective_id=2, has_side_effects=True),
        cost_estimate=cost(0, 400 * MIB),
        name="finish",
    )(
        part, a.reshape(line, chips, 2, rows, lanes), b.reshape(chips, 2, rows, width), block, gain,
        slope, gains,
    )


def swap_plane(rows):
    return lax.all_to_all(rows, "expert", split_axis=0, concat_axis=0, tiled=True)


def small_line_sum(array, line):
    total = array
    for d in range(1, line):
        total = total + lax.ppermute(array, "fsdp", [(i, (i + d) % line) for i in range(line)])
    return total


def as_row(column, second):
    lane = lax.broadcasted_iota(jnp.int32, (column.shape[0], 128), 1)
    return jnp.where(lane == 0, column, second).T[:2, :]


def as_column(row):
    return jnp.broadcast_to(row, (128, row.shape[1])).T


def project_kernel(x_ref, gain_ref, columns_ref, normed_ref, raw_ref, value_ref, squares_ref):
    x = x_ref[...].astype(F32)
    scale = lax.rsqrt(jnp.mean(x * x, axis=-1, keepdims=True) + EPSILON)
    normed = (x * scale * gain_ref[...]).astype(BF)
    normed_ref[...] = normed
    own = value_ref.shape[1]
    query = dot(normed, columns_ref[:, :own])
    key = dot(normed, columns_ref[:, own:2 * own])
    value_ref[...] = dot(normed, columns_ref[:, 2 * own:]).astype(BF)
    raw_ref[:, :own] = query
    raw_ref[:, own:] = key
    squares_ref[...] = as_row(
        jnp.sum(query * query, axis=-1, keepdims=True), jnp.sum(key * key, axis=-1, keepdims=True)
    )


def project(block, gain, columns, tile):
    group, width = block.shape
    own = columns.shape[1] // 3
    rows = lambda count: pl.BlockSpec((tile, count), lambda i: (i, 0))
    return pl.pallas_call(
        project_kernel,
        grid=(group // tile,),
        out_shape=(
            shape_of((group, width), BF), shape_of((group, 2 * own), F32),
            shape_of((group, own), BF), shape_of((2, group), F32),
        ),
        in_specs=[
            rows(width), pl.BlockSpec((1, width), lambda i: (0, 0)),
            pl.BlockSpec((width, 3 * own), lambda i: (0, 0)),
        ],
        out_specs=(rows(width), rows(2 * own), rows(own), pl.BlockSpec((2, tile), lambda i: (0, i))),
        compiler_params=params(48),
        cost_estimate=cost(6 * group * width * own, 14 * group * own),
        name="project",
    )(block, gain, columns)


def scales_of(squares_ref, width):
    scales = lax.rsqrt(squares_ref[...] / width + EPSILON)
    return [as_column(scales[i:i + 1, :]) for i in range(2)]


def turn_kernel(width, raw_ref, squares_ref, gain_ref, cos_ref, sin_ref, q_ref, k_ref):
    own = q_ref.shape[1]
    scales = scales_of(squares_ref, width)
    cosine, sine = cos_ref[...], sin_ref[...]
    for which, out in enumerate((q_ref, k_ref)):
        for j in range(0, own, 128):
            place = slice(which * own + j, which * own + j + 128)
            v = raw_ref[:, place] * scales[which] * gain_ref[:, place]
            out[:, j:j + 128] = (v * cosine + pltpu.roll(v, 64, 1) * sine).astype(BF)


def turn(raw, squares, gain, cosine, sine, width, tile):
    group, double = raw.shape
    own = double // 2
    rows = lambda count: pl.BlockSpec((tile, count), lambda i: (i, 0))
    return pl.pallas_call(
        functools.partial(turn_kernel, width),
        grid=(group // tile,),
        out_shape=(shape_of((group, own), BF),) * 2,
        in_specs=[
            rows(double), pl.BlockSpec((2, tile), lambda i: (0, i)),
            pl.BlockSpec((1, double), lambda i: (0, 0)), rows(128), rows(128),
        ],
        out_specs=(rows(own), rows(own)),
        compiler_params=params(32),
        cost_estimate=cost(20 * group * double, 8 * group * double),
        name="turn",
    )(raw, squares, gain, cosine, sine)


def turn_back_kernel(
    width, dq_ref, dk_ref, raw_ref, squares_ref, gain_ref, cos_ref, sin_ref, dots_ref, grad_ref
):
    own = dq_ref.shape[1]
    scales = scales_of(squares_ref, width)
    cosine, sine = cos_ref[...], sin_ref[...]

    @pl.when(pl.program_id(0) == 0)
    def _():
        grad_ref[...] = jnp.zeros_like(grad_ref)

    dots = []
    for which, slope in enumerate((dq_ref, dk_ref)):
        total = 0.0
        for j in range(0, own, 128):
            place = slice(which * own + j, which * own + j + 128)
            v = slope[:, j:j + 128].astype(F32)
            turned = (v * cosine - pltpu.roll(v, 64, 1) * sine) * raw_ref[:, place]
            total = total + jnp.sum(turned * gain_ref[:, place], axis=-1, keepdims=True)
            grad_ref[:, place] += jnp.sum(turned * scales[which], axis=0, keepdims=True)
        dots.append(total)
    dots_ref[...] = as_row(*dots)


def turn_back(dq, dk, raw, squares, gain, cosine, sine, width, tile):
    group, double = raw.shape
    own = double // 2
    rows = lambda count: pl.BlockSpec((tile, count), lambda i: (i, 0))
    pair = pl.BlockSpec((2, tile), lambda i: (0, i))
    flat = pl.BlockSpec((1, double), lambda i: (0, 0))
    return pl.pallas_call(
        functools.partial(turn_back_kernel, width),
        grid=(group // tile,),
        out_shape=(shape_of((2, group), F32), shape_of((1, double), F32)),
        in_specs=[rows(own), rows(own), rows(double), pair, flat, rows(128), rows(128)],
        out_specs=(pair, flat),
        compiler_params=params(32),
        cost_estimate=cost(20 * group * double, 8 * group * double),
        name="turn_back",
    )(dq, dk, raw, squares, gain, cosine, sine)


def join_kernel(
    width, dq_ref, dk_ref, dv_ref, raw_ref, squares_ref, dots_ref, gain_ref, cos_ref, sin_ref,
    columns_ref, joint_ref, part_ref,
):
    own = dq_ref.shape[1]
    scales = scales_of(squares_ref, width)
    dots = [as_column(dots_ref[i:i + 1, :]) for i in range(2)]
    cosine, sine = cos_ref[...], sin_ref[...]
    for which, slope in enumerate((dq_ref, dk_ref)):
        scale = scales[which]
        factor = scale * scale * scale * dots[which] / width
        for j in range(0, own, 128):
            place = slice(which * own + j, which * own + j + 128)
            v = slope[:, j:j + 128].astype(F32)
            turned = (v * cosine - pltpu.roll(v, 64, 1) * sine) * gain_ref[:, place]
            joint_ref[:, place] = (scale * turned - raw_ref[:, place] * factor).astype(BF)
    joint_ref[:, 2 * own:] = dv_ref[...]
    part_ref[...] = dot_nt(joint_ref[...], columns_ref[...]).astype(BF)


def join_slopes(dq, dk, dv, raw, squares, dots, gain, cosine, sine, columns, tile):
    group, double = raw.shape
    own = double // 2
    width = columns.shape[0]
    rows = lambda count: pl.BlockSpec((tile, count), lambda i: (i, 0))
    pair = pl.BlockSpec((2, tile), lambda i: (0, i))
    flat = pl.BlockSpec((1, double), lambda i: (0, 0))
    return pl.pallas_call(
        functools.partial(join_kernel, width),
        grid=(group // tile,),
        out_shape=(shape_of((group, 3 * own), BF), shape_of((group, width), BF)),
        in_specs=[
            rows(own), rows(own), rows(own), rows(double), pair, pair, flat, rows(128), rows(128),
            pl.BlockSpec((width, 3 * own), lambda i: (0, 0)),
        ],
        out_specs=(rows(3 * own), rows(width)),
        compiler_params=params(48),
        cost_estimate=cost(6 * group * width * own, 8 * group * width),
        name="join_slopes",
    )(dq, dk, dv, raw, squares, dots, gain, cosine, sine, columns)


def allowed_scores(queries, key_rows, start_ref, place_ref, key_place_ref, inv_root):
    scores = dot_nt(key_rows, queries) * (inv_root * LOG2E)
    key_place = key_place_ref[...]
    allowed = (key_place >= start_ref[...]) & (key_place <= place_ref[...])
    return jnp.where(allowed, scores, MASKED)


def attend_kernel(size, q_ref, k_ref, v_ref, start_ref, place_ref, kp_ref, o_ref, log_ref):
    for j in range(q_ref.shape[1] // size):
        at = slice(j * size, (j + 1) * size)
        scores = allowed_scores(
            q_ref[:, at], k_ref[:, at], start_ref, place_ref, kp_ref, size ** (-0.5)
        )
        highest = jnp.max(scores, axis=0, keepdims=True)
        powers = jnp.exp2(scores - highest)
        summed = jnp.sum(powers, axis=0, keepdims=True)
        blended = dot_tn(v_ref[:, at], powers.astype(BF)) / summed
        o_ref[:, at] = blended.T.astype(BF)
        log_ref[j] = highest + jnp.log2(summed)


def attend(query, key, value, start_row, place_row, place_column, heads, tile, together=2):
    group, own_width = query.shape
    size = own_width // heads
    wide = together * size
    whole = pl.BlockSpec((group, wide), lambda h, i: (0, h))
    row = pl.BlockSpec((1, tile), lambda h, i: (0, i))
    return pl.pallas_call(
        functools.partial(attend_kernel, size),
        grid=(heads // together, group // tile),
        out_shape=(shape_of((group, own_width), BF), shape_of((heads, 1, group), F32)),
        in_specs=[
            pl.BlockSpec((tile, wide), lambda h, i: (i, h)), whole, whole, row, row,
            pl.BlockSpec((group, 1), lambda h, i: (0, 0)),
        ],
        out_specs=(
            pl.BlockSpec((tile, wide), lambda h, i: (i, h)),
            pl.BlockSpec((together, 1, tile), lambda h, i: (h, 0, i)),
        ),
        compiler_params=params(58),
        cost_estimate=cost(4 * heads * group * group * size * 4, 8 * group * own_width),
        name="attend",
    )(query, key, value, start_row, place_row, place_column)


def attend_back_kernel(
    size, q_ref, k_ref, v_ref, g_ref, log_ref, start_ref, place_ref, kp_ref,
    dq_ref, dk_ref, dv_ref, dk_sum, dv_sum,
):
    i = pl.program_id(1)
    inv_root = size ** (-0.5)

    @pl.when(i == 0)
    def _():
        dk_sum[...] = jnp.zeros_like(dk_sum)
        dv_sum[...] = jnp.zeros_like(dv_sum)

    for j in range(q_ref.shape[1] // size):
        at = slice(j * size, (j + 1) * size)
        queries, key_rows, slope = q_ref[:, at], k_ref[:, at], g_ref[:, at]
        scores = allowed_scores(queries, key_rows, start_ref, place_ref, kp_ref, inv_root)
        probability = jnp.exp2(scores - log_ref[j])
        prob_slope = dot_nt(v_ref[:, at], slope)
        product = probability * prob_slope
        row_dot = jnp.sum(product, axis=0, keepdims=True)
        score_slope = (product - probability * row_dot).astype(BF)
        dq_ref[:, at] = (dot_tn(key_rows, score_slope) * inv_root).T.astype(BF)
        dk_sum[:, at] += dot(score_slope, queries) * inv_root
        dv_sum[:, at] += dot(probability.astype(BF), slope)

    @pl.when(i == pl.num_programs(1) - 1)
    def _():
        dk_ref[...] = dk_sum[...].astype(BF)
        dv_ref[...] = dv_sum[...].astype(BF)


def attend_back(
    query, key, value, slope, log_total, start_row, place_row, place_column, heads, tile, together=2
):
    group, own_width = query.shape
    size = own_width // heads
    wide = together * size
    whole = pl.BlockSpec((group, wide), lambda h, i: (0, h))
    row = pl.BlockSpec((1, tile), lambda h, i: (0, i))
    tiled = pl.BlockSpec((tile, wide), lambda h, i: (i, h))
    return pl.pallas_call(
        functools.partial(attend_back_kernel, size),
        grid=(heads // together, group // tile),
        out_shape=(shape_of((group, own_width), BF),) * 3,
        in_specs=[
            tiled, whole, whole, tiled, pl.BlockSpec((together, 1, tile), lambda h, i: (h, 0, i)),
            row, row, pl.BlockSpec((group, 1), lambda h, i: (0, 0)),
        ],
        out_specs=(tiled, whole, whole),
        scratch_shapes=[pltpu.VMEM((group, wide), F32)] * 2,
        compiler_params=params(60),
        cost_estimate=cost(10 * heads * group * group * size * 3, 16 * group * own_width),
        name="attend_back",
    )(query, key, value, slope, log_total, start_row, place_row, place_column)


def hide_kernel(x_ref, attended_ref, gain_ref, kept_ref, hidden_ref, normed_ref):
    hidden = x_ref[...].astype(F32) + attended_ref[...]
    hidden_ref[...] = hidden
    scale = lax.rsqrt(jnp.mean(hidden * hidden, axis=-1, keepdims=True) + EPSILON)
    normed_ref[...] = (hidden * scale * gain_ref[...]).astype(BF)


def hide(block, attended, gain, offset, tile, kept):
    count, width = attended.shape
    rows = pl.BlockSpec((tile, width), lambda i: (i, 0))
    placed = pl.BlockSpec((tile, width), lambda i: (i + offset // tile, 0))
    return pl.pallas_call(
        hide_kernel,
        grid=(count // tile,),
        out_shape=(shape_of(block.shape, F32), shape_of((count, width), BF)),
        in_specs=[
            placed, rows, pl.BlockSpec((1, width), lambda i: (0, 0)),
            pl.BlockSpec(memory_space=pl.ANY),
        ],
        out_specs=(placed, rows),
        input_output_aliases={3: 0} if offset else {},
        compiler_params=params(48),
        cost_estimate=cost(8 * count * width, 12 * count * width),
        name="hide",
    )(block, attended, gain, kept)


def hide_back_kernel(
    slope_ref, hidden_ref, ca_ref, cb_ref, gain_ref, weight_ref, kept0, kept1, kept2,
    total_ref, low_ref, blend_ref, grad_ref,
):
    slope, hidden = slope_ref[...].astype(F32), hidden_ref[...]
    scale = lax.rsqrt(jnp.mean(hidden * hidden, axis=-1, keepdims=True) + EPSILON)
    part = jnp.sum(slope * hidden * scale, axis=0, keepdims=True)

    @pl.when(pl.program_id(0) == 0)
    def _():
        grad_ref[...] = part

    @pl.when(pl.program_id(0) > 0)
    def _():
        grad_ref[...] += part

    slope = slope * gain_ref[...]
    along = jnp.sum(slope * hidden, axis=-1, keepdims=True) / hidden.shape[1]
    incoming = jnp.concatenate([ca_ref[...], cb_ref[...]], axis=1).astype(F32)
    total = incoming + (
        scale * slope - hidden * (scale * scale * scale * along)
    )
    total_ref[...] = total
    low = total.astype(BF)
    low_ref[...] = low
    blend_ref[...] = dot_nt(low, weight_ref[...]).astype(BF)


def hide_back(slope, hidden, incoming, gain, weight, offset, tile, kept):
    count, width = slope.shape
    group = hidden.shape[0]
    own = weight.shape[0]
    flat = pl.BlockSpec((1, width), lambda i: (0, 0))

    def placed(size):
        return pl.BlockSpec((tile, size), lambda i: (i + offset // tile, 0))

    return pl.pallas_call(
        hide_back_kernel,
        grid=(count // tile,),
        out_shape=(
            shape_of((group, width), F32), shape_of((group, width), BF),
            shape_of((group, own), BF), shape_of((1, width), F32),
        ),
        in_specs=[
            pl.BlockSpec((tile, width), lambda i: (i, 0)), placed(width), placed(width // 2),
            placed(width // 2), flat, pl.BlockSpec((own, width), lambda i: (0, 0)),
        ]
        + [pl.BlockSpec(memory_space=pl.ANY)] * 3,
        out_specs=(placed(width), placed(width), placed(own), flat),
        input_output_aliases={6: 0, 7: 1, 8: 2} if offset else {},
        compiler_params=params(56),
        cost_estimate=cost(2 * count * width * own, 18 * count * width),
        name="hide_back",
    )(slope, hidden, *incoming, gain, weight, *kept)


def widen_kernel(own, a_ref, b_ref, query_ref, key_ref, value_ref, out_ref, router_ref):
    line, _, _, rows, _ = a_ref.shape
    for f in range(line):
        for which, o_ref in enumerate((query_ref, key_ref, value_ref)):
            o_ref[:, f * own:(f + 1) * own] = a_ref[
                f, 0, 0, :, which * own:(which + 1) * own
            ].astype(F32)
    out_ref[...] = b_ref[0, 0].astype(F32)
    routing = a_ref[0, 0, 0, :, 3 * own:].astype(F32)
    for f in range(1, line):
        routing = routing + a_ref[f, 0, 0, :, 3 * own:].astype(F32)
    router_ref[...] = routing


def widen(a, b, own):
    line, chips, _, rows, lanes = a.shape
    width = b.shape[-1]
    extra = lanes - 3 * own
    count = 2 * chips * rows
    full, part = shape_of((count, width), F32), shape_of((count, extra), F32)
    wide = pl.BlockSpec((rows, width), lambda i: (i, 0))
    return pl.pallas_call(
        functools.partial(widen_kernel, own),
        grid=(2 * chips,),
        out_shape=(full,) * 4 + (part,),
        in_specs=[
            pl.BlockSpec((line, 1, 1, rows, lanes), lambda i: (0, i // 2, i % 2, 0, 0)),
            pl.BlockSpec((1, 1, rows, width), lambda i: (i // 2, i % 2, 0, 0)),
        ],
        out_specs=(wide,) * 4 + (pl.BlockSpec((rows, extra), lambda i: (i, 0)),),
        compiler_params=params(32),
        cost_estimate=cost(8 * count * width, 24 * count * width),
        name="widen",
    )(a, b)


def joint_grad_kernel(normed_ref, joint_ref, router_ref, o_ref):
    size = joint_ref.shape[1]
    o_ref[:, :size] = dot(normed_ref[...].T, joint_ref[...]).astype(BF)
    o_ref[:, size:] = router_ref[...]


def joint_grad(normed, joint, router):
    group, width = normed.shape
    size, extra = joint.shape[1], router.shape[1]
    tile = 512
    return pl.pallas_call(
        joint_grad_kernel,
        grid=(width // tile,),
        out_shape=shape_of((width, size + extra), BF),
        in_specs=[
            pl.BlockSpec((group, tile), lambda j: (0, j)),
            pl.BlockSpec((group, size), lambda j: (0, 0)),
            pl.BlockSpec((tile, extra), lambda j: (j, 0)),
        ],
        out_specs=pl.BlockSpec((tile, size + extra), lambda j: (j, 0)),
        compiler_params=params(56),
        cost_estimate=cost(2 * group * width * size, 6 * group * width),
        name="joint_grad",
    )(normed, joint, router)


def dispatch_kernel(slots, code_ref, rows_ref, o_ref, select):
    pairs = code_ref.shape[1]

    @pl.when(pl.program_id(1) == 0)
    def _():
        for i in range(pairs):
            row = code_ref[0, i:i + 1, :]
            slot = lax.broadcasted_iota(jnp.int32, (slots, row.shape[1]), 0).astype(F32)
            select[i * slots:(i + 1) * slots, :] = (slot == row).astype(BF)

    chosen = dot(select[...], rows_ref[...]).astype(BF)
    o_ref[...] = chosen.reshape(o_ref.shape)


def dispatch(codes, rows, planes, local, slots):
    chunks, pairs, count = codes.shape
    width = rows.shape[1]
    tile = 512
    return pl.pallas_call(
        functools.partial(dispatch_kernel, slots),
        grid=(chunks, width // tile),
        out_shape=shape_of((planes, local, chunks * slots, width), BF),
        in_specs=[
            pl.BlockSpec((1, pairs, count), lambda k, j: (k, 0, 0)),
            pl.BlockSpec((count, tile), lambda k, j: (k, j)),
        ],
        out_specs=pl.BlockSpec((planes, local, slots, tile), lambda k, j: (0, 0, k, j)),
        scratch_shapes=[pltpu.VMEM((pairs * slots, count), BF)],
        compiler_params=params(48),
        cost_estimate=cost(2 * pairs * slots * chunks * count * width, 4 * pairs * slots * width),
        name="dispatch",
    )(codes, rows)


def combine_kernel(slots, code_ref, rows_ref, o_ref, select):
    pairs = code_ref.shape[2]

    @pl.when(pl.program_id(1) == 0)
    def _():
        total = pairs * slots
        lane = lax.broadcasted_iota(jnp.int32, (pairs, total), 1)
        start = lax.broadcasted_iota(jnp.int32, (pairs, total), 0) * slots
        within = (lane >= start) & (lane < start + slots)
        spread = dot(code_ref[0], within.astype(BF))
        slot = jnp.sum(jnp.where(within, lane - start, 0), axis=0, keepdims=True)
        select[...] = (spread == slot.astype(F32)).astype(BF)

    rows = rows_ref[...].reshape(pairs * slots, rows_ref.shape[-1])
    o_ref[...] = dot(select[...], rows).astype(BF)


def combine(codes, rows, slots):
    planes, local, _, width = rows.shape
    chunks, count, pairs = codes.shape
    tile = 512
    return pl.pallas_call(
        functools.partial(combine_kernel, slots),
        grid=(chunks, width // tile),
        out_shape=shape_of((chunks * count, width), BF),
        in_specs=[
            pl.BlockSpec((1, count, pairs), lambda k, j: (k, 0, 0)),
            pl.BlockSpec((planes, local, slots, tile), lambda k, j: (0, 0, k, j)),
        ],
        out_specs=pl.BlockSpec((count, tile), lambda k, j: (k, j)),
        scratch_shapes=[pltpu.VMEM((count, pairs * slots), BF)],
        compiler_params=params(56),
        cost_estimate=cost(2 * pairs * slots * chunks * count * width, 4 * pairs * slots * width),
        name="combine",
    )(codes, rows)


def expert_kernel(
    halves, x_ref, ca_ref, cb_ref, gate_ref, up_ref, down_ref, router_ref, named_ref, kept_ref,
    weighted_ref, slope_ref, act_ref, gslope_ref, uslope_ref, logit_ref,
):
    width = x_ref.shape[-1]
    x = x_ref[...].reshape(-1, width)
    c = jnp.concatenate(
        [ref[...].reshape(-1, width // 2) for ref in (ca_ref, cb_ref)], axis=1
    ).astype(F32)
    router = router_ref[...]
    logits = dot(x, router)
    powers = jnp.exp(logits - jnp.max(logits, axis=-1, keepdims=True))
    chance = powers / jnp.sum(powers, axis=-1, keepdims=True)
    named = named_ref[0]
    gating = jnp.sum(chance * named, axis=-1, keepdims=True)
    joined = None
    kept = []
    for h in range(halves):
        gate_pre = dot(x, gate_ref[h])
        up_pre = dot(x, up_ref[h])
        squashed = jax.nn.sigmoid(gate_pre)
        swished = gate_pre * squashed
        activation = swished * up_pre
        act_ref[h] = (gating * activation).astype(BF)
        part = dot(activation.astype(BF), down_ref[h])
        joined = part if joined is None else joined + part
        kept.append((up_pre * squashed * (1.0 + gate_pre * (1.0 - squashed)), swished))
    gating_slope = jnp.sum(c * joined, axis=-1, keepdims=True)
    weighted_ref[...] = (gating * joined).astype(BF).reshape(weighted_ref.shape)
    unit_slope = (gating * c).astype(BF)
    logit_slope = (gating_slope * gating * (named - chance)).astype(BF)
    logit_ref[...] = logit_slope[None]
    slope = dot_nt(logit_slope, router)
    for h in range(halves):
        activation_slope = dot_nt(unit_slope, down_ref[h])
        gate_slope = (activation_slope * kept[h][0]).astype(BF)
        up_slope = (activation_slope * kept[h][1]).astype(BF)
        gslope_ref[h] = gate_slope
        uslope_ref[h] = up_slope
        slope = slope + dot_nt(gate_slope, gate_ref[h]) + dot_nt(up_slope, up_ref[h])
    slope_ref[...] = slope.astype(BF).reshape(slope_ref.shape)


def experts(x, cs, at, gates, ups, downs, router, named, halves, kept):
    planes, local, slots, width = x.shape
    hidden = gates.shape[-1]
    sources = max(1, 448 // slots)
    tile = sources * slots
    steps = planes // sources
    count = planes * slots
    expert_total = router.shape[1]
    units = local * halves
    row_spec = pl.BlockSpec((sources, 1, slots, width), lambda n, t: (t, n, 0, 0))
    half_spec = pl.BlockSpec((sources, 1, slots, width // 2), lambda n, t: (t, n, at, 0))
    unit_spec = pl.BlockSpec((halves, tile, hidden), lambda n, t: (n, t, 0))
    once = pl.Buffered(1)
    wide = pl.BlockSpec((halves, width, hidden), lambda n, t: (n, 0, 0), pipeline_mode=once)
    tall = pl.BlockSpec((halves, hidden, width), lambda n, t: (n, 0, 0), pipeline_mode=once)
    return pl.pallas_call(
        functools.partial(expert_kernel, halves),
        grid=(local, steps),
        out_shape=(
            shape_of((planes, local, CHUNKS * slots, width), BF), shape_of(x.shape, BF),
            shape_of((units, count, hidden), BF), shape_of((units, count, hidden), BF),
            shape_of((units, count, hidden), BF), shape_of((local, count, expert_total), BF),
        ),
        in_specs=[
            row_spec, half_spec, half_spec, wide, wide, tall,
            pl.BlockSpec((width, expert_total), lambda n, t: (0, 0)),
            pl.BlockSpec((1, 1, expert_total), lambda n, t: (n, 0, 0)),
            pl.BlockSpec(memory_space=pl.ANY),
        ],
        out_specs=(
            pl.BlockSpec((sources, 1, slots, width), lambda n, t: (t, n, at, 0)), row_spec, unit_spec, unit_spec, unit_spec,
            pl.BlockSpec((1, tile, expert_total), lambda n, t: (n, t, 0)),
        ),
        input_output_aliases={8: 0} if at else {},
        compiler_params=params(62),
        cost_estimate=cost(12 * units * count * hidden * width, 10 * local * count * width),
        name="experts",
    )(x, *cs, gates, ups, downs, router, named, kept)


def wide_grad_kernel(x0_ref, x1_ref, g0_ref, g1_ref, u0_ref, u1_ref, dg_ref, du_ref):
    tile = x0_ref.shape[-1]
    x0 = x0_ref[...].reshape(-1, tile).T
    x1 = x1_ref[...].reshape(-1, tile).T
    dg_ref[0] = dot(x0, g0_ref[0]) + dot(x1, g1_ref[0])
    du_ref[0] = dot(x0, u0_ref[0]) + dot(x1, u1_ref[0])


def wide_grad(xs, gslopes, uslopes, halves):
    planes, local, slots, width = xs[0].shape
    units, count, hidden = gslopes[0].shape
    tile = 1024 if planes * slots <= 1024 else 512
    x_spec = pl.BlockSpec((planes, 1, slots, tile), lambda u, j: (0, u // halves, 0, j))
    s_spec = pl.BlockSpec((1, count, hidden), lambda u, j: (u, 0, 0))
    o_spec = pl.BlockSpec((1, tile, hidden), lambda u, j: (u, j, 0))
    out = shape_of((units, width, hidden), F32)
    return pl.pallas_call(
        wide_grad_kernel,
        grid=(units, width // tile),
        out_shape=(out, out),
        in_specs=[x_spec] * 2 + [s_spec] * 4,
        out_specs=(o_spec, o_spec),
        compiler_params=params(60),
        cost_estimate=cost(8 * units * count * hidden * width, 8 * units * hidden * width),
        name="wide_grad",
    )(*xs, *gslopes, *uslopes)


def down_grad_kernel(a0_ref, a1_ref, ca_ref, cb_ref, d_ref):
    tile, slots = ca_ref.shape[-1], ca_ref.shape[2] // 2

    def part(c_ref):
        d_ref[0] = dot(a0_ref[0].T, c_ref[:, :, :slots].reshape(-1, tile)) + dot(
            a1_ref[0].T, c_ref[:, :, slots:].reshape(-1, tile)
        )

    first = pl.program_id(1) < pl.num_programs(1) // 2
    pl.when(first)(lambda: part(ca_ref))
    pl.when(jnp.logical_not(first))(lambda: part(cb_ref))


def down_grad(acts, cs, halves):
    planes, local, double, half = cs[0].shape
    units, count, hidden = acts[0].shape
    tile = half if planes * double <= 2048 else 512
    steps = half // tile
    a_spec = pl.BlockSpec((1, count, hidden), lambda u, j: (u, 0, 0))
    shape = (planes, 1, double, tile)
    return pl.pallas_call(
        down_grad_kernel,
        grid=(units, 2 * steps),
        out_shape=shape_of((units, hidden, 2 * half), F32),
        in_specs=[
            a_spec, a_spec,
            pl.BlockSpec(shape, lambda u, j: (0, u // halves, 0, jnp.minimum(j, steps - 1))),
            pl.BlockSpec(shape, lambda u, j: (0, u // halves, 0, jnp.maximum(j - steps, 0))),
        ],
        out_specs=pl.BlockSpec((1, hidden, tile), lambda u, j: (u, 0, j)),
        compiler_params=params(60),
        cost_estimate=cost(8 * units * count * hidden * half, 8 * units * hidden * half),
        name="down_grad",
    )(*acts, *cs)


def per_device(
    inputs,
    query_weight,
    key_weight,
    value_weight,
    output_weight,
    router_weight,
    first_gain,
    query_gain,
    key_gain,
    second_gain,
    gate_weight,
    up_weight,
    down_weight,
    routes,
    lengths,
    dealing,
    cotangent,
):
    planes, line = lax.axis_size("expert"), lax.axis_size("fsdp")
    plane_at, line_at = lax.axis_index("expert"), lax.axis_index("fsdp")
    tokens, width = inputs.shape
    group = line * tokens
    own_heads = HEADS // line
    head_size = width // HEADS
    own_width = own_heads * head_size
    weight_rows = query_weight.shape[0]
    slice_rows = weight_rows // planes
    units = gate_weight.shape[0]
    local = max(1, units // 2)
    halves = units // local
    expert_count = router_weight.shape[1]
    blocks = line // CHUNKS
    chunk_rows = blocks * tokens
    slots = blocks * CAP

    def own_slice(weight):
        return lax.dynamic_slice_in_dim(weight, plane_at * slice_rows, slice_rows, 0)

    sent = jnp.stack([own_slice(w) for w in (query_weight, key_weight, value_weight)], axis=1)
    sent = jnp.moveaxis(sent.reshape(slice_rows, 3, line, own_width), 2, 0)
    sent = sent.reshape(line, slice_rows, 3 * own_width)
    top_count = routes.shape[1]
    packed = [router_weight, first_gain, second_gain, routes.astype(BF)]
    sizes = [array.size for array in packed]
    fill = -sum(sizes) % (16 * 128)
    small = jnp.concatenate([array.reshape(-1) for array in packed] + [jnp.zeros((fill,), BF)])
    block_in, first_half, small_all, columns, _ = gather_start(
        inputs, cotangent, small.reshape(-1, 128), sent, planes, line
    )
    columns = columns.reshape(width, 3 * own_width)
    small_all = small_all.reshape(line, -1)
    ends = [sum(sizes[:i]) for i in range(5)]
    full_router, gain_first, gain_second, routes_all = (
        small_all[:, ends[i]:ends[i + 1]] for i in range(4)
    )
    full_router = full_router.reshape(width, expert_count)
    gain_first, gain_second = (g.reshape(width).astype(F32) for g in (gain_first, gain_second))
    routes_all = routes_all.reshape(line, tokens, top_count).astype(jnp.int32)
    later, _ = lax.optimization_barrier((cotangent, block_in))
    second_half = lax.all_gather(later[:, width // 2:], "fsdp", axis=0, tiled=True)
    incoming = [first_half, second_half]

    seq_start, positions = places(lengths[0], dealing)
    start_row, place_row, place_column = seq_start[None, :], dealing[None, :], dealing[:, None]
    cosine, sine = angles(positions, head_size)
    per_plane = expert_count // planes
    first_local = (line_at * units) // 2
    member = jnp.sum(
        (routes_all[..., None] == jnp.arange(expert_count, dtype=jnp.int32)).astype(F32), axis=2
    )
    earlier = jnp.tril(jnp.ones((tokens, tokens), BF), -1)
    rank = contract("ts,bse->bte", earlier, member.astype(BF))
    rank = rank + ((jnp.arange(line) % blocks) * CAP).astype(F32)[:, None, None]
    coded = jnp.where(member > 0, rank, -1.0).reshape(line, tokens, planes, per_plane)
    coded = lax.dynamic_slice_in_dim(coded, first_local, local, 3)
    coded = coded.reshape(CHUNKS, chunk_rows, planes * local)
    by_token = coded.astype(BF)
    by_pair = jnp.swapaxes(coded, 1, 2)

    def chunk(array, k):
        return lax.slice_in_dim(array, k * chunk_rows, (k + 1) * chunk_rows)

    rows = dispatch(by_pair, incoming[0], planes, local, slots)
    normed_low, raw, value_low, squares = project(block_in, gain_first[None], columns, tokens)
    squares = small_line_sum(squares, line)
    both_gains = jnp.concatenate([query_gain, key_gain])[None].astype(F32)
    rotary = (jnp.concatenate([cosine, cosine], -1), jnp.concatenate([-sine, sine], -1))
    query_low, key_low = turn(raw, squares, both_gains, *rotary, width, tokens)
    blended, log_total = attend(
        query_low, key_low, value_low, start_row, place_row, place_column, own_heads, tokens
    )
    attention_part = dot(blended, output_weight).astype(BF)

    named = (
        (((plane_at * line + line_at) * units) // 2 + jnp.arange(local))[:, None, None]
        == jnp.arange(expert_count)
    ).astype(F32)
    attention_parts = [chunk(attention_part, k) for k in range(CHUNKS)]
    arrived_slopes = [swap_plane(rows)]
    rows = dispatch(by_pair, incoming[1], planes, local, slots)
    attended, swapped = line_swap(attention_parts[0], rows, line, 4)
    arrived_slopes.append(swapped)
    hidden, arrived = block_in, []
    for k in range(CHUNKS):
        hidden, normed = hide(block_in, attended, gain_second[None], k * chunk_rows, tokens, hidden)
        rows = dispatch(by_pair[k:k + 1], normed, planes, local, slots)
        if k + 1 < CHUNKS:
            attended, swapped = line_swap(attention_parts[k + 1], rows, line, 3)
            arrived.append(swapped)
        else:
            rows, arrived_slopes[0] = lax.optimization_barrier((rows, arrived_slopes[0]))
            arrived.append(swap_plane(rows))
    weighted = arrived_slopes[0]
    row_slopes, acts, gslopes, uslopes, logit_slopes = [], [], [], [], []
    for k in range(CHUNKS):
        results = experts(
            arrived[k], arrived_slopes, k, gate_weight, up_weight, down_weight, full_router,
            named, halves, weighted,
        )
        weighted = results[0]
        for store, result in zip((row_slopes, acts, gslopes, uslopes, logit_slopes), results[1:]):
            store.append(result)
    returned = []
    behind = arrived[-1]
    for k in range(CHUNKS):
        rows, _ = lax.optimization_barrier((row_slopes[k], behind))
        behind = swap_plane(rows)
        returned.append(behind)

    second_gain_grad = 0.0
    kept = (block_in,) * 3
    for k in range(CHUNKS):
        returned[k], _ = lax.optimization_barrier((returned[k], summed if k else row_slopes[-1]))
        part = combine(by_token[k:k + 1], returned[k], slots)
        if k:
            rows, _ = lax.optimization_barrier((weighted, returned[k]))
            mixed_rows = swap_plane(rows)
        summed = line_sum(part, line)
        *kept, gain_part = hide_back(
            summed, hidden, incoming, gain_second[None], output_weight, k * chunk_rows, tokens, kept
        )
        second_gain_grad = second_gain_grad + gain_part
    hidden_slope, attention_slope, blended_slope = kept
    slopes = attend_back(
        query_low, key_low, value_low, blended_slope, log_total, start_row,
        place_row, place_column, own_heads, tokens,
    )
    dots, gain_grads = turn_back(*slopes[:2], raw, squares, both_gains, *rotary, width, tokens)
    dots = small_line_sum(dots, line)
    mixed_rows, _ = lax.optimization_barrier((mixed_rows, gain_grads))
    mixed = combine(by_token, mixed_rows, slots)
    acts, gslopes, uslopes, logit_slopes, attention_slope, _ = lax.optimization_barrier(
        (acts, gslopes, uslopes, logit_slopes, attention_slope, mixed)
    )
    mixed = lax.psum_scatter(mixed, "fsdp", scatter_dimension=0, tiled=True)
    expert_grads = [
        *wide_grad(arrived, gslopes, uslopes, halves),
        down_grad(acts, arrived_slopes, halves),
    ]
    router_grad = sum(
        contract(
            "ensd,nesq->dq", arrived[k],
            logit_slopes[k].reshape(local, planes, slots, expert_count),
        )
        for k in range(CHUNKS)
    )
    output_grad = contract("tc,td->cd", blended, attention_slope).astype(BF)
    dots, _ = lax.optimization_barrier((dots, expert_grads))
    joint, normed_part = join_slopes(
        *slopes, raw, squares, dots, both_gains, *rotary, columns, tokens
    )
    router_lanes = -expert_count % 128
    router_pad = jnp.pad(router_grad.astype(BF), ((0, 0), (0, router_lanes)))
    joint_total = joint_grad(normed_low, joint, router_pad)
    mine = line_at * weight_rows
    second_own = lax.dynamic_slice_in_dim(second_gain_grad, mine, weight_rows, 1)
    gain_rows = jnp.concatenate(
        [
            jnp.zeros((1, weight_rows), F32), second_own, gain_grads.reshape(2, own_width),
            jnp.zeros((4, weight_rows), F32),
        ]
    )
    input_gradient, totals, output_total, gain_totals = finish(
        normed_part, joint_total.reshape(line, planes, slice_rows, -1),
        output_grad.reshape(planes, slice_rows, width), inputs, gain_first[None],
        hidden_slope, gain_rows, planes, line,
    )
    hidden_own = lax.dynamic_slice_in_dim(hidden, line_at * tokens, tokens, 0)
    block_output = (hidden_own + mixed.astype(F32)).astype(BF)
    *weight_grads, router_total = widen(
        totals.reshape(line, planes // 2, 2, slice_rows, -1),
        output_total.reshape(planes // 2, 2, slice_rows, width), own_width,
    )
    router_total = router_total[:, :expert_count]
    return (
        block_output,
        input_gradient,
        *weight_grads,
        router_total,
        gain_totals[0],
        gain_totals[2],
        gain_totals[3],
        gain_totals[1],
        *expert_grads,
    )


def solution(mesh):
    both = ("expert", "fsdp")
    rows, cube, shard, gain = P(both, None), P(both, None, None), P("fsdp", None), P("fsdp")
    return jax.shard_map(
        per_device,
        mesh=mesh,
        in_specs=(rows,)
        + (shard,) * 5
        + (gain,) * 4
        + (cube,) * 3
        + (rows, P("expert", None), P("expert"), rows),
        out_specs=(rows, rows) + (shard,) * 5 + (gain,) * 4 + (cube,) * 3,
        check_vma=False,
    )
```

```python
import functools

import jax
import jax.numpy as jnp
from jax import lax
from jax.experimental import pallas as pl
from jax.experimental.pallas import tpu as pltpu
from jax.sharding import PartitionSpec as P

HEADS = 16
CAP = 56
EPSILON = 1e-05
THETA = 10000.0
MASKED = -1e30
LOG2E = 1.4426950408889634
BF = jnp.bfloat16
F32 = jnp.float32
MESH = pl.DeviceIdType.MESH
MIB = 1 << 20
CHUNKS = 2


def dot(a, b):
    return jnp.dot(a, b, preferred_element_type=F32)


def dot_nt(a, b):
    return lax.dot_general(a, b, (((1,), (1,)), ((), ())), preferred_element_type=F32)


def dot_tn(a, b):
    return lax.dot_general(a, b, (((0,), (0,)), ((), ())), preferred_element_type=F32)


def contract(spec, *operands):
    return jnp.einsum(spec, *operands, preferred_element_type=F32)


def shape_of(dims, dtype):
    return jax.ShapeDtypeStruct(dims, dtype)


def cost(flops, moved):
    return pl.CostEstimate(flops=int(flops) // 64, bytes_accessed=int(moved) // 64, transcendentals=0)


def params(mib, **kwargs):
    return pltpu.CompilerParams(vmem_limit_bytes=mib * MIB, **kwargs)


def places(lengths_row, stream):
    seq_ends = jnp.cumsum(lengths_row)
    before = (seq_ends[None, :] <= stream[:, None]).astype(jnp.int32)
    offset = jnp.sum(before * lengths_row[None, :], axis=1)
    return offset, stream - offset


def angles(positions, head_width):
    exponent = jnp.arange(0, head_width, 2).astype(F32) / head_width
    phases = positions.astype(F32)[:, None] * (THETA ** (-exponent))[None, :]
    return jnp.cos(phases), jnp.sin(phases)


def gather_kernel(
    planes, line, pieces, x_ref, c_ref, small_ref, sent_ref,
    x_all, c_all, small_all, columns_ref, swapped_ref,
    x_send, x_recv, s_send, s_recv, z_send, z_recv, p_send, p_recv, own_sem,
):
    e, f = lax.axis_index("expert"), lax.axis_index("fsdp")
    barrier = pltpu.get_barrier_semaphore()
    for d in range(1, line):
        pl.semaphore_signal(
            barrier, inc=1, device_id={"fsdp": lax.rem(f + d, line)}, device_id_type=MESH
        )
    for d in range(1, planes):
        pl.semaphore_signal(
            barrier, inc=1, device_id={"expert": lax.rem(e + d, planes)}, device_id_type=MESH
        )
    pl.semaphore_wait(barrier, line + planes - 2)
    rows = x_ref.shape[0]
    part = rows // pieces
    small_rows = small_ref.shape[0]

    swaps, smalls = [], []
    for d in range(1, line):
        to = lax.rem(f + d, line)
        swaps.append(pltpu.make_async_remote_copy(
            src_ref=sent_ref.at[to], dst_ref=swapped_ref.at[f],
            send_sem=z_send.at[d - 1], recv_sem=z_recv.at[d - 1],
            device_id={"fsdp": to}, device_id_type=MESH,
        ))
        smalls.append(pltpu.make_async_remote_copy(
            src_ref=small_ref, dst_ref=small_all.at[pl.ds(f * small_rows, small_rows)],
            send_sem=s_send.at[d - 1], recv_sem=s_recv.at[d - 1],
            device_id={"fsdp": to}, device_id_type=MESH,
        ))
    for copy in swaps:
        copy.start()

    def hop(direction, step, c):
        own_ref, all_ref = (x_ref, x_all) if c < pieces else (c_ref, c_all)
        origin = f - direction * step
        place = pl.ds(origin * rows + c % pieces * part, part)
        cut = pl.ds(0, all_ref.shape[1])
        source = own_ref.at[pl.ds(c % pieces * part, part), cut] if step == 0 else all_ref.at[place]
        side = 0 if direction == 1 else 1
        return pltpu.make_async_remote_copy(
            src_ref=source, dst_ref=all_ref.at[place],
            send_sem=x_send.at[side, step, c], recv_sem=x_recv.at[side, step, c],
            device_id={"fsdp": f + direction}, device_id_type=MESH,
        )

    def sends(direction, step):
        origin, to = f - direction * step, f + direction
        return (origin >= 0) & (origin < line) & (to >= 0) & (to < line)

    def receives(direction, step):
        origin = f - direction * (step + 1)
        return (origin >= 0) & (origin < line)

    for direction in (1, -1):
        @pl.when(sends(direction, 0))
        def _(direction=direction):
            for c in range(2 * pieces):
                hop(direction, 0, c).start()

    for copy in smalls:
        copy.start()
    locals_ = [
        pltpu.make_async_copy(x_ref, x_all.at[pl.ds(f * rows, rows)], own_sem.at[0]),
        pltpu.make_async_copy(
            c_ref.at[:, pl.ds(0, c_all.shape[1])], c_all.at[pl.ds(f * rows, rows)], own_sem.at[4]
        ),
        pltpu.make_async_copy(
            small_ref, small_all.at[pl.ds(f * small_rows, small_rows)], own_sem.at[1]
        ),
        pltpu.make_async_copy(sent_ref.at[f], swapped_ref.at[f], own_sem.at[2]),
    ]
    for copy in locals_:
        copy.start()
    for copy in swaps:
        copy.wait_recv()
    locals_[3].wait()
    spread = []
    for d in range(1, planes):
        spread.append(pltpu.make_async_remote_copy(
            src_ref=swapped_ref, dst_ref=columns_ref.at[:, e],
            send_sem=p_send.at[d - 1], recv_sem=p_recv.at[d - 1],
            device_id={"expert": lax.rem(e + d, planes)}, device_id_type=MESH,
        ))
        spread[-1].start()
    own = pltpu.make_async_copy(swapped_ref, columns_ref.at[:, e], own_sem.at[3])
    own.start()

    for step in range(line - 1):
        for c in range(2 * pieces):
            for direction in (1, -1):
                @pl.when(receives(direction, step))
                def _(direction=direction, step=step, c=c):
                    origin = f - direction * (step + 1)
                    all_ref = x_all if c < pieces else c_all
                    place = pl.ds(origin * rows + c % pieces * part, part)
                    side = 0 if direction == 1 else 1
                    pltpu.make_async_remote_copy(
                        src_ref=all_ref.at[place], dst_ref=all_ref.at[place],
                        send_sem=x_send.at[side, step, c], recv_sem=x_recv.at[side, step, c],
                        device_id={"fsdp": f - direction}, device_id_type=MESH,
                    ).wait_recv()
                if step < line - 2:
                    @pl.when(sends(direction, step + 1))
                    def _(direction=direction, step=step, c=c):
                        hop(direction, step + 1, c).start()
    for step in range(line - 1):
        for direction in (1, -1):
            @pl.when(sends(direction, step))
            def _(direction=direction, step=step):
                for c in range(2 * pieces):
                    hop(direction, step, c).wait_send()
    for copy in swaps:
        copy.wait_send()
    for copy in smalls + spread:
        copy.wait()
    for copy in locals_[:3] + [own]:
        copy.wait()


def gather_start(block, half, small, sent, planes, line):
    rows, width = block.shape
    pieces = 4
    anywhere = pl.BlockSpec(memory_space=pl.ANY)
    sems = pltpu.SemaphoreType.DMA
    return pl.pallas_call(
        functools.partial(gather_kernel, planes, line, pieces),
        out_shape=(
            shape_of((line * rows, width), BF),
            shape_of((line * rows, half.shape[1] // 2), BF),
            shape_of((line * small.shape[0], small.shape[1]), BF),
            shape_of((line, planes) + sent.shape[1:], BF),
            shape_of(sent.shape, BF),
        ),
        in_specs=[anywhere] * 4,
        out_specs=[anywhere] * 5,
        scratch_shapes=[
            sems((2, line - 1, 2 * pieces)), sems((2, line - 1, 2 * pieces)),
            sems((line - 1,)), sems((line - 1,)), sems((line - 1,)), sems((line - 1,)),
            sems((planes - 1,)), sems((planes - 1,)), sems((5,)),
        ],
        compiler_params=pltpu.CompilerParams(collective_id=0, has_side_effects=True),
        name="gather_start",
    )(block, half, small, sent)


def line_steps(line, pieces, lag, p_ref, o_ref, right_in, left_in, send_sem, recv_sem, complete):
    f = lax.axis_index("fsdp")
    last = line - 1
    part = p_ref.shape[0] // pieces

    def greet():
        barrier = pltpu.get_barrier_semaphore()

        @pl.when(f > 0)
        def _():
            pl.semaphore_signal(barrier, inc=1, device_id={"fsdp": f - 1}, device_id_type=MESH)

        @pl.when(f < last)
        def _():
            pl.semaphore_signal(barrier, inc=1, device_id={"fsdp": f + 1}, device_id_type=MESH)

    neighbours = jnp.where((f > 0) & (f < last), 2, 1)

    def copy(side, source, c):
        buffer = right_in if side == 0 else left_in
        place = pl.ds(c * part, part)
        return pltpu.make_async_remote_copy(
            src_ref=(p_ref if source else buffer).at[place], dst_ref=buffer.at[place],
            send_sem=send_sem.at[side, c], recv_sem=recv_sem.at[side, c],
            device_id={"fsdp": f + 1 if side == 0 else f - 1}, device_id_type=MESH,
        )

    def enter():
        for side in range(2):
            @pl.when(f == (0 if side == 0 else last))
            def _(side=side):
                def one(c, carry):
                    copy(side, True, c).start()
                    return carry

                lax.fori_loop(0, pieces, one, 0)

    def arrive(side, c):
        place = pl.ds(pl.multiple_of(c * part, part), part)
        buffer = right_in if side == 0 else left_in
        origin, end = (0, last) if side == 0 else (last, 0)
        leads = (2 * f <= last) if side == 0 else (2 * f > last)

        @pl.when(f == origin)
        def _():
            o_ref[place, :] = p_ref[place, :].astype(F32)

        @pl.when(f != origin)
        def _():
            copy(side, False, c).wait_recv()
            came = buffer[place, :].astype(F32)

            @pl.when(f != end)
            def _():
                buffer[place, :] = (came + p_ref[place, :].astype(F32)).astype(BF)
                copy(side, False, c).start()

            @pl.when(leads)
            def _():
                o_ref[place, :] = came + p_ref[place, :].astype(F32)

            @pl.when(jnp.logical_not(leads))
            def _():
                o_ref[place, :] += came
                complete(place, c)

    def body(s, carry):
        for side in range(2):
            c = s - lag * (f if side == 0 else last - f)

            @pl.when((c >= 0) & (c < pieces))
            def _(side=side, c=c):
                arrive(side, c)

        return carry

    def drain():
        def one(c, carry):
            @pl.when(f < last)
            def _():
                copy(0, True, c).wait_send()

            @pl.when(f > 0)
            def _():
                copy(1, True, c).wait_send()

            return carry

        lax.fori_loop(0, pieces, one, 0)

    return greet, neighbours, enter, body, drain, pieces + lag * last


def line_scratch(rows, width, pieces):
    return [
        pltpu.VMEM((rows, width), BF),
        pltpu.VMEM((rows, width), BF),
        pltpu.SemaphoreType.DMA((2, pieces)),
        pltpu.SemaphoreType.DMA((2, pieces)),
    ]


def store_pieces(pairs, sems, pieces, height):
    def copies(c):
        place = pl.ds(pl.multiple_of(c * height, height), height)
        return [
            pltpu.make_async_copy(source.at[place], target.at[place], sems.at[i, c])
            for i, (source, target) in enumerate(pairs)
        ]

    def start(c):
        for copy in copies(c):
            copy.start()

    def wait():
        def one(c, carry):
            for copy in copies(c):
                copy.wait()
            return carry

        lax.fori_loop(0, pieces, one, 0)

    return start, wait


def hide_kernel(
    planes, line, pieces, lag, at, p_ref, x_ref, gain_ref, rows_ref, hidden_ref, normed_ref, swapped_ref,
    right_in, left_in, send_sem, recv_sem, w_send, w_recv, own_sem, x_own, total_own, normed_own, store_sem,
):
    e = lax.axis_index("expert")
    rows = p_ref.shape[0]
    load = pltpu.make_async_copy(x_ref.at[pl.ds(at * rows, rows)], x_own, own_sem.at[1])
    load.start()
    start_store, wait_stores = store_pieces(
        [(total_own, hidden_ref), (normed_own, normed_ref)], store_sem, pieces, rows // pieces
    )

    def complete(place, c):
        hidden = x_own[place, :].astype(F32) + total_own[place, :]
        total_own[place, :] = hidden
        scale = lax.rsqrt(jnp.mean(hidden * hidden, axis=-1, keepdims=True) + EPSILON)
        normed_own[place, :] = (hidden * scale * gain_ref[...]).astype(BF)
        start_store(c)

    greet, neighbours, enter, body, drain, total = line_steps(
        line, pieces, lag, p_ref, total_own, right_in, left_in, send_sem, recv_sem, complete
    )
    greet()
    barrier = pltpu.get_barrier_semaphore()
    for d in range(1, planes):
        pl.semaphore_signal(
            barrier, inc=1, device_id={"expert": lax.rem(e + d, planes)}, device_id_type=MESH
        )
    pl.semaphore_wait(barrier, neighbours + planes - 1)
    enter()
    swaps = []
    for d in range(1, planes):
        to = lax.rem(e + d, planes)
        swaps.append(pltpu.make_async_remote_copy(
            src_ref=rows_ref.at[to], dst_ref=swapped_ref.at[e],
            send_sem=w_send.at[d - 1], recv_sem=w_recv.at[d - 1],
            device_id={"expert": to}, device_id_type=MESH,
        ))
    own = pltpu.make_async_copy(rows_ref.at[e], swapped_ref.at[e], own_sem.at[0])
    for copy in swaps + [own]:
        copy.start()
    load.wait()
    lax.fori_loop(0, total, body, 0)
    drain()
    for copy in swaps + [own]:
        copy.wait()
    wait_stores()


def hide(part, block, gain, rows_sent, at, line, identity, height=32, lag=2):
    rows, width = part.shape
    planes = rows_sent.shape[0]
    pieces = rows // height
    sems = pltpu.SemaphoreType.DMA
    anywhere = pl.BlockSpec(memory_space=pl.ANY)
    vmem = pl.BlockSpec(memory_space=pltpu.VMEM)
    return pl.pallas_call(
        functools.partial(hide_kernel, planes, line, pieces, lag, at),
        out_shape=(
            shape_of((rows, width), F32), shape_of((rows, width), BF),
            shape_of(rows_sent.shape, BF),
        ),
        in_specs=[vmem, anywhere, vmem, anywhere],
        out_specs=(anywhere, anywhere, anywhere),
        scratch_shapes=line_scratch(rows, width, pieces)
        + [
            sems((planes - 1,)), sems((planes - 1,)), sems((2,)),
            pltpu.VMEM((rows, width), BF), pltpu.VMEM((rows, width), F32),
            pltpu.VMEM((rows, width), BF), sems((2, pieces)),
        ],
        compiler_params=params(60, collective_id=identity, has_side_effects=True),
        cost_estimate=cost(0, 300 * MIB),
        name="hide",
    )(part, block, gain, rows_sent)


def hide_back_kernel(
    line, pieces, lag, at, p_ref, hidden_ref, ca_ref, cb_ref, gain_ref, total_ref, low_ref, grad_ref,
    right_in, left_in, send_sem, recv_sem, hidden_own, ca_own, cb_own, total_own, low_own, load_sem, store_sem,
):
    rows = p_ref.shape[0]
    half = ca_ref.shape[1]
    mine = pl.ds(at * rows, rows)
    loads = [
        pltpu.make_async_copy(hidden_ref, hidden_own, load_sem.at[0]),
        pltpu.make_async_copy(ca_ref.at[mine], ca_own, load_sem.at[1]),
        pltpu.make_async_copy(cb_ref.at[mine], cb_own, load_sem.at[2]),
    ]
    for copy in loads:
        copy.start()
    start_store, wait_stores = store_pieces(
        [(total_own, total_ref), (low_own, low_ref)], store_sem, pieces, rows // pieces
    )

    def complete(place, c):
        slope, hidden = total_own[place, :], hidden_own[place, :]
        scale = lax.rsqrt(jnp.mean(hidden * hidden, axis=-1, keepdims=True) + EPSILON)
        grad_ref[...] += jnp.sum(slope * hidden * scale, axis=0, keepdims=True)
        slope = slope * gain_ref[...]
        along = jnp.sum(slope * hidden, axis=-1, keepdims=True) / hidden.shape[1]
        part = scale * slope - hidden * (scale * scale * scale * along)
        for ref, lanes in ((ca_own, slice(0, half)), (cb_own, slice(half, 2 * half))):
            total = ref[place, :].astype(F32) + part[:, lanes]
            total_own[place, lanes] = total
            low_own[place, lanes] = total.astype(BF)
        start_store(c)

    greet, neighbours, enter, body, drain, total = line_steps(
        line, pieces, lag, p_ref, total_own, right_in, left_in, send_sem, recv_sem, complete
    )
    greet()
    grad_ref[...] = jnp.zeros_like(grad_ref)
    pl.semaphore_wait(pltpu.get_barrier_semaphore(), neighbours)
    enter()
    for copy in loads:
        copy.wait()
    lax.fori_loop(0, total, body, 0)
    drain()
    wait_stores()


def hide_back(part, hidden, incoming, gain, at, line, height=32, lag=2):
    rows, width = part.shape
    pieces = rows // height
    sems = pltpu.SemaphoreType.DMA
    anywhere = pl.BlockSpec(memory_space=pl.ANY)
    vmem = pl.BlockSpec(memory_space=pltpu.VMEM)
    return pl.pallas_call(
        functools.partial(hide_back_kernel, line, pieces, lag, at),
        out_shape=(
            shape_of((rows, width), F32), shape_of((rows, width), BF), shape_of((1, width), F32),
        ),
        in_specs=[vmem, anywhere, anywhere, anywhere, vmem],
        out_specs=(anywhere, anywhere, vmem),
        scratch_shapes=line_scratch(rows, width, pieces)
        + [
            pltpu.VMEM((rows, width), F32), pltpu.VMEM((rows, width // 2), BF),
            pltpu.VMEM((rows, width // 2), BF), pltpu.VMEM((rows, width), F32),
            pltpu.VMEM((rows, width), BF), sems((3,)), sems((2, pieces)),
        ],
        compiler_params=params(62, collective_id=5 + at, has_side_effects=True),
        cost_estimate=cost(0, 260 * MIB),
        name="hide_back",
    )(part, hidden, *incoming, gain)


def finish_kernel(
    planes, line, height, lag, p_ref, a_ref, b_ref, x_ref, gain_ref, slope0_ref, slope1_ref, gains_ref,
    o_ref, a_out, b_out, gains_out,
    right_in, left_in, a_own, a_half, a_in, a_sum, a_cols, b_own, b_half, b_in, b_sum, gain_part, gain_in, gain_own, gain_all,
    z_send, z_recv, h_send, h_recv, r_send, r_recv, s_send, s_recv, g_send, g_recv,
    w_send, w_recv, n_send, n_recv, m_send, m_recv, own_sem, slope_own,
):
    e, f = lax.axis_index("expert"), lax.axis_index("fsdp")
    chips, last = planes // 2, line - 1
    c, k = e // 2, e % 2
    mate = e + 1 - 2 * k
    barrier = pltpu.get_barrier_semaphore()

    def greet(**device):
        pl.semaphore_signal(barrier, inc=1, device_id=device, device_id_type=MESH)

    for d in range(1, planes):
        greet(expert=lax.rem(e + d, planes))
    for d in range(1, line):
        greet(fsdp=lax.rem(f + d, line))
    pl.semaphore_wait(barrier, planes - 1 + last)

    rows = p_ref.shape[0] // line
    pieces = rows // height
    ahead = 4

    def remote(source, target, send, recv, **device):
        return pltpu.make_async_remote_copy(
            src_ref=source, dst_ref=target, send_sem=send, recv_sem=recv,
            device_id=device, device_id_type=MESH,
        )

    lanes_a = a_ref.shape[-1]
    cut = lanes_a // 128 * 9 // 13 * 128
    spans = (pl.ds(0, cut), pl.ds(cut, lanes_a - cut))

    to_mate = [
        remote(
            a_ref.at[:, :, 1 - k, :, span], a_half.at[:, :, :, span], h_send.at[i], h_recv.at[i],
            expert=mate,
        )
        for i, span in enumerate(spans)
    ]
    to_mate.append(remote(b_ref.at[:, 1 - k], b_half, h_send.at[2], h_recv.at[2], expert=mate))
    own_half = [
        pltpu.make_async_copy(a_ref.at[:, :, k], a_own, own_sem.at[0]),
        pltpu.make_async_copy(b_ref.at[:, k], b_own, own_sem.at[1]),
    ]
    blocks = line // 2

    def slope_load(which):
        source = (slope0_ref, slope1_ref)[which]
        place = pl.ds(pl.multiple_of((f - which * blocks) * rows, rows), rows)
        return pltpu.make_async_copy(source.at[place], slope_own, own_sem.at[4])

    pl.when(f < blocks)(lambda: slope_load(0).start())
    pl.when(f >= blocks)(lambda: slope_load(1).start())
    for copy in to_mate + own_half:
        copy.start()

    def place_of(side, s):
        target = last - s // pieces if side == 0 else s // pieces
        return target, pl.ds(pl.multiple_of(target * rows + lax.rem(s, pieces) * height, height), height)

    def copy_line(side, source, s):
        buffer = right_in if side == 0 else left_in
        place = place_of(side, s)[1]
        return remote(
            (p_ref if source else buffer).at[place], buffer.at[place],
            z_send.at[side, s], z_recv.at[side, s], fsdp=f + 1 if side == 0 else f - 1,
        )

    def begin(side, s):
        @pl.when(s >= ahead)
        def _():
            copy_line(side, True, s - ahead).wait_send()

        copy_line(side, True, s).start()

    def arrive(side, s):
        buffer = right_in if side == 0 else left_in
        target, place = place_of(side, s)
        copy_line(side, False, s).wait_recv()

        @pl.when(target != f)
        def _():
            buffer[place, :] = (buffer[place, :].astype(F32) + p_ref[place, :].astype(F32)).astype(BF)
            copy_line(side, False, s).start()

    def body(s, carry):
        right = s - lag * f
        left = s - lag * (last - f)

        @pl.when((f == 0) & (s < last * pieces))
        def _():
            begin(0, s)

        @pl.when((f == last) & (s < last * pieces))
        def _():
            begin(1, s)

        @pl.when((f > 0) & (right >= 0) & (right < (last - f + 1) * pieces))
        def _():
            arrive(0, right)

        @pl.when((f < last) & (left >= 0) & (left < (f + 1) * pieces))
        def _():
            arrive(1, left)

        return carry

    total = last * pieces + lag * last
    shares, swaps, spread = [], [], []
    sent = []

    def add_pairs():
        for copy in own_half:
            copy.wait()
        for copy in to_mate:
            copy.wait_recv()

        def one(i, carry):
            for j in range(chips):
                a_own[i, j] = (a_own[i, j].astype(F32) + a_half[i, j].astype(F32)).astype(BF)
            return carry

        lax.fori_loop(0, line, one, 0)
        for j in range(chips):
            b_own[j] = (b_own[j].astype(F32) + b_half[j].astype(F32)).astype(BF)

    def share(which):
        span = spans[which]
        mine = []
        for d in range(1, chips):
            to = lax.rem(c + d, chips)
            mine.append(remote(
                a_own.at[:, to, :, span], a_in.at[d - 1, :, :, span],
                r_send.at[which, d - 1], r_recv.at[which, d - 1], expert=to * 2 + k,
            ))
            if which:
                mine.append(remote(
                    b_own.at[to], b_in.at[d - 1], r_send.at[2, d - 1], r_recv.at[2, d - 1],
                    expert=to * 2 + k,
                ))
        for copy in mine:
            copy.start()
        shares.append(mine)

    def swap(which):
        span = spans[which]

        def one(i, carry):
            summed = a_own[i, c, :, span].astype(F32)
            for d in range(1, chips):
                summed = summed + a_in[d - 1, i, :, span].astype(F32)
            a_sum[i, :, span] = summed.astype(BF)
            return carry

        lax.fori_loop(0, line, one, 0)
        if which:
            summed = b_own[c].astype(F32)
            for d in range(1, chips):
                summed = summed + b_in[d - 1].astype(F32)
            b_sum[...] = summed.astype(BF)
        mine = []
        for d in range(1, line):
            to = lax.rem(f + d, line)
            mine.append(remote(
                a_sum.at[to, :, span], a_cols.at[f, :, span],
                s_send.at[which, d - 1], s_recv.at[which, d - 1], fsdp=to,
            ))
        for copy in mine:
            copy.start()
        a_cols[f, :, span] = a_sum[f, :, span]
        swaps.append(mine)

    def spread_out(which):
        span = spans[which]
        for copy in swaps[which]:
            copy.wait_recv()
        mine = []
        for d in range(chips):
            to = lax.rem(c + d, chips) * 2 + k if d else mate
            pair = [remote(
                a_cols.at[:, :, span], a_out.at[:, e, :, span],
                g_send.at[which, d], g_recv.at[which, d], expert=to,
            )]
            if which:
                pair.append(remote(
                    b_sum, b_out.at[e], g_send.at[2, d], g_recv.at[2, d], expert=to
                ))
            for copy in pair:
                copy.start()
            mine.append(pair)
        spread.append(mine)

    def pass_on(which):
        span = spans[which]
        for d in range(1, chips):
            for copy in spread[which][d]:
                copy.wait_recv()
            source = lax.rem(c + chips - d, chips) * 2 + k
            place = a_out.at[:, source, :, span]
            pair = [remote(
                place, place, w_send.at[which, d - 1], w_recv.at[which, d - 1], expert=mate
            )]
            if which:
                place = b_out.at[source]
                pair.append(remote(
                    place, place, w_send.at[2, d - 1], w_recv.at[2, d - 1], expert=mate
                ))
            for copy in pair:
                copy.start()
            sent.extend(pair)

    stops = [total // 10, total * 3 // 10, total // 2, total * 3 // 5, total * 3 // 4, total]
    lax.fori_loop(0, stops[0], body, 0)
    add_pairs()
    share(0)
    lax.fori_loop(stops[0], stops[1], body, 0)
    for copy in shares[0]:
        copy.wait_recv()
    share(1)
    swap(0)
    lax.fori_loop(stops[1], stops[2], body, 0)
    spread_out(0)
    lax.fori_loop(stops[2], stops[3], body, 0)
    for copy in shares[1]:
        copy.wait_recv()
    swap(1)
    lax.fori_loop(stops[3], stops[4], body, 0)
    spread_out(1)
    lax.fori_loop(stops[4], stops[5], body, 0)
    own_out = [
        pltpu.make_async_copy(a_cols, a_out.at[:, e], own_sem.at[2]),
        pltpu.make_async_copy(b_sum, b_out.at[e], own_sem.at[3]),
    ]
    for copy in own_out:
        copy.start()
    pass_on(0)

    gain = gain_ref[...]
    width = gain.shape[1]
    gain_part[...] = jnp.zeros_like(gain_part)
    pl.when(f < blocks)(lambda: slope_load(0).wait())
    pl.when(f >= blocks)(lambda: slope_load(1).wait())

    def tile(i, carry):
        place = pl.ds(pl.multiple_of(i * height, height), height)
        mine = pl.ds(pl.multiple_of(f * rows + i * height, height), height)
        right = jnp.where(f > 0, right_in[mine, :].astype(F32), 0.0)
        left = jnp.where(f < last, left_in[mine, :].astype(F32), 0.0)
        slope = p_ref[mine, :].astype(F32) + right + left
        x = x_ref[place, :].astype(F32)
        scale = lax.rsqrt(jnp.mean(x * x, axis=-1, keepdims=True) + EPSILON)
        gain_part[0:1, :] += jnp.sum(slope * x * scale, axis=0, keepdims=True)
        slope = slope * gain
        along = jnp.sum(slope * x, axis=-1, keepdims=True) / width
        part = scale * slope - x * (scale * scale * scale * along)
        o_ref[place, :] = (slope_own[place, :] + part).astype(BF)
        return carry

    lax.fori_loop(0, pieces, tile, 0)

    lanes = gains_ref.shape[1]

    def share_of(which):
        return gain_part.at[:, pl.ds(pl.multiple_of(which * lanes, lanes), lanes)]

    to_shards = []
    for d in range(1, line):
        to = lax.rem(f + d, line)
        to_shards.append(remote(
            share_of(to), gain_in.at[d - 1], n_send.at[d - 1], n_recv.at[d - 1], fsdp=to
        ))
    for copy in to_shards:
        copy.start()
    for copy in to_shards:
        copy.wait_recv()
    summed = share_of(f)[...] + gains_ref[...]
    for d in range(1, line):
        summed = summed + gain_in[d - 1]
    gain_own[...] = summed
    to_plane = []
    for d in range(1, planes):
        to_plane.append(remote(
            gain_own, gain_all.at[d - 1], m_send.at[d - 1], m_recv.at[d - 1],
            expert=lax.rem(e + d, planes),
        ))
    for copy in to_plane:
        copy.start()

    pass_on(1)
    for copy in to_plane:
        copy.wait_recv()
    total_gain = gain_own[...]
    for d in range(1, planes):
        total_gain = total_gain + gain_all[d - 1]
    gains_out[...] = total_gain
    for mine in spread:
        for copy in mine[0]:
            copy.wait_recv()
    for copy in sent + own_out:
        copy.wait()
    for mine in spread:
        for copy in sum(mine, []):
            copy.wait_send()
    for copy in to_shards + to_plane + to_mate + sum(shares + swaps, []):
        copy.wait_send()

    def drain(side, start, stop):
        def one(s, carry):
            copy_line(side, True, s).wait_send()
            return carry

        lax.fori_loop(start, stop, one, 0)

    for side, origin in ((0, 0), (1, last)):
        count = ((last - f) if side == 0 else f) * pieces

        @pl.when(f == origin)
        def _(side=side):
            drain(side, last * pieces - ahead, last * pieces)

        @pl.when(f != origin)
        def _(side=side, count=count):
            drain(side, 0, count)


def finish(part, a, b, block, gain, slopes, gains, planes, line, height=32, lag=2):
    group, width = part.shape
    tokens = group // line
    chips, last = planes // 2, line - 1
    items = last * (tokens // height)
    rows, lanes = a.shape[2:]
    share = gains.shape[1]
    vmem = pl.BlockSpec(memory_space=pltpu.VMEM)
    anywhere = pl.BlockSpec(memory_space=pl.ANY)
    sems = pltpu.SemaphoreType.DMA
    return pl.pallas_call(
        functools.partial(finish_kernel, planes, line, height, lag),
        out_shape=(
            shape_of((tokens, width), BF), shape_of(a.shape, BF), shape_of(b.shape, BF),
            shape_of(gains.shape, F32),
        ),
        in_specs=[vmem, anywhere, anywhere, vmem, vmem, anywhere, anywhere, vmem],
        out_specs=(vmem, anywhere, anywhere, vmem),
        scratch_shapes=[
            pltpu.VMEM((group, width), BF), pltpu.VMEM((group, width), BF),
            pltpu.VMEM((line, chips, rows, lanes), BF), pltpu.VMEM((line, chips, rows, lanes), BF),
            pltpu.VMEM((chips - 1, line, rows, lanes), BF),
            pltpu.VMEM((line, rows, lanes), BF), pltpu.VMEM((line, rows, lanes), BF),
            pltpu.VMEM((chips, rows, width), BF), pltpu.VMEM((chips, rows, width), BF),
            pltpu.VMEM((chips - 1, rows, width), BF), pltpu.VMEM((rows, width), BF),
            pltpu.VMEM((8, width), F32), pltpu.VMEM((last, 8, share), F32),
            pltpu.VMEM((8, share), F32), pltpu.VMEM((planes - 1, 8, share), F32),
            sems((2, items)), sems((2, items)), sems((3,)), sems((3,)),
            sems((3, chips - 1)), sems((3, chips - 1)), sems((2, last)), sems((2, last)),
            sems((3, chips)), sems((3, chips)), sems((3, chips - 1)), sems((3, chips - 1)),
            sems((last,)), sems((last,)), sems((planes - 1,)), sems((planes - 1,)),
            sems((5,)), pltpu.VMEM((tokens, width), F32),
        ],
        compiler_params=params(60, collective_id=2, has_side_effects=True),
        cost_estimate=cost(0, 400 * MIB),
        name="finish",
    )(
        part, a.reshape(line, chips, 2, rows, lanes), b.reshape(chips, 2, rows, width), block, gain,
        *slopes, gains,
    )


def swap_plane(rows):
    return lax.all_to_all(rows, "expert", split_axis=0, concat_axis=0, tiled=True)


def small_line_sum(array, line):
    total = array
    for d in range(1, line):
        total = total + lax.ppermute(array, "fsdp", [(i, (i + d) % line) for i in range(line)])
    return total


def as_row(column, second):
    lane = lax.broadcasted_iota(jnp.int32, (column.shape[0], 128), 1)
    return jnp.where(lane == 0, column, second).T[:2, :]


def as_column(row):
    return jnp.broadcast_to(row, (128, row.shape[1])).T


def project_kernel(x_ref, gain_ref, columns_ref, normed_ref, raw_ref, value_ref, squares_ref):
    x = x_ref[...].astype(F32)
    scale = lax.rsqrt(jnp.mean(x * x, axis=-1, keepdims=True) + EPSILON)
    normed = (x * scale * gain_ref[...]).astype(BF)
    normed_ref[...] = normed
    own = value_ref.shape[1]
    query = dot(normed, columns_ref[:, :own])
    key = dot(normed, columns_ref[:, own:2 * own])
    value_ref[...] = dot(normed, columns_ref[:, 2 * own:]).astype(BF)
    raw_ref[:, :own] = query
    raw_ref[:, own:] = key
    squares_ref[...] = as_row(
        jnp.sum(query * query, axis=-1, keepdims=True), jnp.sum(key * key, axis=-1, keepdims=True)
    )


def project(block, gain, columns, tile):
    group, width = block.shape
    own = columns.shape[1] // 3
    rows = lambda count: pl.BlockSpec((tile, count), lambda i: (i, 0))
    return pl.pallas_call(
        project_kernel,
        grid=(group // tile,),
        out_shape=(
            shape_of((group, width), BF), shape_of((group, 2 * own), F32),
            shape_of((group, own), BF), shape_of((2, group), F32),
        ),
        in_specs=[
            rows(width), pl.BlockSpec((1, width), lambda i: (0, 0)),
            pl.BlockSpec((width, 3 * own), lambda i: (0, 0)),
        ],
        out_specs=(rows(width), rows(2 * own), rows(own), pl.BlockSpec((2, tile), lambda i: (0, i))),
        compiler_params=params(48),
        cost_estimate=cost(6 * group * width * own, 14 * group * own),
        name="project",
    )(block, gain, columns)


def scales_of(squares_ref, width):
    scales = lax.rsqrt(squares_ref[...] / width + EPSILON)
    return [as_column(scales[i:i + 1, :]) for i in range(2)]


def turn_kernel(width, raw_ref, squares_ref, gain_ref, cos_ref, sin_ref, q_ref, k_ref):
    own = q_ref.shape[1]
    scales = scales_of(squares_ref, width)
    cosine, sine = cos_ref[...], sin_ref[...]
    for which, out in enumerate((q_ref, k_ref)):
        for j in range(0, own, 128):
            place = slice(which * own + j, which * own + j + 128)
            v = raw_ref[:, place] * scales[which] * gain_ref[:, place]
            out[:, j:j + 128] = (v * cosine + pltpu.roll(v, 64, 1) * sine).astype(BF)


def turn(raw, squares, gain, cosine, sine, width, tile):
    group, double = raw.shape
    own = double // 2
    rows = lambda count: pl.BlockSpec((tile, count), lambda i: (i, 0))
    return pl.pallas_call(
        functools.partial(turn_kernel, width),
        grid=(group // tile,),
        out_shape=(shape_of((group, own), BF),) * 2,
        in_specs=[
            rows(double), pl.BlockSpec((2, tile), lambda i: (0, i)),
            pl.BlockSpec((1, double), lambda i: (0, 0)), rows(128), rows(128),
        ],
        out_specs=(rows(own), rows(own)),
        compiler_params=params(32),
        cost_estimate=cost(20 * group * double, 8 * group * double),
        name="turn",
    )(raw, squares, gain, cosine, sine)


def turn_back_kernel(
    width, dq_ref, dk_ref, raw_ref, squares_ref, gain_ref, cos_ref, sin_ref, dots_ref, grad_ref
):
    own = dq_ref.shape[1]
    scales = scales_of(squares_ref, width)
    cosine, sine = cos_ref[...], sin_ref[...]

    @pl.when(pl.program_id(0) == 0)
    def _():
        grad_ref[...] = jnp.zeros_like(grad_ref)

    dots = []
    for which, slope in enumerate((dq_ref, dk_ref)):
        total = 0.0
        for j in range(0, own, 128):
            place = slice(which * own + j, which * own + j + 128)
            v = slope[:, j:j + 128].astype(F32)
            turned = (v * cosine - pltpu.roll(v, 64, 1) * sine) * raw_ref[:, place]
            total = total + jnp.sum(turned * gain_ref[:, place], axis=-1, keepdims=True)
            grad_ref[:, place] += jnp.sum(turned * scales[which], axis=0, keepdims=True)
        dots.append(total)
    dots_ref[...] = as_row(*dots)


def turn_back(dq, dk, raw, squares, gain, cosine, sine, width, tile):
    group, double = raw.shape
    own = double // 2
    rows = lambda count: pl.BlockSpec((tile, count), lambda i: (i, 0))
    pair = pl.BlockSpec((2, tile), lambda i: (0, i))
    flat = pl.BlockSpec((1, double), lambda i: (0, 0))
    return pl.pallas_call(
        functools.partial(turn_back_kernel, width),
        grid=(group // tile,),
        out_shape=(shape_of((2, group), F32), shape_of((1, double), F32)),
        in_specs=[rows(own), rows(own), rows(double), pair, flat, rows(128), rows(128)],
        out_specs=(pair, flat),
        compiler_params=params(32),
        cost_estimate=cost(20 * group * double, 8 * group * double),
        name="turn_back",
    )(dq, dk, raw, squares, gain, cosine, sine)


def join_kernel(
    width, dq_ref, dk_ref, dv_ref, raw_ref, squares_ref, dots_ref, gain_ref, cos_ref, sin_ref,
    columns_ref, joint_ref, part_ref,
):
    own = dq_ref.shape[1]
    scales = scales_of(squares_ref, width)
    dots = [as_column(dots_ref[i:i + 1, :]) for i in range(2)]
    cosine, sine = cos_ref[...], sin_ref[...]
    for which, slope in enumerate((dq_ref, dk_ref)):
        scale = scales[which]
        factor = scale * scale * scale * dots[which] / width
        for j in range(0, own, 128):
            place = slice(which * own + j, which * own + j + 128)
            v = slope[:, j:j + 128].astype(F32)
            turned = (v * cosine - pltpu.roll(v, 64, 1) * sine) * gain_ref[:, place]
            joint_ref[:, place] = (scale * turned - raw_ref[:, place] * factor).astype(BF)
    joint_ref[:, 2 * own:] = dv_ref[...]
    part_ref[...] = dot_nt(joint_ref[...], columns_ref[...]).astype(BF)


def join_slopes(dq, dk, dv, raw, squares, dots, gain, cosine, sine, columns, tile):
    group, double = raw.shape
    own = double // 2
    width = columns.shape[0]
    rows = lambda count: pl.BlockSpec((tile, count), lambda i: (i, 0))
    pair = pl.BlockSpec((2, tile), lambda i: (0, i))
    flat = pl.BlockSpec((1, double), lambda i: (0, 0))
    return pl.pallas_call(
        functools.partial(join_kernel, width),
        grid=(group // tile,),
        out_shape=(shape_of((group, 3 * own), BF), shape_of((group, width), BF)),
        in_specs=[
            rows(own), rows(own), rows(own), rows(double), pair, pair, flat, rows(128), rows(128),
            pl.BlockSpec((width, 3 * own), lambda i: (0, 0)),
        ],
        out_specs=(rows(3 * own), rows(width)),
        compiler_params=params(48),
        cost_estimate=cost(6 * group * width * own, 8 * group * width),
        name="join_slopes",
    )(dq, dk, dv, raw, squares, dots, gain, cosine, sine, columns)


def allowed_scores(queries, key_rows, start_ref, place_ref, key_place_ref, inv_root):
    scores = dot_nt(key_rows, queries) * (inv_root * LOG2E)
    key_place = key_place_ref[...]
    allowed = (key_place >= start_ref[...]) & (key_place <= place_ref[...])
    return jnp.where(allowed, scores, MASKED)


def attend_kernel(size, q_ref, k_ref, v_ref, start_ref, place_ref, kp_ref, o_ref, log_ref):
    for j in range(q_ref.shape[1] // size):
        at = slice(j * size, (j + 1) * size)
        scores = allowed_scores(
            q_ref[:, at], k_ref[:, at], start_ref, place_ref, kp_ref, size ** (-0.5)
        )
        highest = jnp.max(scores, axis=0, keepdims=True)
        powers = jnp.exp2(scores - highest)
        summed = jnp.sum(powers, axis=0, keepdims=True)
        blended = dot_tn(v_ref[:, at], powers.astype(BF)) / summed
        o_ref[:, at] = blended.T.astype(BF)
        log_ref[j] = highest + jnp.log2(summed)


def attend(query, key, value, start_row, place_row, place_column, heads, tile, together=2):
    group, own_width = query.shape
    size = own_width // heads
    wide = together * size
    whole = pl.BlockSpec((group, wide), lambda h, i: (0, h))
    row = pl.BlockSpec((1, tile), lambda h, i: (0, i))
    return pl.pallas_call(
        functools.partial(attend_kernel, size),
        grid=(heads // together, group // tile),
        out_shape=(shape_of((group, own_width), BF), shape_of((heads, 1, group), F32)),
        in_specs=[
            pl.BlockSpec((tile, wide), lambda h, i: (i, h)), whole, whole, row, row,
            pl.BlockSpec((group, 1), lambda h, i: (0, 0)),
        ],
        out_specs=(
            pl.BlockSpec((tile, wide), lambda h, i: (i, h)),
            pl.BlockSpec((together, 1, tile), lambda h, i: (h, 0, i)),
        ),
        compiler_params=params(58),
        cost_estimate=cost(4 * heads * group * group * size * 4, 8 * group * own_width),
        name="attend",
    )(query, key, value, start_row, place_row, place_column)


def attend_back_kernel(
    size, q_ref, k_ref, v_ref, g_ref, log_ref, start_ref, place_ref, kp_ref,
    dq_ref, dk_ref, dv_ref, dk_sum, dv_sum,
):
    i = pl.program_id(1)
    inv_root = size ** (-0.5)

    @pl.when(i == 0)
    def _():
        dk_sum[...] = jnp.zeros_like(dk_sum)
        dv_sum[...] = jnp.zeros_like(dv_sum)

    for j in range(q_ref.shape[1] // size):
        at = slice(j * size, (j + 1) * size)
        queries, key_rows, slope = q_ref[:, at], k_ref[:, at], g_ref[:, at]
        scores = allowed_scores(queries, key_rows, start_ref, place_ref, kp_ref, inv_root)
        probability = jnp.exp2(scores - log_ref[j])
        prob_slope = dot_nt(v_ref[:, at], slope)
        product = probability * prob_slope
        row_dot = jnp.sum(product, axis=0, keepdims=True)
        score_slope = (product - probability * row_dot).astype(BF)
        dq_ref[:, at] = (dot_tn(key_rows, score_slope) * inv_root).T.astype(BF)
        dk_sum[:, at] += dot(score_slope, queries) * inv_root
        dv_sum[:, at] += dot(probability.astype(BF), slope)

    @pl.when(i == pl.num_programs(1) - 1)
    def _():
        dk_ref[...] = dk_sum[...].astype(BF)
        dv_ref[...] = dv_sum[...].astype(BF)


def attend_back(
    query, key, value, slope, log_total, start_row, place_row, place_column, heads, tile, together=2
):
    group, own_width = query.shape
    size = own_width // heads
    wide = together * size
    whole = pl.BlockSpec((group, wide), lambda h, i: (0, h))
    row = pl.BlockSpec((1, tile), lambda h, i: (0, i))
    tiled = pl.BlockSpec((tile, wide), lambda h, i: (i, h))
    return pl.pallas_call(
        functools.partial(attend_back_kernel, size),
        grid=(heads // together, group // tile),
        out_shape=(shape_of((group, own_width), BF),) * 3,
        in_specs=[
            tiled, whole, whole, tiled, pl.BlockSpec((together, 1, tile), lambda h, i: (h, 0, i)),
            row, row, pl.BlockSpec((group, 1), lambda h, i: (0, 0)),
        ],
        out_specs=(tiled, whole, whole),
        scratch_shapes=[pltpu.VMEM((group, wide), F32)] * 2,
        compiler_params=params(60),
        cost_estimate=cost(10 * heads * group * group * size * 3, 16 * group * own_width),
        name="attend_back",
    )(query, key, value, slope, log_total, start_row, place_row, place_column)


def widen_kernel(own, a_ref, b_ref, query_ref, key_ref, value_ref, out_ref, router_ref):
    line, _, _, rows, _ = a_ref.shape
    for f in range(line):
        for which, o_ref in enumerate((query_ref, key_ref, value_ref)):
            o_ref[:, f * own:(f + 1) * own] = a_ref[
                f, 0, 0, :, which * own:(which + 1) * own
            ].astype(F32)
    out_ref[...] = b_ref[0, 0].astype(F32)
    routing = a_ref[0, 0, 0, :, 3 * own:].astype(F32)
    for f in range(1, line):
        routing = routing + a_ref[f, 0, 0, :, 3 * own:].astype(F32)
    router_ref[...] = routing


def widen(a, b, own):
    line, chips, _, rows, lanes = a.shape
    width = b.shape[-1]
    extra = lanes - 3 * own
    count = 2 * chips * rows
    full, part = shape_of((count, width), F32), shape_of((count, extra), F32)
    wide = pl.BlockSpec((rows, width), lambda i: (i, 0))
    return pl.pallas_call(
        functools.partial(widen_kernel, own),
        grid=(2 * chips,),
        out_shape=(full,) * 4 + (part,),
        in_specs=[
            pl.BlockSpec((line, 1, 1, rows, lanes), lambda i: (0, i // 2, i % 2, 0, 0)),
            pl.BlockSpec((1, 1, rows, width), lambda i: (i // 2, i % 2, 0, 0)),
        ],
        out_specs=(wide,) * 4 + (pl.BlockSpec((rows, extra), lambda i: (i, 0)),),
        compiler_params=params(32),
        cost_estimate=cost(8 * count * width, 24 * count * width),
        name="widen",
    )(a, b)


def joint_grad_kernel(normed_ref, joint_ref, router_ref, o_ref):
    size = joint_ref.shape[1]
    o_ref[:, :size] = dot(normed_ref[...].T, joint_ref[...]).astype(BF)
    o_ref[:, size:] = router_ref[...]


def joint_grad(normed, joint, router):
    group, width = normed.shape
    size, extra = joint.shape[1], router.shape[1]
    tile = 512
    return pl.pallas_call(
        joint_grad_kernel,
        grid=(width // tile,),
        out_shape=shape_of((width, size + extra), BF),
        in_specs=[
            pl.BlockSpec((group, tile), lambda j: (0, j)),
            pl.BlockSpec((group, size), lambda j: (0, 0)),
            pl.BlockSpec((tile, extra), lambda j: (j, 0)),
        ],
        out_specs=pl.BlockSpec((tile, size + extra), lambda j: (j, 0)),
        compiler_params=params(56),
        cost_estimate=cost(2 * group * width * size, 6 * group * width),
        name="joint_grad",
    )(normed, joint, router)


def dispatch_kernel(slots, code_ref, rows_ref, o_ref, select):
    pairs = code_ref.shape[1]

    @pl.when(pl.program_id(1) == 0)
    def _():
        for i in range(pairs):
            row = code_ref[0, i:i + 1, :]
            slot = lax.broadcasted_iota(jnp.int32, (slots, row.shape[1]), 0).astype(F32)
            select[i * slots:(i + 1) * slots, :] = (slot == row).astype(BF)

    chosen = dot(select[...], rows_ref[...]).astype(BF)
    o_ref[...] = chosen.reshape(o_ref.shape)


def dispatch(codes, rows, planes, local, slots):
    chunks, pairs, count = codes.shape
    width = rows.shape[1]
    tile = 512
    return pl.pallas_call(
        functools.partial(dispatch_kernel, slots),
        grid=(chunks, width // tile),
        out_shape=shape_of((planes, local, chunks * slots, width), BF),
        in_specs=[
            pl.BlockSpec((1, pairs, count), lambda k, j: (k, 0, 0)),
            pl.BlockSpec((count, tile), lambda k, j: (k, j)),
        ],
        out_specs=pl.BlockSpec((planes, local, slots, tile), lambda k, j: (0, 0, k, j)),
        scratch_shapes=[pltpu.VMEM((pairs * slots, count), BF)],
        compiler_params=params(48),
        cost_estimate=cost(2 * pairs * slots * chunks * count * width, 4 * pairs * slots * width),
        name="dispatch",
    )(codes, rows)


def combine_kernel(slots, code_ref, rows_ref, o_ref, select):
    pairs = code_ref.shape[2]

    @pl.when(pl.program_id(1) == 0)
    def _():
        total = pairs * slots
        lane = lax.broadcasted_iota(jnp.int32, (pairs, total), 1)
        start = lax.broadcasted_iota(jnp.int32, (pairs, total), 0) * slots
        within = (lane >= start) & (lane < start + slots)
        spread = dot(code_ref[0], within.astype(BF))
        slot = jnp.sum(jnp.where(within, lane - start, 0), axis=0, keepdims=True)
        select[...] = (spread == slot.astype(F32)).astype(BF)

    rows = rows_ref[...].reshape(pairs * slots, rows_ref.shape[-1])
    o_ref[...] = dot(select[...], rows).astype(BF)


def combine(codes, rows, slots):
    planes, local, _, width = rows.shape
    chunks, count, pairs = codes.shape
    tile = 512
    return pl.pallas_call(
        functools.partial(combine_kernel, slots),
        grid=(chunks, width // tile),
        out_shape=shape_of((chunks * count, width), BF),
        in_specs=[
            pl.BlockSpec((1, count, pairs), lambda k, j: (k, 0, 0)),
            pl.BlockSpec((planes, local, slots, tile), lambda k, j: (0, 0, k, j)),
        ],
        out_specs=pl.BlockSpec((count, tile), lambda k, j: (k, j)),
        scratch_shapes=[pltpu.VMEM((count, pairs * slots), BF)],
        compiler_params=params(56),
        cost_estimate=cost(2 * pairs * slots * chunks * count * width, 4 * pairs * slots * width),
        name="combine",
    )(codes, rows)


def expert_kernel(
    halves, x_ref, ca_ref, cb_ref, gate_ref, up_ref, down_ref, router_ref, named_ref, kept_ref,
    weighted_ref, slope_ref, act_ref, gslope_ref, uslope_ref, logit_ref,
):
    width = x_ref.shape[-1]
    x = x_ref[...].reshape(-1, width)
    c = jnp.concatenate(
        [ref[...].reshape(-1, width // 2) for ref in (ca_ref, cb_ref)], axis=1
    ).astype(F32)
    router = router_ref[...]
    logits = dot(x, router)
    powers = jnp.exp(logits - jnp.max(logits, axis=-1, keepdims=True))
    chance = powers / jnp.sum(powers, axis=-1, keepdims=True)
    named = named_ref[0]
    gating = jnp.sum(chance * named, axis=-1, keepdims=True)
    joined = None
    kept = []
    for h in range(halves):
        gate_pre = dot(x, gate_ref[h])
        up_pre = dot(x, up_ref[h])
        squashed = jax.nn.sigmoid(gate_pre)
        swished = gate_pre * squashed
        activation = swished * up_pre
        act_ref[h] = (gating * activation).astype(BF)
        part = dot(activation.astype(BF), down_ref[h])
        joined = part if joined is None else joined + part
        kept.append((up_pre * squashed * (1.0 + gate_pre * (1.0 - squashed)), swished))
    gating_slope = jnp.sum(c * joined, axis=-1, keepdims=True)
    weighted_ref[...] = (gating * joined).astype(BF).reshape(weighted_ref.shape)
    unit_slope = (gating * c).astype(BF)
    logit_slope = (gating_slope * gating * (named - chance)).astype(BF)
    logit_ref[...] = logit_slope[None]
    slope = dot_nt(logit_slope, router)
    for h in range(halves):
        activation_slope = dot_nt(unit_slope, down_ref[h])
        gate_slope = (activation_slope * kept[h][0]).astype(BF)
        up_slope = (activation_slope * kept[h][1]).astype(BF)
        gslope_ref[h] = gate_slope
        uslope_ref[h] = up_slope
        slope = slope + dot_nt(gate_slope, gate_ref[h]) + dot_nt(up_slope, up_ref[h])
    slope_ref[...] = slope.astype(BF).reshape(slope_ref.shape)


def experts(x, cs, at, gates, ups, downs, router, named, halves, kept):
    planes, local, slots, width = x.shape
    hidden = gates.shape[-1]
    sources = max(1, 448 // slots)
    tile = sources * slots
    steps = planes // sources
    count = planes * slots
    expert_total = router.shape[1]
    units = local * halves
    row_spec = pl.BlockSpec((sources, 1, slots, width), lambda n, t: (t, n, 0, 0))
    half_spec = pl.BlockSpec((sources, 1, slots, width // 2), lambda n, t: (t, n, at, 0))
    unit_spec = pl.BlockSpec((halves, tile, hidden), lambda n, t: (n, t, 0))
    once = pl.Buffered(1)
    wide = pl.BlockSpec((halves, width, hidden), lambda n, t: (n, 0, 0), pipeline_mode=once)
    tall = pl.BlockSpec((halves, hidden, width), lambda n, t: (n, 0, 0), pipeline_mode=once)
    return pl.pallas_call(
        functools.partial(expert_kernel, halves),
        grid=(local, steps),
        out_shape=(
            shape_of((planes, local, CHUNKS * slots, width), BF), shape_of(x.shape, BF),
            shape_of((units, count, hidden), BF), shape_of((units, count, hidden), BF),
            shape_of((units, count, hidden), BF), shape_of((local, count, expert_total), BF),
        ),
        in_specs=[
            row_spec, half_spec, half_spec, wide, wide, tall,
            pl.BlockSpec((width, expert_total), lambda n, t: (0, 0)),
            pl.BlockSpec((1, 1, expert_total), lambda n, t: (n, 0, 0)),
            pl.BlockSpec(memory_space=pl.ANY),
        ],
        out_specs=(
            pl.BlockSpec((sources, 1, slots, width), lambda n, t: (t, n, at, 0)), row_spec, unit_spec, unit_spec, unit_spec,
            pl.BlockSpec((1, tile, expert_total), lambda n, t: (n, t, 0)),
        ),
        input_output_aliases={8: 0} if at else {},
        compiler_params=params(62),
        cost_estimate=cost(12 * units * count * hidden * width, 10 * local * count * width),
        name="experts",
    )(x, *cs, gates, ups, downs, router, named, kept)


def wide_grad_kernel(
    x0_ref, x1_ref, g0_ref, g1_ref, u0_ref, u1_ref, l0_ref, l1_ref, dg_ref, du_ref, dr_ref
):
    tile = x0_ref.shape[-1]
    x0 = x0_ref[...].reshape(-1, tile).T
    x1 = x1_ref[...].reshape(-1, tile).T
    dg_ref[0] = dot(x0, g0_ref[0]) + dot(x1, g1_ref[0])
    du_ref[0] = dot(x0, u0_ref[0]) + dot(x1, u1_ref[0])
    dr_ref[0] = dot(x0, l0_ref[0]) + dot(x1, l1_ref[0])


def wide_grad(xs, gslopes, uslopes, logit_slopes, halves):
    planes, local, slots, width = xs[0].shape
    units, count, hidden = gslopes[0].shape
    tile = 1024 if planes * slots <= 1024 else 512
    x_spec = pl.BlockSpec((planes, 1, slots, tile), lambda u, j: (0, u // halves, 0, j))
    s_spec = pl.BlockSpec((1, count, hidden), lambda u, j: (u, 0, 0))
    o_spec = pl.BlockSpec((1, tile, hidden), lambda u, j: (u, j, 0))
    out = shape_of((units, width, hidden), F32)
    experts_all = logit_slopes[0].shape[2]
    return pl.pallas_call(
        wide_grad_kernel,
        grid=(units, width // tile),
        out_shape=(out, out, shape_of((local, width, experts_all), F32)),
        in_specs=[x_spec] * 2
        + [s_spec] * 4
        + [pl.BlockSpec((1, count, experts_all), lambda u, j: (u // halves, 0, 0))] * 2,
        out_specs=(
            o_spec, o_spec, pl.BlockSpec((1, tile, experts_all), lambda u, j: (u // halves, j, 0)),
        ),
        compiler_params=params(60),
        cost_estimate=cost(8 * units * count * hidden * width, 8 * units * hidden * width),
        name="wide_grad",
    )(*xs, *gslopes, *uslopes, *logit_slopes)


def down_grad_kernel(a0_ref, a1_ref, ca_ref, cb_ref, d_ref):
    tile, slots = ca_ref.shape[-1], ca_ref.shape[2] // 2

    def part(c_ref):
        d_ref[0] = dot(a0_ref[0].T, c_ref[:, :, :slots].reshape(-1, tile)) + dot(
            a1_ref[0].T, c_ref[:, :, slots:].reshape(-1, tile)
        )

    first = pl.program_id(1) < pl.num_programs(1) // 2
    pl.when(first)(lambda: part(ca_ref))
    pl.when(jnp.logical_not(first))(lambda: part(cb_ref))


def down_grad(acts, cs, halves):
    planes, local, double, half = cs[0].shape
    units, count, hidden = acts[0].shape
    tile = half if planes * double <= 2048 else 512
    steps = half // tile
    a_spec = pl.BlockSpec((1, count, hidden), lambda u, j: (u, 0, 0))
    shape = (planes, 1, double, tile)
    return pl.pallas_call(
        down_grad_kernel,
        grid=(units, 2 * steps),
        out_shape=shape_of((units, hidden, 2 * half), F32),
        in_specs=[
            a_spec, a_spec,
            pl.BlockSpec(shape, lambda u, j: (0, u // halves, 0, jnp.minimum(j, steps - 1))),
            pl.BlockSpec(shape, lambda u, j: (0, u // halves, 0, jnp.maximum(j - steps, 0))),
        ],
        out_specs=pl.BlockSpec((1, hidden, tile), lambda u, j: (u, 0, j)),
        compiler_params=params(60),
        cost_estimate=cost(8 * units * count * hidden * half, 8 * units * hidden * half),
        name="down_grad",
    )(*acts, *cs)


def per_device(
    inputs,
    query_weight,
    key_weight,
    value_weight,
    output_weight,
    router_weight,
    first_gain,
    query_gain,
    key_gain,
    second_gain,
    gate_weight,
    up_weight,
    down_weight,
    routes,
    lengths,
    dealing,
    cotangent,
):
    planes, line = lax.axis_size("expert"), lax.axis_size("fsdp")
    plane_at, line_at = lax.axis_index("expert"), lax.axis_index("fsdp")
    tokens, width = inputs.shape
    group = line * tokens
    own_heads = HEADS // line
    head_size = width // HEADS
    own_width = own_heads * head_size
    weight_rows = query_weight.shape[0]
    slice_rows = weight_rows // planes
    units = gate_weight.shape[0]
    local = max(1, units // 2)
    halves = units // local
    expert_count = router_weight.shape[1]
    blocks = line // CHUNKS
    chunk_rows = blocks * tokens
    slots = blocks * CAP

    def own_slice(weight):
        return lax.dynamic_slice_in_dim(weight, plane_at * slice_rows, slice_rows, 0)

    sent = jnp.stack([own_slice(w) for w in (query_weight, key_weight, value_weight)], axis=1)
    sent = jnp.moveaxis(sent.reshape(slice_rows, 3, line, own_width), 2, 0)
    sent = sent.reshape(line, slice_rows, 3 * own_width)
    top_count = routes.shape[1]
    packed = [router_weight, first_gain, second_gain, routes.astype(BF)]
    sizes = [array.size for array in packed]
    fill = -sum(sizes) % (16 * 128)
    small = jnp.concatenate([array.reshape(-1) for array in packed] + [jnp.zeros((fill,), BF)])
    block_in, first_half, small_all, columns, _ = gather_start(
        inputs, cotangent, small.reshape(-1, 128), sent, planes, line
    )
    columns = columns.reshape(width, 3 * own_width)
    small_all = small_all.reshape(line, -1)
    ends = [sum(sizes[:i]) for i in range(5)]
    full_router, gain_first, gain_second, routes_all = (
        small_all[:, ends[i]:ends[i + 1]] for i in range(4)
    )
    full_router = full_router.reshape(width, expert_count)
    gain_first, gain_second = (g.reshape(width).astype(F32) for g in (gain_first, gain_second))
    routes_all = routes_all.reshape(line, tokens, top_count).astype(jnp.int32)
    later, _ = lax.optimization_barrier((cotangent, block_in))
    second_half = lax.all_gather(later[:, width // 2:], "fsdp", axis=0, tiled=True)
    incoming = [first_half, second_half]

    seq_start, positions = places(lengths[0], dealing)
    start_row, place_row, place_column = seq_start[None, :], dealing[None, :], dealing[:, None]
    cosine, sine = angles(positions, head_size)
    per_plane = expert_count // planes
    first_local = (line_at * units) // 2
    member = jnp.sum(
        (routes_all[..., None] == jnp.arange(expert_count, dtype=jnp.int32)).astype(F32), axis=2
    )
    earlier = jnp.tril(jnp.ones((tokens, tokens), BF), -1)
    rank = contract("ts,bse->bte", earlier, member.astype(BF))
    rank = rank + ((jnp.arange(line) % blocks) * CAP).astype(F32)[:, None, None]
    coded = jnp.where(member > 0, rank, -1.0).reshape(line, tokens, planes, per_plane)
    coded = lax.dynamic_slice_in_dim(coded, first_local, local, 3)
    coded = coded.reshape(CHUNKS, chunk_rows, planes * local)
    by_token = coded.astype(BF)
    by_pair = jnp.swapaxes(coded, 1, 2)

    def chunk(array, k):
        return lax.slice_in_dim(array, k * chunk_rows, (k + 1) * chunk_rows)

    rows = dispatch(by_pair, incoming[0], planes, local, slots)
    normed_low, raw, value_low, squares = project(block_in, gain_first[None], columns, tokens)
    squares = small_line_sum(squares, line)
    both_gains = jnp.concatenate([query_gain, key_gain])[None].astype(F32)
    rotary = (jnp.concatenate([cosine, cosine], -1), jnp.concatenate([-sine, sine], -1))
    query_low, key_low = turn(raw, squares, both_gains, *rotary, width, tokens)
    blended, log_total = attend(
        query_low, key_low, value_low, start_row, place_row, place_column, own_heads, tokens
    )
    attention_part = dot(blended, output_weight).astype(BF)

    named = (
        (((plane_at * line + line_at) * units) // 2 + jnp.arange(local))[:, None, None]
        == jnp.arange(expert_count)
    ).astype(F32)
    attention_parts = [chunk(attention_part, k) for k in range(CHUNKS)]
    arrived_slopes = [swap_plane(rows)]
    rows = dispatch(by_pair, incoming[1], planes, local, slots)
    held, normed, swapped = hide(
        attention_parts[0], block_in, gain_second[None], rows, 0, line, 4
    )
    arrived_slopes.append(swapped)
    rows = dispatch(by_pair[:1], normed, planes, local, slots)
    held_next, normed, swapped = hide(
        attention_parts[1], block_in, gain_second[None], rows, 1, line, 3
    )
    hidden, arrived = [held, held_next], [swapped]
    rows = dispatch(by_pair[1:], normed, planes, local, slots)
    rows, arrived_slopes[0] = lax.optimization_barrier((rows, arrived_slopes[0]))
    arrived.append(swap_plane(rows))
    weighted = arrived_slopes[0]
    row_slopes, acts, gslopes, uslopes, logit_slopes = [], [], [], [], []
    for k in range(CHUNKS):
        results = experts(
            arrived[k], arrived_slopes, k, gate_weight, up_weight, down_weight, full_router,
            named, halves, weighted,
        )
        weighted = results[0]
        for store, result in zip((row_slopes, acts, gslopes, uslopes, logit_slopes), results[1:]):
            store.append(result)
    returned = []
    behind = arrived[-1]
    for k in range(CHUNKS):
        rows, _ = lax.optimization_barrier((row_slopes[k], behind))
        behind = swap_plane(rows)
        returned.append(behind)

    hidden_slopes, attention_slopes, blended_slopes, second_parts = [], [], [], []
    for k in range(CHUNKS):
        returned[k], _ = lax.optimization_barrier(
            (returned[k], hidden_slopes[0] if k else row_slopes[-1])
        )
        part = combine(by_token[k:k + 1], returned[k], slots)
        if k:
            rows, _ = lax.optimization_barrier((weighted, returned[k]))
            mixed_rows = swap_plane(rows)
        results = hide_back(part, hidden[k], incoming, gain_second[None], k, line)
        for store, result in zip((hidden_slopes, attention_slopes, second_parts), results):
            store.append(result)
    second_gain_grad = second_parts[0] + second_parts[1]
    blended_slope = jnp.concatenate(
        [contract("td,cd->tc", low, output_weight).astype(BF) for low in attention_slopes]
    )
    slopes = attend_back(
        query_low, key_low, value_low, blended_slope, log_total, start_row,
        place_row, place_column, own_heads, tokens,
    )
    dots, gain_grads = turn_back(*slopes[:2], raw, squares, both_gains, *rotary, width, tokens)
    dots = small_line_sum(dots, line)
    mixed_rows, _ = lax.optimization_barrier((mixed_rows, gain_grads))
    mixed = combine(by_token, mixed_rows, slots)
    acts, gslopes, uslopes, logit_slopes, attention_slopes, _ = lax.optimization_barrier(
        (acts, gslopes, uslopes, logit_slopes, attention_slopes, mixed)
    )
    mixed = lax.psum_scatter(mixed, "fsdp", scatter_dimension=0, tiled=True)
    *expert_grads, router_parts = wide_grad(arrived, gslopes, uslopes, logit_slopes, halves)
    expert_grads.append(down_grad(acts, arrived_slopes, halves))
    router_grad = jnp.sum(router_parts, axis=0)
    output_grad = sum(
        contract("tc,td->cd", chunk(blended, k), attention_slopes[k]) for k in range(CHUNKS)
    ).astype(BF)
    dots, _ = lax.optimization_barrier((dots, expert_grads))
    joint, normed_part = join_slopes(
        *slopes, raw, squares, dots, both_gains, *rotary, columns, tokens
    )
    router_lanes = -expert_count % 128
    router_pad = jnp.pad(router_grad.astype(BF), ((0, 0), (0, router_lanes)))
    joint_total = joint_grad(normed_low, joint, router_pad)
    mine = line_at * weight_rows
    second_own = lax.dynamic_slice_in_dim(second_gain_grad, mine, weight_rows, 1)
    gain_rows = jnp.concatenate(
        [
            jnp.zeros((1, weight_rows), F32), second_own, gain_grads.reshape(2, own_width),
            jnp.zeros((4, weight_rows), F32),
        ]
    )
    input_gradient, totals, output_total, gain_totals = finish(
        normed_part, joint_total.reshape(line, planes, slice_rows, -1),
        output_grad.reshape(planes, slice_rows, width), inputs, gain_first[None],
        hidden_slopes, gain_rows, planes, line,
    )
    start = (line_at % blocks) * tokens
    hidden_own = jnp.where(
        line_at < blocks, *(lax.dynamic_slice_in_dim(held, start, tokens, 0) for held in hidden)
    )
    block_output = (hidden_own + mixed.astype(F32)).astype(BF)
    *weight_grads, router_total = widen(
        totals.reshape(line, planes // 2, 2, slice_rows, -1),
        output_total.reshape(planes // 2, 2, slice_rows, width), own_width,
    )
    router_total = router_total[:, :expert_count]
    return (
        block_output,
        input_gradient,
        *weight_grads,
        router_total,
        gain_totals[0],
        gain_totals[2],
        gain_totals[3],
        gain_totals[1],
        *expert_grads,
    )


def solution(mesh):
    both = ("expert", "fsdp")
    rows, cube, shard, gain = P(both, None), P(both, None, None), P("fsdp", None), P("fsdp")
    return jax.shard_map(
        per_device,
        mesh=mesh,
        in_specs=(rows,)
        + (shard,) * 5
        + (gain,) * 4
        + (cube,) * 3
        + (rows, P("expert", None), P("expert"), rows),
        out_specs=(rows, rows) + (shard,) * 5 + (gain,) * 4 + (cube,) * 3,
        check_vma=False,
    )
```

```python
import functools

import jax
import jax.numpy as jnp
from jax import lax
from jax.experimental import pallas as pl
from jax.experimental.pallas import tpu as pltpu
from jax.sharding import PartitionSpec as P

HEADS = 16
CAP = 56
EPSILON = 1e-05
THETA = 10000.0
MASKED = -1e30
LOG2E = 1.4426950408889634
BF = jnp.bfloat16
F32 = jnp.float32
MESH = pl.DeviceIdType.MESH
MIB = 1 << 20
CHUNKS = 2


def dot(a, b):
    return jnp.dot(a, b, preferred_element_type=F32)


def dot_nt(a, b):
    return lax.dot_general(a, b, (((1,), (1,)), ((), ())), preferred_element_type=F32)


def dot_tn(a, b):
    return lax.dot_general(a, b, (((0,), (0,)), ((), ())), preferred_element_type=F32)


def contract(spec, *operands):
    return jnp.einsum(spec, *operands, preferred_element_type=F32)


def shape_of(dims, dtype):
    return jax.ShapeDtypeStruct(dims, dtype)


def cost(flops, moved):
    return pl.CostEstimate(flops=int(flops) // 64, bytes_accessed=int(moved) // 64, transcendentals=0)


def params(mib, **kwargs):
    return pltpu.CompilerParams(vmem_limit_bytes=mib * MIB, **kwargs)


def places(lengths_row, stream):
    seq_ends = jnp.cumsum(lengths_row)
    before = (seq_ends[None, :] <= stream[:, None]).astype(jnp.int32)
    offset = jnp.sum(before * lengths_row[None, :], axis=1)
    return offset, stream - offset


def angles(positions, head_width):
    exponent = jnp.arange(0, head_width, 2).astype(F32) / head_width
    phases = positions.astype(F32)[:, None] * (THETA ** (-exponent))[None, :]
    return jnp.cos(phases), jnp.sin(phases)


def gather_kernel(
    planes, line, pieces, x_ref, c_ref, small_ref, sent_ref,
    x_all, c_all, small_all, columns_ref, swapped_ref,
    x_send, x_recv, s_send, s_recv, z_send, z_recv, p_send, p_recv, own_sem,
):
    e, f = lax.axis_index("expert"), lax.axis_index("fsdp")
    barrier = pltpu.get_barrier_semaphore()
    for d in range(1, line):
        pl.semaphore_signal(
            barrier, inc=1, device_id={"fsdp": lax.rem(f + d, line)}, device_id_type=MESH
        )
    for d in range(1, planes):
        pl.semaphore_signal(
            barrier, inc=1, device_id={"expert": lax.rem(e + d, planes)}, device_id_type=MESH
        )
    pl.semaphore_wait(barrier, line + planes - 2)
    rows = x_ref.shape[0]
    part = rows // pieces
    small_rows = small_ref.shape[0]

    swaps, smalls = [], []
    for d in range(1, line):
        to = lax.rem(f + d, line)
        swaps.append(pltpu.make_async_remote_copy(
            src_ref=sent_ref.at[to], dst_ref=swapped_ref.at[f],
            send_sem=z_send.at[d - 1], recv_sem=z_recv.at[d - 1],
            device_id={"fsdp": to}, device_id_type=MESH,
        ))
        smalls.append(pltpu.make_async_remote_copy(
            src_ref=small_ref, dst_ref=small_all.at[pl.ds(f * small_rows, small_rows)],
            send_sem=s_send.at[d - 1], recv_sem=s_recv.at[d - 1],
            device_id={"fsdp": to}, device_id_type=MESH,
        ))
    for copy in swaps:
        copy.start()

    def hop(direction, step, c):
        own_ref, all_ref = (x_ref, x_all) if c < pieces else (c_ref, c_all)
        origin = f - direction * step
        place = pl.ds(origin * rows + c % pieces * part, part)
        cut = pl.ds(0, all_ref.shape[1])
        source = own_ref.at[pl.ds(c % pieces * part, part), cut] if step == 0 else all_ref.at[place]
        side = 0 if direction == 1 else 1
        return pltpu.make_async_remote_copy(
            src_ref=source, dst_ref=all_ref.at[place],
            send_sem=x_send.at[side, step, c], recv_sem=x_recv.at[side, step, c],
            device_id={"fsdp": f + direction}, device_id_type=MESH,
        )

    def sends(direction, step):
        origin, to = f - direction * step, f + direction
        return (origin >= 0) & (origin < line) & (to >= 0) & (to < line)

    def receives(direction, step):
        origin = f - direction * (step + 1)
        return (origin >= 0) & (origin < line)

    for direction in (1, -1):
        @pl.when(sends(direction, 0))
        def _(direction=direction):
            for c in range(2 * pieces):
                hop(direction, 0, c).start()

    for copy in smalls:
        copy.start()
    locals_ = [
        pltpu.make_async_copy(x_ref, x_all.at[pl.ds(f * rows, rows)], own_sem.at[0]),
        pltpu.make_async_copy(
            c_ref.at[:, pl.ds(0, c_all.shape[1])], c_all.at[pl.ds(f * rows, rows)], own_sem.at[4]
        ),
        pltpu.make_async_copy(
            small_ref, small_all.at[pl.ds(f * small_rows, small_rows)], own_sem.at[1]
        ),
        pltpu.make_async_copy(sent_ref.at[f], swapped_ref.at[f], own_sem.at[2]),
    ]
    for copy in locals_:
        copy.start()
    for copy in swaps:
        copy.wait_recv()
    locals_[3].wait()
    spread = []
    for d in range(1, planes):
        spread.append(pltpu.make_async_remote_copy(
            src_ref=swapped_ref, dst_ref=columns_ref.at[:, e],
            send_sem=p_send.at[d - 1], recv_sem=p_recv.at[d - 1],
            device_id={"expert": lax.rem(e + d, planes)}, device_id_type=MESH,
        ))
        spread[-1].start()
    own = pltpu.make_async_copy(swapped_ref, columns_ref.at[:, e], own_sem.at[3])
    own.start()

    for step in range(line - 1):
        for c in range(2 * pieces):
            for direction in (1, -1):
                @pl.when(receives(direction, step))
                def _(direction=direction, step=step, c=c):
                    origin = f - direction * (step + 1)
                    all_ref = x_all if c < pieces else c_all
                    place = pl.ds(origin * rows + c % pieces * part, part)
                    side = 0 if direction == 1 else 1
                    pltpu.make_async_remote_copy(
                        src_ref=all_ref.at[place], dst_ref=all_ref.at[place],
                        send_sem=x_send.at[side, step, c], recv_sem=x_recv.at[side, step, c],
                        device_id={"fsdp": f - direction}, device_id_type=MESH,
                    ).wait_recv()
                if step < line - 2:
                    @pl.when(sends(direction, step + 1))
                    def _(direction=direction, step=step, c=c):
                        hop(direction, step + 1, c).start()
    for step in range(line - 1):
        for direction in (1, -1):
            @pl.when(sends(direction, step))
            def _(direction=direction, step=step):
                for c in range(2 * pieces):
                    hop(direction, step, c).wait_send()
    for copy in swaps:
        copy.wait_send()
    for copy in smalls + spread:
        copy.wait()
    for copy in locals_[:3] + [own]:
        copy.wait()


def gather_start(block, half, small, sent, planes, line):
    rows, width = block.shape
    pieces = 4
    anywhere = pl.BlockSpec(memory_space=pl.ANY)
    sems = pltpu.SemaphoreType.DMA
    return pl.pallas_call(
        functools.partial(gather_kernel, planes, line, pieces),
        out_shape=(
            shape_of((line * rows, width), BF),
            shape_of((line * rows, half.shape[1] // 2), BF),
            shape_of((line * small.shape[0], small.shape[1]), BF),
            shape_of((line, planes) + sent.shape[1:], BF),
            shape_of(sent.shape, BF),
        ),
        in_specs=[anywhere] * 4,
        out_specs=[anywhere] * 5,
        scratch_shapes=[
            sems((2, line - 1, 2 * pieces)), sems((2, line - 1, 2 * pieces)),
            sems((line - 1,)), sems((line - 1,)), sems((line - 1,)), sems((line - 1,)),
            sems((planes - 1,)), sems((planes - 1,)), sems((5,)),
        ],
        compiler_params=pltpu.CompilerParams(collective_id=0, has_side_effects=True),
        name="gather_start",
    )(block, half, small, sent)


def line_steps(line, pieces, lag, p_ref, o_ref, right_in, left_in, send_sem, recv_sem, complete):
    f = lax.axis_index("fsdp")
    last = line - 1
    part = p_ref.shape[0] // pieces

    def greet():
        barrier = pltpu.get_barrier_semaphore()

        @pl.when(f > 0)
        def _():
            pl.semaphore_signal(barrier, inc=1, device_id={"fsdp": f - 1}, device_id_type=MESH)

        @pl.when(f < last)
        def _():
            pl.semaphore_signal(barrier, inc=1, device_id={"fsdp": f + 1}, device_id_type=MESH)

    neighbours = jnp.where((f > 0) & (f < last), 2, 1)

    def copy(side, source, c):
        buffer = right_in if side == 0 else left_in
        place = pl.ds(c * part, part)
        return pltpu.make_async_remote_copy(
            src_ref=(p_ref if source else buffer).at[place], dst_ref=buffer.at[place],
            send_sem=send_sem.at[side, c], recv_sem=recv_sem.at[side, c],
            device_id={"fsdp": f + 1 if side == 0 else f - 1}, device_id_type=MESH,
        )

    def enter():
        for side in range(2):
            @pl.when(f == (0 if side == 0 else last))
            def _(side=side):
                def one(c, carry):
                    copy(side, True, c).start()
                    return carry

                lax.fori_loop(0, pieces, one, 0)

    def arrive(side, c):
        place = pl.ds(pl.multiple_of(c * part, part), part)
        buffer = right_in if side == 0 else left_in
        origin, end = (0, last) if side == 0 else (last, 0)
        leads = (2 * f <= last) if side == 0 else (2 * f > last)

        @pl.when(f == origin)
        def _():
            o_ref[place, :] = p_ref[place, :].astype(F32)

        @pl.when(f != origin)
        def _():
            copy(side, False, c).wait_recv()
            came = buffer[place, :].astype(F32)

            @pl.when(f != end)
            def _():
                buffer[place, :] = (came + p_ref[place, :].astype(F32)).astype(BF)
                copy(side, False, c).start()

            @pl.when(leads)
            def _():
                o_ref[place, :] = came + p_ref[place, :].astype(F32)

            @pl.when(jnp.logical_not(leads))
            def _():
                o_ref[place, :] += came
                complete(place, c)

    def body(s, carry):
        for side in range(2):
            c = s - lag * (f if side == 0 else last - f)

            @pl.when((c >= 0) & (c < pieces))
            def _(side=side, c=c):
                arrive(side, c)

        return carry

    def drain():
        def one(c, carry):
            @pl.when(f < last)
            def _():
                copy(0, True, c).wait_send()

            @pl.when(f > 0)
            def _():
                copy(1, True, c).wait_send()

            return carry

        lax.fori_loop(0, pieces, one, 0)

    return greet, neighbours, enter, body, drain, pieces + lag * last


def line_scratch(rows, width, pieces):
    return [
        pltpu.VMEM((rows, width), BF),
        pltpu.VMEM((rows, width), BF),
        pltpu.SemaphoreType.DMA((2, pieces)),
        pltpu.SemaphoreType.DMA((2, pieces)),
    ]


def store_pieces(pairs, sems, pieces, height):
    def copies(c):
        place = pl.ds(pl.multiple_of(c * height, height), height)
        return [
            pltpu.make_async_copy(source.at[place], target.at[place], sems.at[i, c])
            for i, (source, target) in enumerate(pairs)
        ]

    def start(c):
        for copy in copies(c):
            copy.start()

    def wait():
        def one(c, carry):
            for copy in copies(c):
                copy.wait()
            return carry

        lax.fori_loop(0, pieces, one, 0)

    return start, wait


def hide_kernel(
    planes, line, pieces, lag, at, p_ref, x_ref, gain_ref, rows_ref, hidden_ref, normed_ref, swapped_ref,
    right_in, left_in, send_sem, recv_sem, w_send, w_recv, own_sem, x_own, total_own, normed_own, store_sem,
):
    e = lax.axis_index("expert")
    rows = p_ref.shape[0]
    load = pltpu.make_async_copy(x_ref.at[pl.ds(at * rows, rows)], x_own, own_sem.at[1])
    load.start()
    start_store, wait_stores = store_pieces(
        [(total_own, hidden_ref), (normed_own, normed_ref)], store_sem, pieces, rows // pieces
    )

    def complete(place, c):
        hidden = x_own[place, :].astype(F32) + total_own[place, :]
        total_own[place, :] = hidden
        scale = lax.rsqrt(jnp.mean(hidden * hidden, axis=-1, keepdims=True) + EPSILON)
        normed_own[place, :] = (hidden * scale * gain_ref[...]).astype(BF)
        start_store(c)

    greet, neighbours, enter, body, drain, total = line_steps(
        line, pieces, lag, p_ref, total_own, right_in, left_in, send_sem, recv_sem, complete
    )
    greet()
    barrier = pltpu.get_barrier_semaphore()
    for d in range(1, planes):
        pl.semaphore_signal(
            barrier, inc=1, device_id={"expert": lax.rem(e + d, planes)}, device_id_type=MESH
        )
    pl.semaphore_wait(barrier, neighbours + planes - 1)
    enter()
    swaps = []
    for d in range(1, planes):
        to = lax.rem(e + d, planes)
        swaps.append(pltpu.make_async_remote_copy(
            src_ref=rows_ref.at[to], dst_ref=swapped_ref.at[e],
            send_sem=w_send.at[d - 1], recv_sem=w_recv.at[d - 1],
            device_id={"expert": to}, device_id_type=MESH,
        ))
    own = pltpu.make_async_copy(rows_ref.at[e], swapped_ref.at[e], own_sem.at[0])
    for copy in swaps + [own]:
        copy.start()
    load.wait()
    lax.fori_loop(0, total, body, 0)
    drain()
    for copy in swaps + [own]:
        copy.wait()
    wait_stores()


def hide(part, block, gain, rows_sent, at, line, identity, height=32, lag=2):
    rows, width = part.shape
    planes = rows_sent.shape[0]
    pieces = rows // height
    sems = pltpu.SemaphoreType.DMA
    anywhere = pl.BlockSpec(memory_space=pl.ANY)
    vmem = pl.BlockSpec(memory_space=pltpu.VMEM)
    return pl.pallas_call(
        functools.partial(hide_kernel, planes, line, pieces, lag, at),
        out_shape=(
            shape_of((rows, width), F32), shape_of((rows, width), BF),
            shape_of(rows_sent.shape, BF),
        ),
        in_specs=[vmem, anywhere, vmem, anywhere],
        out_specs=(anywhere, anywhere, anywhere),
        scratch_shapes=line_scratch(rows, width, pieces)
        + [
            sems((planes - 1,)), sems((planes - 1,)), sems((2,)),
            pltpu.VMEM((rows, width), BF), pltpu.VMEM((rows, width), F32),
            pltpu.VMEM((rows, width), BF), sems((2, pieces)),
        ],
        compiler_params=params(60, collective_id=identity, has_side_effects=True),
        cost_estimate=cost(0, 300 * MIB),
        name="hide",
    )(part, block, gain, rows_sent)


def hide_back_kernel(
    line, pieces, lag, at, p_ref, hidden_ref, ca_ref, cb_ref, gain_ref, total_ref, low_ref, grad_ref,
    right_in, left_in, send_sem, recv_sem, hidden_own, ca_own, cb_own, total_own, low_own, load_sem, store_sem,
):
    rows = p_ref.shape[0]
    half = ca_ref.shape[1]
    mine = pl.ds(at * rows, rows)
    loads = [
        pltpu.make_async_copy(hidden_ref, hidden_own, load_sem.at[0]),
        pltpu.make_async_copy(ca_ref.at[mine], ca_own, load_sem.at[1]),
        pltpu.make_async_copy(cb_ref.at[mine], cb_own, load_sem.at[2]),
    ]
    for copy in loads:
        copy.start()
    start_store, wait_stores = store_pieces(
        [(total_own, total_ref), (low_own, low_ref)], store_sem, pieces, rows // pieces
    )

    def complete(place, c):
        slope, hidden = total_own[place, :], hidden_own[place, :]
        scale = lax.rsqrt(jnp.mean(hidden * hidden, axis=-1, keepdims=True) + EPSILON)
        grad_ref[...] += jnp.sum(slope * hidden * scale, axis=0, keepdims=True)
        slope = slope * gain_ref[...]
        along = jnp.sum(slope * hidden, axis=-1, keepdims=True) / hidden.shape[1]
        part = scale * slope - hidden * (scale * scale * scale * along)
        for ref, lanes in ((ca_own, slice(0, half)), (cb_own, slice(half, 2 * half))):
            total = ref[place, :].astype(F32) + part[:, lanes]
            total_own[place, lanes] = total
            low_own[place, lanes] = total.astype(BF)
        start_store(c)

    greet, neighbours, enter, body, drain, total = line_steps(
        line, pieces, lag, p_ref, total_own, right_in, left_in, send_sem, recv_sem, complete
    )
    greet()
    grad_ref[...] = jnp.zeros_like(grad_ref)
    pl.semaphore_wait(pltpu.get_barrier_semaphore(), neighbours)
    enter()
    for copy in loads:
        copy.wait()
    lax.fori_loop(0, total, body, 0)
    drain()
    wait_stores()


def hide_back(part, hidden, incoming, gain, at, line, height=32, lag=2):
    rows, width = part.shape
    pieces = rows // height
    sems = pltpu.SemaphoreType.DMA
    anywhere = pl.BlockSpec(memory_space=pl.ANY)
    vmem = pl.BlockSpec(memory_space=pltpu.VMEM)
    return pl.pallas_call(
        functools.partial(hide_back_kernel, line, pieces, lag, at),
        out_shape=(
            shape_of((rows, width), F32), shape_of((rows, width), BF), shape_of((1, width), F32),
        ),
        in_specs=[vmem, anywhere, anywhere, anywhere, vmem],
        out_specs=(anywhere, anywhere, vmem),
        scratch_shapes=line_scratch(rows, width, pieces)
        + [
            pltpu.VMEM((rows, width), F32), pltpu.VMEM((rows, width // 2), BF),
            pltpu.VMEM((rows, width // 2), BF), pltpu.VMEM((rows, width), F32),
            pltpu.VMEM((rows, width), BF), sems((3,)), sems((2, pieces)),
        ],
        compiler_params=params(62, collective_id=5 + at, has_side_effects=True),
        cost_estimate=cost(0, 260 * MIB),
        name="hide_back",
    )(part, hidden, *incoming, gain)


def finish_kernel(
    planes, line, height, lag, p_ref, a_ref, b_ref, x_ref, gain_ref, slope0_ref, slope1_ref, gains_ref,
    o_ref, a_out, b_out, gains_out,
    right_in, left_in, a_own, a_half, a_in, a_sum, a_cols, b_own, b_half, b_in, b_sum, gain_part, gain_in, gain_own, gain_all,
    z_send, z_recv, h_send, h_recv, r_send, r_recv, s_send, s_recv, g_send, g_recv,
    w_send, w_recv, n_send, n_recv, m_send, m_recv, own_sem, slope_own,
):
    e, f = lax.axis_index("expert"), lax.axis_index("fsdp")
    chips, last = planes // 2, line - 1
    c, k = e // 2, e % 2
    mate = e + 1 - 2 * k
    barrier = pltpu.get_barrier_semaphore()

    def greet(**device):
        pl.semaphore_signal(barrier, inc=1, device_id=device, device_id_type=MESH)

    for d in range(1, planes):
        greet(expert=lax.rem(e + d, planes))
    for d in range(1, line):
        greet(fsdp=lax.rem(f + d, line))
    pl.semaphore_wait(barrier, planes - 1 + last)

    rows = p_ref.shape[0] // line
    pieces = rows // height
    ahead = 4

    def remote(source, target, send, recv, **device):
        return pltpu.make_async_remote_copy(
            src_ref=source, dst_ref=target, send_sem=send, recv_sem=recv,
            device_id=device, device_id_type=MESH,
        )

    lanes_a = a_ref.shape[-1]
    cut = lanes_a // 128 * 9 // 13 * 128
    spans = (pl.ds(0, cut), pl.ds(cut, lanes_a - cut))

    to_mate = [
        remote(
            a_ref.at[:, :, 1 - k, :, span], a_half.at[:, :, :, span], h_send.at[i], h_recv.at[i],
            expert=mate,
        )
        for i, span in enumerate(spans)
    ]
    to_mate.append(remote(b_ref.at[:, 1 - k], b_half, h_send.at[2], h_recv.at[2], expert=mate))
    own_half = [
        pltpu.make_async_copy(a_ref.at[:, :, k], a_own, own_sem.at[0]),
        pltpu.make_async_copy(b_ref.at[:, k], b_own, own_sem.at[1]),
    ]
    blocks = line // 2

    def slope_load(which):
        source = (slope0_ref, slope1_ref)[which]
        place = pl.ds(pl.multiple_of((f - which * blocks) * rows, rows), rows)
        return pltpu.make_async_copy(source.at[place], slope_own, own_sem.at[4])

    pl.when(f < blocks)(lambda: slope_load(0).start())
    pl.when(f >= blocks)(lambda: slope_load(1).start())
    for copy in to_mate + own_half:
        copy.start()

    def place_of(side, s):
        target = last - s // pieces if side == 0 else s // pieces
        return target, pl.ds(pl.multiple_of(target * rows + lax.rem(s, pieces) * height, height), height)

    def copy_line(side, source, s):
        buffer = right_in if side == 0 else left_in
        place = place_of(side, s)[1]
        return remote(
            (p_ref if source else buffer).at[place], buffer.at[place],
            z_send.at[side, s], z_recv.at[side, s], fsdp=f + 1 if side == 0 else f - 1,
        )

    def begin(side, s):
        @pl.when(s >= ahead)
        def _():
            copy_line(side, True, s - ahead).wait_send()

        copy_line(side, True, s).start()

    def arrive(side, s):
        buffer = right_in if side == 0 else left_in
        target, place = place_of(side, s)
        copy_line(side, False, s).wait_recv()

        @pl.when(target != f)
        def _():
            buffer[place, :] = (buffer[place, :].astype(F32) + p_ref[place, :].astype(F32)).astype(BF)
            copy_line(side, False, s).start()

    def body(s, carry):
        right = s - lag * f
        left = s - lag * (last - f)

        @pl.when((f == 0) & (s < last * pieces))
        def _():
            begin(0, s)

        @pl.when((f == last) & (s < last * pieces))
        def _():
            begin(1, s)

        @pl.when((f > 0) & (right >= 0) & (right < (last - f + 1) * pieces))
        def _():
            arrive(0, right)

        @pl.when((f < last) & (left >= 0) & (left < (f + 1) * pieces))
        def _():
            arrive(1, left)

        return carry

    total = last * pieces + lag * last
    shares, swaps, spread = [], [], []
    sent = []

    def add_pairs():
        for copy in own_half:
            copy.wait()
        for copy in to_mate:
            copy.wait_recv()

        def one(i, carry):
            for j in range(chips):
                a_own[i, j] = (a_own[i, j].astype(F32) + a_half[i, j].astype(F32)).astype(BF)
            return carry

        lax.fori_loop(0, line, one, 0)
        for j in range(chips):
            b_own[j] = (b_own[j].astype(F32) + b_half[j].astype(F32)).astype(BF)

    def share(which):
        span = spans[which]
        mine = []
        for d in range(1, chips):
            to = lax.rem(c + d, chips)
            mine.append(remote(
                a_own.at[:, to, :, span], a_in.at[d - 1, :, :, span],
                r_send.at[which, d - 1], r_recv.at[which, d - 1], expert=to * 2 + k,
            ))
            if which:
                mine.append(remote(
                    b_own.at[to], b_in.at[d - 1], r_send.at[2, d - 1], r_recv.at[2, d - 1],
                    expert=to * 2 + k,
                ))
        for copy in mine:
            copy.start()
        shares.append(mine)

    def swap(which):
        span = spans[which]

        def one(i, carry):
            summed = a_own[i, c, :, span].astype(F32)
            for d in range(1, chips):
                summed = summed + a_in[d - 1, i, :, span].astype(F32)
            a_sum[i, :, span] = summed.astype(BF)
            return carry

        lax.fori_loop(0, line, one, 0)
        if which:
            summed = b_own[c].astype(F32)
            for d in range(1, chips):
                summed = summed + b_in[d - 1].astype(F32)
            b_sum[...] = summed.astype(BF)
        mine = []
        for d in range(1, line):
            to = lax.rem(f + d, line)
            mine.append(remote(
                a_sum.at[to, :, span], a_cols.at[f, :, span],
                s_send.at[which, d - 1], s_recv.at[which, d - 1], fsdp=to,
            ))
        for copy in mine:
            copy.start()
        a_cols[f, :, span] = a_sum[f, :, span]
        swaps.append(mine)

    def spread_out(which):
        span = spans[which]
        for copy in swaps[which]:
            copy.wait_recv()
        mine = []
        for d in range(chips):
            to = lax.rem(c + d, chips) * 2 + k if d else mate
            pair = [remote(
                a_cols.at[:, :, span], a_out.at[:, e, :, span],
                g_send.at[which, d], g_recv.at[which, d], expert=to,
            )]
            if which:
                pair.append(remote(
                    b_sum, b_out.at[e], g_send.at[2, d], g_recv.at[2, d], expert=to
                ))
            for copy in pair:
                copy.start()
            mine.append(pair)
        spread.append(mine)

    def pass_on(which):
        span = spans[which]
        for d in range(1, chips):
            for copy in spread[which][d]:
                copy.wait_recv()
            source = lax.rem(c + chips - d, chips) * 2 + k
            place = a_out.at[:, source, :, span]
            pair = [remote(
                place, place, w_send.at[which, d - 1], w_recv.at[which, d - 1], expert=mate
            )]
            if which:
                place = b_out.at[source]
                pair.append(remote(
                    place, place, w_send.at[2, d - 1], w_recv.at[2, d - 1], expert=mate
                ))
            for copy in pair:
                copy.start()
            sent.extend(pair)

    stops = [total // 10, total * 3 // 10, total // 2, total * 3 // 5, total * 3 // 4, total]
    lax.fori_loop(0, stops[0], body, 0)
    add_pairs()
    share(0)
    lax.fori_loop(stops[0], stops[1], body, 0)
    for copy in shares[0]:
        copy.wait_recv()
    share(1)
    swap(0)
    lax.fori_loop(stops[1], stops[2], body, 0)
    spread_out(0)
    lax.fori_loop(stops[2], stops[3], body, 0)
    for copy in shares[1]:
        copy.wait_recv()
    swap(1)
    lax.fori_loop(stops[3], stops[4], body, 0)
    spread_out(1)
    lax.fori_loop(stops[4], stops[5], body, 0)
    own_out = [
        pltpu.make_async_copy(a_cols, a_out.at[:, e], own_sem.at[2]),
        pltpu.make_async_copy(b_sum, b_out.at[e], own_sem.at[3]),
    ]
    for copy in own_out:
        copy.start()
    pass_on(0)

    gain = gain_ref[...]
    width = gain.shape[1]
    gain_part[...] = jnp.zeros_like(gain_part)
    pl.when(f < blocks)(lambda: slope_load(0).wait())
    pl.when(f >= blocks)(lambda: slope_load(1).wait())

    def tile(i, carry):
        place = pl.ds(pl.multiple_of(i * height, height), height)
        mine = pl.ds(pl.multiple_of(f * rows + i * height, height), height)
        right = jnp.where(f > 0, right_in[mine, :].astype(F32), 0.0)
        left = jnp.where(f < last, left_in[mine, :].astype(F32), 0.0)
        slope = p_ref[mine, :].astype(F32) + right + left
        x = x_ref[place, :].astype(F32)
        scale = lax.rsqrt(jnp.mean(x * x, axis=-1, keepdims=True) + EPSILON)
        gain_part[0:1, :] += jnp.sum(slope * x * scale, axis=0, keepdims=True)
        slope = slope * gain
        along = jnp.sum(slope * x, axis=-1, keepdims=True) / width
        part = scale * slope - x * (scale * scale * scale * along)
        o_ref[place, :] = (slope_own[place, :] + part).astype(BF)
        return carry

    lax.fori_loop(0, pieces, tile, 0)

    lanes = gains_ref.shape[1]

    def share_of(which):
        return gain_part.at[:, pl.ds(pl.multiple_of(which * lanes, lanes), lanes)]

    to_shards = []
    for d in range(1, line):
        to = lax.rem(f + d, line)
        to_shards.append(remote(
            share_of(to), gain_in.at[d - 1], n_send.at[d - 1], n_recv.at[d - 1], fsdp=to
        ))
    for copy in to_shards:
        copy.start()
    for copy in to_shards:
        copy.wait_recv()
    summed = share_of(f)[...] + gains_ref[...]
    for d in range(1, line):
        summed = summed + gain_in[d - 1]
    gain_own[...] = summed
    to_plane = []
    for d in range(1, planes):
        to_plane.append(remote(
            gain_own, gain_all.at[d - 1], m_send.at[d - 1], m_recv.at[d - 1],
            expert=lax.rem(e + d, planes),
        ))
    for copy in to_plane:
        copy.start()

    pass_on(1)
    for copy in to_plane:
        copy.wait_recv()
    total_gain = gain_own[...]
    for d in range(1, planes):
        total_gain = total_gain + gain_all[d - 1]
    gains_out[...] = total_gain
    for mine in spread:
        for copy in mine[0]:
            copy.wait_recv()
    for copy in sent + own_out:
        copy.wait()
    for mine in spread:
        for copy in sum(mine, []):
            copy.wait_send()
    for copy in to_shards + to_plane + to_mate + sum(shares + swaps, []):
        copy.wait_send()

    def drain(side, start, stop):
        def one(s, carry):
            copy_line(side, True, s).wait_send()
            return carry

        lax.fori_loop(start, stop, one, 0)

    for side, origin in ((0, 0), (1, last)):
        count = ((last - f) if side == 0 else f) * pieces

        @pl.when(f == origin)
        def _(side=side):
            drain(side, last * pieces - ahead, last * pieces)

        @pl.when(f != origin)
        def _(side=side, count=count):
            drain(side, 0, count)


def finish(part, a, b, block, gain, slopes, gains, planes, line, height=32, lag=2):
    group, width = part.shape
    tokens = group // line
    chips, last = planes // 2, line - 1
    items = last * (tokens // height)
    rows, lanes = a.shape[2:]
    share = gains.shape[1]
    vmem = pl.BlockSpec(memory_space=pltpu.VMEM)
    anywhere = pl.BlockSpec(memory_space=pl.ANY)
    sems = pltpu.SemaphoreType.DMA
    return pl.pallas_call(
        functools.partial(finish_kernel, planes, line, height, lag),
        out_shape=(
            shape_of((tokens, width), BF), shape_of(a.shape, BF), shape_of(b.shape, BF),
            shape_of(gains.shape, F32),
        ),
        in_specs=[vmem, anywhere, anywhere, vmem, vmem, anywhere, anywhere, vmem],
        out_specs=(vmem, anywhere, anywhere, vmem),
        scratch_shapes=[
            pltpu.VMEM((group, width), BF), pltpu.VMEM((group, width), BF),
            pltpu.VMEM((line, chips, rows, lanes), BF), pltpu.VMEM((line, chips, rows, lanes), BF),
            pltpu.VMEM((chips - 1, line, rows, lanes), BF),
            pltpu.VMEM((line, rows, lanes), BF), pltpu.VMEM((line, rows, lanes), BF),
            pltpu.VMEM((chips, rows, width), BF), pltpu.VMEM((chips, rows, width), BF),
            pltpu.VMEM((chips - 1, rows, width), BF), pltpu.VMEM((rows, width), BF),
            pltpu.VMEM((8, width), F32), pltpu.VMEM((last, 8, share), F32),
            pltpu.VMEM((8, share), F32), pltpu.VMEM((planes - 1, 8, share), F32),
            sems((2, items)), sems((2, items)), sems((3,)), sems((3,)),
            sems((3, chips - 1)), sems((3, chips - 1)), sems((2, last)), sems((2, last)),
            sems((3, chips)), sems((3, chips)), sems((3, chips - 1)), sems((3, chips - 1)),
            sems((last,)), sems((last,)), sems((planes - 1,)), sems((planes - 1,)),
            sems((5,)), pltpu.VMEM((tokens, width), F32),
        ],
        compiler_params=params(60, collective_id=2, has_side_effects=True),
        cost_estimate=cost(0, 400 * MIB),
        name="finish",
    )(
        part, a.reshape(line, chips, 2, rows, lanes), b.reshape(chips, 2, rows, width), block, gain,
        *slopes, gains,
    )


def swap_plane(rows):
    return lax.all_to_all(rows, "expert", split_axis=0, concat_axis=0, tiled=True)


def small_line_sum(array, line):
    total = array
    for d in range(1, line):
        total = total + lax.ppermute(array, "fsdp", [(i, (i + d) % line) for i in range(line)])
    return total


def as_row(column, second):
    lane = lax.broadcasted_iota(jnp.int32, (column.shape[0], 128), 1)
    return jnp.where(lane == 0, column, second).T[:2, :]


def as_column(row):
    return jnp.broadcast_to(row, (128, row.shape[1])).T


def project_kernel(x_ref, gain_ref, columns_ref, normed_ref, raw_ref, value_ref, squares_ref):
    x = x_ref[...].astype(F32)
    scale = lax.rsqrt(jnp.mean(x * x, axis=-1, keepdims=True) + EPSILON)
    normed = (x * scale * gain_ref[...]).astype(BF)
    normed_ref[...] = normed
    own = value_ref.shape[1]
    query = dot(normed, columns_ref[:, :own])
    key = dot(normed, columns_ref[:, own:2 * own])
    value_ref[...] = dot(normed, columns_ref[:, 2 * own:]).astype(BF)
    raw_ref[:, :own] = query
    raw_ref[:, own:] = key
    squares_ref[...] = as_row(
        jnp.sum(query * query, axis=-1, keepdims=True), jnp.sum(key * key, axis=-1, keepdims=True)
    )


def project(block, gain, columns, tile):
    group, width = block.shape
    own = columns.shape[1] // 3
    rows = lambda count: pl.BlockSpec((tile, count), lambda i: (i, 0))
    return pl.pallas_call(
        project_kernel,
        grid=(group // tile,),
        out_shape=(
            shape_of((group, width), BF), shape_of((group, 2 * own), F32),
            shape_of((group, own), BF), shape_of((2, group), F32),
        ),
        in_specs=[
            rows(width), pl.BlockSpec((1, width), lambda i: (0, 0)),
            pl.BlockSpec((width, 3 * own), lambda i: (0, 0)),
        ],
        out_specs=(rows(width), rows(2 * own), rows(own), pl.BlockSpec((2, tile), lambda i: (0, i))),
        compiler_params=params(48),
        cost_estimate=cost(6 * group * width * own, 14 * group * own),
        name="project",
    )(block, gain, columns)


def scales_of(squares_ref, width):
    scales = lax.rsqrt(squares_ref[...] / width + EPSILON)
    return [as_column(scales[i:i + 1, :]) for i in range(2)]


def turn_kernel(width, raw_ref, squares_ref, gain_ref, cos_ref, sin_ref, q_ref, k_ref):
    own = q_ref.shape[1]
    scales = scales_of(squares_ref, width)
    cosine, sine = cos_ref[...], sin_ref[...]
    for which, out in enumerate((q_ref, k_ref)):
        for j in range(0, own, 128):
            place = slice(which * own + j, which * own + j + 128)
            v = raw_ref[:, place] * scales[which] * gain_ref[:, place]
            out[:, j:j + 128] = (v * cosine + pltpu.roll(v, 64, 1) * sine).astype(BF)


def turn(raw, squares, gain, cosine, sine, width, tile):
    group, double = raw.shape
    own = double // 2
    rows = lambda count: pl.BlockSpec((tile, count), lambda i: (i, 0))
    return pl.pallas_call(
        functools.partial(turn_kernel, width),
        grid=(group // tile,),
        out_shape=(shape_of((group, own), BF),) * 2,
        in_specs=[
            rows(double), pl.BlockSpec((2, tile), lambda i: (0, i)),
            pl.BlockSpec((1, double), lambda i: (0, 0)), rows(128), rows(128),
        ],
        out_specs=(rows(own), rows(own)),
        compiler_params=params(32),
        cost_estimate=cost(20 * group * double, 8 * group * double),
        name="turn",
    )(raw, squares, gain, cosine, sine)


def turn_back_kernel(
    width, dq_ref, dk_ref, raw_ref, squares_ref, gain_ref, cos_ref, sin_ref, dots_ref, grad_ref
):
    own = dq_ref.shape[1]
    scales = scales_of(squares_ref, width)
    cosine, sine = cos_ref[...], sin_ref[...]

    @pl.when(pl.program_id(0) == 0)
    def _():
        grad_ref[...] = jnp.zeros_like(grad_ref)

    dots = []
    for which, slope in enumerate((dq_ref, dk_ref)):
        total = 0.0
        for j in range(0, own, 128):
            place = slice(which * own + j, which * own + j + 128)
            v = slope[:, j:j + 128].astype(F32)
            turned = (v * cosine - pltpu.roll(v, 64, 1) * sine) * raw_ref[:, place]
            total = total + jnp.sum(turned * gain_ref[:, place], axis=-1, keepdims=True)
            grad_ref[:, place] += jnp.sum(turned * scales[which], axis=0, keepdims=True)
        dots.append(total)
    dots_ref[...] = as_row(*dots)


def turn_back(dq, dk, raw, squares, gain, cosine, sine, width, tile):
    group, double = raw.shape
    own = double // 2
    rows = lambda count: pl.BlockSpec((tile, count), lambda i: (i, 0))
    pair = pl.BlockSpec((2, tile), lambda i: (0, i))
    flat = pl.BlockSpec((1, double), lambda i: (0, 0))
    return pl.pallas_call(
        functools.partial(turn_back_kernel, width),
        grid=(group // tile,),
        out_shape=(shape_of((2, group), F32), shape_of((1, double), F32)),
        in_specs=[rows(own), rows(own), rows(double), pair, flat, rows(128), rows(128)],
        out_specs=(pair, flat),
        compiler_params=params(32),
        cost_estimate=cost(20 * group * double, 8 * group * double),
        name="turn_back",
    )(dq, dk, raw, squares, gain, cosine, sine)


def join_kernel(
    width, dq_ref, dk_ref, dv_ref, raw_ref, squares_ref, dots_ref, gain_ref, cos_ref, sin_ref,
    columns_ref, joint_ref, part_ref,
):
    own = dq_ref.shape[1]
    scales = scales_of(squares_ref, width)
    dots = [as_column(dots_ref[i:i + 1, :]) for i in range(2)]
    cosine, sine = cos_ref[...], sin_ref[...]
    for which, slope in enumerate((dq_ref, dk_ref)):
        scale = scales[which]
        factor = scale * scale * scale * dots[which] / width
        for j in range(0, own, 128):
            place = slice(which * own + j, which * own + j + 128)
            v = slope[:, j:j + 128].astype(F32)
            turned = (v * cosine - pltpu.roll(v, 64, 1) * sine) * gain_ref[:, place]
            joint_ref[:, place] = (scale * turned - raw_ref[:, place] * factor).astype(BF)
    joint_ref[:, 2 * own:] = dv_ref[...]
    part_ref[...] = dot_nt(joint_ref[...], columns_ref[...]).astype(BF)


def join_slopes(dq, dk, dv, raw, squares, dots, gain, cosine, sine, columns, tile):
    group, double = raw.shape
    own = double // 2
    width = columns.shape[0]
    rows = lambda count: pl.BlockSpec((tile, count), lambda i: (i, 0))
    pair = pl.BlockSpec((2, tile), lambda i: (0, i))
    flat = pl.BlockSpec((1, double), lambda i: (0, 0))
    return pl.pallas_call(
        functools.partial(join_kernel, width),
        grid=(group // tile,),
        out_shape=(shape_of((group, 3 * own), BF), shape_of((group, width), BF)),
        in_specs=[
            rows(own), rows(own), rows(own), rows(double), pair, pair, flat, rows(128), rows(128),
            pl.BlockSpec((width, 3 * own), lambda i: (0, 0)),
        ],
        out_specs=(rows(3 * own), rows(width)),
        compiler_params=params(48),
        cost_estimate=cost(6 * group * width * own, 8 * group * width),
        name="join_slopes",
    )(dq, dk, dv, raw, squares, dots, gain, cosine, sine, columns)


def allowed_scores(queries, key_rows, start_ref, place_ref, key_place_ref, inv_root):
    scores = dot_nt(key_rows, queries) * (inv_root * LOG2E)
    key_place = key_place_ref[...]
    allowed = (key_place >= start_ref[...]) & (key_place <= place_ref[...])
    return jnp.where(allowed, scores, MASKED)


def attend_kernel(size, q_ref, k_ref, v_ref, start_ref, place_ref, kp_ref, o_ref, log_ref):
    for j in range(q_ref.shape[1] // size):
        at = slice(j * size, (j + 1) * size)
        scores = allowed_scores(
            q_ref[:, at], k_ref[:, at], start_ref, place_ref, kp_ref, size ** (-0.5)
        )
        highest = jnp.max(scores, axis=0, keepdims=True)
        powers = jnp.exp2(scores - highest)
        summed = jnp.sum(powers, axis=0, keepdims=True)
        blended = dot_tn(v_ref[:, at], powers.astype(BF)) / summed
        o_ref[:, at] = blended.T.astype(BF)
        log_ref[j] = highest + jnp.log2(summed)


def attend(query, key, value, start_row, place_row, place_column, heads, tile, together=2):
    group, own_width = query.shape
    size = own_width // heads
    wide = together * size
    whole = pl.BlockSpec((group, wide), lambda h, i: (0, h))
    row = pl.BlockSpec((1, tile), lambda h, i: (0, i))
    return pl.pallas_call(
        functools.partial(attend_kernel, size),
        grid=(heads // together, group // tile),
        out_shape=(shape_of((group, own_width), BF), shape_of((heads, 1, group), F32)),
        in_specs=[
            pl.BlockSpec((tile, wide), lambda h, i: (i, h)), whole, whole, row, row,
            pl.BlockSpec((group, 1), lambda h, i: (0, 0)),
        ],
        out_specs=(
            pl.BlockSpec((tile, wide), lambda h, i: (i, h)),
            pl.BlockSpec((together, 1, tile), lambda h, i: (h, 0, i)),
        ),
        compiler_params=params(58),
        cost_estimate=cost(4 * heads * group * group * size * 4, 8 * group * own_width),
        name="attend",
    )(query, key, value, start_row, place_row, place_column)


def attend_back_kernel(
    size, q_ref, k_ref, v_ref, g_ref, log_ref, start_ref, place_ref, kp_ref,
    dq_ref, dk_ref, dv_ref, dk_sum, dv_sum,
):
    i = pl.program_id(1)
    inv_root = size ** (-0.5)

    @pl.when(i == 0)
    def _():
        dk_sum[...] = jnp.zeros_like(dk_sum)
        dv_sum[...] = jnp.zeros_like(dv_sum)

    for j in range(q_ref.shape[1] // size):
        at = slice(j * size, (j + 1) * size)
        queries, key_rows, slope = q_ref[:, at], k_ref[:, at], g_ref[:, at]
        scores = allowed_scores(queries, key_rows, start_ref, place_ref, kp_ref, inv_root)
        probability = jnp.exp2(scores - log_ref[j])
        prob_slope = dot_nt(v_ref[:, at], slope)
        product = probability * prob_slope
        row_dot = jnp.sum(product, axis=0, keepdims=True)
        score_slope = (product - probability * row_dot).astype(BF)
        dq_ref[:, at] = (dot_tn(key_rows, score_slope) * inv_root).T.astype(BF)
        dk_sum[:, at] += dot(score_slope, queries) * inv_root
        dv_sum[:, at] += dot(probability.astype(BF), slope)

    @pl.when(i == pl.num_programs(1) - 1)
    def _():
        dk_ref[...] = dk_sum[...].astype(BF)
        dv_ref[...] = dv_sum[...].astype(BF)


def attend_back(
    query, key, value, slope, log_total, start_row, place_row, place_column, heads, tile, together=2
):
    group, own_width = query.shape
    size = own_width // heads
    wide = together * size
    whole = pl.BlockSpec((group, wide), lambda h, i: (0, h))
    row = pl.BlockSpec((1, tile), lambda h, i: (0, i))
    tiled = pl.BlockSpec((tile, wide), lambda h, i: (i, h))
    return pl.pallas_call(
        functools.partial(attend_back_kernel, size),
        grid=(heads // together, group // tile),
        out_shape=(shape_of((group, own_width), BF),) * 3,
        in_specs=[
            tiled, whole, whole, tiled, pl.BlockSpec((together, 1, tile), lambda h, i: (h, 0, i)),
            row, row, pl.BlockSpec((group, 1), lambda h, i: (0, 0)),
        ],
        out_specs=(tiled, whole, whole),
        scratch_shapes=[pltpu.VMEM((group, wide), F32)] * 2,
        compiler_params=params(60),
        cost_estimate=cost(10 * heads * group * group * size * 3, 16 * group * own_width),
        name="attend_back",
    )(query, key, value, slope, log_total, start_row, place_row, place_column)


def widen_kernel(own, a_ref, b_ref, query_ref, key_ref, value_ref, out_ref, router_ref):
    line, _, _, rows, _ = a_ref.shape
    for f in range(line):
        for which, o_ref in enumerate((query_ref, key_ref, value_ref)):
            o_ref[:, f * own:(f + 1) * own] = a_ref[
                f, 0, 0, :, which * own:(which + 1) * own
            ].astype(F32)
    out_ref[...] = b_ref[0, 0].astype(F32)
    routing = a_ref[0, 0, 0, :, 3 * own:].astype(F32)
    for f in range(1, line):
        routing = routing + a_ref[f, 0, 0, :, 3 * own:].astype(F32)
    router_ref[...] = routing


def widen(a, b, own):
    line, chips, _, rows, lanes = a.shape
    width = b.shape[-1]
    extra = lanes - 3 * own
    count = 2 * chips * rows
    full, part = shape_of((count, width), F32), shape_of((count, extra), F32)
    wide = pl.BlockSpec((rows, width), lambda i: (i, 0))
    return pl.pallas_call(
        functools.partial(widen_kernel, own),
        grid=(2 * chips,),
        out_shape=(full,) * 4 + (part,),
        in_specs=[
            pl.BlockSpec((line, 1, 1, rows, lanes), lambda i: (0, i // 2, i % 2, 0, 0)),
            pl.BlockSpec((1, 1, rows, width), lambda i: (i // 2, i % 2, 0, 0)),
        ],
        out_specs=(wide,) * 4 + (pl.BlockSpec((rows, extra), lambda i: (i, 0)),),
        compiler_params=params(32),
        cost_estimate=cost(8 * count * width, 24 * count * width),
        name="widen",
    )(a, b)


def joint_grad_kernel(normed_ref, joint_ref, router_ref, o_ref):
    size = joint_ref.shape[1]
    o_ref[:, :size] = dot(normed_ref[...].T, joint_ref[...]).astype(BF)
    o_ref[:, size:] = router_ref[...]


def joint_grad(normed, joint, router):
    group, width = normed.shape
    size, extra = joint.shape[1], router.shape[1]
    tile = 512
    return pl.pallas_call(
        joint_grad_kernel,
        grid=(width // tile,),
        out_shape=shape_of((width, size + extra), BF),
        in_specs=[
            pl.BlockSpec((group, tile), lambda j: (0, j)),
            pl.BlockSpec((group, size), lambda j: (0, 0)),
            pl.BlockSpec((tile, extra), lambda j: (j, 0)),
        ],
        out_specs=pl.BlockSpec((tile, size + extra), lambda j: (j, 0)),
        compiler_params=params(56),
        cost_estimate=cost(2 * group * width * size, 6 * group * width),
        name="joint_grad",
    )(normed, joint, router)


def dispatch_kernel(code_ref, rows_ref, o_ref, select):
    pairs = code_ref.shape[1]
    blocks, _, tokens = select.shape
    tile = rows_ref.shape[1]

    @pl.when(pl.program_id(1) == 0)
    def _():
        for b in range(blocks):
            row = code_ref[0, :, b * tokens:(b + 1) * tokens][:, None, :]
            slot = lax.broadcasted_iota(jnp.int32, (pairs, CAP, tokens), 1) + b * CAP
            chosen = jnp.where(slot.astype(F32) == row, 1.0, 0.0)
            select[b] = chosen.reshape(pairs * CAP, tokens).astype(BF)

    parts = [
        dot(select[b], rows_ref[b * tokens:(b + 1) * tokens, :]).reshape(pairs, CAP, tile)
        for b in range(blocks)
    ]
    o_ref[...] = jnp.concatenate(parts, axis=1).astype(BF).reshape(o_ref.shape)


def dispatch(codes, rows, planes, local, slots):
    chunks, pairs, count = codes.shape
    width = rows.shape[1]
    tile = 512
    return pl.pallas_call(
        dispatch_kernel,
        grid=(chunks, width // tile),
        out_shape=shape_of((planes, local, chunks * slots, width), BF),
        in_specs=[
            pl.BlockSpec((1, pairs, count), lambda k, j: (k, 0, 0)),
            pl.BlockSpec((count, tile), lambda k, j: (k, j)),
        ],
        out_specs=pl.BlockSpec((planes, local, slots, tile), lambda k, j: (0, 0, k, j)),
        scratch_shapes=[pltpu.VMEM((slots // CAP, pairs * CAP, count * CAP // slots), BF)],
        compiler_params=params(48),
        cost_estimate=cost(2 * pairs * slots * chunks * count * width, 4 * pairs * slots * width),
        name="dispatch",
    )(codes, rows)


def combine_kernel(slots, code_ref, rows_ref, o_ref, select):
    pairs = code_ref.shape[2]

    @pl.when(pl.program_id(1) == 0)
    def _():
        total = pairs * slots
        lane = lax.broadcasted_iota(jnp.int32, (pairs, total), 1)
        start = lax.broadcasted_iota(jnp.int32, (pairs, total), 0) * slots
        within = (lane >= start) & (lane < start + slots)
        spread = dot(code_ref[0], within.astype(BF))
        slot = jnp.sum(jnp.where(within, lane - start, 0), axis=0, keepdims=True)
        select[...] = (spread == slot.astype(F32)).astype(BF)

    rows = rows_ref[...].reshape(pairs * slots, rows_ref.shape[-1])
    o_ref[...] = dot(select[...], rows).astype(BF)


def combine(codes, rows, slots):
    planes, local, _, width = rows.shape
    chunks, count, pairs = codes.shape
    tile = 512
    return pl.pallas_call(
        functools.partial(combine_kernel, slots),
        grid=(chunks, width // tile),
        out_shape=shape_of((chunks * count, width), BF),
        in_specs=[
            pl.BlockSpec((1, count, pairs), lambda k, j: (k, 0, 0)),
            pl.BlockSpec((planes, local, slots, tile), lambda k, j: (0, 0, k, j)),
        ],
        out_specs=pl.BlockSpec((count, tile), lambda k, j: (k, j)),
        scratch_shapes=[pltpu.VMEM((count, pairs * slots), BF)],
        compiler_params=params(56),
        cost_estimate=cost(2 * pairs * slots * chunks * count * width, 4 * pairs * slots * width),
        name="combine",
    )(codes, rows)


def expert_kernel(
    halves, x_ref, ca_ref, cb_ref, gate_ref, up_ref, down_ref, router_ref, named_ref, kept_ref,
    weighted_ref, slope_ref, act_ref, gslope_ref, uslope_ref, logit_ref,
):
    width = x_ref.shape[-1]
    x = x_ref[...].reshape(-1, width)
    c = jnp.concatenate(
        [ref[...].reshape(-1, width // 2) for ref in (ca_ref, cb_ref)], axis=1
    ).astype(F32)
    router = router_ref[...]
    logits = dot(x, router)
    powers = jnp.exp(logits - jnp.max(logits, axis=-1, keepdims=True))
    chance = powers / jnp.sum(powers, axis=-1, keepdims=True)
    named = named_ref[0]
    gating = jnp.sum(chance * named, axis=-1, keepdims=True)
    joined = None
    kept = []
    for h in range(halves):
        gate_pre = dot(x, gate_ref[h])
        up_pre = dot(x, up_ref[h])
        squashed = jax.nn.sigmoid(gate_pre)
        swished = gate_pre * squashed
        activation = swished * up_pre
        act_ref[h] = (gating * activation).astype(BF)
        part = dot(activation.astype(BF), down_ref[h])
        joined = part if joined is None else joined + part
        kept.append((up_pre * squashed * (1.0 + gate_pre * (1.0 - squashed)), swished))
    gating_slope = jnp.sum(c * joined, axis=-1, keepdims=True)
    weighted_ref[...] = (gating * joined).astype(BF).reshape(weighted_ref.shape)
    unit_slope = (gating * c).astype(BF)
    logit_slope = (gating_slope * gating * (named - chance)).astype(BF)
    logit_ref[...] = logit_slope[None]
    slope = dot_nt(logit_slope, router)
    for h in range(halves):
        activation_slope = dot_nt(unit_slope, down_ref[h])
        gate_slope = (activation_slope * kept[h][0]).astype(BF)
        up_slope = (activation_slope * kept[h][1]).astype(BF)
        gslope_ref[h] = gate_slope
        uslope_ref[h] = up_slope
        slope = slope + dot_nt(gate_slope, gate_ref[h]) + dot_nt(up_slope, up_ref[h])
    slope_ref[...] = slope.astype(BF).reshape(slope_ref.shape)


def experts(x, cs, at, gates, ups, downs, router, named, halves, kept):
    planes, local, slots, width = x.shape
    hidden = gates.shape[-1]
    sources = max(1, 448 // slots)
    tile = sources * slots
    steps = planes // sources
    count = planes * slots
    expert_total = router.shape[1]
    units = local * halves
    row_spec = pl.BlockSpec((sources, 1, slots, width), lambda n, t: (t, n, 0, 0))
    half_spec = pl.BlockSpec((sources, 1, slots, width // 2), lambda n, t: (t, n, at, 0))
    unit_spec = pl.BlockSpec((halves, tile, hidden), lambda n, t: (n, t, 0))
    once = pl.Buffered(1)
    wide = pl.BlockSpec((halves, width, hidden), lambda n, t: (n, 0, 0), pipeline_mode=once)
    tall = pl.BlockSpec((halves, hidden, width), lambda n, t: (n, 0, 0), pipeline_mode=once)
    return pl.pallas_call(
        functools.partial(expert_kernel, halves),
        grid=(local, steps),
        out_shape=(
            shape_of((planes, local, CHUNKS * slots, width), BF), shape_of(x.shape, BF),
            shape_of((units, count, hidden), BF), shape_of((units, count, hidden), BF),
            shape_of((units, count, hidden), BF), shape_of((local, count, expert_total), BF),
        ),
        in_specs=[
            row_spec, half_spec, half_spec, wide, wide, tall,
            pl.BlockSpec((width, expert_total), lambda n, t: (0, 0)),
            pl.BlockSpec((1, 1, expert_total), lambda n, t: (n, 0, 0)),
            pl.BlockSpec(memory_space=pl.ANY),
        ],
        out_specs=(
            pl.BlockSpec((sources, 1, slots, width), lambda n, t: (t, n, at, 0)), row_spec, unit_spec, unit_spec, unit_spec,
            pl.BlockSpec((1, tile, expert_total), lambda n, t: (n, t, 0)),
        ),
        input_output_aliases={8: 0} if at else {},
        compiler_params=params(62),
        cost_estimate=cost(12 * units * count * hidden * width, 10 * local * count * width),
        name="experts",
    )(x, *cs, gates, ups, downs, router, named, kept)


def wide_grad_kernel(
    x0_ref, x1_ref, g0_ref, g1_ref, u0_ref, u1_ref, l0_ref, l1_ref, dg_ref, du_ref, dr_ref
):
    tile = x0_ref.shape[-1]
    x0 = x0_ref[...].reshape(-1, tile).T
    x1 = x1_ref[...].reshape(-1, tile).T
    for h in range(dg_ref.shape[0]):
        dg_ref[h] = dot(x0, g0_ref[h]) + dot(x1, g1_ref[h])
        du_ref[h] = dot(x0, u0_ref[h]) + dot(x1, u1_ref[h])
    dr_ref[0] = dot(x0, l0_ref[0]) + dot(x1, l1_ref[0])


def wide_grad(xs, gslopes, uslopes, logit_slopes, halves):
    planes, local, slots, width = xs[0].shape
    units, count, hidden = gslopes[0].shape
    tile = 1024 if planes * slots <= 1024 else 512
    x_spec = pl.BlockSpec((planes, 1, slots, tile), lambda n, j: (0, n, 0, j))
    s_spec = pl.BlockSpec((halves, count, hidden), lambda n, j: (n, 0, 0))
    o_spec = pl.BlockSpec((halves, tile, hidden), lambda n, j: (n, j, 0))
    out = shape_of((units, width, hidden), F32)
    experts_all = logit_slopes[0].shape[2]
    return pl.pallas_call(
        wide_grad_kernel,
        grid=(local, width // tile),
        out_shape=(out, out, shape_of((local, width, experts_all), F32)),
        in_specs=[x_spec] * 2
        + [s_spec] * 4
        + [pl.BlockSpec((1, count, experts_all), lambda n, j: (n, 0, 0))] * 2,
        out_specs=(
            o_spec, o_spec, pl.BlockSpec((1, tile, experts_all), lambda n, j: (n, j, 0)),
        ),
        compiler_params=params(60),
        cost_estimate=cost(8 * units * count * hidden * width, 8 * units * hidden * width),
        name="wide_grad",
    )(*xs, *gslopes, *uslopes, *logit_slopes)


def down_grad_kernel(a0_ref, a1_ref, ca_ref, cb_ref, d_ref):
    tile, slots = ca_ref.shape[-1], ca_ref.shape[2] // 2

    def part(c_ref):
        d_ref[0] = dot(a0_ref[0].T, c_ref[:, :, :slots].reshape(-1, tile)) + dot(
            a1_ref[0].T, c_ref[:, :, slots:].reshape(-1, tile)
        )

    first = pl.program_id(1) < pl.num_programs(1) // 2
    pl.when(first)(lambda: part(ca_ref))
    pl.when(jnp.logical_not(first))(lambda: part(cb_ref))


def down_grad(acts, cs, halves):
    planes, local, double, half = cs[0].shape
    units, count, hidden = acts[0].shape
    tile = half if planes * double <= 2048 else 512
    steps = half // tile
    a_spec = pl.BlockSpec((1, count, hidden), lambda u, j: (u, 0, 0))
    shape = (planes, 1, double, tile)
    return pl.pallas_call(
        down_grad_kernel,
        grid=(units, 2 * steps),
        out_shape=shape_of((units, hidden, 2 * half), F32),
        in_specs=[
            a_spec, a_spec,
            pl.BlockSpec(shape, lambda u, j: (0, u // halves, 0, jnp.minimum(j, steps - 1))),
            pl.BlockSpec(shape, lambda u, j: (0, u // halves, 0, jnp.maximum(j - steps, 0))),
        ],
        out_specs=pl.BlockSpec((1, hidden, tile), lambda u, j: (u, 0, j)),
        compiler_params=params(60),
        cost_estimate=cost(8 * units * count * hidden * half, 8 * units * hidden * half),
        name="down_grad",
    )(*acts, *cs)


def per_device(
    inputs,
    query_weight,
    key_weight,
    value_weight,
    output_weight,
    router_weight,
    first_gain,
    query_gain,
    key_gain,
    second_gain,
    gate_weight,
    up_weight,
    down_weight,
    routes,
    lengths,
    dealing,
    cotangent,
):
    planes, line = lax.axis_size("expert"), lax.axis_size("fsdp")
    plane_at, line_at = lax.axis_index("expert"), lax.axis_index("fsdp")
    tokens, width = inputs.shape
    group = line * tokens
    own_heads = HEADS // line
    head_size = width // HEADS
    own_width = own_heads * head_size
    weight_rows = query_weight.shape[0]
    slice_rows = weight_rows // planes
    units = gate_weight.shape[0]
    local = max(1, units // 2)
    halves = units // local
    expert_count = router_weight.shape[1]
    blocks = line // CHUNKS
    chunk_rows = blocks * tokens
    slots = blocks * CAP

    def own_slice(weight):
        return lax.dynamic_slice_in_dim(weight, plane_at * slice_rows, slice_rows, 0)

    sent = jnp.stack([own_slice(w) for w in (query_weight, key_weight, value_weight)], axis=1)
    sent = jnp.moveaxis(sent.reshape(slice_rows, 3, line, own_width), 2, 0)
    sent = sent.reshape(line, slice_rows, 3 * own_width)
    top_count = routes.shape[1]
    packed = [router_weight, first_gain, second_gain, routes.astype(BF)]
    sizes = [array.size for array in packed]
    fill = -sum(sizes) % (16 * 128)
    small = jnp.concatenate([array.reshape(-1) for array in packed] + [jnp.zeros((fill,), BF)])
    block_in, first_half, small_all, columns, _ = gather_start(
        inputs, cotangent, small.reshape(-1, 128), sent, planes, line
    )
    columns = columns.reshape(width, 3 * own_width)
    small_all = small_all.reshape(line, -1)
    ends = [sum(sizes[:i]) for i in range(5)]
    full_router, gain_first, gain_second, routes_all = (
        small_all[:, ends[i]:ends[i + 1]] for i in range(4)
    )
    full_router = full_router.reshape(width, expert_count)
    gain_first, gain_second = (g.reshape(width).astype(F32) for g in (gain_first, gain_second))
    routes_all = routes_all.reshape(line, tokens, top_count).astype(jnp.int32)
    later, _ = lax.optimization_barrier((cotangent, block_in))
    second_half = lax.all_gather(later[:, width // 2:], "fsdp", axis=0, tiled=True)
    incoming = [first_half, second_half]

    seq_start, positions = places(lengths[0], dealing)
    start_row, place_row, place_column = seq_start[None, :], dealing[None, :], dealing[:, None]
    cosine, sine = angles(positions, head_size)
    per_plane = expert_count // planes
    first_local = (line_at * units) // 2
    member = jnp.sum(
        (routes_all[..., None] == jnp.arange(expert_count, dtype=jnp.int32)).astype(F32), axis=2
    )
    earlier = jnp.tril(jnp.ones((tokens, tokens), BF), -1)
    rank = contract("ts,bse->bte", earlier, member.astype(BF))
    rank = rank + ((jnp.arange(line) % blocks) * CAP).astype(F32)[:, None, None]
    coded = jnp.where(member > 0, rank, -1.0).reshape(line, tokens, planes, per_plane)
    coded = lax.dynamic_slice_in_dim(coded, first_local, local, 3)
    coded = coded.reshape(CHUNKS, chunk_rows, planes * local)
    by_token = coded.astype(BF)
    by_pair = jnp.swapaxes(coded, 1, 2)

    def chunk(array, k):
        return lax.slice_in_dim(array, k * chunk_rows, (k + 1) * chunk_rows)

    rows = dispatch(by_pair, incoming[0], planes, local, slots)
    normed_low, raw, value_low, squares = project(block_in, gain_first[None], columns, tokens)
    squares = small_line_sum(squares, line)
    both_gains = jnp.concatenate([query_gain, key_gain])[None].astype(F32)
    rotary = (jnp.concatenate([cosine, cosine], -1), jnp.concatenate([-sine, sine], -1))
    query_low, key_low = turn(raw, squares, both_gains, *rotary, width, tokens)
    blended, log_total = attend(
        query_low, key_low, value_low, start_row, place_row, place_column, own_heads, tokens
    )
    attention_part = dot(blended, output_weight).astype(BF)

    named = (
        (((plane_at * line + line_at) * units) // 2 + jnp.arange(local))[:, None, None]
        == jnp.arange(expert_count)
    ).astype(F32)
    attention_parts = [chunk(attention_part, k) for k in range(CHUNKS)]
    arrived_slopes = [swap_plane(rows)]
    rows = dispatch(by_pair, incoming[1], planes, local, slots)
    held, normed, swapped = hide(
        attention_parts[0], block_in, gain_second[None], rows, 0, line, 4
    )
    arrived_slopes.append(swapped)
    rows = dispatch(by_pair[:1], normed, planes, local, slots)
    held_next, normed, swapped = hide(
        attention_parts[1], block_in, gain_second[None], rows, 1, line, 3
    )
    hidden, arrived = [held, held_next], [swapped]
    rows = dispatch(by_pair[1:], normed, planes, local, slots)
    rows, arrived_slopes[0] = lax.optimization_barrier((rows, arrived_slopes[0]))
    arrived.append(swap_plane(rows))
    weighted = arrived_slopes[0]
    row_slopes, acts, gslopes, uslopes, logit_slopes = [], [], [], [], []
    for k in range(CHUNKS):
        results = experts(
            arrived[k], arrived_slopes, k, gate_weight, up_weight, down_weight, full_router,
            named, halves, weighted,
        )
        weighted = results[0]
        for store, result in zip((row_slopes, acts, gslopes, uslopes, logit_slopes), results[1:]):
            store.append(result)
    returned = []
    behind = arrived[-1]
    for k in range(CHUNKS):
        rows, _ = lax.optimization_barrier((row_slopes[k], behind))
        behind = swap_plane(rows)
        returned.append(behind)

    hidden_slopes, attention_slopes, blended_slopes, second_parts = [], [], [], []
    for k in range(CHUNKS):
        returned[k], _ = lax.optimization_barrier(
            (returned[k], hidden_slopes[0] if k else row_slopes[-1])
        )
        part = combine(by_token[k:k + 1], returned[k], slots)
        if k:
            rows, _ = lax.optimization_barrier((weighted, returned[k]))
            mixed_rows = swap_plane(rows)
        results = hide_back(part, hidden[k], incoming, gain_second[None], k, line)
        for store, result in zip((hidden_slopes, attention_slopes, second_parts), results):
            store.append(result)
    second_gain_grad = second_parts[0] + second_parts[1]
    blended_slope = jnp.concatenate(
        [contract("td,cd->tc", low, output_weight).astype(BF) for low in attention_slopes]
    )
    slopes = attend_back(
        query_low, key_low, value_low, blended_slope, log_total, start_row,
        place_row, place_column, own_heads, tokens,
    )
    dots, gain_grads = turn_back(*slopes[:2], raw, squares, both_gains, *rotary, width, tokens)
    dots = small_line_sum(dots, line)
    mixed_rows, _ = lax.optimization_barrier((mixed_rows, gain_grads))
    mixed = combine(by_token, mixed_rows, slots)
    acts, gslopes, uslopes, logit_slopes, attention_slopes, _ = lax.optimization_barrier(
        (acts, gslopes, uslopes, logit_slopes, attention_slopes, mixed)
    )
    mixed = lax.psum_scatter(mixed, "fsdp", scatter_dimension=0, tiled=True)
    *expert_grads, router_parts = wide_grad(arrived, gslopes, uslopes, logit_slopes, halves)
    expert_grads.append(down_grad(acts, arrived_slopes, halves))
    router_grad = jnp.sum(router_parts, axis=0)
    output_grad = sum(
        contract("tc,td->cd", chunk(blended, k), attention_slopes[k]) for k in range(CHUNKS)
    ).astype(BF)
    dots, _ = lax.optimization_barrier((dots, expert_grads))
    joint, normed_part = join_slopes(
        *slopes, raw, squares, dots, both_gains, *rotary, columns, tokens
    )
    router_lanes = -expert_count % 128
    router_pad = jnp.pad(router_grad.astype(BF), ((0, 0), (0, router_lanes)))
    joint_total = joint_grad(normed_low, joint, router_pad)
    mine = line_at * weight_rows
    second_own = lax.dynamic_slice_in_dim(second_gain_grad, mine, weight_rows, 1)
    gain_rows = jnp.concatenate(
        [
            jnp.zeros((1, weight_rows), F32), second_own, gain_grads.reshape(2, own_width),
            jnp.zeros((4, weight_rows), F32),
        ]
    )
    input_gradient, totals, output_total, gain_totals = finish(
        normed_part, joint_total.reshape(line, planes, slice_rows, -1),
        output_grad.reshape(planes, slice_rows, width), inputs, gain_first[None],
        hidden_slopes, gain_rows, planes, line,
    )
    start = (line_at % blocks) * tokens
    hidden_own = jnp.where(
        line_at < blocks, *(lax.dynamic_slice_in_dim(held, start, tokens, 0) for held in hidden)
    )
    block_output = (hidden_own + mixed.astype(F32)).astype(BF)
    *weight_grads, router_total = widen(
        totals.reshape(line, planes // 2, 2, slice_rows, -1),
        output_total.reshape(planes // 2, 2, slice_rows, width), own_width,
    )
    router_total = router_total[:, :expert_count]
    return (
        block_output,
        input_gradient,
        *weight_grads,
        router_total,
        gain_totals[0],
        gain_totals[2],
        gain_totals[3],
        gain_totals[1],
        *expert_grads,
    )


def solution(mesh):
    both = ("expert", "fsdp")
    rows, cube, shard, gain = P(both, None), P(both, None, None), P("fsdp", None), P("fsdp")
    return jax.shard_map(
        per_device,
        mesh=mesh,
        in_specs=(rows,)
        + (shard,) * 5
        + (gain,) * 4
        + (cube,) * 3
        + (rows, P("expert", None), P("expert"), rows),
        out_specs=(rows, rows) + (shard,) * 5 + (gain,) * 4 + (cube,) * 3,
        check_vma=False,
    )
```

```python
import functools

import jax
import jax.numpy as jnp
from jax import lax
from jax.experimental import pallas as pl
from jax.experimental.pallas import tpu as pltpu
from jax.sharding import PartitionSpec as P

HEADS = 16
CAP = 56
EPSILON = 1e-05
THETA = 10000.0
MASKED = -1e30
LOG2E = 1.4426950408889634
BF = jnp.bfloat16
F32 = jnp.float32
MESH = pl.DeviceIdType.MESH
MIB = 1 << 20
CHUNKS = 2


def dot(a, b):
    return jnp.dot(a, b, preferred_element_type=F32)


def dot_nt(a, b):
    return lax.dot_general(a, b, (((1,), (1,)), ((), ())), preferred_element_type=F32)


def dot_tn(a, b):
    return lax.dot_general(a, b, (((0,), (0,)), ((), ())), preferred_element_type=F32)


def contract(spec, *operands):
    return jnp.einsum(spec, *operands, preferred_element_type=F32)


def shape_of(dims, dtype):
    return jax.ShapeDtypeStruct(dims, dtype)


def cost(flops, moved):
    return pl.CostEstimate(flops=int(flops) // 64, bytes_accessed=int(moved) // 64, transcendentals=0)


def params(mib, **kwargs):
    return pltpu.CompilerParams(vmem_limit_bytes=mib * MIB, **kwargs)


def places(lengths_row, stream):
    seq_ends = jnp.cumsum(lengths_row)
    before = (seq_ends[None, :] <= stream[:, None]).astype(jnp.int32)
    offset = jnp.sum(before * lengths_row[None, :], axis=1)
    return offset, stream - offset


def angles(positions, head_width):
    exponent = jnp.arange(0, head_width, 2).astype(F32) / head_width
    phases = positions.astype(F32)[:, None] * (THETA ** (-exponent))[None, :]
    return jnp.cos(phases), jnp.sin(phases)


def gather_kernel(
    planes, line, pieces, x_ref, c_ref, small_ref, sent_ref,
    x_all, c_all, small_all, columns_ref, swapped_ref,
    x_send, x_recv, s_send, s_recv, z_send, z_recv, p_send, p_recv, own_sem,
):
    e, f = lax.axis_index("expert"), lax.axis_index("fsdp")
    barrier = pltpu.get_barrier_semaphore()
    for d in range(1, line):
        pl.semaphore_signal(
            barrier, inc=1, device_id={"fsdp": lax.rem(f + d, line)}, device_id_type=MESH
        )
    for d in range(1, planes):
        pl.semaphore_signal(
            barrier, inc=1, device_id={"expert": lax.rem(e + d, planes)}, device_id_type=MESH
        )
    pl.semaphore_wait(barrier, line + planes - 2)
    rows = x_ref.shape[0]
    part = rows // pieces
    small_rows = small_ref.shape[0]

    swaps, smalls = [], []
    for d in range(1, line):
        to = lax.rem(f + d, line)
        swaps.append(pltpu.make_async_remote_copy(
            src_ref=sent_ref.at[to], dst_ref=swapped_ref.at[f],
            send_sem=z_send.at[d - 1], recv_sem=z_recv.at[d - 1],
            device_id={"fsdp": to}, device_id_type=MESH,
        ))
        smalls.append(pltpu.make_async_remote_copy(
            src_ref=small_ref, dst_ref=small_all.at[pl.ds(f * small_rows, small_rows)],
            send_sem=s_send.at[d - 1], recv_sem=s_recv.at[d - 1],
            device_id={"fsdp": to}, device_id_type=MESH,
        ))
    for copy in swaps:
        copy.start()

    def hop(direction, step, c):
        own_ref, all_ref = (x_ref, x_all) if c < pieces else (c_ref, c_all)
        origin = f - direction * step
        place = pl.ds(origin * rows + c % pieces * part, part)
        cut = pl.ds(0, all_ref.shape[1])
        source = own_ref.at[pl.ds(c % pieces * part, part), cut] if step == 0 else all_ref.at[place]
        side = 0 if direction == 1 else 1
        return pltpu.make_async_remote_copy(
            src_ref=source, dst_ref=all_ref.at[place],
            send_sem=x_send.at[side, step, c], recv_sem=x_recv.at[side, step, c],
            device_id={"fsdp": f + direction}, device_id_type=MESH,
        )

    def sends(direction, step):
        origin, to = f - direction * step, f + direction
        return (origin >= 0) & (origin < line) & (to >= 0) & (to < line)

    def receives(direction, step):
        origin = f - direction * (step + 1)
        return (origin >= 0) & (origin < line)

    for direction in (1, -1):
        @pl.when(sends(direction, 0))
        def _(direction=direction):
            for c in range(2 * pieces):
                hop(direction, 0, c).start()

    for copy in smalls:
        copy.start()
    locals_ = [
        pltpu.make_async_copy(x_ref, x_all.at[pl.ds(f * rows, rows)], own_sem.at[0]),
        pltpu.make_async_copy(
            c_ref.at[:, pl.ds(0, c_all.shape[1])], c_all.at[pl.ds(f * rows, rows)], own_sem.at[4]
        ),
        pltpu.make_async_copy(
            small_ref, small_all.at[pl.ds(f * small_rows, small_rows)], own_sem.at[1]
        ),
        pltpu.make_async_copy(sent_ref.at[f], swapped_ref.at[f], own_sem.at[2]),
    ]
    for copy in locals_:
        copy.start()
    for copy in swaps:
        copy.wait_recv()
    locals_[3].wait()
    spread = []
    for d in range(1, planes):
        spread.append(pltpu.make_async_remote_copy(
            src_ref=swapped_ref, dst_ref=columns_ref.at[:, e],
            send_sem=p_send.at[d - 1], recv_sem=p_recv.at[d - 1],
            device_id={"expert": lax.rem(e + d, planes)}, device_id_type=MESH,
        ))
        spread[-1].start()
    own = pltpu.make_async_copy(swapped_ref, columns_ref.at[:, e], own_sem.at[3])
    own.start()

    for step in range(line - 1):
        for c in range(2 * pieces):
            for direction in (1, -1):
                @pl.when(receives(direction, step))
                def _(direction=direction, step=step, c=c):
                    origin = f - direction * (step + 1)
                    all_ref = x_all if c < pieces else c_all
                    place = pl.ds(origin * rows + c % pieces * part, part)
                    side = 0 if direction == 1 else 1
                    pltpu.make_async_remote_copy(
                        src_ref=all_ref.at[place], dst_ref=all_ref.at[place],
                        send_sem=x_send.at[side, step, c], recv_sem=x_recv.at[side, step, c],
                        device_id={"fsdp": f - direction}, device_id_type=MESH,
                    ).wait_recv()
                if step < line - 2:
                    @pl.when(sends(direction, step + 1))
                    def _(direction=direction, step=step, c=c):
                        hop(direction, step + 1, c).start()
    for step in range(line - 1):
        for direction in (1, -1):
            @pl.when(sends(direction, step))
            def _(direction=direction, step=step):
                for c in range(2 * pieces):
                    hop(direction, step, c).wait_send()
    for copy in swaps:
        copy.wait_send()
    for copy in smalls + spread:
        copy.wait()
    for copy in locals_[:3] + [own]:
        copy.wait()


def gather_start(block, half, small, sent, planes, line):
    rows, width = block.shape
    pieces = 4
    anywhere = pl.BlockSpec(memory_space=pl.ANY)
    sems = pltpu.SemaphoreType.DMA
    return pl.pallas_call(
        functools.partial(gather_kernel, planes, line, pieces),
        out_shape=(
            shape_of((line * rows, width), BF),
            shape_of((line * rows, half.shape[1] // 2), BF),
            shape_of((line * small.shape[0], small.shape[1]), BF),
            shape_of((line, planes) + sent.shape[1:], BF),
            shape_of(sent.shape, BF),
        ),
        in_specs=[anywhere] * 4,
        out_specs=[anywhere] * 5,
        scratch_shapes=[
            sems((2, line - 1, 2 * pieces)), sems((2, line - 1, 2 * pieces)),
            sems((line - 1,)), sems((line - 1,)), sems((line - 1,)), sems((line - 1,)),
            sems((planes - 1,)), sems((planes - 1,)), sems((5,)),
        ],
        compiler_params=pltpu.CompilerParams(collective_id=0, has_side_effects=True),
        name="gather_start",
    )(block, half, small, sent)


def line_steps(line, pieces, lag, p_ref, o_ref, right_in, left_in, send_sem, recv_sem, complete):
    f = lax.axis_index("fsdp")
    last = line - 1
    part = p_ref.shape[0] // pieces

    def greet():
        barrier = pltpu.get_barrier_semaphore()

        @pl.when(f > 0)
        def _():
            pl.semaphore_signal(barrier, inc=1, device_id={"fsdp": f - 1}, device_id_type=MESH)

        @pl.when(f < last)
        def _():
            pl.semaphore_signal(barrier, inc=1, device_id={"fsdp": f + 1}, device_id_type=MESH)

    neighbours = jnp.where((f > 0) & (f < last), 2, 1)

    def copy(side, source, c):
        buffer = right_in if side == 0 else left_in
        place = pl.ds(c * part, part)
        return pltpu.make_async_remote_copy(
            src_ref=(p_ref if source else buffer).at[place], dst_ref=buffer.at[place],
            send_sem=send_sem.at[side, c], recv_sem=recv_sem.at[side, c],
            device_id={"fsdp": f + 1 if side == 0 else f - 1}, device_id_type=MESH,
        )

    def enter():
        for side in range(2):
            @pl.when(f == (0 if side == 0 else last))
            def _(side=side):
                def one(c, carry):
                    copy(side, True, c).start()
                    return carry

                lax.fori_loop(0, pieces, one, 0)

    def arrive(side, c):
        place = pl.ds(pl.multiple_of(c * part, part), part)
        buffer = right_in if side == 0 else left_in
        origin, end = (0, last) if side == 0 else (last, 0)
        leads = (2 * f <= last) if side == 0 else (2 * f > last)

        @pl.when(f == origin)
        def _():
            o_ref[place, :] = p_ref[place, :].astype(F32)

        @pl.when(f != origin)
        def _():
            copy(side, False, c).wait_recv()
            came = buffer[place, :].astype(F32)

            @pl.when(f != end)
            def _():
                buffer[place, :] = (came + p_ref[place, :].astype(F32)).astype(BF)
                copy(side, False, c).start()

            @pl.when(leads)
            def _():
                o_ref[place, :] = came + p_ref[place, :].astype(F32)

            @pl.when(jnp.logical_not(leads))
            def _():
                o_ref[place, :] += came
                complete(place, c)

    def body(s, carry):
        for side in range(2):
            c = s - lag * (f if side == 0 else last - f)

            @pl.when((c >= 0) & (c < pieces))
            def _(side=side, c=c):
                arrive(side, c)

        return carry

    def drain():
        def one(c, carry):
            @pl.when(f < last)
            def _():
                copy(0, True, c).wait_send()

            @pl.when(f > 0)
            def _():
                copy(1, True, c).wait_send()

            return carry

        lax.fori_loop(0, pieces, one, 0)

    return greet, neighbours, enter, body, drain, pieces + lag * last


def line_scratch(rows, width, pieces):
    return [
        pltpu.VMEM((rows, width), BF),
        pltpu.VMEM((rows, width), BF),
        pltpu.SemaphoreType.DMA((2, pieces)),
        pltpu.SemaphoreType.DMA((2, pieces)),
    ]


def store_pieces(pairs, sems, pieces, height):
    def copies(c):
        place = pl.ds(pl.multiple_of(c * height, height), height)
        return [
            pltpu.make_async_copy(source.at[place], target.at[place], sems.at[i, c])
            for i, (source, target) in enumerate(pairs)
        ]

    def start(c):
        for copy in copies(c):
            copy.start()

    def wait():
        def one(c, carry):
            for copy in copies(c):
                copy.wait()
            return carry

        lax.fori_loop(0, pieces, one, 0)

    return start, wait


def hide_kernel(
    planes, line, pieces, lag, at, p_ref, x_ref, gain_ref, rows_ref, hidden_ref, normed_ref, swapped_ref,
    right_in, left_in, send_sem, recv_sem, w_send, w_recv, own_sem, x_own, total_own, normed_own, store_sem,
):
    e = lax.axis_index("expert")
    rows = p_ref.shape[0]
    load = pltpu.make_async_copy(x_ref.at[pl.ds(at * rows, rows)], x_own, own_sem.at[1])
    load.start()
    start_store, wait_stores = store_pieces(
        [(total_own, hidden_ref), (normed_own, normed_ref)], store_sem, pieces, rows // pieces
    )

    def complete(place, c):
        hidden = x_own[place, :].astype(F32) + total_own[place, :]
        total_own[place, :] = hidden
        scale = lax.rsqrt(jnp.mean(hidden * hidden, axis=-1, keepdims=True) + EPSILON)
        normed_own[place, :] = (hidden * scale * gain_ref[...]).astype(BF)
        start_store(c)

    greet, neighbours, enter, body, drain, total = line_steps(
        line, pieces, lag, p_ref, total_own, right_in, left_in, send_sem, recv_sem, complete
    )
    greet()
    barrier = pltpu.get_barrier_semaphore()
    for d in range(1, planes):
        pl.semaphore_signal(
            barrier, inc=1, device_id={"expert": lax.rem(e + d, planes)}, device_id_type=MESH
        )
    pl.semaphore_wait(barrier, neighbours + planes - 1)
    enter()
    swaps = []
    for d in range(1, planes):
        to = lax.rem(e + d, planes)
        swaps.append(pltpu.make_async_remote_copy(
            src_ref=rows_ref.at[to], dst_ref=swapped_ref.at[e],
            send_sem=w_send.at[d - 1], recv_sem=w_recv.at[d - 1],
            device_id={"expert": to}, device_id_type=MESH,
        ))
    own = pltpu.make_async_copy(rows_ref.at[e], swapped_ref.at[e], own_sem.at[0])
    for copy in swaps + [own]:
        copy.start()
    load.wait()
    lax.fori_loop(0, total, body, 0)
    drain()
    for copy in swaps + [own]:
        copy.wait()
    wait_stores()


def hide(part, block, gain, rows_sent, at, line, identity, height=32, lag=2):
    rows, width = part.shape
    planes = rows_sent.shape[0]
    pieces = rows // height
    sems = pltpu.SemaphoreType.DMA
    anywhere = pl.BlockSpec(memory_space=pl.ANY)
    vmem = pl.BlockSpec(memory_space=pltpu.VMEM)
    return pl.pallas_call(
        functools.partial(hide_kernel, planes, line, pieces, lag, at),
        out_shape=(
            shape_of((rows, width), F32), shape_of((rows, width), BF),
            shape_of(rows_sent.shape, BF),
        ),
        in_specs=[vmem, anywhere, vmem, anywhere],
        out_specs=(anywhere, anywhere, anywhere),
        scratch_shapes=line_scratch(rows, width, pieces)
        + [
            sems((planes - 1,)), sems((planes - 1,)), sems((2,)),
            pltpu.VMEM((rows, width), BF), pltpu.VMEM((rows, width), F32),
            pltpu.VMEM((rows, width), BF), sems((2, pieces)),
        ],
        compiler_params=params(60, collective_id=identity, has_side_effects=True),
        cost_estimate=cost(0, 300 * MIB),
        name="hide",
    )(part, block, gain, rows_sent)


def hide_back_kernel(
    line, pieces, lag, at, p_ref, hidden_ref, ca_ref, cb_ref, gain_ref, total_ref, low_ref, grad_ref,
    right_in, left_in, send_sem, recv_sem, hidden_own, ca_own, cb_own, total_own, low_own, load_sem, store_sem,
):
    rows = p_ref.shape[0]
    half = ca_ref.shape[1]
    mine = pl.ds(at * rows, rows)
    loads = [
        pltpu.make_async_copy(hidden_ref, hidden_own, load_sem.at[0]),
        pltpu.make_async_copy(ca_ref.at[mine], ca_own, load_sem.at[1]),
        pltpu.make_async_copy(cb_ref.at[mine], cb_own, load_sem.at[2]),
    ]
    for copy in loads:
        copy.start()
    start_store, wait_stores = store_pieces(
        [(total_own, total_ref), (low_own, low_ref)], store_sem, pieces, rows // pieces
    )

    def complete(place, c):
        slope, hidden = total_own[place, :], hidden_own[place, :]
        scale = lax.rsqrt(jnp.mean(hidden * hidden, axis=-1, keepdims=True) + EPSILON)
        grad_ref[...] += jnp.sum(slope * hidden * scale, axis=0, keepdims=True)
        slope = slope * gain_ref[...]
        along = jnp.sum(slope * hidden, axis=-1, keepdims=True) / hidden.shape[1]
        part = scale * slope - hidden * (scale * scale * scale * along)
        for ref, lanes in ((ca_own, slice(0, half)), (cb_own, slice(half, 2 * half))):
            total = ref[place, :].astype(F32) + part[:, lanes]
            total_own[place, lanes] = total
            low_own[place, lanes] = total.astype(BF)
        start_store(c)

    greet, neighbours, enter, body, drain, total = line_steps(
        line, pieces, lag, p_ref, total_own, right_in, left_in, send_sem, recv_sem, complete
    )
    greet()
    grad_ref[...] = jnp.zeros_like(grad_ref)
    pl.semaphore_wait(pltpu.get_barrier_semaphore(), neighbours)
    enter()
    for copy in loads:
        copy.wait()
    lax.fori_loop(0, total, body, 0)
    drain()
    wait_stores()


def hide_back(part, hidden, incoming, gain, at, line, height=32, lag=2):
    rows, width = part.shape
    pieces = rows // height
    sems = pltpu.SemaphoreType.DMA
    anywhere = pl.BlockSpec(memory_space=pl.ANY)
    vmem = pl.BlockSpec(memory_space=pltpu.VMEM)
    return pl.pallas_call(
        functools.partial(hide_back_kernel, line, pieces, lag, at),
        out_shape=(
            shape_of((rows, width), F32), shape_of((rows, width), BF), shape_of((1, width), F32),
        ),
        in_specs=[vmem, anywhere, anywhere, anywhere, vmem],
        out_specs=(anywhere, anywhere, vmem),
        scratch_shapes=line_scratch(rows, width, pieces)
        + [
            pltpu.VMEM((rows, width), F32), pltpu.VMEM((rows, width // 2), BF),
            pltpu.VMEM((rows, width // 2), BF), pltpu.VMEM((rows, width), F32),
            pltpu.VMEM((rows, width), BF), sems((3,)), sems((2, pieces)),
        ],
        compiler_params=params(62, collective_id=5 + at, has_side_effects=True),
        cost_estimate=cost(0, 260 * MIB),
        name="hide_back",
    )(part, hidden, *incoming, gain)


def finish_kernel(
    planes, line, height, lag, p_ref, a_ref, b_ref, x_ref, gain_ref, slope0_ref, slope1_ref, gains_ref,
    o_ref, a_out, b_out, gains_out,
    right_in, left_in, a_own, a_half, a_in, a_sum, a_cols, b_own, b_half, b_in, b_sum, gain_part, gain_in, gain_own, gain_all,
    z_send, z_recv, h_send, h_recv, r_send, r_recv, s_send, s_recv, g_send, g_recv,
    w_send, w_recv, n_send, n_recv, m_send, m_recv, own_sem, slope_own,
):
    e, f = lax.axis_index("expert"), lax.axis_index("fsdp")
    chips, last = planes // 2, line - 1
    c, k = e // 2, e % 2
    mate = e + 1 - 2 * k
    barrier = pltpu.get_barrier_semaphore()

    def greet(**device):
        pl.semaphore_signal(barrier, inc=1, device_id=device, device_id_type=MESH)

    for d in range(1, planes):
        greet(expert=lax.rem(e + d, planes))
    for d in range(1, line):
        greet(fsdp=lax.rem(f + d, line))
    pl.semaphore_wait(barrier, planes - 1 + last)

    rows = p_ref.shape[0] // line
    pieces = rows // height
    ahead = 4

    def remote(source, target, send, recv, **device):
        return pltpu.make_async_remote_copy(
            src_ref=source, dst_ref=target, send_sem=send, recv_sem=recv,
            device_id=device, device_id_type=MESH,
        )

    lanes_a = a_ref.shape[-1]
    cut = lanes_a // 128 * 9 // 13 * 128
    spans = (pl.ds(0, cut), pl.ds(cut, lanes_a - cut))

    to_mate = [
        remote(
            a_ref.at[:, :, 1 - k, :, span], a_half.at[:, :, :, span], h_send.at[i], h_recv.at[i],
            expert=mate,
        )
        for i, span in enumerate(spans)
    ]
    to_mate.append(remote(b_ref.at[:, 1 - k], b_half, h_send.at[2], h_recv.at[2], expert=mate))
    own_half = [
        pltpu.make_async_copy(a_ref.at[:, :, k], a_own, own_sem.at[0]),
        pltpu.make_async_copy(b_ref.at[:, k], b_own, own_sem.at[1]),
    ]
    blocks = line // 2

    def slope_load(which):
        source = (slope0_ref, slope1_ref)[which]
        place = pl.ds(pl.multiple_of((f - which * blocks) * rows, rows), rows)
        return pltpu.make_async_copy(source.at[place], slope_own, own_sem.at[4])

    pl.when(f < blocks)(lambda: slope_load(0).start())
    pl.when(f >= blocks)(lambda: slope_load(1).start())
    for copy in to_mate + own_half:
        copy.start()

    def place_of(side, s):
        target = last - s // pieces if side == 0 else s // pieces
        return target, pl.ds(pl.multiple_of(target * rows + lax.rem(s, pieces) * height, height), height)

    def copy_line(side, source, s):
        buffer = right_in if side == 0 else left_in
        place = place_of(side, s)[1]
        return remote(
            (p_ref if source else buffer).at[place], buffer.at[place],
            z_send.at[side, s], z_recv.at[side, s], fsdp=f + 1 if side == 0 else f - 1,
        )

    def begin(side, s):
        @pl.when(s >= ahead)
        def _():
            copy_line(side, True, s - ahead).wait_send()

        copy_line(side, True, s).start()

    def arrive(side, s):
        buffer = right_in if side == 0 else left_in
        target, place = place_of(side, s)
        copy_line(side, False, s).wait_recv()

        @pl.when(target != f)
        def _():
            buffer[place, :] = (buffer[place, :].astype(F32) + p_ref[place, :].astype(F32)).astype(BF)
            copy_line(side, False, s).start()

    def body(s, carry):
        right = s - lag * f
        left = s - lag * (last - f)

        @pl.when((f == 0) & (s < last * pieces))
        def _():
            begin(0, s)

        @pl.when((f == last) & (s < last * pieces))
        def _():
            begin(1, s)

        @pl.when((f > 0) & (right >= 0) & (right < (last - f + 1) * pieces))
        def _():
            arrive(0, right)

        @pl.when((f < last) & (left >= 0) & (left < (f + 1) * pieces))
        def _():
            arrive(1, left)

        return carry

    total = last * pieces + lag * last
    shares, swaps, spread = [], [], []
    sent = []

    def add_pairs():
        for copy in own_half:
            copy.wait()
        for copy in to_mate:
            copy.wait_recv()

        def one(i, carry):
            for j in range(chips):
                a_own[i, j] = (a_own[i, j].astype(F32) + a_half[i, j].astype(F32)).astype(BF)
            return carry

        lax.fori_loop(0, line, one, 0)
        for j in range(chips):
            b_own[j] = (b_own[j].astype(F32) + b_half[j].astype(F32)).astype(BF)

    def share(which):
        span = spans[which]
        mine = []
        for d in range(1, chips):
            to = lax.rem(c + d, chips)
            mine.append(remote(
                a_own.at[:, to, :, span], a_in.at[d - 1, :, :, span],
                r_send.at[which, d - 1], r_recv.at[which, d - 1], expert=to * 2 + k,
            ))
            if which:
                mine.append(remote(
                    b_own.at[to], b_in.at[d - 1], r_send.at[2, d - 1], r_recv.at[2, d - 1],
                    expert=to * 2 + k,
                ))
        for copy in mine:
            copy.start()
        shares.append(mine)

    def swap(which):
        span = spans[which]

        def one(i, carry):
            summed = a_own[i, c, :, span].astype(F32)
            for d in range(1, chips):
                summed = summed + a_in[d - 1, i, :, span].astype(F32)
            a_sum[i, :, span] = summed.astype(BF)
            return carry

        lax.fori_loop(0, line, one, 0)
        if which:
            summed = b_own[c].astype(F32)
            for d in range(1, chips):
                summed = summed + b_in[d - 1].astype(F32)
            b_sum[...] = summed.astype(BF)
        mine = []
        for d in range(1, line):
            to = lax.rem(f + d, line)
            mine.append(remote(
                a_sum.at[to, :, span], a_cols.at[f, :, span],
                s_send.at[which, d - 1], s_recv.at[which, d - 1], fsdp=to,
            ))
        for copy in mine:
            copy.start()
        a_cols[f, :, span] = a_sum[f, :, span]
        swaps.append(mine)

    def spread_out(which):
        span = spans[which]
        for copy in swaps[which]:
            copy.wait_recv()
        mine = []
        for d in range(chips):
            to = lax.rem(c + d, chips) * 2 + k if d else mate
            pair = [remote(
                a_cols.at[:, :, span], a_out.at[:, e, :, span],
                g_send.at[which, d], g_recv.at[which, d], expert=to,
            )]
            if which:
                pair.append(remote(
                    b_sum, b_out.at[e], g_send.at[2, d], g_recv.at[2, d], expert=to
                ))
            for copy in pair:
                copy.start()
            mine.append(pair)
        spread.append(mine)

    def pass_on(which):
        span = spans[which]
        for d in range(1, chips):
            for copy in spread[which][d]:
                copy.wait_recv()
            source = lax.rem(c + chips - d, chips) * 2 + k
            place = a_out.at[:, source, :, span]
            pair = [remote(
                place, place, w_send.at[which, d - 1], w_recv.at[which, d - 1], expert=mate
            )]
            if which:
                place = b_out.at[source]
                pair.append(remote(
                    place, place, w_send.at[2, d - 1], w_recv.at[2, d - 1], expert=mate
                ))
            for copy in pair:
                copy.start()
            sent.extend(pair)

    stops = [total // 10, total * 3 // 10, total // 2, total * 3 // 5, total * 3 // 4, total]
    lax.fori_loop(0, stops[0], body, 0)
    add_pairs()
    share(0)
    lax.fori_loop(stops[0], stops[1], body, 0)
    for copy in shares[0]:
        copy.wait_recv()
    share(1)
    swap(0)
    lax.fori_loop(stops[1], stops[2], body, 0)
    spread_out(0)
    lax.fori_loop(stops[2], stops[3], body, 0)
    for copy in shares[1]:
        copy.wait_recv()
    swap(1)
    lax.fori_loop(stops[3], stops[4], body, 0)
    spread_out(1)
    lax.fori_loop(stops[4], stops[5], body, 0)
    own_out = [
        pltpu.make_async_copy(a_cols, a_out.at[:, e], own_sem.at[2]),
        pltpu.make_async_copy(b_sum, b_out.at[e], own_sem.at[3]),
    ]
    for copy in own_out:
        copy.start()
    pass_on(0)

    gain = gain_ref[...]
    width = gain.shape[1]
    gain_part[...] = jnp.zeros_like(gain_part)
    pl.when(f < blocks)(lambda: slope_load(0).wait())
    pl.when(f >= blocks)(lambda: slope_load(1).wait())

    def tile(i, carry):
        place = pl.ds(pl.multiple_of(i * height, height), height)
        mine = pl.ds(pl.multiple_of(f * rows + i * height, height), height)
        right = jnp.where(f > 0, right_in[mine, :].astype(F32), 0.0)
        left = jnp.where(f < last, left_in[mine, :].astype(F32), 0.0)
        slope = p_ref[mine, :].astype(F32) + right + left
        x = x_ref[place, :].astype(F32)
        scale = lax.rsqrt(jnp.mean(x * x, axis=-1, keepdims=True) + EPSILON)
        gain_part[0:1, :] += jnp.sum(slope * x * scale, axis=0, keepdims=True)
        slope = slope * gain
        along = jnp.sum(slope * x, axis=-1, keepdims=True) / width
        part = scale * slope - x * (scale * scale * scale * along)
        o_ref[place, :] = (slope_own[place, :] + part).astype(BF)
        return carry

    lax.fori_loop(0, pieces, tile, 0)

    lanes = gains_ref.shape[1]

    def share_of(which):
        return gain_part.at[:, pl.ds(pl.multiple_of(which * lanes, lanes), lanes)]

    to_shards = []
    for d in range(1, line):
        to = lax.rem(f + d, line)
        to_shards.append(remote(
            share_of(to), gain_in.at[d - 1], n_send.at[d - 1], n_recv.at[d - 1], fsdp=to
        ))
    for copy in to_shards:
        copy.start()
    for copy in to_shards:
        copy.wait_recv()
    summed = share_of(f)[...] + gains_ref[...]
    for d in range(1, line):
        summed = summed + gain_in[d - 1]
    gain_own[...] = summed
    to_plane = []
    for d in range(1, planes):
        to_plane.append(remote(
            gain_own, gain_all.at[d - 1], m_send.at[d - 1], m_recv.at[d - 1],
            expert=lax.rem(e + d, planes),
        ))
    for copy in to_plane:
        copy.start()

    pass_on(1)
    for copy in to_plane:
        copy.wait_recv()
    total_gain = gain_own[...]
    for d in range(1, planes):
        total_gain = total_gain + gain_all[d - 1]
    gains_out[...] = total_gain
    for mine in spread:
        for copy in mine[0]:
            copy.wait_recv()
    for copy in sent + own_out:
        copy.wait()
    for mine in spread:
        for copy in sum(mine, []):
            copy.wait_send()
    for copy in to_shards + to_plane + to_mate + sum(shares + swaps, []):
        copy.wait_send()

    def drain(side, start, stop):
        def one(s, carry):
            copy_line(side, True, s).wait_send()
            return carry

        lax.fori_loop(start, stop, one, 0)

    for side, origin in ((0, 0), (1, last)):
        count = ((last - f) if side == 0 else f) * pieces

        @pl.when(f == origin)
        def _(side=side):
            drain(side, last * pieces - ahead, last * pieces)

        @pl.when(f != origin)
        def _(side=side, count=count):
            drain(side, 0, count)


def finish(part, a, b, block, gain, slopes, gains, planes, line, height=32, lag=2):
    group, width = part.shape
    tokens = group // line
    chips, last = planes // 2, line - 1
    items = last * (tokens // height)
    rows, lanes = a.shape[2:]
    share = gains.shape[1]
    vmem = pl.BlockSpec(memory_space=pltpu.VMEM)
    anywhere = pl.BlockSpec(memory_space=pl.ANY)
    sems = pltpu.SemaphoreType.DMA
    return pl.pallas_call(
        functools.partial(finish_kernel, planes, line, height, lag),
        out_shape=(
            shape_of((tokens, width), BF), shape_of(a.shape, BF), shape_of(b.shape, BF),
            shape_of(gains.shape, F32),
        ),
        in_specs=[vmem, anywhere, anywhere, vmem, vmem, anywhere, anywhere, vmem],
        out_specs=(vmem, anywhere, anywhere, vmem),
        scratch_shapes=[
            pltpu.VMEM((group, width), BF), pltpu.VMEM((group, width), BF),
            pltpu.VMEM((line, chips, rows, lanes), BF), pltpu.VMEM((line, chips, rows, lanes), BF),
            pltpu.VMEM((chips - 1, line, rows, lanes), BF),
            pltpu.VMEM((line, rows, lanes), BF), pltpu.VMEM((line, rows, lanes), BF),
            pltpu.VMEM((chips, rows, width), BF), pltpu.VMEM((chips, rows, width), BF),
            pltpu.VMEM((chips - 1, rows, width), BF), pltpu.VMEM((rows, width), BF),
            pltpu.VMEM((8, width), F32), pltpu.VMEM((last, 8, share), F32),
            pltpu.VMEM((8, share), F32), pltpu.VMEM((planes - 1, 8, share), F32),
            sems((2, items)), sems((2, items)), sems((3,)), sems((3,)),
            sems((3, chips - 1)), sems((3, chips - 1)), sems((2, last)), sems((2, last)),
            sems((3, chips)), sems((3, chips)), sems((3, chips - 1)), sems((3, chips - 1)),
            sems((last,)), sems((last,)), sems((planes - 1,)), sems((planes - 1,)),
            sems((5,)), pltpu.VMEM((tokens, width), F32),
        ],
        compiler_params=params(60, collective_id=2, has_side_effects=True),
        cost_estimate=cost(0, 400 * MIB),
        name="finish",
    )(
        part, a.reshape(line, chips, 2, rows, lanes), b.reshape(chips, 2, rows, width), block, gain,
        *slopes, gains,
    )


def swap_plane(rows):
    return lax.all_to_all(rows, "expert", split_axis=0, concat_axis=0, tiled=True)


def small_line_sum(array, line):
    total = array
    for d in range(1, line):
        total = total + lax.ppermute(array, "fsdp", [(i, (i + d) % line) for i in range(line)])
    return total


def as_row(column, second):
    lane = lax.broadcasted_iota(jnp.int32, (column.shape[0], 128), 1)
    return jnp.where(lane == 0, column, second).T[:2, :]


def as_column(row):
    return jnp.broadcast_to(row, (128, row.shape[1])).T


def project_kernel(x_ref, gain_ref, columns_ref, normed_ref, raw_ref, value_ref, squares_ref):
    x = x_ref[...].astype(F32)
    scale = lax.rsqrt(jnp.mean(x * x, axis=-1, keepdims=True) + EPSILON)
    normed = (x * scale * gain_ref[...]).astype(BF)
    normed_ref[...] = normed
    own = value_ref.shape[1]
    query = dot(normed, columns_ref[:, :own])
    key = dot(normed, columns_ref[:, own:2 * own])
    value_ref[...] = dot(normed, columns_ref[:, 2 * own:]).astype(BF)
    raw_ref[:, :own] = query
    raw_ref[:, own:] = key
    squares_ref[...] = as_row(
        jnp.sum(query * query, axis=-1, keepdims=True), jnp.sum(key * key, axis=-1, keepdims=True)
    )


def project(block, gain, columns, tile):
    group, width = block.shape
    own = columns.shape[1] // 3 // 128 * 128
    rows = lambda count: pl.BlockSpec((tile, count), lambda i: (i, 0))
    return pl.pallas_call(
        project_kernel,
        grid=(group // tile,),
        out_shape=(
            shape_of((group, width), BF), shape_of((group, 2 * own), F32),
            shape_of((group, own), BF), shape_of((2, group), F32),
        ),
        in_specs=[
            rows(width), pl.BlockSpec((1, width), lambda i: (0, 0)),
            pl.BlockSpec((width, 3 * own), lambda i: (0, 0)),
        ],
        out_specs=(rows(width), rows(2 * own), rows(own), pl.BlockSpec((2, tile), lambda i: (0, i))),
        compiler_params=params(48),
        cost_estimate=cost(6 * group * width * own, 14 * group * own),
        name="project",
    )(block, gain, columns)


def scales_of(squares_ref, width):
    scales = lax.rsqrt(squares_ref[...] / width + EPSILON)
    return [as_column(scales[i:i + 1, :]) for i in range(2)]


def turn_kernel(width, raw_ref, squares_ref, gain_ref, cos_ref, sin_ref, q_ref, k_ref):
    own = q_ref.shape[1]
    scales = scales_of(squares_ref, width)
    cosine, sine = cos_ref[...], sin_ref[...]
    for which, out in enumerate((q_ref, k_ref)):
        for j in range(0, own, 128):
            place = slice(which * own + j, which * own + j + 128)
            v = raw_ref[:, place] * scales[which] * gain_ref[:, place]
            out[:, j:j + 128] = (v * cosine + pltpu.roll(v, 64, 1) * sine).astype(BF)


def turn(raw, squares, gain, cosine, sine, width, tile):
    group, double = raw.shape
    own = double // 2
    rows = lambda count: pl.BlockSpec((tile, count), lambda i: (i, 0))
    return pl.pallas_call(
        functools.partial(turn_kernel, width),
        grid=(group // tile,),
        out_shape=(shape_of((group, own), BF),) * 2,
        in_specs=[
            rows(double), pl.BlockSpec((2, tile), lambda i: (0, i)),
            pl.BlockSpec((1, double), lambda i: (0, 0)), rows(128), rows(128),
        ],
        out_specs=(rows(own), rows(own)),
        compiler_params=params(32),
        cost_estimate=cost(20 * group * double, 8 * group * double),
        name="turn",
    )(raw, squares, gain, cosine, sine)


def turn_back_kernel(
    width, dq_ref, dk_ref, raw_ref, squares_ref, gain_ref, cos_ref, sin_ref, dots_ref, grad_ref
):
    own = dq_ref.shape[1]
    scales = scales_of(squares_ref, width)
    cosine, sine = cos_ref[...], sin_ref[...]

    @pl.when(pl.program_id(0) == 0)
    def _():
        grad_ref[...] = jnp.zeros_like(grad_ref)

    dots = []
    for which, slope in enumerate((dq_ref, dk_ref)):
        total = 0.0
        for j in range(0, own, 128):
            place = slice(which * own + j, which * own + j + 128)
            v = slope[:, j:j + 128].astype(F32)
            turned = (v * cosine - pltpu.roll(v, 64, 1) * sine) * raw_ref[:, place]
            total = total + jnp.sum(turned * gain_ref[:, place], axis=-1, keepdims=True)
            grad_ref[:, place] += jnp.sum(turned * scales[which], axis=0, keepdims=True)
        dots.append(total)
    dots_ref[...] = as_row(*dots)


def turn_back(dq, dk, raw, squares, gain, cosine, sine, width, tile):
    group, double = raw.shape
    own = double // 2
    rows = lambda count: pl.BlockSpec((tile, count), lambda i: (i, 0))
    pair = pl.BlockSpec((2, tile), lambda i: (0, i))
    flat = pl.BlockSpec((1, double), lambda i: (0, 0))
    return pl.pallas_call(
        functools.partial(turn_back_kernel, width),
        grid=(group // tile,),
        out_shape=(shape_of((2, group), F32), shape_of((1, double), F32)),
        in_specs=[rows(own), rows(own), rows(double), pair, flat, rows(128), rows(128)],
        out_specs=(pair, flat),
        compiler_params=params(32),
        cost_estimate=cost(20 * group * double, 8 * group * double),
        name="turn_back",
    )(dq, dk, raw, squares, gain, cosine, sine)


def join_kernel(
    width, dq_ref, dk_ref, dv_ref, raw_ref, squares_ref, dots_ref, gain_ref, cos_ref, sin_ref,
    columns_ref, joint_ref, part_ref,
):
    own = dq_ref.shape[1]
    scales = scales_of(squares_ref, width)
    dots = [as_column(dots_ref[i:i + 1, :]) for i in range(2)]
    cosine, sine = cos_ref[...], sin_ref[...]
    for which, slope in enumerate((dq_ref, dk_ref)):
        scale = scales[which]
        factor = scale * scale * scale * dots[which] / width
        for j in range(0, own, 128):
            place = slice(which * own + j, which * own + j + 128)
            v = slope[:, j:j + 128].astype(F32)
            turned = (v * cosine - pltpu.roll(v, 64, 1) * sine) * gain_ref[:, place]
            joint_ref[:, place] = (scale * turned - raw_ref[:, place] * factor).astype(BF)
    joint_ref[:, 2 * own:] = dv_ref[...]
    part_ref[...] = dot_nt(joint_ref[...], columns_ref[...]).astype(BF)


def join_slopes(dq, dk, dv, raw, squares, dots, gain, cosine, sine, columns, tile):
    group, double = raw.shape
    own = double // 2
    width = columns.shape[0]
    rows = lambda count: pl.BlockSpec((tile, count), lambda i: (i, 0))
    pair = pl.BlockSpec((2, tile), lambda i: (0, i))
    flat = pl.BlockSpec((1, double), lambda i: (0, 0))
    return pl.pallas_call(
        functools.partial(join_kernel, width),
        grid=(group // tile,),
        out_shape=(shape_of((group, 3 * own), BF), shape_of((group, width), BF)),
        in_specs=[
            rows(own), rows(own), rows(own), rows(double), pair, pair, flat, rows(128), rows(128),
            pl.BlockSpec((width, 3 * own), lambda i: (0, 0)),
        ],
        out_specs=(rows(3 * own), rows(width)),
        compiler_params=params(48),
        cost_estimate=cost(6 * group * width * own, 8 * group * width),
        name="join_slopes",
    )(dq, dk, dv, raw, squares, dots, gain, cosine, sine, columns)


def allowed_scores(queries, key_rows, start_ref, place_ref, key_place_ref, inv_root):
    scores = dot_nt(key_rows, queries) * (inv_root * LOG2E)
    key_place = key_place_ref[...]
    allowed = (key_place >= start_ref[...]) & (key_place <= place_ref[...])
    return jnp.where(allowed, scores, MASKED)


def attend_kernel(size, q_ref, k_ref, v_ref, start_ref, place_ref, kp_ref, o_ref, log_ref):
    for j in range(q_ref.shape[1] // size):
        at = slice(j * size, (j + 1) * size)
        scores = allowed_scores(
            q_ref[:, at], k_ref[:, at], start_ref, place_ref, kp_ref, size ** (-0.5)
        )
        highest = jnp.max(scores, axis=0, keepdims=True)
        powers = jnp.exp2(scores - highest)
        summed = jnp.sum(powers, axis=0, keepdims=True)
        blended = dot_tn(v_ref[:, at], powers.astype(BF)) / summed
        o_ref[:, at] = blended.T.astype(BF)
        log_ref[j] = highest + jnp.log2(summed)


def attend(query, key, value, start_row, place_row, place_column, heads, tile, together=2):
    group, own_width = query.shape
    size = own_width // heads
    wide = together * size
    whole = pl.BlockSpec((group, wide), lambda h, i: (0, h))
    row = pl.BlockSpec((1, tile), lambda h, i: (0, i))
    return pl.pallas_call(
        functools.partial(attend_kernel, size),
        grid=(heads // together, group // tile),
        out_shape=(shape_of((group, own_width), BF), shape_of((heads, 1, group), F32)),
        in_specs=[
            pl.BlockSpec((tile, wide), lambda h, i: (i, h)), whole, whole, row, row,
            pl.BlockSpec((group, 1), lambda h, i: (0, 0)),
        ],
        out_specs=(
            pl.BlockSpec((tile, wide), lambda h, i: (i, h)),
            pl.BlockSpec((together, 1, tile), lambda h, i: (h, 0, i)),
        ),
        compiler_params=params(58),
        cost_estimate=cost(4 * heads * group * group * size * 4, 8 * group * own_width),
        name="attend",
    )(query, key, value, start_row, place_row, place_column)


def attend_back_kernel(
    size, q_ref, k_ref, v_ref, g_ref, log_ref, start_ref, place_ref, kp_ref,
    dq_ref, dk_ref, dv_ref, dk_sum, dv_sum,
):
    i = pl.program_id(1)
    inv_root = size ** (-0.5)

    @pl.when(i == 0)
    def _():
        dk_sum[...] = jnp.zeros_like(dk_sum)
        dv_sum[...] = jnp.zeros_like(dv_sum)

    for j in range(q_ref.shape[1] // size):
        at = slice(j * size, (j + 1) * size)
        queries, key_rows, slope = q_ref[:, at], k_ref[:, at], g_ref[:, at]
        scores = allowed_scores(queries, key_rows, start_ref, place_ref, kp_ref, inv_root)
        probability = jnp.exp2(scores - log_ref[j])
        prob_slope = dot_nt(v_ref[:, at], slope)
        product = probability * prob_slope
        row_dot = jnp.sum(product, axis=0, keepdims=True)
        score_slope = (product - probability * row_dot).astype(BF)
        dq_ref[:, at] = (dot_tn(key_rows, score_slope) * inv_root).T.astype(BF)
        dk_sum[:, at] += dot(score_slope, queries) * inv_root
        dv_sum[:, at] += dot(probability.astype(BF), slope)

    @pl.when(i == pl.num_programs(1) - 1)
    def _():
        dk_ref[...] = dk_sum[...].astype(BF)
        dv_ref[...] = dv_sum[...].astype(BF)


def attend_back(
    query, key, value, slope, log_total, start_row, place_row, place_column, heads, tile, together=2
):
    group, own_width = query.shape
    size = own_width // heads
    wide = together * size
    whole = pl.BlockSpec((group, wide), lambda h, i: (0, h))
    row = pl.BlockSpec((1, tile), lambda h, i: (0, i))
    tiled = pl.BlockSpec((tile, wide), lambda h, i: (i, h))
    return pl.pallas_call(
        functools.partial(attend_back_kernel, size),
        grid=(heads // together, group // tile),
        out_shape=(shape_of((group, own_width), BF),) * 3,
        in_specs=[
            tiled, whole, whole, tiled, pl.BlockSpec((together, 1, tile), lambda h, i: (h, 0, i)),
            row, row, pl.BlockSpec((group, 1), lambda h, i: (0, 0)),
        ],
        out_specs=(tiled, whole, whole),
        scratch_shapes=[pltpu.VMEM((group, wide), F32)] * 2,
        compiler_params=params(60),
        cost_estimate=cost(10 * heads * group * group * size * 3, 16 * group * own_width),
        name="attend_back",
    )(query, key, value, slope, log_total, start_row, place_row, place_column)


def widen_kernel(own, a_ref, b_ref, query_ref, key_ref, value_ref, out_ref, router_ref):
    line, _, _, rows, _ = a_ref.shape
    for f in range(line):
        for which, o_ref in enumerate((query_ref, key_ref, value_ref)):
            o_ref[:, f * own:(f + 1) * own] = a_ref[
                f, 0, 0, :, which * own:(which + 1) * own
            ].astype(F32)
    out_ref[...] = b_ref[0, 0].astype(F32)
    routing = a_ref[0, 0, 0, :, 3 * own:].astype(F32)
    for f in range(1, line):
        routing = routing + a_ref[f, 0, 0, :, 3 * own:].astype(F32)
    router_ref[...] = routing


def widen(a, b, own):
    line, chips, _, rows, lanes = a.shape
    width = b.shape[-1]
    extra = lanes - 3 * own
    count = 2 * chips * rows
    full, part = shape_of((count, width), F32), shape_of((count, extra), F32)
    wide = pl.BlockSpec((rows, width), lambda i: (i, 0))
    return pl.pallas_call(
        functools.partial(widen_kernel, own),
        grid=(2 * chips,),
        out_shape=(full,) * 4 + (part,),
        in_specs=[
            pl.BlockSpec((line, 1, 1, rows, lanes), lambda i: (0, i // 2, i % 2, 0, 0)),
            pl.BlockSpec((1, 1, rows, width), lambda i: (i // 2, i % 2, 0, 0)),
        ],
        out_specs=(wide,) * 4 + (pl.BlockSpec((rows, extra), lambda i: (i, 0)),),
        compiler_params=params(32),
        cost_estimate=cost(8 * count * width, 24 * count * width),
        name="widen",
    )(a, b)


def joint_grad_kernel(normed_ref, joint_ref, router_ref, o_ref):
    size = joint_ref.shape[1]
    o_ref[:, :size] = dot(normed_ref[...].T, joint_ref[...]).astype(BF)
    o_ref[:, size:] = router_ref[...]


def joint_grad(normed, joint, router):
    group, width = normed.shape
    size, extra = joint.shape[1], router.shape[1]
    tile = 512
    return pl.pallas_call(
        joint_grad_kernel,
        grid=(width // tile,),
        out_shape=shape_of((width, size + extra), BF),
        in_specs=[
            pl.BlockSpec((group, tile), lambda j: (0, j)),
            pl.BlockSpec((group, size), lambda j: (0, 0)),
            pl.BlockSpec((tile, extra), lambda j: (j, 0)),
        ],
        out_specs=pl.BlockSpec((tile, size + extra), lambda j: (j, 0)),
        compiler_params=params(56),
        cost_estimate=cost(2 * group * width * size, 6 * group * width),
        name="joint_grad",
    )(normed, joint, router)


def dispatch_kernel(code_ref, rows_ref, o_ref, select):
    pairs = code_ref.shape[1]
    blocks, _, tokens = select.shape
    tile = rows_ref.shape[1]

    @pl.when(pl.program_id(1) == 0)
    def _():
        for b in range(blocks):
            row = code_ref[0, :, b * tokens:(b + 1) * tokens][:, None, :]
            slot = lax.broadcasted_iota(jnp.int32, (pairs, CAP, tokens), 1) + b * CAP
            chosen = jnp.where(slot.astype(F32) == row, 1.0, 0.0)
            select[b] = chosen.reshape(pairs * CAP, tokens).astype(BF)

    parts = [
        dot(select[b], rows_ref[b * tokens:(b + 1) * tokens, :]).reshape(pairs, CAP, tile)
        for b in range(blocks)
    ]
    o_ref[...] = jnp.concatenate(parts, axis=1).astype(BF).reshape(o_ref.shape)


def dispatch(codes, rows, planes, local, slots):
    chunks, pairs, count = codes.shape
    width = rows.shape[1]
    tile = 512
    return pl.pallas_call(
        dispatch_kernel,
        grid=(chunks, width // tile),
        out_shape=shape_of((planes, local, chunks * slots, width), BF),
        in_specs=[
            pl.BlockSpec((1, pairs, count), lambda k, j: (k, 0, 0)),
            pl.BlockSpec((count, tile), lambda k, j: (k, j)),
        ],
        out_specs=pl.BlockSpec((planes, local, slots, tile), lambda k, j: (0, 0, k, j)),
        scratch_shapes=[pltpu.VMEM((slots // CAP, pairs * CAP, count * CAP // slots), BF)],
        compiler_params=params(48),
        cost_estimate=cost(2 * pairs * slots * chunks * count * width, 4 * pairs * slots * width),
        name="dispatch",
    )(codes, rows)


def combine_kernel(slots, code_ref, rows_ref, o_ref, select):
    pairs = code_ref.shape[2]

    @pl.when(pl.program_id(1) == 0)
    def _():
        total = pairs * slots
        lane = lax.broadcasted_iota(jnp.int32, (pairs, total), 1)
        start = lax.broadcasted_iota(jnp.int32, (pairs, total), 0) * slots
        within = (lane >= start) & (lane < start + slots)
        spread = dot(code_ref[0], within.astype(BF))
        slot = jnp.sum(jnp.where(within, lane - start, 0), axis=0, keepdims=True)
        select[...] = (spread == slot.astype(F32)).astype(BF)

    rows = rows_ref[...].reshape(pairs * slots, rows_ref.shape[-1])
    o_ref[...] = dot(select[...], rows).astype(BF)


def combine(codes, rows, slots):
    planes, local, _, width = rows.shape
    chunks, count, pairs = codes.shape
    tile = 512
    return pl.pallas_call(
        functools.partial(combine_kernel, slots),
        grid=(chunks, width // tile),
        out_shape=shape_of((chunks * count, width), BF),
        in_specs=[
            pl.BlockSpec((1, count, pairs), lambda k, j: (k, 0, 0)),
            pl.BlockSpec((planes, local, slots, tile), lambda k, j: (0, 0, k, j)),
        ],
        out_specs=pl.BlockSpec((count, tile), lambda k, j: (k, j)),
        scratch_shapes=[pltpu.VMEM((count, pairs * slots), BF)],
        compiler_params=params(56),
        cost_estimate=cost(2 * pairs * slots * chunks * count * width, 4 * pairs * slots * width),
        name="combine",
    )(codes, rows)


def expert_kernel(
    halves, x_ref, ca_ref, cb_ref, gate_ref, up_ref, down_ref, router_ref, named_ref, kept_ref,
    weighted_ref, slope_ref, act_ref, gslope_ref, uslope_ref, logit_ref,
):
    width = x_ref.shape[-1]
    x = x_ref[...].reshape(-1, width)
    c = jnp.concatenate(
        [ref[...].reshape(-1, width // 2) for ref in (ca_ref, cb_ref)], axis=1
    ).astype(F32)
    router = router_ref[...]
    logits = dot(x, router)
    powers = jnp.exp(logits - jnp.max(logits, axis=-1, keepdims=True))
    chance = powers / jnp.sum(powers, axis=-1, keepdims=True)
    named = named_ref[0]
    gating = jnp.sum(chance * named, axis=-1, keepdims=True)
    joined = None
    kept = []
    for h in range(halves):
        gate_pre = dot(x, gate_ref[h])
        up_pre = dot(x, up_ref[h])
        squashed = jax.nn.sigmoid(gate_pre)
        swished = gate_pre * squashed
        activation = swished * up_pre
        act_ref[h] = (gating * activation).astype(BF)
        part = dot(activation.astype(BF), down_ref[h])
        joined = part if joined is None else joined + part
        kept.append((up_pre * squashed * (1.0 + gate_pre * (1.0 - squashed)), swished))
    gating_slope = jnp.sum(c * joined, axis=-1, keepdims=True)
    weighted_ref[...] = (gating * joined).astype(BF).reshape(weighted_ref.shape)
    unit_slope = (gating * c).astype(BF)
    logit_slope = (gating_slope * gating * (named - chance)).astype(BF)
    logit_ref[...] = logit_slope[None]
    slope = dot_nt(logit_slope, router)
    for h in range(halves):
        activation_slope = dot_nt(unit_slope, down_ref[h])
        gate_slope = (activation_slope * kept[h][0]).astype(BF)
        up_slope = (activation_slope * kept[h][1]).astype(BF)
        gslope_ref[h] = gate_slope
        uslope_ref[h] = up_slope
        slope = slope + dot_nt(gate_slope, gate_ref[h]) + dot_nt(up_slope, up_ref[h])
    slope_ref[...] = slope.astype(BF).reshape(slope_ref.shape)


def experts(x, cs, at, gates, ups, downs, router, named, halves, kept):
    planes, local, slots, width = x.shape
    hidden = gates.shape[-1]
    sources = max(1, 448 // slots)
    tile = sources * slots
    steps = planes // sources
    count = planes * slots
    expert_total = router.shape[1]
    units = local * halves
    row_spec = pl.BlockSpec((sources, 1, slots, width), lambda n, t: (t, n, 0, 0))
    half_spec = pl.BlockSpec((sources, 1, slots, width // 2), lambda n, t: (t, n, at, 0))
    unit_spec = pl.BlockSpec((halves, tile, hidden), lambda n, t: (n, t, 0))
    once = pl.Buffered(1)
    wide = pl.BlockSpec((halves, width, hidden), lambda n, t: (n, 0, 0), pipeline_mode=once)
    tall = pl.BlockSpec((halves, hidden, width), lambda n, t: (n, 0, 0), pipeline_mode=once)
    return pl.pallas_call(
        functools.partial(expert_kernel, halves),
        grid=(local, steps),
        out_shape=(
            shape_of((planes, local, CHUNKS * slots, width), BF), shape_of(x.shape, BF),
            shape_of((units, count, hidden), BF), shape_of((units, count, hidden), BF),
            shape_of((units, count, hidden), BF), shape_of((local, count, expert_total), BF),
        ),
        in_specs=[
            row_spec, half_spec, half_spec, wide, wide, tall,
            pl.BlockSpec((width, expert_total), lambda n, t: (0, 0)),
            pl.BlockSpec((1, 1, expert_total), lambda n, t: (n, 0, 0)),
            pl.BlockSpec(memory_space=pl.ANY),
        ],
        out_specs=(
            pl.BlockSpec((sources, 1, slots, width), lambda n, t: (t, n, at, 0)), row_spec, unit_spec, unit_spec, unit_spec,
            pl.BlockSpec((1, tile, expert_total), lambda n, t: (n, t, 0)),
        ),
        input_output_aliases={8: 0} if at else {},
        compiler_params=params(62),
        cost_estimate=cost(12 * units * count * hidden * width, 10 * local * count * width),
        name="experts",
    )(x, *cs, gates, ups, downs, router, named, kept)


def wide_grad_kernel(
    x0_ref, x1_ref, g0_ref, g1_ref, u0_ref, u1_ref, l0_ref, l1_ref, dg_ref, du_ref, dr_ref
):
    tile = x0_ref.shape[-1]
    x0 = x0_ref[...].reshape(-1, tile).T
    x1 = x1_ref[...].reshape(-1, tile).T
    for h in range(dg_ref.shape[0]):
        dg_ref[h] = dot(x0, g0_ref[h]) + dot(x1, g1_ref[h])
        du_ref[h] = dot(x0, u0_ref[h]) + dot(x1, u1_ref[h])
    dr_ref[0] = dot(x0, l0_ref[0]) + dot(x1, l1_ref[0])


def wide_grad(xs, gslopes, uslopes, logit_slopes, halves):
    planes, local, slots, width = xs[0].shape
    units, count, hidden = gslopes[0].shape
    tile = 1024 if planes * slots <= 1024 else 512
    x_spec = pl.BlockSpec((planes, 1, slots, tile), lambda n, j: (0, n, 0, j))
    s_spec = pl.BlockSpec((halves, count, hidden), lambda n, j: (n, 0, 0))
    o_spec = pl.BlockSpec((halves, tile, hidden), lambda n, j: (n, j, 0))
    out = shape_of((units, width, hidden), F32)
    experts_all = logit_slopes[0].shape[2]
    return pl.pallas_call(
        wide_grad_kernel,
        grid=(local, width // tile),
        out_shape=(out, out, shape_of((local, width, experts_all), F32)),
        in_specs=[x_spec] * 2
        + [s_spec] * 4
        + [pl.BlockSpec((1, count, experts_all), lambda n, j: (n, 0, 0))] * 2,
        out_specs=(
            o_spec, o_spec, pl.BlockSpec((1, tile, experts_all), lambda n, j: (n, j, 0)),
        ),
        compiler_params=params(60),
        cost_estimate=cost(8 * units * count * hidden * width, 8 * units * hidden * width),
        name="wide_grad",
    )(*xs, *gslopes, *uslopes, *logit_slopes)


def down_grad_unit_kernel(a0_ref, a1_ref, ca_ref, cb_ref, d_ref):
    half, slots = ca_ref.shape[-1], ca_ref.shape[2] // 2
    a0, a1 = a0_ref[0].T, a1_ref[0].T
    for which, c_ref in enumerate((ca_ref, cb_ref)):
        d_ref[0, :, which * half:(which + 1) * half] = dot(
            a0, c_ref[:, :, :slots].reshape(-1, half)
        ) + dot(a1, c_ref[:, :, slots:].reshape(-1, half))


def down_grad_kernel(a0_ref, a1_ref, ca_ref, cb_ref, d_ref):
    tile, slots = ca_ref.shape[-1], ca_ref.shape[2] // 2

    def part(c_ref):
        d_ref[0] = dot(a0_ref[0].T, c_ref[:, :, :slots].reshape(-1, tile)) + dot(
            a1_ref[0].T, c_ref[:, :, slots:].reshape(-1, tile)
        )

    first = pl.program_id(1) < pl.num_programs(1) // 2
    pl.when(first)(lambda: part(ca_ref))
    pl.when(jnp.logical_not(first))(lambda: part(cb_ref))


def down_grad(acts, cs, halves):
    planes, local, double, half = cs[0].shape
    units, count, hidden = acts[0].shape
    if planes * double <= 2048:
        a_spec = pl.BlockSpec((1, count, hidden), lambda u: (u, 0, 0))
        c_spec = pl.BlockSpec((planes, 1, double, half), lambda u: (0, u // halves, 0, 0))
        return pl.pallas_call(
            down_grad_unit_kernel,
            grid=(units,),
            out_shape=shape_of((units, hidden, 2 * half), F32),
            in_specs=[a_spec, a_spec, c_spec, c_spec],
            out_specs=pl.BlockSpec((1, hidden, 2 * half), lambda u: (u, 0, 0)),
            compiler_params=params(60),
            cost_estimate=cost(8 * units * count * hidden * half, 8 * units * hidden * half),
            name="down_grad",
        )(*acts, *cs)
    tile = 512
    steps = half // tile
    a_spec = pl.BlockSpec((1, count, hidden), lambda u, j: (u, 0, 0))
    shape = (planes, 1, double, tile)
    return pl.pallas_call(
        down_grad_kernel,
        grid=(units, 2 * steps),
        out_shape=shape_of((units, hidden, 2 * half), F32),
        in_specs=[
            a_spec, a_spec,
            pl.BlockSpec(shape, lambda u, j: (0, u // halves, 0, jnp.minimum(j, steps - 1))),
            pl.BlockSpec(shape, lambda u, j: (0, u // halves, 0, jnp.maximum(j - steps, 0))),
        ],
        out_specs=pl.BlockSpec((1, hidden, tile), lambda u, j: (u, 0, j)),
        compiler_params=params(60),
        cost_estimate=cost(8 * units * count * hidden * half, 8 * units * hidden * half),
        name="down_grad",
    )(*acts, *cs)


def per_device(
    inputs,
    query_weight,
    key_weight,
    value_weight,
    output_weight,
    router_weight,
    first_gain,
    query_gain,
    key_gain,
    second_gain,
    gate_weight,
    up_weight,
    down_weight,
    routes,
    lengths,
    dealing,
    cotangent,
):
    planes, line = lax.axis_size("expert"), lax.axis_size("fsdp")
    plane_at, line_at = lax.axis_index("expert"), lax.axis_index("fsdp")
    tokens, width = inputs.shape
    group = line * tokens
    own_heads = HEADS // line
    head_size = width // HEADS
    own_width = own_heads * head_size
    weight_rows = query_weight.shape[0]
    slice_rows = weight_rows // planes
    units = gate_weight.shape[0]
    local = max(1, units // 2)
    halves = units // local
    expert_count = router_weight.shape[1]
    blocks = line // CHUNKS
    chunk_rows = blocks * tokens
    slots = blocks * CAP

    def own_slice(weight):
        return lax.dynamic_slice_in_dim(weight, plane_at * slice_rows, slice_rows, 0)

    sent = jnp.stack([own_slice(w) for w in (query_weight, key_weight, value_weight)], axis=1)
    sent = jnp.moveaxis(sent.reshape(slice_rows, 3, line, own_width), 2, 0)
    routing = jnp.pad(own_slice(router_weight), ((0, 0), (0, -expert_count % 128)))
    sent = jnp.concatenate(
        [
            sent.reshape(line, slice_rows, 3 * own_width),
            jnp.broadcast_to(routing, (line,) + routing.shape),
        ],
        axis=2,
    )
    top_count = routes.shape[1]
    packed = [first_gain, second_gain, routes.astype(BF)]
    sizes = [array.size for array in packed]
    fill = -sum(sizes) % (16 * 128)
    small = jnp.concatenate([array.reshape(-1) for array in packed] + [jnp.zeros((fill,), BF)])
    block_in, first_half, small_all, columns, _ = gather_start(
        inputs, cotangent, small.reshape(-1, 128), sent, planes, line
    )
    columns = columns.reshape(width, -1)
    full_router = columns[:, 3 * own_width:3 * own_width + expert_count]
    small_all = small_all.reshape(line, -1)
    ends = [sum(sizes[:i]) for i in range(4)]
    gain_first, gain_second, routes_all = (
        small_all[:, ends[i]:ends[i + 1]] for i in range(3)
    )
    gain_first, gain_second = (g.reshape(width).astype(F32) for g in (gain_first, gain_second))
    routes_all = routes_all.reshape(line, tokens, top_count).astype(jnp.int32)
    later, _ = lax.optimization_barrier((cotangent, block_in))
    second_half = lax.all_gather(later[:, width // 2:], "fsdp", axis=0, tiled=True)
    incoming = [first_half, second_half]

    seq_start, positions = places(lengths[0], dealing)
    start_row, place_row, place_column = seq_start[None, :], dealing[None, :], dealing[:, None]
    cosine, sine = angles(positions, head_size)
    per_plane = expert_count // planes
    first_local = (line_at * units) // 2
    member = jnp.sum(
        (routes_all[..., None] == jnp.arange(expert_count, dtype=jnp.int32)).astype(F32), axis=2
    )
    earlier = jnp.tril(jnp.ones((tokens, tokens), BF), -1)
    rank = contract("ts,bse->bte", earlier, member.astype(BF))
    rank = rank + ((jnp.arange(line) % blocks) * CAP).astype(F32)[:, None, None]
    coded = jnp.where(member > 0, rank, -1.0).reshape(line, tokens, planes, per_plane)
    coded = lax.dynamic_slice_in_dim(coded, first_local, local, 3)
    coded = coded.reshape(CHUNKS, chunk_rows, planes * local)
    by_token = coded.astype(BF)
    by_pair = jnp.swapaxes(coded, 1, 2)

    def chunk(array, k):
        return lax.slice_in_dim(array, k * chunk_rows, (k + 1) * chunk_rows)

    rows = dispatch(by_pair, incoming[0], planes, local, slots)
    normed_low, raw, value_low, squares = project(block_in, gain_first[None], columns, tokens)
    squares = small_line_sum(squares, line)
    both_gains = jnp.concatenate([query_gain, key_gain])[None].astype(F32)
    rotary = (jnp.concatenate([cosine, cosine], -1), jnp.concatenate([-sine, sine], -1))
    query_low, key_low = turn(raw, squares, both_gains, *rotary, width, tokens)
    blended, log_total = attend(
        query_low, key_low, value_low, start_row, place_row, place_column, own_heads, tokens
    )
    attention_part = dot(blended, output_weight).astype(BF)

    named = (
        (((plane_at * line + line_at) * units) // 2 + jnp.arange(local))[:, None, None]
        == jnp.arange(expert_count)
    ).astype(F32)
    attention_parts = [chunk(attention_part, k) for k in range(CHUNKS)]
    arrived_slopes = [swap_plane(rows)]
    rows = dispatch(by_pair, incoming[1], planes, local, slots)
    held, normed, swapped = hide(
        attention_parts[0], block_in, gain_second[None], rows, 0, line, 4
    )
    arrived_slopes.append(swapped)
    rows = dispatch(by_pair[:1], normed, planes, local, slots)
    held_next, normed, swapped = hide(
        attention_parts[1], block_in, gain_second[None], rows, 1, line, 3
    )
    hidden, arrived = [held, held_next], [swapped]
    rows = dispatch(by_pair[1:], normed, planes, local, slots)
    rows, arrived_slopes[0] = lax.optimization_barrier((rows, arrived_slopes[0]))
    arrived.append(swap_plane(rows))
    weighted = arrived_slopes[0]
    row_slopes, acts, gslopes, uslopes, logit_slopes = [], [], [], [], []
    for k in range(CHUNKS):
        results = experts(
            arrived[k], arrived_slopes, k, gate_weight, up_weight, down_weight, full_router,
            named, halves, weighted,
        )
        weighted = results[0]
        for store, result in zip((row_slopes, acts, gslopes, uslopes, logit_slopes), results[1:]):
            store.append(result)
    returned = []
    behind = arrived[-1]
    for k in range(CHUNKS):
        rows, _ = lax.optimization_barrier((row_slopes[k], behind))
        behind = swap_plane(rows)
        returned.append(behind)

    hidden_slopes, attention_slopes, blended_slopes, second_parts = [], [], [], []
    for k in range(CHUNKS):
        returned[k], _ = lax.optimization_barrier(
            (returned[k], hidden_slopes[0] if k else row_slopes[-1])
        )
        part = combine(by_token[k:k + 1], returned[k], slots)
        if k:
            rows, _ = lax.optimization_barrier((weighted, returned[k]))
            mixed_rows = swap_plane(rows)
        results = hide_back(part, hidden[k], incoming, gain_second[None], k, line)
        for store, result in zip((hidden_slopes, attention_slopes, second_parts), results):
            store.append(result)
    second_gain_grad = second_parts[0] + second_parts[1]
    blended_slope = jnp.concatenate(
        [contract("td,cd->tc", low, output_weight).astype(BF) for low in attention_slopes]
    )
    slopes = attend_back(
        query_low, key_low, value_low, blended_slope, log_total, start_row,
        place_row, place_column, own_heads, tokens,
    )
    dots, gain_grads = turn_back(*slopes[:2], raw, squares, both_gains, *rotary, width, tokens)
    dots = small_line_sum(dots, line)
    mixed_rows, _ = lax.optimization_barrier((mixed_rows, gain_grads))
    mixed = combine(by_token, mixed_rows, slots)
    acts, gslopes, uslopes, logit_slopes, attention_slopes, _ = lax.optimization_barrier(
        (acts, gslopes, uslopes, logit_slopes, attention_slopes, mixed)
    )
    mixed = lax.psum_scatter(mixed, "fsdp", scatter_dimension=0, tiled=True)
    *expert_grads, router_parts = wide_grad(arrived, gslopes, uslopes, logit_slopes, halves)
    expert_grads.append(down_grad(acts, arrived_slopes, halves))
    router_grad = jnp.sum(router_parts, axis=0)
    output_grad = sum(
        contract("tc,td->cd", chunk(blended, k), attention_slopes[k]) for k in range(CHUNKS)
    ).astype(BF)
    dots, _ = lax.optimization_barrier((dots, expert_grads))
    joint, normed_part = join_slopes(
        *slopes, raw, squares, dots, both_gains, *rotary, columns, tokens
    )
    router_lanes = -expert_count % 128
    router_pad = jnp.pad(router_grad.astype(BF), ((0, 0), (0, router_lanes)))
    joint_total = joint_grad(normed_low, joint, router_pad)
    mine = line_at * weight_rows
    second_own = lax.dynamic_slice_in_dim(second_gain_grad, mine, weight_rows, 1)
    gain_rows = jnp.concatenate(
        [
            jnp.zeros((1, weight_rows), F32), second_own, gain_grads.reshape(2, own_width),
            jnp.zeros((4, weight_rows), F32),
        ]
    )
    input_gradient, totals, output_total, gain_totals = finish(
        normed_part, joint_total.reshape(line, planes, slice_rows, -1),
        output_grad.reshape(planes, slice_rows, width), inputs, gain_first[None],
        hidden_slopes, gain_rows, planes, line,
    )
    start = (line_at % blocks) * tokens
    hidden_own = jnp.where(
        line_at < blocks, *(lax.dynamic_slice_in_dim(held, start, tokens, 0) for held in hidden)
    )
    block_output = (hidden_own + mixed.astype(F32)).astype(BF)
    *weight_grads, router_total = widen(
        totals.reshape(line, planes // 2, 2, slice_rows, -1),
        output_total.reshape(planes // 2, 2, slice_rows, width), own_width,
    )
    router_total = router_total[:, :expert_count]
    return (
        block_output,
        input_gradient,
        *weight_grads,
        router_total,
        gain_totals[0],
        gain_totals[2],
        gain_totals[3],
        gain_totals[1],
        *expert_grads,
    )


def solution(mesh):
    both = ("expert", "fsdp")
    rows, cube, shard, gain = P(both, None), P(both, None, None), P("fsdp", None), P("fsdp")
    return jax.shard_map(
        per_device,
        mesh=mesh,
        in_specs=(rows,)
        + (shard,) * 5
        + (gain,) * 4
        + (cube,) * 3
        + (rows, P("expert", None), P("expert"), rows),
        out_specs=(rows, rows) + (shard,) * 5 + (gain,) * 4 + (cube,) * 3,
        check_vma=False,
    )
```
